32 devices in a mesh: rep: 4 (over y, x), wide: 8 (over z, core).
Axes of the slice: x: 2, y: 2, z: 4, core: 2. Of those that a mesh axis runs over, the one named last changes fastest.
Arguments:
- doc_tokens: bfloat16 [16384, 768], P(('rep', 'wide')), may hold values from -6 to 6
- query_tokens: bfloat16 [8192, 768], P(('rep', 'wide')), may hold values from -6 to 6
- doc_cotangent: bfloat16 [16384, 128], P(('rep', 'wide')), may hold values from -0.017944336 to 0.017944336
- query_cotangent: bfloat16 [8192, 128], P(('rep', 'wide')), may hold values from -0.017944336 to 0.017944336
- retrieved: int32 [16384, 64], P(('rep', 'wide')), may hold values from 0 to 1, as said below
- pos_ids: int32 [256, 4], P(('rep', 'wide')), may hold values from 0 to 7
- pos_count: int32 [256], P(('rep', 'wide')), may hold values from 1 to 4
- w_query: bfloat16 [768, 768], replicated, may hold values from -0.078125 to 0.078125
- w_key: bfloat16 [768, 768], replicated, may hold values from -0.078125 to 0.078125
- carried_content_weights: bfloat16 [768, 768], replicated, may hold values from -0.21875 to 0.21875
- w_out: bfloat16 [768, 768], replicated, may hold values from -0.875 to 0.875
- w_gate: bfloat16 [768, 2048], replicated, may hold values from -0.21875 to 0.21875
- w_up: bfloat16 [768, 2048], replicated, may hold values from -0.21875 to 0.21875
- w_down: bfloat16 [2048, 768], replicated, may hold values from -0.25 to 0.25
- w_proj: bfloat16 [768, 128], replicated, may hold values from -0.21875 to 0.21875
- gain_attn: bfloat16 [768], replicated, may hold values from 0.5 to 1.5
- gain_ffn: bfloat16 [768], replicated, may hold values from 0.5 to 1.5
- gain_final: bfloat16 [768], replicated, may hold values from 0.5 to 1.5
- rel_bias: bfloat16 [32, 12], replicated, may hold values from -4 to 4
Outputs:
- doc_emb: bfloat16 [16384, 128], P(('rep', 'wide'))
- query_emb: bfloat16 [8192, 128], P(('rep', 'wide'))
- doc_grad: bfloat16 [16384, 768], P(('rep', 'wide'))
- query_grad: bfloat16 [8192, 768], P(('rep', 'wide'))
- grad_query: float32 [768, 768], P('wide')
- grad_key: float32 [768, 768], P('wide')
- grad_value: float32 [768, 768], P('wide')
- grad_out: float32 [768, 768], P('wide')
- grad_gate: float32 [768, 2048], P('wide')
- grad_up: float32 [768, 2048], P('wide')
- grad_down: float32 [2048, 768], P('wide')
- grad_proj: float32 [768, 128], P('wide')
- grad_gain_attn: float32 [768], replicated
- grad_gain_ffn: float32 [768], replicated
- grad_gain_final: float32 [768], replicated
- grad_rel_bias: float32 [32, 12], replicated
- loss: float32 [], replicated
- fraction: float32 [], replicated
The draws below stay inside these ranges and needn't reach their ends.
Inputs may be any that keep to these rules, and one draw needn't show every extreme that they name: Entry (t, q) is 1 where document token t is among the tokens retrieved for query q of the same rep group; queries are numbered within the group. `pos_ids`: the positives of a query are the distinct documents among its first pos_count entries, numbered within its rep group.
All inputs are finite; a program needn't handle non-finite values.
Results may differ from the reference program's by a relative error of at most 0.017.
Values may be sent and summed in bfloat16 or wider, within the bound.
No kernel may reach another device: no remote copies, remote signals or barrier semaphores. Data moves between devices by JAX's collectives and lax.ppermute only.
A program may use at most 192 MiB of HBM per device.

```python
import math
import jax
import jax.numpy as jnp
import numpy as np
from jax import lax

D = 768
HEADS = 12
HD = 64
FF = 2048
EMB = 128
BUCKETS = 32
DL = 512
QUERY_LENGTH = 32
POSITIVES = 4
DOCG = 8
QGROUP = 64
DOCS = 32
QUERIES = 256
N_REP = 4


def topic_table(key):
    return jnp.clip(jax.random.normal(key, (8, D), jnp.float32), -4.0, 4.0)


def noise_rows(key, shape):
    return jnp.clip(jax.random.normal(key, shape, jnp.float32), -4.0, 4.0)


def draw_doc_tokens(key, part):
    topics = topic_table(key)
    key = jax.random.fold_in(key, 11)
    choice_key, noise_key = jax.random.split(key)
    picked = jax.random.randint(choice_key, (DOCS,), 0, 8)
    noise = noise_rows(noise_key, (DOCS, DL, D))
    rows = 0.3 * topics[picked][:, None, :] + 0.95 * noise
    return rows.reshape(DOCS * DL, D).astype(jnp.bfloat16)


def draw_query_tokens(key, part):
    topics = topic_table(key)
    key = jax.random.fold_in(key, 13)
    choice_key, noise_key = jax.random.split(key)
    picked = jax.random.randint(choice_key, (QUERIES,), 0, 8)
    noise = noise_rows(noise_key, (QUERIES, QUERY_LENGTH, D))
    rows = 0.3 * topics[picked][:, None, :] + 0.95 * noise
    return rows.reshape(QUERIES * QUERY_LENGTH, D).astype(jnp.bfloat16)


def draw_retrieved(key, part):
    key = jax.random.fold_in(key, 7)
    level_key, ticket_key = jax.random.split(key)
    levels = jax.random.randint(level_key, (DOCS, 1, QGROUP), 0, 6)
    limit = jnp.right_shift(jnp.full((DOCS, 1, QGROUP), 2048, jnp.int32), levels)
    ticket = jax.random.randint(ticket_key, (DOCS, DL, QGROUP), 0, 4096)
    return (ticket < limit).astype(jnp.int32).reshape(DOCS * DL, QGROUP)


def set_ends(array, key, smallest, top_value):
    index_at = [jax.random.randint(jax.random.fold_in(key, axis), (), 0, length) for axis, length in enumerate(array.shape)]
    longest = array.shape.index(max(array.shape))
    neighbour = index_at[:longest] + [(index_at[longest] + 1) % array.shape[longest]] + index_at[longest + 1:]
    return array.at[tuple(index_at)].set(smallest).at[tuple(neighbour)].set(top_value)


def steps_of(rng, extent, shards, low, largest):
    level = 1.0
    for dim, blocks in shards:
        heights = jax.random.uniform(jax.random.fold_in(jax.random.fold_in(rng, 6), dim), (blocks,), jnp.float32, low / len(shards), largest / len(shards))
        level = level * jnp.repeat(jnp.exp(heights), extent[dim] // blocks).reshape((-1,) + (1,) * (len(extent) - 1 - dim))
    return level


def bell_draw(own_key, dims, spread, most, pieces=(), kind=jnp.bfloat16):
    drawn = jax.random.normal(own_key, dims, jnp.float32) * spread
    if len(pieces) > 0:
        drawn = steps_of(own_key, dims, pieces, -0.22, 0.18) * drawn
    return jnp.clip(drawn, min=-most, max=most).astype(kind)


def setup_inputs(seed: int = 0) -> dict:
    streams_of = jax.random.split(jax.random.key(seed), 20)
    doc_tokens = draw_doc_tokens(jax.random.fold_in(streams_of[19], 71), 0)
    query_tokens = draw_query_tokens(jax.random.fold_in(streams_of[19], 71), 0)
    doc_cotangent = bell_draw(streams_of[2], (DOCS * DL, EMB), 0.003, 0.017944336, ((0, 32),))
    query_cotangent = bell_draw(streams_of[3], (QUERIES * QUERY_LENGTH, EMB), 0.003, 0.017944336, ((0, 32),))
    retrieved = draw_retrieved(jax.random.fold_in(streams_of[19], 71), 0)
    pos_ids = set_ends(jax.random.randint(streams_of[5], (QUERIES, POSITIVES), 0, DOCG), jax.random.fold_in(streams_of[5], 1), 0, DOCG - 1).astype(jnp.int32)
    pos_count = set_ends(jax.random.randint(streams_of[6], (QUERIES,), 1, POSITIVES + 1), jax.random.fold_in(streams_of[6], 1), 1, POSITIVES).astype(jnp.int32)
    w_query = bell_draw(streams_of[7], (D, D), (8 * D) ** -0.5, 0.078125)
    w_key = bell_draw(streams_of[8], (D, D), (8 * D) ** -0.5, 0.078125)
    carried_content_weights = bell_draw(streams_of[9], (D, D), D ** -0.5, 0.21875)
    w_out = bell_draw(streams_of[10], (D, D), (D // 16) ** -0.5, 0.875)
    w_gate = bell_draw(streams_of[11], (D, FF), D ** -0.5, 0.21875)
    w_up = bell_draw(streams_of[12], (D, FF), D ** -0.5, 0.21875)
    w_down = bell_draw(streams_of[13], (FF, D), (FF // 4) ** -0.5, 0.25)
    w_proj = bell_draw(streams_of[14], (D, EMB), D ** -0.5, 0.21875)
    gain_attn = jnp.clip(1.0 + 0.1 * jax.random.normal(streams_of[15], (D,), jnp.float32), 0.5, 1.5).astype(jnp.bfloat16)
    gain_ffn = jnp.clip(1.0 + 0.1 * jax.random.normal(streams_of[16], (D,), jnp.float32), 0.5, 1.5).astype(jnp.bfloat16)
    gain_final = jnp.clip(1.0 + 0.1 * jax.random.normal(streams_of[17], (D,), jnp.float32), 0.5, 1.5).astype(jnp.bfloat16)
    rel_bias = bell_draw(streams_of[18], (BUCKETS, HEADS), 1.0, 4.0)
    return {"doc_tokens": doc_tokens, "query_tokens": query_tokens, "doc_cotangent": doc_cotangent, "query_cotangent": query_cotangent, "retrieved": retrieved, "pos_ids": pos_ids, "pos_count": pos_count, "w_query": w_query, "w_key": w_key, "carried_content_weights": carried_content_weights, "w_out": w_out, "w_gate": w_gate, "w_up": w_up, "w_down": w_down, "w_proj": w_proj, "gain_attn": gain_attn, "gain_ffn": gain_ffn, "gain_final": gain_final, "rel_bias": rel_bias}


@jax.custom_vjp
def low(v):
    return lax.optimization_barrier(v.astype(jnp.bfloat16)).astype(jnp.float32)

@jax.custom_vjp
def low_back(v):
    return v

def low_keep(v):
    return (low(v), None)

def low_pass(kept, grad):
    return (grad,)

def back_keep(v):
    return (v, None)

def back_low(kept, grad):
    return (low(grad),)
low.defvjp(low_keep, low_pass)
low_back.defvjp(back_keep, back_low)
logit_divisor = 0.1
epsilon = 1e-06
peak_logit = lax.Precision.HIGHEST

def bucket_table(length, buckets):
    half = buckets // 2
    exact = half // 2
    context_pos = np.arange(length)[:, None]
    memory_pos = np.arange(length)[None, :]
    relative = memory_pos - context_pos
    base = (relative > 0).astype(np.int64) * half
    distance = np.abs(relative)
    large = exact + (np.log(np.maximum(distance, 1) / float(exact)) / np.log(128.0 / exact) * (half - exact)).astype(np.int64)
    large = np.minimum(large, half - 1)
    return (base + np.where(distance < exact, distance, large)).astype(np.int32)

def rms_norm(values, gain):
    return values * lax.rsqrt(lax.optimization_barrier(jnp.mean(values * values, axis=-1, keepdims=True)) + epsilon) * gain

def matmul_high(left, right):
    return jnp.dot(left, right, precision=peak_logit)

def encode(tokens, weights, length):
    w_query, w_key, carried_content_weights, w_out, w_gate, w_up, w_down, w_proj, gain_attn, gain_ffn, gain_final, rel_bias = weights
    batch = tokens.shape[0]
    flat = tokens.reshape(-1, D)
    normed_one = low(rms_norm(flat, gain_attn))
    query = low_back(low(matmul_high(normed_one, w_query))).reshape(batch, length, HEADS, HD)
    keys = low_back(low(matmul_high(normed_one, w_key))).reshape(batch, length, HEADS, HD)
    values = low_back(low(matmul_high(normed_one, carried_content_weights))).reshape(batch, length, HEADS, HD)
    table = jnp.asarray(bucket_table(length, BUCKETS))
    bias = jnp.transpose(jnp.take(rel_bias, table, axis=0), (2, 0, 1))
    scores = low_back(jnp.einsum('bihd,bjhd->bhij', query, keys, precision=peak_logit) + bias[None])
    probs = low(jax.nn.softmax(scores, axis=-1))
    context = low_back(low(jnp.einsum('bhij,bjhd->bihd', probs, values, precision=peak_logit)))
    hidden = flat + low_back(matmul_high(context.reshape(-1, D), w_out))
    normed_two = low(rms_norm(hidden, gain_ffn))
    gate = low_back(matmul_high(normed_two, w_gate))
    up = low_back(matmul_high(normed_two, w_up))
    act = low(jax.nn.gelu(gate, approximate=True) * up)
    hidden_two = hidden + low_back(matmul_high(act, w_down))
    normed_three = low(rms_norm(hidden_two, gain_final))
    proj = low_back(matmul_high(normed_three, w_proj))
    emb = low(proj * lax.rsqrt(lax.optimization_barrier(jnp.sum(proj * proj, axis=-1, keepdims=True)) + epsilon))
    return emb.reshape(batch, length, EMB)

def encode_all(sequences, weights, length):
    count = sequences.shape[0]
    group_size = math.gcd(count, max(1, 4096 // length))
    grouped = sequences.reshape(count // group_size, group_size, length, D)

    def encode_group(group_rows):
        return encode(group_rows, weights, length)
    encoded = lax.map(jax.checkpoint(encode_group), grouped)
    return encoded.reshape(count, length, EMB)

def group_scores(query_emb, doc_emb, mask_group):

    def column(inputs):
        doc_one, positive_indicator = inputs
        pairwise_logits = low_back(jnp.einsum('qie,je->qij', query_emb, doc_one, precision=peak_logit))
        accumulated_sum = jnp.einsum('mtr,rm->mt', jnp.exp(pairwise_logits / logit_divisor), positive_indicator, precision=peak_logit)
        return lax.optimization_barrier(jnp.mean(jnp.log(1.0 + accumulated_sum), axis=1))
    return jnp.transpose(lax.map(jax.checkpoint(column), (doc_emb, mask_group)))

def query_losses(scores, positive_hot):
    peak = lax.optimization_barrier(jnp.max(scores, axis=1, keepdims=True))
    power_of_e_factor = jnp.exp(scores - peak)
    return jnp.log(lax.optimization_barrier(jnp.sum(power_of_e_factor, axis=1))) - jnp.log(lax.optimization_barrier(jnp.sum(positive_hot * power_of_e_factor, axis=1)))

def reference(doc_tokens, query_tokens, doc_cotangent, query_cotangent, retrieved, pos_ids, pos_count, w_query, w_key, carried_content_weights, w_out, w_gate, w_up, w_down, w_proj, gain_attn, gain_ffn, gain_final, rel_bias):
    weights = tuple((item.astype(jnp.float32) for item in (w_query, w_key, carried_content_weights, w_out, w_gate, w_up, w_down, w_proj, gain_attn, gain_ffn, gain_final, rel_bias)))
    docs = doc_tokens.astype(jnp.float32).reshape(DOCS, DL, D)
    queries = query_tokens.astype(jnp.float32).reshape(QUERIES, QUERY_LENGTH, D)
    doc_cot = doc_cotangent.astype(jnp.float32).reshape(DOCS, DL, EMB)
    query_cot = query_cotangent.astype(jnp.float32).reshape(QUERIES, QUERY_LENGTH, EMB)
    mask = retrieved.astype(jnp.float32).reshape(N_REP, DOCG, DL, QGROUP)
    numbers = jnp.arange(DOCG, dtype=jnp.int32)
    slots = jnp.arange(POSITIVES, dtype=jnp.int32)
    matches = (pos_ids[:, :, None] == numbers[None, None, :]) & (slots[None, :, None] < pos_count[:, None, None])
    positive_hot = jnp.any(matches, axis=1).astype(jnp.float32)
    counts = jnp.transpose(lax.optimization_barrier(jnp.sum(mask, axis=2)), (0, 2, 1)).reshape(QUERIES, DOCG)

    def objective(docs, queries, weights):
        doc_emb = encode_all(docs, weights, DL)
        query_emb = encode_all(queries, weights, QUERY_LENGTH)
        loss_sum = jnp.zeros((), jnp.float32)
        for group in range(N_REP):
            scores = group_scores(query_emb[group * QGROUP:(group + 1) * QGROUP], doc_emb[group * DOCG:(group + 1) * DOCG], mask[group])
            loss_sum = loss_sum + jnp.sum(query_losses(scores, positive_hot[group * QGROUP:(group + 1) * QGROUP]))
        value = loss_sum + jnp.sum(doc_emb * doc_cot) + jnp.sum(query_emb * query_cot)
        return (value, (doc_emb, query_emb, loss_sum))
    value, vjp_fun, (doc_emb, query_emb, loss_sum) = jax.vjp(objective, docs, queries, weights, has_aux=True)
    d_docs, d_queries, d_weights = vjp_fun(jnp.ones_like(value))
    fraction = jnp.sum(positive_hot * counts) / (DL * jnp.sum(positive_hot))
    return (doc_emb.reshape(DOCS * DL, EMB).astype(jnp.bfloat16), query_emb.reshape(QUERIES * QUERY_LENGTH, EMB).astype(jnp.bfloat16), d_docs.reshape(DOCS * DL, D).astype(jnp.bfloat16), d_queries.reshape(QUERIES * QUERY_LENGTH, D).astype(jnp.bfloat16), d_weights[0], d_weights[1], d_weights[2], d_weights[3], d_weights[4], d_weights[5], d_weights[6], d_weights[7], d_weights[8], d_weights[9], d_weights[10], d_weights[11], loss_sum / QUERIES, fraction)
```

```python
import functools

import jax
import jax.numpy as jnp
import numpy as np
from jax import lax
from jax.experimental import pallas as pl
from jax.experimental.pallas import tpu as pltpu
from jax.sharding import PartitionSpec as P

DL = 512
QUERY_LENGTH = 32
EPS = 1e-06
SCALE = 10.0
BF = jnp.bfloat16
F = jnp.float32
TABLE = 1024
SHIFT = 384
VMEM_LIMIT = 60 * 1024 * 1024

SAVED = (
    "n1", "q", "k", "v", "p", "li", "ctx", "hid", "n2", "gv", "us", "act", "h2", "n3", "proj", "emb",
)

SM = pl.BlockSpec(memory_space=pltpu.SMEM)
ANY = pl.BlockSpec(memory_space=pl.ANY)
VM = pl.BlockSpec(memory_space=pltpu.VMEM)


def mm(a, b):
    return jnp.dot(a, b, preferred_element_type=F)


def mm_nt(a, b):
    return lax.dot_general(a, b, (((1,), (1,)), ((), ())), preferred_element_type=F)


def mm_tn(a, b):
    return lax.dot_general(a, b, (((0,), (0,)), ((), ())), preferred_element_type=F)


def bucket_hot(buckets):
    half = buckets // 2
    exact = half // 2
    column = np.arange(TABLE)
    relative = np.where(column < TABLE - 128, column, column - TABLE) - SHIFT
    base = (relative > 0).astype(np.int64) * half
    distance = np.abs(relative)
    large = exact + (
        np.log(np.maximum(distance, 1) / float(exact)) / np.log(128.0 / exact) * (half - exact)
    ).astype(np.int64)
    large = np.minimum(large, half - 1)
    number = base + np.where(distance < exact, distance, large)
    return (np.arange(buckets)[:, None] == number[None, :]).astype(np.float32)


def query_hot(queries):
    tokens = np.arange(queries * QUERY_LENGTH)
    return (np.arange(queries)[:, None] == tokens[None, :] // QUERY_LENGTH).astype(np.float32)


def cost(flops, moved):
    large = flops > 1e8
    return pl.CostEstimate(flops=int(1e12 if large else 1), bytes_accessed=1, transcendentals=0)


def sds(shape, dtype):
    return jax.ShapeDtypeStruct(shape, dtype)


def rows_loop(count, block, fn):
    def step(i, carry):
        fn(pl.ds(pl.multiple_of(i * block, block), block))
        return carry

    lax.fori_loop(0, count // block, step, 0)


def half_masks():
    lane = lax.broadcasted_iota(jnp.int32, (1, 128), 1)
    low = (lane < 64).astype(F)
    high = 1.0 - low
    one_low = (lane == 0).astype(F)
    one_high = (lane == 64).astype(F)
    return low, high, one_low, one_high


def rms(values):
    return lax.rsqrt(jnp.mean(values * values, axis=-1, keepdims=True) + EPS)


def rms_back(values, gain, d_result):
    inverse = rms(values)
    scaled = values * inverse
    grad_gain = jnp.sum(d_result * scaled, axis=0, keepdims=True)
    gained = d_result * gain
    d_values = inverse * (gained - scaled * jnp.mean(gained * scaled, axis=-1, keepdims=True))
    return d_values, grad_gain


def gelu_parts(gate):
    square = gate * gate
    tangent = jnp.tanh(gate * (0.7978845608028654 + (0.7978845608028654 * 0.044715) * square))
    half_plus = 0.5 + 0.5 * tangent
    value = gate * half_plus
    slope = half_plus + 0.5 * gate * (1.0 - tangent * tangent) * (
        0.7978845608028654 + (3.0 * 0.7978845608028654 * 0.044715) * square
    )
    return value, slope


def fwd_kernel(
    seq,
    heads,
    n_after,
    tok, gains, rel, hot, wq_h, wk_h, wv_h, wo_h, wg_h, wu_h, wd_h, wp_h,
    *refs,
):
    (
    n1_h, q_h, k_h, v_h, p_h, li_h, ctx_h, hid_h, n2_h, gv_h, us_h, act_h, h2_h, n3_h, proj_h, emb,
    wq, wk, wv, wo, wg, wu, wd, wp,
    n1, q, k, v, p, li, ctx, hid, n2, gv, us, act, h2, n3, proj,
    tbl, bs, sem_in, sem_out,
    ) = refs[n_after:]
    count = tok.shape[0]
    loads = [
        pltpu.make_async_copy(src, dst, sem_in.at[i])
        for i, (src, dst) in enumerate(
            zip((wq_h, wk_h, wv_h, wo_h, wg_h, wu_h, wd_h, wp_h), (wq, wk, wv, wo, wg, wu, wd, wp))
        )
    ]
    for copy in loads:
        copy.start()
    outs = {}

    def push(i, src, dst):
        outs[i] = pltpu.make_async_copy(src, dst, sem_out.at[i])
        outs[i].start()

    gain_a = gains[0:1, :]
    gain_f = gains[1:2, :]
    gain_l = gains[2:3, :]

    def norm_one(rows):
        x = tok[rows, :].astype(F)
        n1[rows, :] = (x * rms(x) * gain_a).astype(BF)

    rows_loop(count, 128, norm_one)
    push(0, n1, n1_h)
    tbl[0:heads, :] = mm(rel[...], hot[...])
    for i, (w, r, r_h) in enumerate(((wq, q, q_h), (wk, k, k_h), (wv, v, v_h))):
        loads[i].wait()
        r[...] = mm(n1[...], w[...]).astype(BF)
        push(1 + i, r, r_h)

    low, high, one_low, one_high = half_masks()
    is_low = low > 0.5

    def pair(index, carry):
        lanes = pl.ds(pl.multiple_of(index * 128, 128), 128)
        q2 = q[:, lanes]
        k2 = k[:, lanes]
        v2 = v[:, lanes]
        parts = []
        for e, (keep, one) in enumerate(((low, one_high), (high, one_low))):
            head = 2 * index + e
            km = k2 * keep.astype(BF)
            vm = v2 * keep.astype(BF) + one.astype(BF)
            row = jnp.broadcast_to(tbl[pl.ds(head, 1), :], (128, TABLE))
            base = pltpu.roll(row, 0, 1, stride=1, stride_axis=0)
            if seq == DL:
                bs[...] = base
            else:
                ri = lax.broadcasted_iota(jnp.int32, (128, 128), 0) // seq
                ci = lax.broadcasted_iota(jnp.int32, (128, 128), 1) // seq
                bs[:, 0:128] = jnp.where(ri == ci, base[:, SHIFT : SHIFT + 128], -1e30)
            blocks = []
            for i in range(count // 128):
                qb = q2[128 * i : 128 * i + 128]
                if seq == DL:
                    kb, vb = km, vm
                    bias = bs[:, SHIFT - 128 * i : SHIFT - 128 * i + DL]
                else:
                    kb = km[128 * i : 128 * i + 128]
                    vb = vm[128 * i : 128 * i + 128]
                    bias = bs[:, 0:128]
                scores = mm_nt(qb, kb) + bias
                peak = jnp.max(scores, axis=1, keepdims=True)
                pb = jnp.exp(scores - peak).astype(BF)
                p[head, 128 * i : 128 * i + 128, :] = pb
                o = mm(pb, vb)
                total = o[:, 64:65] if e == 0 else o[:, 0:1]
                blocks.append((o, 1.0 / total))
            parts.append(blocks)
        for i in range(count // 128):
            (o0, i0), (o1, i1) = parts[0][i], parts[1][i]
            inv = jnp.where(is_low, i0, i1)
            li[128 * i : 128 * i + 128, lanes] = inv
            ctx[128 * i : 128 * i + 128, lanes] = (jnp.where(is_low, o0, o1) * inv).astype(BF)
        return carry

    lax.fori_loop(0, heads // 2, pair, 0)
    push(4, p, p_h)
    push(5, li, li_h)
    push(6, ctx, ctx_h)

    loads[3].wait()

    def middle(rows):
        h = tok[rows, :].astype(F) + mm(ctx[rows, :], wo[...])
        hid[rows, :] = h
        h2[rows, :] = h
        n2[rows, :] = (h * rms(h) * gain_f).astype(BF)

    rows_loop(count, 256, middle)
    push(7, hid, hid_h)
    push(8, n2, n2_h)
    loads[4].wait()
    loads[5].wait()
    loads[6].wait()

    def ffn(t, carry):
        cols = pl.ds(pl.multiple_of(t * 512, 512), 512)
        for b in range(count // 256):
            rows = slice(256 * b, 256 * b + 256)
            gate = mm(n2[rows, :], wg[:, cols])
            up = mm(n2[rows, :], wu[:, cols])
            value, slope = gelu_parts(gate)
            a = (value * up).astype(BF)
            gv[rows, cols] = value.astype(BF)
            us[rows, cols] = (up * slope).astype(BF)
            act[rows, cols] = a
            h2[rows, :] += mm(a, wd[cols, :])
        return carry

    lax.fori_loop(0, wg.shape[1] // 512, ffn, 0)
    push(9, gv, gv_h)
    push(10, us, us_h)
    push(11, act, act_h)
    loads[7].wait()

    def top(rows):
        h = h2[rows, :]
        n = (h * rms(h) * gain_l).astype(BF)
        n3[rows, :] = n
        pr = mm(n, wp[...])
        proj[rows, :] = pr
        emb[rows, :] = (pr * lax.rsqrt(jnp.sum(pr * pr, axis=-1, keepdims=True) + EPS)).astype(BF)

    rows_loop(count, 256, top)
    push(12, h2, h2_h)
    push(13, n3, n3_h)
    push(14, proj, proj_h)
    for copy in outs.values():
        copy.wait()


def layer_forward(tokens, weights, gains, rel, hot, seq, after=()):
    count, width = tokens.shape
    wq, wk, wv, wo, wg, wu, wd, wp = weights
    hidden = wg.shape[1]
    emb = wp.shape[1]
    heads = rel.shape[0]
    keys = DL if seq == DL else 128
    saved = (
        sds((count, width), BF),
        sds((count, width), BF),
        sds((count, width), BF),
        sds((count, width), BF),
        sds((heads, count, keys), BF),
        sds((count, width), F),
        sds((count, width), BF),
        sds((count, width), F),
        sds((count, width), BF),
        sds((count, hidden), BF),
        sds((count, hidden), BF),
        sds((count, hidden), BF),
        sds((count, width), F),
        sds((count, width), BF),
        sds((count, emb), F),
    )
    outs = pl.pallas_call(
        functools.partial(fwd_kernel, seq, heads, len(after)),
        out_shape=saved + (sds((count, emb), BF),),
        in_specs=[VM] * 4 + [ANY] * (8 + len(after)),
        out_specs=[ANY] * 15 + [VM],
        scratch_shapes=[pltpu.VMEM(w.shape, BF) for w in weights]
        + [pltpu.VMEM(s.shape, s.dtype) for s in saved]
        + [
            pltpu.VMEM((16, TABLE), F),
            pltpu.VMEM((128, TABLE), F),
            pltpu.SemaphoreType.DMA((8,)),
            pltpu.SemaphoreType.DMA((15,)),
        ],
        compiler_params=pltpu.CompilerParams(vmem_limit_bytes=VMEM_LIMIT),
        cost_estimate=cost(count * 14e6, 40e6),
        name="layer_forward_%d" % seq,
    )(tokens, gains, rel, hot, *weights, *after)
    return dict(zip(SAVED, outs))


def each_block(arrays, block, fn):
    first = 0
    for array in arrays:
        number = array.shape[0] // block
        if number == 1:
            fn(first, array[...])
        else:

            def step(i, carry, array=array, first=first):
                fn(first + i, array[pl.ds(pl.multiple_of(i * block, block), block), :])
                return carry

            lax.fori_loop(0, number, step, 0)
        first += number


def query_sims_kernel(n_arrays, number, qemb, mask, ids, used, cot, *refs):
    docs = refs[:n_arrays]
    coef, d_emb, parts, es, total, counts = refs[n_arrays:]
    n_docs = mask.shape[0]
    tokens = qemb.shape[0]
    queries = tokens // QUERY_LENGTH
    lane = lax.broadcasted_iota(jnp.int32, (tokens, 128), 1)
    lane_q = lax.broadcasted_iota(jnp.int32, (queries, 128), 1)
    total[...] = jnp.zeros_like(total)
    counts[...] = jnp.zeros_like(counts)

    def forward(slot, rows):
        d = number[slot]
        m = mask[d]
        wide = jnp.broadcast_to(m[:, None, :], (queries, QUERY_LENGTH, DL)).reshape(tokens, DL)
        e = jnp.exp(mm_nt(qemb[...], rows) * SCALE) * wide
        es[slot] = e
        total[...] = jnp.where(lane == d, jnp.sum(e, axis=1, keepdims=True), total[...])
        counts[...] = jnp.where(lane_q == d, jnp.sum(m, axis=1, keepdims=True), counts[...])

    each_block(docs, DL, forward)
    inside = lane_q < n_docs
    z = jnp.sum(jnp.log(1.0 + total[...]).reshape(queries, QUERY_LENGTH, 128), axis=1)
    z = z * (1.0 / QUERY_LENGTH)
    hot = jnp.zeros((queries, 128), F)
    for s in range(ids.shape[1]):
        here = (ids[:, s : s + 1] == lane_q) & (used[...] > s)
        hot = jnp.where(here, 1.0, hot)
    peak = jnp.max(jnp.where(inside, z, -1e30), axis=1, keepdims=True)
    power = jnp.where(inside, jnp.exp(jnp.where(inside, z - peak, 0.0)), 0.0)
    whole = jnp.sum(power, axis=1, keepdims=True)
    positive = jnp.sum(hot * power, axis=1, keepdims=True)
    loss = jnp.sum(jnp.log(whole) - jnp.log(positive))
    hits = jnp.sum(hot * counts[...])
    found = jnp.sum(hot)
    lane_p = lax.broadcasted_iota(jnp.int32, (8, 128), 1)
    parts[...] = jnp.where(
        lane_p == 0, loss, jnp.where(lane_p == 1, hits, jnp.where(lane_p == 2, found, 0.0))
    )
    d_z = power / whole - hot * power / positive
    d_wide = jnp.broadcast_to(d_z[:, None, :], (queries, QUERY_LENGTH, 128)).reshape(tokens, 128)
    c = d_wide * (SCALE / QUERY_LENGTH) / (1.0 + total[...])
    coef[...] = jnp.transpose(c)[0:n_docs, :]
    d_emb[...] = cot[...].astype(F)

    def backward(slot, rows):
        column = jnp.sum(jnp.where(lane == number[slot], c, 0.0), axis=1, keepdims=True)
        d_emb[...] += mm((es[slot] * column).astype(BF), rows)

    each_block(docs, DL, backward)


def query_sims(number, qemb, docs, mask, ids, used, cot):
    n_docs = mask.shape[0]
    tokens, emb = qemb.shape
    queries = tokens // QUERY_LENGTH
    return pl.pallas_call(
        functools.partial(query_sims_kernel, len(docs)),
        out_shape=(sds((n_docs, tokens), F), sds((tokens, emb), F), sds((8, 128), F)),
        in_specs=[SM] + [VM] * (5 + len(docs)),
        out_specs=[VM] * 3,
        scratch_shapes=[
            pltpu.VMEM((n_docs, tokens, DL), F),
            pltpu.VMEM((tokens, 128), F),
            pltpu.VMEM((queries, 128), F),
        ],
        compiler_params=pltpu.CompilerParams(vmem_limit_bytes=VMEM_LIMIT),
        cost_estimate=cost(n_docs * 67e6 * 10, n_docs * 1e6),
        name="query_sims",
    )(number, qemb, mask, ids, used, cot, *docs)


def top_rows(d_emb, proj, h2, gain, wp):
    inv = lax.rsqrt(jnp.sum(proj * proj, axis=-1, keepdims=True) + EPS)
    along = jnp.sum(proj * d_emb, axis=-1, keepdims=True)
    d_proj = (inv * d_emb - proj * (inv * inv * inv) * along).astype(BF)
    d_h2, grad_gain = rms_back(h2, gain, mm_nt(d_proj, wp))
    return d_proj, d_h2, grad_gain


def query_back_kernel(
    d_emb, proj, gains,
    h2_h, hid_h, gv_h, us_h, wp_h, wd_h, wg_h, wu_h, after,
    d_proj, d_ffn, d_gate_h, d_up_h, d_hid, g_gains,
    h2, hid, gv, us, wp, wd, wg, wu, d_gate, d_up, d_h2, d_n2, sem_in, sem_out,
):
    count = d_emb.shape[0]
    loads = [
        pltpu.make_async_copy(src, dst, sem_in.at[i])
        for i, (src, dst) in enumerate(
            zip((h2_h, wp_h, wd_h, us_h, gv_h, wg_h, wu_h, hid_h), (h2, wp, wd, us, gv, wg, wu, hid))
        )
    ]
    for copy in loads:
        copy.start()
    gain_f = gains[1:2, :]
    gain_l = gains[2:3, :]
    loads[0].wait()
    loads[1].wait()
    dp, dh, gg = top_rows(d_emb[...], proj[...], h2[...], gain_l, wp[...])
    d_proj[...] = dp
    d_h2[...] = dh
    g_gains[...] = jnp.zeros_like(g_gains)
    g_gains[1:2, :] = gg
    d_ffn[...] = dh.astype(BF)
    d_n2[...] = jnp.zeros_like(d_n2)
    for i in range(2, 7):
        loads[i].wait()

    def ffn(t, carry):
        cols = pl.ds(pl.multiple_of(t * 512, 512), 512)
        d_act = mm_nt(d_ffn[...], wd[cols, :])
        dg = (d_act * us[:, cols].astype(F)).astype(BF)
        du = (d_act * gv[:, cols].astype(F)).astype(BF)
        d_gate[:, cols] = dg
        d_up[:, cols] = du
        d_n2[...] += mm_nt(dg, wg[:, cols]) + mm_nt(du, wu[:, cols])
        return carry

    lax.fori_loop(0, wg.shape[1] // 512, ffn, 0)
    out_gate = pltpu.make_async_copy(d_gate, d_gate_h, sem_out.at[0])
    out_up = pltpu.make_async_copy(d_up, d_up_h, sem_out.at[1])
    out_gate.start()
    out_up.start()
    loads[7].wait()
    dm, gg = rms_back(hid[...], gain_f, d_n2[...])
    d_hid[...] = d_h2[...] + dm
    g_gains[0:1, :] = gg
    out_gate.wait()
    out_up.wait()


def query_back(d_emb, saved, weights, gains, after):
    wq, wk, wv, wo, wg, wu, wd, wp = weights
    count, emb = d_emb.shape
    width, hidden = wg.shape
    return pl.pallas_call(
        query_back_kernel,
        out_shape=(
            sds((count, emb), BF),
            sds((count, width), BF),
            sds((count, hidden), BF),
            sds((count, hidden), BF),
            sds((count, width), F),
            sds((8, width), F),
        ),
        in_specs=[VM] * 3 + [ANY] * 9,
        out_specs=[VM, VM, ANY, ANY, VM, VM],
        scratch_shapes=[
            pltpu.VMEM((count, width), F),
            pltpu.VMEM((count, width), F),
            pltpu.VMEM((count, hidden), BF),
            pltpu.VMEM((count, hidden), BF),
            pltpu.VMEM(wp.shape, BF),
            pltpu.VMEM(wd.shape, BF),
            pltpu.VMEM(wg.shape, BF),
            pltpu.VMEM(wu.shape, BF),
            pltpu.VMEM((count, hidden), BF),
            pltpu.VMEM((count, hidden), BF),
            pltpu.VMEM((count, width), F),
            pltpu.VMEM((count, width), F),
            pltpu.SemaphoreType.DMA((8,)),
            pltpu.SemaphoreType.DMA((2,)),
        ],
        compiler_params=pltpu.CompilerParams(vmem_limit_bytes=VMEM_LIMIT),
        cost_estimate=cost(4e9, 30e6),
        name="query_back",
    )(d_emb, saved["proj"], gains, saved["h2"], saved["hid"], saved["gv"], saved["us"], wp, wd, wg, wu, after)


def split_out(own, grads, keep_h, send_h, sem):
    first = pltpu.make_async_copy(grads.at[own], keep_h, sem.at[0])
    second = pltpu.make_async_copy(grads.at[1 - own], send_h, sem.at[1])
    first.start()
    second.start()
    return first, second


def doc_top_kernel(
    n_arrays, own, number, d_emb_in, demb, mask, rep, coef, proj, gains, wp, d_proj_q, d_ffn_q,
    h2_h, act_h, act_qh, n3_h, n3_qh,
    *refs,
):
    every = refs[:n_arrays]
    (
    d_h2, d_ffn, g_gain, keep_h, send_h,
    h2, act, n3, d_proj, d_all, acc, grads, sem_in, sem_out,
    ) = refs[n_arrays:]
    count = demb.shape[0]
    rest = d_ffn_q.shape[0]
    loads = [
        pltpu.make_async_copy(src, dst, sem_in.at[i])
        for i, (src, dst) in enumerate(
            (
                (h2_h, h2),
                (act_h, act.at[0:count]),
                (act_qh, act.at[count:]),
                (n3_h, n3.at[0:count]),
                (n3_qh, n3.at[count:]),
            )
        )
    ]
    for copy in loads:
        copy.start()
    acc[...] = d_emb_in[...].astype(F)
    per = mask.shape[2] * QUERY_LENGTH // 256

    def sims(slot, qb):
        row = number[slot]
        e = jnp.exp(mm_nt(demb[...], qb) * SCALE)
        m = mm(mask[row // per], rep[:, pl.ds(pl.multiple_of((row % per) * 256, 256), 256)])
        ds = (e * m * coef[pl.ds(row, 1), :]).astype(BF)
        acc[...] += mm(ds, qb)

    each_block(every, 256, sims)
    loads[0].wait()
    dp, dh, gg = top_rows(acc[...], proj[...], h2[...], gains[2:3, :], wp[...])
    d_proj[0:count, :] = dp
    d_proj[count:, :] = d_proj_q[...]
    d_h2[...] = dh
    g_gain[...] = jnp.zeros_like(g_gain)
    g_gain[0:1, :] = gg
    d_ffn[...] = dh.astype(BF)
    d_all[0:count, :] = dh.astype(BF)
    d_all[count:, :] = d_ffn_q[...]
    for copy in loads[1:]:
        copy.wait()
    gp = mm_tn(n3[...], d_proj[...])
    grads[:, :, :, :, 192:224, :] = jnp.zeros((2, 4, 2, 2, 32, 256), BF)
    for w in range(8):
        for r in range(3):
            lo = 96 * w + 32 * r
            grads[w % 2, w // 2, r // 2, r % 2, 192:224, 0:128] = gp[lo : lo + 32, :].astype(BF)

    def down(w, carry):
        g = mm_tn(act[:, pl.ds(pl.multiple_of(w * 256, 256), 256)], d_all[...])
        for r in range(4):
            for c in range(3):
                grads[w % 2, w // 2, r // 2, r % 2, 64 * c : 64 * c + 64, :] = g[
                    64 * r : 64 * r + 64, 256 * c : 256 * c + 256
                ].astype(BF)
        return carry

    lax.fori_loop(0, 8, down, 0)
    for copy in split_out(own[0], grads, keep_h, send_h, sem_out):
        copy.wait()


def doc_top(own, number, d_emb, demb, every, mask, rep, coef, dsaved, qsaved, gains, wp, d_proj_q, d_ffn_q):
    count, width = dsaved["h2"].shape
    rest = d_ffn_q.shape[0]
    hidden = dsaved["act"].shape[1]
    emb = wp.shape[1]
    piece = sds((4, 2, 2, 224, 256), BF)
    return pl.pallas_call(
        functools.partial(doc_top_kernel, len(every)),
        out_shape=(sds((count, width), F), sds((count, width), BF), sds((8, width), F), piece, piece),
        in_specs=[SM] * 2 + [VM] * 10 + [ANY] * 5 + [VM] * len(every),
        out_specs=[VM] * 3 + [ANY] * 2,
        scratch_shapes=[
            pltpu.VMEM((count, width), F),
            pltpu.VMEM((count + rest, hidden), BF),
            pltpu.VMEM((count + rest, width), BF),
            pltpu.VMEM((count + rest, emb), BF),
            pltpu.VMEM((count + rest, width), BF),
            pltpu.VMEM((count, emb), F),
            pltpu.VMEM((2, 4, 2, 2, 224, 256), BF),
            pltpu.SemaphoreType.DMA((5,)),
            pltpu.SemaphoreType.DMA((2,)),
        ],
        compiler_params=pltpu.CompilerParams(vmem_limit_bytes=VMEM_LIMIT),
        cost_estimate=cost(6e9, 10e6),
        name="doc_top",
    )(
        own, number, d_emb, demb, mask, rep, coef, dsaved["proj"], gains, wp, d_proj_q, d_ffn_q,
        dsaved["h2"], dsaved["act"], qsaved["act"], dsaved["n3"], qsaved["n3"], *every,
    )


def ffn_grads_kernel(
    own, d_ffn, n2_d, n2_q, wd_h, us_h, gv_h, gate_qh, up_qh,
    gate_h, up_h, keep_h, send_h,
    wd, us, gv, gate, up, n2t, grads, sem_in, sem_out,
):
    count = d_ffn.shape[0]
    loads = [
        pltpu.make_async_copy(src, dst, sem_in.at[i])
        for i, (src, dst) in enumerate(
            (
                (wd_h, wd),
                (us_h, us),
                (gv_h, gv),
                (gate_qh, gate.at[count:]),
                (up_qh, up.at[count:]),
            )
        )
    ]
    for copy in loads:
        copy.start()
    n2t[:, 0:count] = jnp.transpose(n2_d[...])
    n2t[:, count:] = jnp.transpose(n2_q[...])
    for copy in loads:
        copy.wait()

    def tile(t, carry):
        cols = pl.ds(pl.multiple_of(t * 512, 512), 512)
        d_act = mm_nt(d_ffn[...], wd[cols, :])
        gate[0:count, cols] = (d_act * us[:, cols].astype(F)).astype(BF)
        up[0:count, cols] = (d_act * gv[:, cols].astype(F)).astype(BF)
        for base, source in ((0, gate), (1, up)):
            g = mm(n2t[...], source[:, cols]).astype(BF)
            for c in range(2):
                start = pl.multiple_of((t % 2) * 192 + 96 * c, 96)
                for w in range(8):
                    grads[w % 2, w // 2, base, t // 2, pl.ds(start, 96), :] = g[
                        96 * w : 96 * w + 96, 256 * c : 256 * c + 256
                    ]
        return carry

    lax.fori_loop(0, wd.shape[0] // 512, tile, 0)
    copies = [
        pltpu.make_async_copy(gate.at[0:count], gate_h, sem_out.at[2]),
        pltpu.make_async_copy(up.at[0:count], up_h, sem_out.at[3]),
    ]
    for copy in copies:
        copy.start()
    for copy in tuple(split_out(own[0], grads, keep_h, send_h, sem_out)) + tuple(copies):
        copy.wait()


def ffn_grads(own, d_ffn, dsaved, qsaved, wd, gate_q, up_q):
    count, width = d_ffn.shape
    rest, hidden = gate_q.shape
    piece = sds((4, 2, 2, 384, 256), BF)
    return pl.pallas_call(
        ffn_grads_kernel,
        out_shape=(sds((count, hidden), BF), sds((count, hidden), BF), piece, piece),
        in_specs=[SM] + [VM] * 3 + [ANY] * 5,
        out_specs=[ANY] * 4,
        scratch_shapes=[
            pltpu.VMEM(wd.shape, BF),
            pltpu.VMEM((count, hidden), BF),
            pltpu.VMEM((count, hidden), BF),
            pltpu.VMEM((count + rest, hidden), BF),
            pltpu.VMEM((count + rest, hidden), BF),
            pltpu.VMEM((width, count + rest), BF),
            pltpu.VMEM((2, 4, 2, 2, 384, 256), BF),
            pltpu.SemaphoreType.DMA((5,)),
            pltpu.SemaphoreType.DMA((4,)),
        ],
        compiler_params=pltpu.CompilerParams(vmem_limit_bytes=VMEM_LIMIT),
        cost_estimate=cost(8e9, 20e6),
        name="ffn_grads",
    )(own, d_ffn, dsaved["n2"], qsaved["n2"], wd, dsaved["us"], dsaved["gv"], gate_q, up_q)


def middle_back_kernel(
    d_h2, hid, d_hid_q, gains,
    wg_h, wu_h, wo_h, gate_h, up_h, li_d, li_q, *refs
):
    d_hid, g_gain, d_attn, g, wg, wu, wo, gate, up, li, sem_in = refs[-11:]
    count = d_h2.shape[0]
    rest = d_hid_q.shape[0]
    loads = [
        pltpu.make_async_copy(src, dst, sem_in.at[i])
        for i, (src, dst) in enumerate(
            (
                (wg_h, wg),
                (gate_h, gate),
                (wu_h, wu),
                (up_h, up),
                (wo_h, wo),
                (li_d, li.at[0:count]),
                (li_q, li.at[count:]),
            )
        )
    ]
    for copy in loads:
        copy.start()
    for copy in loads[0:4]:
        copy.wait()
    gain_f = gains[1:2, :]
    g_gain[...] = jnp.zeros_like(g_gain)

    def through(rows):
        d_n2 = mm_nt(gate[rows, :], wg[...]) + mm_nt(up[rows, :], wu[...])
        dm, gg = rms_back(hid[rows, :], gain_f, d_n2)
        total = d_h2[rows, :] + dm
        d_hid[rows, :] = total
        g_gain[0:1, :] += gg
        d_attn[rows, :] = total.astype(BF)

    rows_loop(count, 256, through)
    d_attn[count:, :] = d_hid_q[...].astype(BF)
    for copy in loads[4:]:
        copy.wait()

    def to_context(rows):
        d_context = mm_nt(d_attn[rows, :], wo[...]).astype(BF).astype(F)
        g[rows, :] = (d_context * li[rows, :]).astype(BF)

    rows_loop(count + rest, 256, to_context)


def middle_back(d_h2, d_hid_q, gate, up, dsaved, qsaved, weights, gains, after):
    wq, wk, wv, wo, wg, wu, wd, wp = weights
    count, width = d_h2.shape
    rows = count + d_hid_q.shape[0]
    hidden = wg.shape[1]
    return pl.pallas_call(
        middle_back_kernel,
        out_shape=(sds((count, width), F), sds((8, width), F), sds((rows, width), BF), sds((rows, width), BF)),
        in_specs=[VM] * 4 + [ANY] * (7 + len(after)),
        out_specs=[VM] * 4,
        scratch_shapes=[
            pltpu.VMEM(wg.shape, BF),
            pltpu.VMEM(wu.shape, BF),
            pltpu.VMEM(wo.shape, BF),
            pltpu.VMEM((count, hidden), BF),
            pltpu.VMEM((count, hidden), BF),
            pltpu.VMEM((rows, width), F),
            pltpu.SemaphoreType.DMA((7,)),
        ],
        compiler_params=pltpu.CompilerParams(vmem_limit_bytes=VMEM_LIMIT),
        cost_estimate=cost(5e9, 20e6),
        name="middle_back",
    )(d_h2, dsaved["hid"], d_hid_q, gains, wg, wu, wo, gate, up, dsaved["li"], qsaved["li"], *after)


def attn_back_kernel(
    own, hot, d_attn, g,
    n1_d, n1_q, q_d, q_q, k_d, k_q, v_d, v_q, li_d, li_q, ctx_d, ctx_q, p_dh, p_qh, *refs
):
    (
    dq_h, dk_h, dv_h, g_rel, keep_h, send_h,
    n1, q, k, v, li, ctx, p_d, p_q,
    dq, dk, dv, ds, acc, sums, n1t, grads, sem_in, sem_out,
    ) = refs[-24:]
    count = q_d.shape[0]
    rest = q_q.shape[0]
    heads = p_d.shape[0]
    loads = [
        pltpu.make_async_copy(src, dst, sem_in.at[i])
        for i, (src, dst) in enumerate(
            (
                (li_d, li.at[0:count]),
                (li_q, li.at[count:]),
                (q_d, q.at[0:count]),
                (q_q, q.at[count:]),
                (k_d, k.at[0:count]),
                (k_q, k.at[count:]),
                (v_d, v.at[0:count]),
                (v_q, v.at[count:]),
                (p_dh, p_d),
                (p_qh, p_q),
                (ctx_d, ctx.at[0:count]),
                (ctx_q, ctx.at[count:]),
                (n1_d, n1.at[0:count]),
                (n1_q, n1.at[count:]),
            )
        )
    ]
    for copy in loads:
        copy.start()

    def put(which, value):
        value = value.astype(BF)
        for w in range(8):
            for c in range(3):
                grads[w % 2, w // 2, which // 2, which % 2, 96 * c : 96 * c + 96, :] = value[
                    96 * w : 96 * w + 96, 256 * c : 256 * c + 256
                ]

    for copy in loads[0:10]:
        copy.wait()
    sums[...] = jnp.zeros_like(sums)
    low, high, _, _ = half_masks()

    def pair(index, carry):
        lanes = pl.ds(pl.multiple_of(index * 128, 128), 128)
        q2 = q[:, lanes]
        k2 = k[:, lanes]
        v2 = v[:, lanes]
        g2 = g[:, lanes]
        l2 = li[:, lanes]
        d_q = jnp.zeros((count, 128), F)
        d_k = jnp.zeros((count, 128), F)
        d_v = jnp.zeros((count, 128), F)
        d_qq = [jnp.zeros((128, 128), F)] * (rest // 128)
        d_kq = [jnp.zeros((128, 128), F)] * (rest // 128)
        d_vq = [jnp.zeros((128, 128), F)] * (rest // 128)
        for e, keep in enumerate((low, high)):
            head = 2 * index + e
            keep = keep.astype(BF)
            km = k2 * keep
            vm = v2 * keep
            qm = q2 * keep
            gm = g2 * keep
            share = l2[:, 64 * e : 64 * e + 1]
            acc[...] = jnp.zeros_like(acc)
            for i in range(count // 128):
                rows = slice(128 * i, 128 * i + 128)
                d_p = mm_nt(g2[rows], vm[0:count])
                pf = p_d[head, rows, :].astype(F)
                t = pf * d_p
                dsb = (t - pf * (share[rows] * jnp.sum(t, axis=1, keepdims=True))).astype(BF)
                ds[rows, :] = dsb
                acc[:, SHIFT - 128 * i : SHIFT - 128 * i + DL] += dsb.astype(F)
            d_q = d_q + mm(ds[...], km[0:count])
            d_k = d_k + mm_tn(ds[...], qm[0:count])
            d_v = d_v + mm_tn(p_d[head], gm[0:count])
            for i in range(rest // 128):
                rows = slice(count + 128 * i, count + 128 * i + 128)
                d_p = mm_nt(g2[rows], vm[rows])
                pb = p_q[head, 128 * i : 128 * i + 128, :]
                pf = pb.astype(F)
                t = pf * d_p
                dsb = (t - pf * (share[rows] * jnp.sum(t, axis=1, keepdims=True))).astype(BF)
                acc[:, SHIFT : SHIFT + 128] += dsb.astype(F)
                d_qq[i] = d_qq[i] + mm(dsb, km[rows])
                d_kq[i] = d_kq[i] + mm_tn(dsb, qm[rows])
                d_vq[i] = d_vq[i] + mm_tn(pb, gm[rows])
            folded = acc[...]
            half = 64
            while half >= 8:
                folded = folded[0:half] + pltpu.roll(folded[half : 2 * half], TABLE - half, 1)
                half //= 2
            line = folded[0:1]
            for i in range(1, 8):
                line = line + pltpu.roll(folded[i : i + 1], TABLE - i, 1)
            sums[pl.ds(head, 1), :] = line
        dq[0:count, lanes] = d_q.astype(BF)
        dk[0:count, lanes] = d_k.astype(BF)
        dv[0:count, lanes] = d_v.astype(BF)
        for i in range(rest // 128):
            rows = slice(count + 128 * i, count + 128 * i + 128)
            dq[rows, lanes] = d_qq[i].astype(BF)
            dk[rows, lanes] = d_kq[i].astype(BF)
            dv[rows, lanes] = d_vq[i].astype(BF)
        return carry

    lax.fori_loop(0, heads // 2, pair, 0)
    copies = [
        pltpu.make_async_copy(src, dst, sem_out.at[2 + i])
        for i, (src, dst) in enumerate(((dq, dq_h), (dk, dk_h), (dv, dv_h)))
    ]
    for copy in copies:
        copy.start()
    for copy in loads[10:]:
        copy.wait()
    n1t[...] = jnp.transpose(n1[...])
    put(0, mm(n1t[...], dq[...]))
    put(1, mm(n1t[...], dk[...]))
    put(2, mm(n1t[...], dv[...]))
    put(3, mm_tn(ctx[...], d_attn[...]))
    out = split_out(own[0], grads, keep_h, send_h, sem_out)
    g_rel[...] = lax.dot_general(
        sums[...], hot[...], (((1,), (1,)), ((), ())),
        preferred_element_type=F, precision=lax.Precision.HIGHEST,
    )
    for copy in tuple(out) + tuple(copies):
        copy.wait()


def attn_back(own, d_attn, g, dsaved, qsaved, hot, after):
    rows, width = d_attn.shape
    heads = dsaved["p"].shape[0]
    buckets = hot.shape[0]
    piece = sds((4, 2, 2, 288, 256), BF)
    full = sds((rows, width), BF)
    both = []
    for name in ("n1", "q", "k", "v", "li", "ctx", "p"):
        both += [dsaved[name], qsaved[name]]
    return pl.pallas_call(
        attn_back_kernel,
        out_shape=(full, full, full, sds((16, buckets), F), piece, piece),
        in_specs=[SM] + [VM] * 3 + [ANY] * (14 + len(after)),
        out_specs=[ANY] * 3 + [VM] + [ANY] * 2,
        scratch_shapes=[pltpu.VMEM((rows, width), BF)] * 4
        + [
            pltpu.VMEM((rows, width), F),
            pltpu.VMEM((rows, width), BF),
            pltpu.VMEM(dsaved["p"].shape, BF),
            pltpu.VMEM(qsaved["p"].shape, BF),
            pltpu.VMEM((rows, width), BF),
            pltpu.VMEM((rows, width), BF),
            pltpu.VMEM((rows, width), BF),
            pltpu.VMEM((DL, DL), BF),
            pltpu.VMEM((128, TABLE), F),
            pltpu.VMEM((16, TABLE), F),
            pltpu.VMEM((width, rows), BF),
            pltpu.VMEM((2, 4, 2, 2, 288, 256), BF),
            pltpu.SemaphoreType.DMA((14,)),
            pltpu.SemaphoreType.DMA((5,)),
        ],
        compiler_params=pltpu.CompilerParams(vmem_limit_bytes=VMEM_LIMIT),
        cost_estimate=cost(15e9, 40e6),
        name="attn_back",
    )(own, hot, d_attn, g, *both, *after)


def input_back_kernel(
    tok_d, tok_q, d_hid_d, d_hid_q, gains, dq, dk, dv, wq, wk, wv, gain_f, gain_l, gains_q, g_rel,
    parts, *refs
):
    out_d, out_q, small, g_gain = refs[-4:]
    count = tok_d.shape[0]
    gain_a = gains[0:1, :]
    g_gain[...] = jnp.zeros_like(g_gain)

    def part(offset, tok, d_hid, out):
        def step(rows):
            at = pl.ds(pl.multiple_of(rows.start + offset, 256), 256)
            d_n1 = mm_nt(dq[at, :], wq[...]) + mm_nt(dk[at, :], wk[...]) + mm_nt(dv[at, :], wv[...])
            d_in, gg = rms_back(tok[rows, :].astype(F), gain_a, d_n1)
            g_gain[0:1, :] += gg
            out[rows, :] = (d_hid[rows, :] + d_in).astype(BF)

        rows_loop(tok.shape[0], 256, step)

    part(0, tok_d, d_hid_d, out_d)
    part(count, tok_q, d_hid_q, out_q)
    small[...] = jnp.zeros_like(small)
    rows = (
        g_gain[0:1, :],
        gain_f[0:1, :] + gains_q[0:1, :],
        gain_l[0:1, :] + gains_q[1:2, :],
    )
    for i, row in enumerate(rows):
        for c in range(6):
            small[8 * i + c : 8 * i + c + 1, :] = row[:, 128 * c : 128 * c + 128]
    small[24:25, :] = parts[0:1, :]
    small[32:48, 0 : g_rel.shape[1]] = g_rel[...]


def input_back(tok_d, tok_q, d_hid_d, d_hid_q, gains, dq, dk, dv, weights, extra, after):
    width = tok_d.shape[1]
    return pl.pallas_call(
        input_back_kernel,
        out_shape=(sds(tok_d.shape, BF), sds(tok_q.shape, BF), sds((48, 128), F)),
        in_specs=[VM] * 16 + [ANY] * len(after),
        out_specs=[VM] * 3,
        scratch_shapes=[pltpu.VMEM((8, width), F)],
        compiler_params=pltpu.CompilerParams(vmem_limit_bytes=VMEM_LIMIT),
        cost_estimate=cost(3e9, 10e6),
        name="input_back",
    )(tok_d, tok_q, d_hid_d, d_hid_q, gains, dq, dk, dv, weights[0], weights[1], weights[2], *extra, *after)


def unpack_kernel(which, me, a_own, a_came, b_own, b_came, *refs):
    stack = refs[-1]
    outs = refs[-1 - (4 if which == "attn" else 2) : -1]
    half = a_own.shape[1]
    y, x = me[0], me[1]
    for i in range(2):
        stack[i, x, 0:half, :] = a_own[i]
        stack[i, 1 - x, 0:half, :] = a_came[i]
        stack[y, i, half:, :] = b_own[i]
        stack[1 - y, i, half:, :] = b_came[i]
    if which == "ffn":
        for r in range(4):
            out = outs[r // 2]
            for c in range(4):
                at = (r % 2) * 1024 + 256 * c
                out[:, at : at + 256] = stack[r // 2, r % 2, 96 * c : 96 * c + 96, :].astype(F)
    elif which == "attn":
        for r in range(4):
            for c in range(3):
                outs[r][:, 256 * c : 256 * c + 256] = stack[
                    r // 2, r % 2, 96 * c : 96 * c + 96, :
                ].astype(F)
    else:
        for r in range(4):
            for c in range(3):
                outs[0][64 * r : 64 * r + 64, 256 * c : 256 * c + 256] = stack[
                    r // 2, r % 2, 64 * c : 64 * c + 64, :
                ].astype(F)
        for r in range(3):
            outs[1][32 * r : 32 * r + 32, :] = stack[r // 2, r % 2, 192:224, 0:128].astype(F)


def unpack(which, me, parts, shapes, after):
    half = parts[0].shape[1]
    return pl.pallas_call(
        functools.partial(unpack_kernel, which),
        out_shape=tuple(sds(s, F) for s in shapes),
        in_specs=[SM] + [VM] * 4 + [ANY] * len(after),
        out_specs=tuple(VM for _ in shapes),
        scratch_shapes=[pltpu.VMEM((2, 2, 2 * half, 256), BF)],
        compiler_params=pltpu.CompilerParams(vmem_limit_bytes=VMEM_LIMIT),
        cost_estimate=cost(1e6, 3e6),
        name="unpack_" + which,
    )(me, *parts, *after)


def swap(values, axis, size, mask):
    return lax.ppermute(values, axis, [(i, i ^ mask) for i in range(size)])


def near_kernel(me, keep, came, *refs):
    send_a, send_b, own_a, own_b = refs[-4:]
    y, x = me[0], me[1]
    half = own_a.shape[2]

    def total(i, k, low):
        part = keep[0, i, k, low : low + half, :].astype(F) + came[0, i, k, low : low + half, :].astype(F)
        return part.astype(BF)

    for i in range(2):
        send_a[0, i] = total(i, 1 - x, 0)
        own_a[0, i] = total(i, x, 0)
        send_b[0, i] = total(1 - y, i, half)
        own_b[0, i] = total(y, i, half)


def line_kernel(me, a, came_a, b, came_b, *refs):
    z = me[2]
    for m, out in enumerate(refs[-4:]):
        out[0] = (a[z ^ m].astype(F) + came_a[z ^ m].astype(F)).astype(BF)
        out[1] = (b[z ^ m].astype(F) + came_b[z ^ m].astype(F)).astype(BF)


def far_kernel(own, one, two, three, *refs):
    for i, out in enumerate(refs[-2:]):
        total = own[i].astype(F) + one[i].astype(F) + two[i].astype(F) + three[i].astype(F)
        out[...] = total.astype(BF)


def back_kernel(a, came_a, b, came_b, *refs):
    out_a, out_b = refs[-2:]
    out_a[...] = (a[...].astype(F) + came_a[...].astype(F)).astype(BF)
    out_b[...] = (b[...].astype(F) + came_b[...].astype(F)).astype(BF)


def sum_two_kernel(a, b, *refs):
    refs[-1][...] = a[...] + b[...]


def sum_two(a, b, after):
    return pl.pallas_call(
        sum_two_kernel,
        out_shape=sds(a.shape, F),
        in_specs=[VM] * 2 + [ANY] * len(after),
        out_specs=VM,
        cost_estimate=cost(1e4, 1e5),
        name="sum_two",
    )(a, b, *after)


def sum_four_kernel(which, me, own, one, two, three, *refs):
    out, stack = refs[-2:]
    for m, part in enumerate((own, one, two, three)):
        stack[me[which] ^ m] = part[...]
    out[...] = stack[0] + stack[1] + stack[2] + stack[3]


def sum_four(me, which, own, came, after):
    return pl.pallas_call(
        functools.partial(sum_four_kernel, which),
        out_shape=sds(own.shape, F),
        in_specs=[SM] + [VM] * 4 + [ANY] * len(after),
        out_specs=VM,
        scratch_shapes=[pltpu.VMEM((4,) + own.shape, F)],
        cost_estimate=cost(1e4, 1e5),
        name="sum_four",
    )(me, own, *came, *after)


class Reduction:
    def __init__(self, name, me, keep, send):
        self.name = name
        self.me = me
        self.half = keep.shape[3] // 2
        self.keep = keep
        self.came = swap(send, "wide", 8, 1)

    def near(self, after):
        rows = 2 * self.half
        whole = pl.BlockSpec((1, 2, 2, rows, 256), lambda i: (i, 0, 0, 0, 0))
        part = pl.BlockSpec((1, 2, self.half, 256), lambda i: (i, 0, 0, 0))
        send_a, send_b, self.a, self.b = pl.pallas_call(
            near_kernel,
            grid=(4,),
            out_shape=(sds((4, 2, self.half, 256), BF),) * 4,
            in_specs=[SM, whole, whole] + [ANY] * len(after),
            out_specs=(part,) * 4,
            compiler_params=pltpu.CompilerParams(vmem_limit_bytes=VMEM_LIMIT),
            cost_estimate=cost(1e6, rows * 256 * 2 * 48),
            name="near_" + self.name,
        )(self.me, self.keep, self.came, *after)
        self.came_a = swap(send_a, "rep", 4, 1)
        self.came_b = swap(send_b, "rep", 4, 2)
        return (self.a,)

    def line(self, after):
        outs = pl.pallas_call(
            line_kernel,
            out_shape=(sds((2, 2, self.half, 256), BF),) * 4,
            in_specs=[SM] + [VM] * 4 + [ANY] * len(after),
            out_specs=(VM,) * 4,
            compiler_params=pltpu.CompilerParams(vmem_limit_bytes=VMEM_LIMIT),
            cost_estimate=cost(1e6, self.half * 256 * 2 * 48),
            name="line_" + self.name,
        )(self.me, self.a, self.came_a, self.b, self.came_b, *after)
        self.own = outs[0]
        self.came = [swap(outs[m], "wide", 8, 2 * m) for m in (1, 2, 3)]
        return (self.own,)

    def far(self, after):
        self.a, self.b = pl.pallas_call(
            far_kernel,
            out_shape=(sds((2, self.half, 256), BF),) * 2,
            in_specs=[VM] * 4 + [ANY] * len(after),
            out_specs=(VM,) * 2,
            compiler_params=pltpu.CompilerParams(vmem_limit_bytes=VMEM_LIMIT),
            cost_estimate=cost(1e6, self.half * 256 * 2 * 20),
            name="far_" + self.name,
        )(self.own, *self.came, *after)
        self.came_a = swap(self.a, "rep", 4, 2)
        self.came_b = swap(self.b, "rep", 4, 1)
        return (self.a,)

    def back(self, after):
        self.a, self.b = pl.pallas_call(
            back_kernel,
            out_shape=(sds((2, self.half, 256), BF),) * 2,
            in_specs=[VM] * 4 + [ANY] * len(after),
            out_specs=(VM,) * 2,
            compiler_params=pltpu.CompilerParams(vmem_limit_bytes=VMEM_LIMIT),
            cost_estimate=cost(1e6, self.half * 256 * 2 * 12),
            name="back_" + self.name,
        )(self.a, self.came_a, self.b, self.came_b, *after)
        self.came_a = swap(self.a, "rep", 4, 1)
        self.came_b = swap(self.b, "rep", 4, 2)
        return (self.a,)

    def unpack(self, shapes, after):
        return unpack(self.name, self.me, (self.a, self.came_a, self.b, self.came_b), shapes, after)


def natural(which, keep, send):
    both = jnp.stack([keep, send])
    both = both.reshape((2, 4, 4) + both.shape[4:])
    if which == "ffn":
        a = both.reshape(2, 4, 4, 4, 96, 256).transpose(1, 0, 4, 2, 3, 5).reshape(768, 4096)
        return [a[:, :2048], a[:, 2048:]]
    if which == "attn":
        a = both.reshape(2, 4, 4, 3, 96, 256).transpose(2, 1, 0, 4, 3, 5).reshape(4, 768, 768)
        return [a[i] for i in range(4)]
    d = both[:, :, :, :192].reshape(2, 4, 4, 3, 64, 256).transpose(1, 0, 2, 4, 3, 5)
    e = both[:, :, :3, 192:224, :128].transpose(1, 0, 2, 3, 4)
    return [d.reshape(2048, 768), e.reshape(768, 128)]


def body(
    doc_tokens, query_tokens, doc_cotangent, query_cotangent, retrieved, pos_ids, pos_count,
    w_query, w_key, carried_content_weights, w_out, w_gate, w_up, w_down, w_proj,
    gain_attn, gain_ffn, gain_final, rel_bias,
):
    n_wide = lax.axis_size("wide")
    n_rep = lax.axis_size("rep")
    fast = n_wide == 8 and n_rep == 4
    weights = (w_query, w_key, carried_content_weights, w_out, w_gate, w_up, w_down, w_proj)
    width = doc_tokens.shape[1]
    gains = jnp.stack([gain_attn, gain_ffn, gain_final]).astype(F)
    buckets, heads = rel_bias.shape
    hot_np = bucket_hot(buckets)
    hot = jnp.asarray(hot_np, BF)
    hot_f = jnp.asarray(hot_np, F)
    rel = jnp.transpose(rel_bias)
    group = retrieved.shape[1]
    queries = pos_ids.shape[0]
    wide = lax.axis_index("wide").astype(jnp.int32)
    z, core = wide // 2, wide % 2

    mask_rows = jnp.transpose(retrieved).astype(F)
    mask_query = lax.all_to_all(mask_rows, "wide", 0, 0, tiled=True).reshape(n_wide, queries, DL)
    blocks = group // 64
    mask_doc = retrieved.astype(BF).reshape(DL, blocks, 64).transpose(1, 0, 2)
    rep_hot = jnp.asarray(query_hot(64), BF)

    def line_swaps(emb):
        return [emb] + [swap(emb, "wide", n_wide, 2 * m) for m in (1, 2, 3)]

    doc = layer_forward(doc_tokens, weights, gains, rel, hot, DL)
    if fast:
        number = jnp.stack(
            [(z ^ m) * 2 + core for m in range(4)] + [(z ^ m) * 2 + 1 - core for m in range(4)]
        )
        docs = line_swaps(doc["emb"])
    else:
        number = jnp.arange(n_wide, dtype=jnp.int32)
        docs = [lax.all_gather(doc["emb"], "wide", axis=0, tiled=True)]
    query = layer_forward(
        query_tokens, weights, gains, rel, hot, QUERY_LENGTH, (doc["emb"], mask_query)
    )
    if fast:
        docs = docs + [swap(d, "wide", n_wide, 1) for d in docs]
        every = line_swaps(query["emb"])
    else:
        every = [lax.all_gather(query["emb"], "wide", axis=0, tiled=True)]

    coef, d_query_emb, parts = query_sims(
        number, query["emb"], docs, mask_query, pos_ids, pos_count.reshape(queries, 1), query_cotangent
    )
    coef_all = lax.all_to_all(coef, "wide", 0, 0, tiled=True)
    if fast:
        every = every + [swap(e, "wide", n_wide, 1) for e in every]
    own = (core if fast else jnp.int32(0)).reshape(1)
    d_proj_q, d_ffn_q, d_gate_q, d_up_q, d_hid_q, gains_q = query_back(
        d_query_emb, query, weights, gains, coef
    )
    d_h2, d_ffn, gain_l, keep_down, send_down = doc_top(
        own, number, doc_cotangent, doc["emb"], every, mask_doc, rep_hot, coef_all, doc, query, gains,
        w_proj, d_proj_q, d_ffn_q,
    )
    d_gate, d_up, keep_ffn, send_ffn = ffn_grads(own, d_ffn, doc, query, w_down, d_gate_q, d_up_q)
    after = ()
    if fast:
        rep = lax.axis_index("rep").astype(jnp.int32)
        me = jnp.stack([rep // 2, rep % 2, z, rep])
        down = Reduction("down", me, keep_down, send_down)
        ffn = Reduction("ffn", me, keep_ffn, send_ffn)
        after = down.near((d_up,))
    d_hid, gain_f, d_attn, g = middle_back(
        d_h2, d_hid_q, d_gate, d_up, doc, query, weights, gains, after
    )
    if fast:
        after = ffn.near((d_attn,))
        after = down.line(after)
    dq, dk, dv, g_rel, keep_attn, send_attn = attn_back(own, d_attn, g, doc, query, hot_f, after)
    if fast:
        attn = Reduction("attn", me, keep_attn, send_attn)
        after = down.far((g_rel,))
        after = ffn.line(after)
    doc_grad, query_grad, small = input_back(
        doc_tokens, query_tokens, d_hid, d_hid_q, gains, dq, dk, dv, weights,
        (gain_f, gain_l, gains_q, g_rel, parts), after,
    )
    if fast:
        after = attn.near((small,))
        small = sum_two(small, swap(small, "wide", 8, 1), after)
        after = down.back((small,))
        came = [swap(small, "rep", 4, m) for m in (1, 2, 3)]
        after = ffn.far(after)
        small = sum_four(me, 3, small, came, after)
        came = [swap(small, "wide", 8, 2 * m) for m in (1, 2, 3)]
        after = attn.line((small,))
        after = grad_down, grad_proj = down.unpack(((256, 768), (96, 128)), after)
        small = sum_four(me, 2, small, came, after[1:])
        after = ffn.back((small,))
        after = attn.far(after)
        after = grad_gate, grad_up = ffn.unpack(((96, 2048), (96, 2048)), after)
        after = attn.back(after[1:])
        grad_query, grad_key, grad_value, grad_out = attn.unpack(((96, 768),) * 4, after)
    else:
        small = lax.psum(small, ("rep", "wide"))
        shards = []
        for which, keep, send in (
            ("attn", keep_attn, send_attn),
            ("ffn", keep_ffn, send_ffn),
            ("down", keep_down, send_down),
        ):
            for whole in natural(which, keep, send):
                part = lax.psum_scatter(whole, "wide", scatter_dimension=0, tiled=True)
                shards.append(lax.psum(part, "rep").astype(F))
        (
            grad_query, grad_key, grad_value, grad_out, grad_gate, grad_up, grad_down, grad_proj,
        ) = shards
    loss = small[24, 0] / (queries * n_wide * n_rep)
    fraction = small[24, 1] / (DL * small[24, 2])
    return (
        doc["emb"],
        query["emb"],
        doc_grad,
        query_grad,
        grad_query,
        grad_key,
        grad_value,
        grad_out,
        grad_gate,
        grad_up,
        grad_down,
        grad_proj,
        small[0:6].reshape(width),
        small[8:14].reshape(width),
        small[16:22].reshape(width),
        jnp.transpose(small[32 : 32 + heads, 0:buckets]),
        loss,
        fraction,
    )


def solution(mesh):
    rows = P(("rep", "wide"), None)
    return jax.shard_map(
        body,
        mesh=mesh,
        in_specs=(rows,) * 6 + (P(("rep", "wide")),) + (P(),) * 12,
        out_specs=(rows,) * 4 + (P("wide", None),) * 8 + (P(),) * 6,
        check_vma=False,
    )
```

```python
import functools

import jax
import jax.numpy as jnp
import numpy as np
from jax import lax
from jax.experimental import pallas as pl
from jax.experimental.pallas import tpu as pltpu
from jax.sharding import PartitionSpec as P

DL = 512
QUERY_LENGTH = 32
EPS = 1e-06
SCALE = 10.0
BF = jnp.bfloat16
F = jnp.float32
TABLE = 512
VMEM_LIMIT = 60 * 1024 * 1024

SAVED = (
    "n1", "q", "k", "v", "p", "li", "ctx", "hid", "n2", "gv", "us", "act", "h2", "n3", "proj", "lr", "emb", "send",
)

SM = pl.BlockSpec(memory_space=pltpu.SMEM)
ANY = pl.BlockSpec(memory_space=pl.ANY)
VM = pl.BlockSpec(memory_space=pltpu.VMEM)


def mm(a, b):
    return jnp.dot(a, b, preferred_element_type=F)


def mm_nt(a, b):
    return lax.dot_general(a, b, (((1,), (1,)), ((), ())), preferred_element_type=F)


def mm_tn(a, b):
    return lax.dot_general(a, b, (((0,), (0,)), ((), ())), preferred_element_type=F)


def bucket_hot(buckets):
    half = buckets // 2
    exact = half // 2
    column = np.arange(TABLE)
    relative = 128 - np.where(column <= TABLE - 128, column, column - TABLE)
    base = (relative > 0).astype(np.int64) * half
    distance = np.abs(relative)
    large = exact + (
        np.log(np.maximum(distance, 1) / float(exact)) / np.log(128.0 / exact) * (half - exact)
    ).astype(np.int64)
    large = np.minimum(large, half - 1)
    number = base + np.where(distance < exact, distance, large)
    return (np.arange(buckets)[:, None] == number[None, :]).astype(np.float32)


def query_hot(queries):
    tokens = np.arange(queries * QUERY_LENGTH)
    return (np.arange(queries)[:, None] == tokens[None, :] // QUERY_LENGTH).astype(np.float32)


def cost(flops, moved):
    large = flops > 1e8
    return pl.CostEstimate(flops=int(1e12 if large else 1), bytes_accessed=1, transcendentals=0)


class Place:
    def __init__(self, fast):
        self.fast = fast
        self.rep = lax.axis_index("rep")
        self.wide = lax.axis_index("wide")
        self.y, self.x = self.rep >> 1, self.rep & 1
        self.z = self.wide >> 1
        self.own = self.wide & 1 if fast else 0

    def doc(self, slot):
        return self.wide ^ (2 * (slot % 4)) ^ (slot // 4) if self.fast else slot

    def source(self, slot):
        return self.wide ^ slot if self.fast else slot


def row_of(gain):
    return gain[...].astype(F).reshape(1, gain.shape[0])


def stack_kernel(n_parts, *refs):
    out = refs[-1]
    row = 0
    for part in refs[:n_parts]:
        out[row : row + part.shape[0], :] = part[...]
        row += part.shape[0]


def stack_rows(parts, after):
    rows = sum(part.shape[0] for part in parts)
    return pl.pallas_call(
        functools.partial(stack_kernel, len(parts)),
        out_shape=sds((rows, 128), BF),
        in_specs=[VM] * len(parts) + [ANY] * len(after),
        out_specs=VM,
        cost_estimate=cost(1, 1),
        name="stack_rows",
    )(*parts, *after)


def sds(shape, dtype):
    return jax.ShapeDtypeStruct(shape, dtype)


def rows_loop(count, block, fn):
    def step(i, carry):
        fn(pl.ds(pl.multiple_of(i * block, block), block))
        return carry

    lax.fori_loop(0, count // block, step, 0)


def half_masks():
    lane = lax.broadcasted_iota(jnp.int32, (1, 128), 1)
    low = (lane < 64).astype(F)
    high = 1.0 - low
    one_low = (lane == 0).astype(F)
    one_high = (lane == 64).astype(F)
    return low, high, one_low, one_high


def rms(values):
    return lax.rsqrt(jnp.mean(values * values, axis=-1, keepdims=True) + EPS)


def rms_back(values, gain, d_result):
    inverse = rms(values)
    scaled = values * inverse
    grad_gain = jnp.sum(d_result * scaled, axis=0, keepdims=True)
    gained = d_result * gain
    d_values = inverse * (gained - scaled * jnp.mean(gained * scaled, axis=-1, keepdims=True))
    return d_values, grad_gain


def gelu_parts(gate):
    square = gate * gate
    tangent = jnp.tanh(gate * (0.7978845608028654 + (0.7978845608028654 * 0.044715) * square))
    half_plus = 0.5 + 0.5 * tangent
    value = gate * half_plus
    slope = half_plus + 0.5 * gate * (1.0 - tangent * tangent) * (
        0.7978845608028654 + (3.0 * 0.7978845608028654 * 0.044715) * square
    )
    return value, slope


def fwd_kernel(
    seq,
    heads,
    n_after,
    columns,
    tok, ga, gf, gl, rel, hot, wq_h, wk_h, wv_h, wo_h, wg_h, wu_h, wd_h, wp_h,
    *refs,
):
    (
    n1_h, q_h, k_h, v_h, p_h, li_h, ctx_h, hid_h, n2_h, gv_h, us_h, act_h, h2_h, n3_h, proj_h, lr_h, emb, send,
    wq, wk, wv, wo, wg, wu, wd, wp,
    n1, q, k, v, p, li, ctx, hid, n2, gv, us, act, h2, n3, proj, lr,
    tbl, bs, sem_in, sem_out,
    ) = refs[n_after + columns :]
    count = tok.shape[0]
    loads = [
        pltpu.make_async_copy(src, dst, sem_in.at[i])
        for i, (src, dst) in enumerate(
            zip((wq_h, wk_h, wv_h, wo_h, wg_h, wu_h, wd_h, wp_h), (wq, wk, wv, wo, wg, wu, wd, wp))
        )
    ]
    for copy in loads:
        copy.start()
    outs = {}

    def push(i, src, dst):
        outs[i] = pltpu.make_async_copy(src, dst, sem_out.at[i])
        outs[i].start()

    gain_a, gain_f, gain_l = row_of(ga), row_of(gf), row_of(gl)

    def norm_one(rows):
        x = tok[rows, :].astype(F)
        n1[rows, :] = (x * rms(x) * gain_a).astype(BF)

    rows_loop(count, 128, norm_one)
    push(0, n1, n1_h)
    lines = mm(rel[...], hot[...])
    for h in range(heads):
        tbl[h] = lines[h : h + 1, :]
    for i, (w, r, r_h) in enumerate(((wq, q, q_h), (wk, k, k_h), (wv, v, v_h))):
        loads[i].wait()
        r[...] = mm(n1[...], w[...]).astype(BF)
        push(1 + i, r, r_h)

    low, high, one_low, one_high = half_masks()
    is_low = low > 0.5

    blocks = count // 128

    def table(head, carry):
        row = jnp.broadcast_to(tbl[head], (128, TABLE))
        base = pltpu.roll(row, 0, 1, stride=1, stride_axis=0)
        if seq == DL:
            bs[head] = base[:, 0:384]
        else:
            rows = lax.broadcasted_iota(jnp.int32, (128, 128), 0) // seq
            columns = lax.broadcasted_iota(jnp.int32, (128, 128), 1) // seq
            bs[head] = jnp.where(rows == columns, base[:, 128:256], -1e30)
        return carry

    lax.fori_loop(0, heads, table, 0)

    def halves(index):
        lanes = pl.ds(pl.multiple_of(index * 128, 128), 128)
        q2 = q[:, lanes]
        k2 = k[:, lanes]
        v2 = v[:, lanes]
        parts = []
        for keep, one in ((low, one_high), (high, one_low)):
            parts.append((k2 * keep.astype(BF), v2 * keep.astype(BF) + one.astype(BF)))
        return lanes, q2, parts

    def join(lanes, o0, o1):
        inv = 1.0 / jnp.where(is_low, o0[:, 64:65], o1[:, 0:1])
        li[:, lanes] = inv
        ctx[:, lanes] = (jnp.where(is_low, o0, o1) * inv).astype(BF)

    def doc_scores(index):
        _, q2, parts = halves(index)
        for e in range(2):
            for half in range(2):
                yield mm_nt(parts[e][0], q2[256 * half : 256 * half + 256])

    def doc_softmax(head, score, i):
        cols = slice(128 * i, 128 * i + 128)
        terms = []
        for j in range(blocks):
            term = score[128 * j : 128 * j + 128, 128 * (i % 2) : 128 * (i % 2) + 128]
            if abs(j - i) <= 1:
                t = 1 - (j - i)
                terms.append(term + bs[head, :, 128 * t : 128 * t + 128])
            else:
                terms.append(term + (tbl[head, :, 0:1] if j > i else tbl[head, :, 256:257]))
        peak = functools.reduce(jnp.maximum, terms)
        peak = jnp.max(peak, axis=0, keepdims=True)
        total = jnp.zeros((128, 128), F)
        probs = []
        for j in range(blocks):
            power = jnp.exp(terms[j] - peak)
            total = total + power
            probs.append(power.astype(BF))
            p[head, 128 * j : 128 * j + 128, cols] = probs[-1]
        lr[head, :, cols] = 1.0 / jnp.sum(total, axis=0, keepdims=True)
        return jnp.concatenate(probs, axis=0)

    def doc_pairs(first, number):
        scores = list(doc_scores(first))
        for index in range(number):
            lanes, _, parts = halves(first + index)
            coming = doc_scores(first + index + 1) if index + 1 < number else iter(())
            following = []
            sides = []
            for e in range(2):
                head = 2 * (first + index) + e
                done = []
                for half in range(2):
                    following += [c for c in [next(coming, None)] if c is not None]
                    probs = [doc_softmax(head, scores[2 * e + half], 2 * half + i) for i in range(2)]
                    done.append(mm_tn(jnp.concatenate(probs, axis=1), parts[e][1]))
                sides.append(jnp.concatenate(done, axis=0))
            join(lanes, *sides)
            scores = following

    def query_group(group, carry):
        pairs = [halves(group * 3 + i) for i in range(3)]
        cells = [(i, e, b) for i in range(3) for e in range(2) for b in range(blocks)]
        rows = [slice(128 * b, 128 * b + 128) for b in range(blocks)]
        scores = [mm_nt(pairs[i][2][e][0][rows[b]], pairs[i][1][rows[b]]) for i, e, b in cells]
        probs = []
        for score, (i, e, b) in zip(scores, cells):
            head = (group * 3 + i) * 2 + e
            term = score + bs[head]
            power = jnp.exp(term - jnp.max(term, axis=0, keepdims=True))
            probs.append(power.astype(BF))
            p[head, rows[b], :] = probs[-1]
            lr[head, :, rows[b]] = 1.0 / jnp.sum(power, axis=0, keepdims=True)
        outs_g = [mm_tn(pb, pairs[i][2][e][1][rows[b]]) for pb, (i, e, b) in zip(probs, cells)]
        for i in range(3):
            sides = [
                jnp.concatenate([outs_g[cells.index((i, e, b))] for b in range(blocks)], axis=0)
                for e in range(2)
            ]
            join(pairs[i][0], *sides)
        return carry

    if seq == DL:
        def doc_group(group, carry):
            doc_pairs(group * 3, 3)
            return carry

        lax.fori_loop(0, heads // 2 // 3, doc_group, 0)
    else:
        lax.fori_loop(0, heads // 6, query_group, 0)
    push(4, p, p_h)
    push(5, li, li_h)
    push(15, lr, lr_h)
    push(6, ctx, ctx_h)

    loads[3].wait()

    def middle(rows):
        h = tok[rows, :].astype(F) + mm(ctx[rows, :], wo[...])
        hid[rows, :] = h
        h2[rows, :] = h
        n2[rows, :] = (h * rms(h) * gain_f).astype(BF)

    rows_loop(count, 256, middle)
    push(7, hid, hid_h)
    push(8, n2, n2_h)
    loads[4].wait()
    loads[5].wait()
    loads[6].wait()

    def ffn(t, carry):
        cols = pl.ds(pl.multiple_of(t * 512, 512), 512)
        for b in range(count // 256):
            rows = slice(256 * b, 256 * b + 256)
            gate = mm(n2[rows, :], wg[:, cols])
            up = mm(n2[rows, :], wu[:, cols])
            value, slope = gelu_parts(gate)
            a = (value * up).astype(BF)
            gv[rows, cols] = value.astype(BF)
            us[rows, cols] = (up * slope).astype(BF)
            act[rows, cols] = a
            h2[rows, :] += mm(a, wd[cols, :])
        return carry

    lax.fori_loop(0, wg.shape[1] // 512, ffn, 0)
    push(9, gv, gv_h)
    push(10, us, us_h)
    push(11, act, act_h)
    loads[7].wait()

    def top(rows):
        h = h2[rows, :]
        n = (h * rms(h) * gain_l).astype(BF)
        n3[rows, :] = n
        pr = mm(n, wp[...])
        proj[rows, :] = pr
        emb[rows, :] = (pr * lax.rsqrt(jnp.sum(pr * pr, axis=-1, keepdims=True) + EPS)).astype(BF)

    rows_loop(count, 256, top)
    if columns:
        send[0:count, :] = emb[...]
        mask = refs[0][...].astype(F).astype(BF)
        for b in range(DL // 128):
            first = count + 64 * b
            send[first : first + 64, :] = mask[:, 128 * b : 128 * b + 128]
    else:
        send[...] = jnp.zeros_like(send)
    push(12, h2, h2_h)
    push(13, n3, n3_h)
    push(14, proj, proj_h)
    for copy in outs.values():
        copy.wait()


def layer_forward(tokens, weights, gains, rel, hot, seq, columns=(), after=()):
    count, width = tokens.shape
    wq, wk, wv, wo, wg, wu, wd, wp = weights
    hidden = wg.shape[1]
    emb = wp.shape[1]
    heads = rel.shape[0]
    keys = DL if seq == DL else 128
    saved = (
        sds((count, width), BF),
        sds((count, width), BF),
        sds((count, width), BF),
        sds((count, width), BF),
        sds((heads, count, keys), BF),
        sds((count, width), F),
        sds((count, width), BF),
        sds((count, width), F),
        sds((count, width), BF),
        sds((count, hidden), BF),
        sds((count, hidden), BF),
        sds((count, hidden), BF),
        sds((count, width), F),
        sds((count, width), BF),
        sds((count, emb), F),
        sds((heads, 1, count), F),
    )
    outs = pl.pallas_call(
        functools.partial(fwd_kernel, seq, heads, len(after), len(columns)),
        out_shape=saved
        + (sds((count, emb), BF), sds((count + 64 * DL // 128 if columns else 16, emb), BF)),
        in_specs=[VM] * 6 + [ANY] * 8 + [VM] * len(columns) + [ANY] * len(after),
        out_specs=[ANY] * 16 + [VM] * 2,
        scratch_shapes=[pltpu.VMEM(w.shape, BF) for w in weights]
        + [pltpu.VMEM(s.shape, s.dtype) for s in saved]
        + [
            pltpu.VMEM((heads, 1, TABLE), F),
            pltpu.VMEM((heads, 128, 384 if seq == DL else 128), F),
            pltpu.SemaphoreType.DMA((8,)),
            pltpu.SemaphoreType.DMA((16,)),
        ],
        compiler_params=pltpu.CompilerParams(vmem_limit_bytes=VMEM_LIMIT),
        cost_estimate=cost(count * 14e6, 40e6),
        name="layer_forward_%d" % seq,
    )(tokens, *gains, rel, hot, *weights, *columns, *after)
    return dict(zip(SAVED, outs))


def each_block(arrays, block, fn):
    first = 0
    for array in arrays:
        number = array.shape[0] // block
        if number == 1:
            fn(first, array[...])
        else:

            def step(i, carry, array=array, first=first):
                fn(first + i, array[pl.ds(pl.multiple_of(i * block, block), block), :])
                return carry

            lax.fori_loop(0, number, step, 0)
        first += number


def query_sims_kernel(fast, n_docs, n_ins, ids, used, qemb, cot, *refs):
    ins = refs[:n_ins]
    coef, d_emb, parts, es, total, counts = refs[n_ins:]
    place = Place(fast)
    tokens = qemb.shape[0]
    queries = tokens // QUERY_LENGTH
    lane = lax.broadcasted_iota(jnp.int32, (tokens, 128), 1)
    lane_q = lax.broadcasted_iota(jnp.int32, (queries, 128), 1)
    total[...] = jnp.zeros_like(total)
    counts[...] = jnp.zeros_like(counts)

    if fast:
        row = lax.broadcasted_iota(jnp.int32, (queries, 64), 0)
        pick = row + queries * place.wide == lax.broadcasted_iota(jnp.int32, (queries, 64), 1)
        pick = jnp.where(pick, 1.0, 0.0).astype(BF)
        per = DL + 64 * DL // 128

        def rows_at(slot, first, last):
            if slot < 5:
                return ins[slot][first:last, :]
            base = per * (slot - 5)
            return ins[5][base + first : base + last, :]

        def doc_at(slot):
            return rows_at(slot, 0, DL)

        def mask_at(slot):
            packed = rows_at(slot, DL, per)
            return jnp.concatenate([mm(pick, packed[64 * b : 64 * b + 64]) for b in range(4)], axis=1)

        def each(fn):
            for slot in range(n_docs):
                fn(slot)

    else:
        docs, mask = ins

        def doc_at(slot):
            return docs[pl.ds(pl.multiple_of(slot * DL, DL), DL), :]

        def mask_at(slot):
            return mask[slot]

        def each(fn):
            def step(i, carry):
                fn(i)
                return carry

            lax.fori_loop(0, n_docs, step, 0)

    def forward(slot):
        d = place.doc(slot)
        m = mask_at(slot)
        wide = jnp.broadcast_to(m[:, None, :], (queries, QUERY_LENGTH, DL)).reshape(tokens, DL)
        e = jnp.exp(mm_nt(qemb[...], doc_at(slot)) * SCALE) * wide
        es[slot] = e
        total[...] = jnp.where(lane == d, jnp.sum(e, axis=1, keepdims=True), total[...])
        counts[...] = jnp.where(lane_q == d, jnp.sum(m, axis=1, keepdims=True), counts[...])

    each(forward)
    inside = lane_q < n_docs
    z = jnp.sum(jnp.log(1.0 + total[...]).reshape(queries, QUERY_LENGTH, 128), axis=1)
    z = z * (1.0 / QUERY_LENGTH)
    hot = jnp.zeros((queries, 128), F)
    row_q = lax.broadcasted_iota(jnp.int32, (queries, 128), 0)
    for q in range(queries):
        for s in range(ids.shape[0]):
            number = jnp.where(s < used[q], ids[s, q], 128)
            hot = jnp.where((row_q == q) & (lane_q == number), 1.0, hot)
    peak = jnp.max(jnp.where(inside, z, -1e30), axis=1, keepdims=True)
    power = jnp.where(inside, jnp.exp(jnp.where(inside, z - peak, 0.0)), 0.0)
    whole = jnp.sum(power, axis=1, keepdims=True)
    positive = jnp.sum(hot * power, axis=1, keepdims=True)
    loss = jnp.sum(jnp.log(whole) - jnp.log(positive))
    hits = jnp.sum(hot * counts[...])
    found = jnp.sum(hot)
    lane_p = lax.broadcasted_iota(jnp.int32, (8, 128), 1)
    parts[...] = jnp.where(
        lane_p == 0, loss, jnp.where(lane_p == 1, hits, jnp.where(lane_p == 2, found, 0.0))
    )
    d_z = power / whole - hot * power / positive
    d_wide = jnp.broadcast_to(d_z[:, None, :], (queries, QUERY_LENGTH, 128)).reshape(tokens, 128)
    c = d_wide * (SCALE / QUERY_LENGTH) / (1.0 + total[...])
    by_doc = jnp.transpose(c)[0:n_docs, :]
    if fast:
        split = jnp.concatenate([by_doc[:, 0:128], by_doc[:, 128:256]], axis=0)
        high_part = split.astype(BF)
        coef[0:tokens, :] = qemb[...]
        coef[tokens : tokens + 16, :] = high_part
        coef[tokens + 16 : tokens + 32, :] = (split - high_part.astype(F)).astype(BF)
    else:
        coef[...] = by_doc
    d_emb[...] = cot[...].astype(F)

    def backward(slot):
        column = jnp.sum(jnp.where(lane == place.doc(slot), c, 0.0), axis=1, keepdims=True)
        d_emb[...] += mm((es[slot] * column).astype(BF), doc_at(slot))

    each(backward)


def query_sims(fast, ids, used, qemb, cot, ins, n_docs):
    tokens, emb = qemb.shape
    queries = tokens // QUERY_LENGTH
    return pl.pallas_call(
        functools.partial(query_sims_kernel, fast, n_docs, len(ins)),
        out_shape=(
            sds((tokens + 32, emb), BF) if fast else sds((n_docs, tokens), F),
            sds((tokens, emb), F),
            sds((8, 128), F),
        ),
        in_specs=[SM] * 2 + [VM] * (2 + len(ins)),
        out_specs=[VM] * 3,
        scratch_shapes=[
            pltpu.VMEM((n_docs, tokens, DL), F),
            pltpu.VMEM((tokens, 128), F),
            pltpu.VMEM((queries, 128), F),
        ],
        compiler_params=pltpu.CompilerParams(vmem_limit_bytes=VMEM_LIMIT),
        cost_estimate=cost(n_docs * 67e6 * 10, n_docs * 1e6),
        name="query_sims",
    )(ids, used, qemb, cot, *ins)


def top_rows(d_emb, proj, h2, gain, wp):
    inv = lax.rsqrt(jnp.sum(proj * proj, axis=-1, keepdims=True) + EPS)
    along = jnp.sum(proj * d_emb, axis=-1, keepdims=True)
    d_proj = (inv * d_emb - proj * (inv * inv * inv) * along).astype(BF)
    d_h2, grad_gain = rms_back(h2, gain, mm_nt(d_proj, wp))
    return d_proj, d_h2, grad_gain


def query_back_kernel(
    d_emb, proj, gf, gl,
    h2_h, hid_h, gv_h, us_h, wp_h, wd_h, wg_h, wu_h, after,
    d_proj, d_ffn, d_gate_h, d_up_h, d_hid, g_gains,
    h2, hid, gv, us, wp, wd, wg, wu, d_gate, d_up, d_h2, d_n2, sem_in, sem_out,
):
    count = d_emb.shape[0]
    loads = [
        pltpu.make_async_copy(src, dst, sem_in.at[i])
        for i, (src, dst) in enumerate(
            zip((h2_h, wp_h, wd_h, us_h, gv_h, wg_h, wu_h, hid_h), (h2, wp, wd, us, gv, wg, wu, hid))
        )
    ]
    for copy in loads:
        copy.start()
    gain_f, gain_l = row_of(gf), row_of(gl)
    loads[0].wait()
    loads[1].wait()
    dp, dh, gg = top_rows(d_emb[...], proj[...], h2[...], gain_l, wp[...])
    d_proj[...] = dp
    d_h2[...] = dh
    g_gains[...] = jnp.zeros_like(g_gains)
    g_gains[1:2, :] = gg
    d_ffn[...] = dh.astype(BF)
    d_n2[...] = jnp.zeros_like(d_n2)
    for i in range(2, 7):
        loads[i].wait()

    def ffn(t, carry):
        cols = pl.ds(pl.multiple_of(t * 512, 512), 512)
        d_act = mm_nt(d_ffn[...], wd[cols, :])
        dg = (d_act * us[:, cols].astype(F)).astype(BF)
        du = (d_act * gv[:, cols].astype(F)).astype(BF)
        d_gate[:, cols] = dg
        d_up[:, cols] = du
        d_n2[...] += mm_nt(dg, wg[:, cols]) + mm_nt(du, wu[:, cols])
        return carry

    lax.fori_loop(0, wg.shape[1] // 512, ffn, 0)
    out_gate = pltpu.make_async_copy(d_gate, d_gate_h, sem_out.at[0])
    out_up = pltpu.make_async_copy(d_up, d_up_h, sem_out.at[1])
    out_gate.start()
    out_up.start()
    loads[7].wait()
    dm, gg = rms_back(hid[...], gain_f, d_n2[...])
    d_hid[...] = d_h2[...] + dm
    g_gains[0:1, :] = gg
    out_gate.wait()
    out_up.wait()


def query_back(d_emb, saved, weights, gains, after):
    wq, wk, wv, wo, wg, wu, wd, wp = weights
    count, emb = d_emb.shape
    width, hidden = wg.shape
    return pl.pallas_call(
        query_back_kernel,
        out_shape=(
            sds((count, emb), BF),
            sds((count, width), BF),
            sds((count, hidden), BF),
            sds((count, hidden), BF),
            sds((count, width), F),
            sds((8, width), F),
        ),
        in_specs=[VM] * 4 + [ANY] * 9,
        out_specs=[VM, VM, ANY, ANY, VM, VM],
        scratch_shapes=[
            pltpu.VMEM((count, width), F),
            pltpu.VMEM((count, width), F),
            pltpu.VMEM((count, hidden), BF),
            pltpu.VMEM((count, hidden), BF),
            pltpu.VMEM(wp.shape, BF),
            pltpu.VMEM(wd.shape, BF),
            pltpu.VMEM(wg.shape, BF),
            pltpu.VMEM(wu.shape, BF),
            pltpu.VMEM((count, hidden), BF),
            pltpu.VMEM((count, hidden), BF),
            pltpu.VMEM((count, width), F),
            pltpu.VMEM((count, width), F),
            pltpu.SemaphoreType.DMA((8,)),
            pltpu.SemaphoreType.DMA((2,)),
        ],
        compiler_params=pltpu.CompilerParams(vmem_limit_bytes=VMEM_LIMIT),
        cost_estimate=cost(4e9, 30e6),
        name="query_back",
    )(d_emb, saved["proj"], gains[1], gains[2], saved["h2"], saved["hid"], saved["gv"], saved["us"], wp, wd, wg, wu, after)


def split_out(own, grads, keep_h, send_h, sem):
    first = pltpu.make_async_copy(grads.at[own], keep_h, sem.at[0])
    second = pltpu.make_async_copy(grads.at[1 - own], send_h, sem.at[1])
    first.start()
    second.start()
    return first, second


def doc_back_kernel(
    fast, n_arrays, d_emb_in, demb, mask, rep, coef, proj, gl, wp, d_proj_q, d_ffn_q, n2_d, n2_q,
    h2_h, n3_h, n3_qh, act_h, act_qh, wd_h, us_h, gv_h, gate_qh, up_qh,
    *refs,
):
    every = refs[:n_arrays]
    (
    d_h2, g_gain, gate_h, up_h, keep_h, send_h,
    h2, n3, act, wd, us, gv, gate, up, n2t, d_proj, d_all, acc, grads, sem_in, sem_out,
    ) = refs[n_arrays:]
    place = Place(fast)
    count = demb.shape[0]
    loads = [
        pltpu.make_async_copy(src, dst, sem_in.at[i])
        for i, (src, dst) in enumerate(
            (
                (h2_h, h2),
                (n3_h, n3.at[0:count]),
                (n3_qh, n3.at[count:]),
                (act_h, act.at[0:count]),
                (act_qh, act.at[count:]),
                (wd_h, wd),
                (us_h, us),
                (gv_h, gv),
                (gate_qh, gate.at[count:]),
                (up_qh, up.at[count:]),
            )
        )
    ]
    for copy in loads:
        copy.start()
    acc[...] = d_emb_in[...].astype(F)
    per = 64 * QUERY_LENGTH // 256

    def sims(slot, qb, line):
        row = place.source(slot)
        e = jnp.exp(mm_nt(demb[...], qb) * SCALE)
        first = pl.multiple_of((row // per) * 64, 64)
        here = mask[pl.ds(first, 64), :].astype(F).astype(BF)
        m = mm_tn(here, rep[:, pl.ds(pl.multiple_of((row % per) * 256, 256), 256)])
        acc[...] += mm((e * m * line).astype(BF), qb)

    if fast:
        row = lax.broadcasted_iota(jnp.int32, (8, 32), 0)
        column = lax.broadcasted_iota(jnp.int32, (8, 32), 1)
        pick = jnp.where((row < 2) & ((column & 15) == 8 * row + place.wide), 1.0, 0.0).astype(BF)
        for slot in range(n_arrays):
            halves = mm(pick, every[slot][256:288, :])
            line = jnp.concatenate([halves[0:1, :], halves[1:2, :]], axis=1)
            sims(slot, every[slot][0:256, :], line)
    else:

        def step(slot, carry):
            rows = pl.ds(pl.multiple_of(slot * 256, 256), 256)
            sims(slot, every[0][rows, :], coef[pl.ds(slot, 1), :])
            return carry

        lax.fori_loop(0, coef.shape[0], step, 0)
    loads[0].wait()
    dp, dh, gg = top_rows(acc[...], proj[...], h2[...], row_of(gl), wp[...])
    d_proj[0:count, :] = dp
    d_proj[count:, :] = d_proj_q[...]
    d_h2[...] = dh
    g_gain[...] = jnp.zeros_like(g_gain)
    g_gain[0:1, :] = gg
    d_all[0:count, :] = dh.astype(BF)
    d_all[count:, :] = d_ffn_q[...]
    n2t[:, 0:count] = jnp.transpose(n2_d[...])
    n2t[:, count:] = jnp.transpose(n2_q[...])
    for copy in loads[1:]:
        copy.wait()
    gp = mm_tn(n3[...], d_proj[...])
    grads[:, :, :, :, 192:224, :] = jnp.zeros((2, 4, 2, 2, 32, 256), BF)
    for w in range(8):
        for r in range(3):
            lo = 96 * w + 32 * r
            grads[w % 2, w // 2, r // 2, r % 2, 192:224, 0:128] = gp[lo : lo + 32, :].astype(BF)

    def tile(t, carry):
        cols = pl.ds(pl.multiple_of(t * 512, 512), 512)
        for half in range(2):
            w = 2 * t + half
            g = mm_tn(act[:, pl.ds(pl.multiple_of(w * 256, 256), 256)], d_all[...])
            for r in range(4):
                for c in range(3):
                    grads[half, t, r // 2, r % 2, 64 * c : 64 * c + 64, :] = g[
                        64 * r : 64 * r + 64, 256 * c : 256 * c + 256
                    ].astype(BF)
        d_act = mm_nt(d_all[0:count, :], wd[cols, :])
        gate[0:count, cols] = (d_act * us[:, cols].astype(F)).astype(BF)
        up[0:count, cols] = (d_act * gv[:, cols].astype(F)).astype(BF)
        for base, source in ((0, gate), (1, up)):
            g = mm(n2t[...], source[:, cols]).astype(BF)
            for c in range(2):
                start = pl.multiple_of(224 + (t % 2) * 192 + 96 * c, 32)
                for w in range(8):
                    grads[w % 2, w // 2, base, t // 2, pl.ds(start, 96), :] = g[
                        96 * w : 96 * w + 96, 256 * c : 256 * c + 256
                    ]
        return carry

    lax.fori_loop(0, 4, tile, 0)
    copies = [
        pltpu.make_async_copy(gate.at[0:count], gate_h, sem_out.at[2]),
        pltpu.make_async_copy(up.at[0:count], up_h, sem_out.at[3]),
    ]
    out = split_out(place.own, grads, keep_h, send_h, sem_out)
    for copy in copies:
        copy.start()
    for copy in tuple(out) + tuple(copies):
        copy.wait()


def doc_back(fast, d_emb, demb, every, mask, rep, coef, dsaved, qsaved, gains, wp, wd, from_query):
    count, width = dsaved["h2"].shape
    d_proj_q, d_ffn_q, gate_q, up_q = from_query
    rows = count + d_ffn_q.shape[0]
    hidden = wd.shape[0]
    emb = wp.shape[1]
    piece = sds((4, 2, 2, 608, 256), BF)
    return pl.pallas_call(
        functools.partial(doc_back_kernel, fast, len(every)),
        out_shape=(
            sds((count, width), F),
            sds((8, width), F),
            sds((count, hidden), BF),
            sds((count, hidden), BF),
            piece,
            piece,
        ),
        in_specs=[VM] * 12 + [ANY] * 10 + [VM] * len(every),
        out_specs=[VM] * 2 + [ANY] * 4,
        scratch_shapes=[
            pltpu.VMEM((count, width), F),
            pltpu.VMEM((rows, width), BF),
            pltpu.VMEM((rows, hidden), BF),
            pltpu.VMEM(wd.shape, BF),
            pltpu.VMEM((count, hidden), BF),
            pltpu.VMEM((count, hidden), BF),
            pltpu.VMEM((rows, hidden), BF),
            pltpu.VMEM((rows, hidden), BF),
            pltpu.VMEM((width, rows), BF),
            pltpu.VMEM((rows, emb), BF),
            pltpu.VMEM((rows, width), BF),
            pltpu.VMEM((count, emb), F),
            pltpu.VMEM((2, 4, 2, 2, 608, 256), BF),
            pltpu.SemaphoreType.DMA((10,)),
            pltpu.SemaphoreType.DMA((4,)),
        ],
        compiler_params=pltpu.CompilerParams(vmem_limit_bytes=VMEM_LIMIT),
        cost_estimate=cost(14e9, 10e6),
        name="doc_back",
    )(
        d_emb, demb, mask, rep, coef, dsaved["proj"], gains[2], wp, d_proj_q, d_ffn_q,
        dsaved["n2"], qsaved["n2"], dsaved["h2"], dsaved["n3"], qsaved["n3"], dsaved["act"], qsaved["act"],
        wd, dsaved["us"], dsaved["gv"], gate_q, up_q, *every,
    )


def middle_back_kernel(
    d_h2, hid, d_hid_q, gf,
    wg_h, wu_h, wo_h, gate_h, up_h, li_d, li_q, *refs
):
    d_hid, g_gain, d_attn, g, wg, wu, wo, gate, up, li, sem_in = refs[-11:]
    count = d_h2.shape[0]
    rest = d_hid_q.shape[0]
    loads = [
        pltpu.make_async_copy(src, dst, sem_in.at[i])
        for i, (src, dst) in enumerate(
            (
                (wg_h, wg),
                (gate_h, gate),
                (wu_h, wu),
                (up_h, up),
                (wo_h, wo),
                (li_d, li.at[0:count]),
                (li_q, li.at[count:]),
            )
        )
    ]
    for copy in loads:
        copy.start()
    for copy in loads[0:4]:
        copy.wait()
    gain_f = row_of(gf)
    g_gain[...] = jnp.zeros_like(g_gain)

    def through(rows):
        d_n2 = mm_nt(gate[rows, :], wg[...]) + mm_nt(up[rows, :], wu[...])
        dm, gg = rms_back(hid[rows, :], gain_f, d_n2)
        total = d_h2[rows, :] + dm
        d_hid[rows, :] = total
        g_gain[0:1, :] += gg
        d_attn[rows, :] = total.astype(BF)

    rows_loop(count, 256, through)
    d_attn[count:, :] = d_hid_q[...].astype(BF)
    for copy in loads[4:]:
        copy.wait()

    def to_context(rows):
        d_context = mm_nt(d_attn[rows, :], wo[...]).astype(BF).astype(F)
        g[rows, :] = (d_context * li[rows, :]).astype(BF)

    rows_loop(count + rest, 256, to_context)


def middle_back(d_h2, d_hid_q, gate, up, dsaved, qsaved, weights, gains, after):
    wq, wk, wv, wo, wg, wu, wd, wp = weights
    count, width = d_h2.shape
    rows = count + d_hid_q.shape[0]
    hidden = wg.shape[1]
    return pl.pallas_call(
        middle_back_kernel,
        out_shape=(sds((count, width), F), sds((8, width), F), sds((rows, width), BF), sds((rows, width), BF)),
        in_specs=[VM] * 4 + [ANY] * (7 + len(after)),
        out_specs=[VM] * 4,
        scratch_shapes=[
            pltpu.VMEM(wg.shape, BF),
            pltpu.VMEM(wu.shape, BF),
            pltpu.VMEM(wo.shape, BF),
            pltpu.VMEM((count, hidden), BF),
            pltpu.VMEM((count, hidden), BF),
            pltpu.VMEM((rows, width), F),
            pltpu.SemaphoreType.DMA((7,)),
        ],
        compiler_params=pltpu.CompilerParams(vmem_limit_bytes=VMEM_LIMIT),
        cost_estimate=cost(5e9, 20e6),
        name="middle_back",
    )(d_h2, dsaved["hid"], d_hid_q, gains[1], wg, wu, wo, gate, up, dsaved["li"], qsaved["li"], *after)


def attn_back_kernel(
    hot, g,
    q_d, q_q, k_d, k_q, v_d, v_q, lr_d, lr_q, p_dh, p_qh, *refs
):
    dq, dk, dv, g_rel, q, k, v, p_d, p_q, lrd, lrq, ds, acc, sums, sem_in = refs[-15:]
    heads = p_d.shape[0]
    count = q_d.shape[0]
    rest = q_q.shape[0]
    blocks = count // 128
    cells_q = rest // 128
    loads = [
        pltpu.make_async_copy(src, dst, sem_in.at[i])
        for i, (src, dst) in enumerate(
            (
                (v_q, v.at[count:]),
                (p_qh, p_q),
                (lr_q, lrq),
                (q_q, q.at[count:]),
                (k_q, k.at[count:]),
                (v_d, v.at[0:count]),
                (p_dh, p_d),
                (lr_d, lrd),
                (q_d, q.at[0:count]),
                (k_d, k.at[0:count]),
            )
        )
    ]
    for copy in loads:
        copy.start()
    low, high, _, _ = half_masks()
    keeps = (low.astype(BF), high.astype(BF))
    for copy in loads[0:5]:
        copy.wait()
    acc[...] = jnp.zeros_like(acc)

    rows_q = [slice(count + 128 * b, count + 128 * b + 128) for b in range(cells_q)]
    cells = [(pair, e, b) for pair in range(heads // 2) for e in range(2) for b in range(cells_q)]
    lanes_of = [slice(128 * pair, 128 * pair + 128) for pair in range(heads // 2)]
    d_ps = [
        mm_nt(v[rows_q[b], lanes_of[pair]] * keeps[e], g[rows_q[b], lanes_of[pair]])
        for pair, e, b in cells
    ]
    dss = []
    for d_p, (pair, e, b) in zip(d_ps, cells):
        head = 2 * pair + e
        pf = p_q[head, 128 * b : 128 * b + 128, :].astype(F)
        t = pf * d_p
        share = lrq[head, :, 128 * b : 128 * b + 128] * jnp.sum(t, axis=0, keepdims=True)
        d_s = t - pf * share
        acc[head, :, 128:256] += d_s
        dss.append(d_s.astype(BF))
    for pair in range(heads // 2):
        lanes = lanes_of[pair]
        for b in range(cells_q):
            rows = rows_q[b]
            at_cell = [cells.index((pair, e, b)) for e in range(2)]
            probs = [p_q[2 * pair + e, 128 * b : 128 * b + 128, :] for e in range(2)]
            parts = [
                (
                    mm_tn(dss[at_cell[e]], k[rows, lanes] * keeps[e]),
                    mm(dss[at_cell[e]], q[rows, lanes] * keeps[e]),
                    mm(probs[e], g[rows, lanes] * keeps[e]),
                )
                for e in range(2)
            ]
            dq[rows, lanes] = (parts[0][0] + parts[1][0]).astype(BF)
            dk[rows, lanes] = (parts[0][1] + parts[1][1]).astype(BF)
            dv[rows, lanes] = (parts[0][2] + parts[1][2]).astype(BF)
    for copy in loads[5:]:
        copy.wait()

    def doc_pair(pair, carry):
        lanes = pl.ds(pl.multiple_of(pair * 128, 128), 128)
        q2 = q[0:count, lanes]
        k2 = k[0:count, lanes]
        v2 = v[0:count, lanes]
        g2 = g[0:count, lanes]
        d_ps = [mm_nt(v2 * keep, g2) for keep in keeps]
        sides = []
        for e, keep in enumerate(keeps):
            head = 2 * pair + e
            for i in range(blocks):
                cols = slice(128 * i, 128 * i + 128)
                pfs = [p_d[head, 128 * j : 128 * j + 128, cols].astype(F) for j in range(blocks)]
                ts = [pfs[j] * d_ps[e][128 * j : 128 * j + 128, cols] for j in range(blocks)]
                total = functools.reduce(jnp.add, ts)
                share = lrd[head, :, cols] * jnp.sum(total, axis=0, keepdims=True)
                for j in range(blocks):
                    d_s = ts[j] - pfs[j] * share
                    t = 1 - (j - i)
                    tile = t if abs(j - i) <= 1 else (3 if j > i else 4)
                    acc[head, :, 128 * tile : 128 * tile + 128] += d_s
                    ds[e, 128 * j : 128 * j + 128, cols] = d_s.astype(BF)
            sides.append(
                (
                    mm_tn(ds[e], k2 * keep),
                    mm(ds[e], q2 * keep),
                    mm(p_d[head], g2 * keep),
                )
            )
        dq[0:count, lanes] = (sides[0][0] + sides[1][0]).astype(BF)
        dk[0:count, lanes] = (sides[0][1] + sides[1][1]).astype(BF)
        dv[0:count, lanes] = (sides[0][2] + sides[1][2]).astype(BF)
        return carry

    lax.fori_loop(0, heads // 2, doc_pair, 0)
    sums[...] = jnp.zeros_like(sums)
    lane = lax.broadcasted_iota(jnp.int32, (1, TABLE), 1)
    for head in range(heads):
        folded = jnp.concatenate([acc[head, :, 0:384], jnp.zeros((128, 128), F)], axis=1)
        half = 64
        while half >= 8:
            folded = folded[0:half] + pltpu.roll(folded[half : 2 * half], TABLE - half, 1)
            half //= 2
        line = folded[0:1]
        for i in range(1, 8):
            line = line + pltpu.roll(folded[i : i + 1], TABLE - i, 1)
        after = jnp.sum(acc[head, :, 384:512])
        before = jnp.sum(acc[head, :, 512:640])
        line = line + jnp.where(lane == 0, after, jnp.where(lane == 256, before, 0.0))
        sums[head : head + 1, :] = line
    g_rel[...] = lax.dot_general(
        sums[...], hot[...], (((1,), (1,)), ((), ())),
        preferred_element_type=F, precision=lax.Precision.HIGHEST,
    )


def attn_back(g, dsaved, qsaved, hot, after):
    rows, width = g.shape
    heads = dsaved["p"].shape[0]
    buckets = hot.shape[0]
    count = dsaved["q"].shape[0]
    rest = rows - count
    both = []
    for name in ("q", "k", "v", "lr", "p"):
        both += [dsaved[name], qsaved[name]]
    return pl.pallas_call(
        attn_back_kernel,
        out_shape=(sds((rows, width), BF),) * 3 + (sds((16, buckets), F),),
        in_specs=[VM] * 2 + [ANY] * (10 + len(after)),
        out_specs=[VM] * 4,
        scratch_shapes=[pltpu.VMEM((rows, width), BF)] * 3
        + [
            pltpu.VMEM((heads, DL, DL), BF),
            pltpu.VMEM((heads, rest, 128), BF),
            pltpu.VMEM((heads, 1, count), F),
            pltpu.VMEM((heads, 1, rest), F),
            pltpu.VMEM((2, DL, DL), BF),
            pltpu.VMEM((heads, 128, 640), F),
            pltpu.VMEM((16, TABLE), F),
            pltpu.SemaphoreType.DMA((10,)),
        ],
        compiler_params=pltpu.CompilerParams(vmem_limit_bytes=VMEM_LIMIT),
        cost_estimate=cost(15e9, 40e6),
        name="attn_back",
    )(hot, g, *both, *after)


def attn_grads_kernel(fast, dq, dk, dv, d_attn, n1_d, n1_q, ctx_d, ctx_q, *refs):
    keep_h, send_h, n1, ctx, grads, sem_in, sem_out = refs[-7:]
    place = Place(fast)
    count = n1_d.shape[0]
    loads = [
        pltpu.make_async_copy(src, dst, sem_in.at[i])
        for i, (src, dst) in enumerate(
            (
                (n1_d, n1.at[0:count]),
                (n1_q, n1.at[count:]),
                (ctx_d, ctx.at[0:count]),
                (ctx_q, ctx.at[count:]),
            )
        )
    ]
    for copy in loads:
        copy.start()
    for copy in loads:
        copy.wait()

    for which, (left, right) in enumerate(((n1, dq), (n1, dk), (n1, dv), (ctx, d_attn))):
        value = mm_tn(left[...], right[...]).astype(BF)
        for w in range(8):
            for c in range(3):
                grads[w % 2, w // 2, which // 2, which % 2, 96 * c : 96 * c + 96, :] = value[
                    96 * w : 96 * w + 96, 256 * c : 256 * c + 256
                ]
    for copy in split_out(place.own, grads, keep_h, send_h, sem_out):
        copy.wait()


def attn_grads(fast, dq, dk, dv, d_attn, dsaved, qsaved, after):
    rows, width = d_attn.shape
    piece = sds((4, 2, 2, 288, 256), BF)
    return pl.pallas_call(
        functools.partial(attn_grads_kernel, fast),
        out_shape=(piece, piece),
        in_specs=[VM] * 4 + [ANY] * (4 + len(after)),
        out_specs=[ANY] * 2,
        scratch_shapes=[
            pltpu.VMEM((rows, width), BF),
            pltpu.VMEM((rows, width), BF),
            pltpu.VMEM((2, 4, 2, 2, 288, 256), BF),
            pltpu.SemaphoreType.DMA((4,)),
            pltpu.SemaphoreType.DMA((2,)),
        ],
        compiler_params=pltpu.CompilerParams(vmem_limit_bytes=VMEM_LIMIT),
        cost_estimate=cost(4e9, 10e6),
        name="attn_grads",
    )(dq, dk, dv, d_attn, dsaved["n1"], qsaved["n1"], dsaved["ctx"], qsaved["ctx"], *after)


def input_back_kernel(
    tok_d, tok_q, d_hid_d, d_hid_q, ga, gain_f, gain_l, gains_q, parts,
    rel, dq, dk, dv, wq, wk, wv, *refs
):
    out_d, out_q, small, g_gain = refs[-4:]
    count = tok_d.shape[0]
    gain_a = row_of(ga)
    g_gain[...] = jnp.zeros_like(g_gain)

    def part(offset, tok, d_hid, out):
        def step(rows):
            at_rows = pl.ds(pl.multiple_of(rows.start + offset, 256), 256)
            d_n1 = mm_nt(dq[at_rows, :], wq[...])
            d_n1 = d_n1 + mm_nt(dk[at_rows, :], wk[...])
            d_n1 = d_n1 + mm_nt(dv[at_rows, :], wv[...])
            d_in, gg = rms_back(tok[rows, :].astype(F), gain_a, d_n1)
            g_gain[0:1, :] += gg
            out[rows, :] = (d_hid[rows, :] + d_in).astype(BF)

        rows_loop(tok.shape[0], 256, step)

    part(0, tok_d, d_hid_d, out_d)
    part(count, tok_q, d_hid_q, out_q)
    small[...] = jnp.zeros_like(small)
    rows = (
        g_gain[0:1, :],
        gain_f[0:1, :] + gains_q[0:1, :],
        gain_l[0:1, :] + gains_q[1:2, :],
    )
    for i, row in enumerate(rows):
        for c in range(6):
            small[8 * i + c : 8 * i + c + 1, :] = row[:, 128 * c : 128 * c + 128]
    small[24:25, :] = parts[0:1, :]
    small[32:48, 0 : rel.shape[1]] = rel[...]


def input_back(tok_d, tok_q, d_hid_d, d_hid_q, gains, extra, from_attn, weights, after):
    width = tok_d.shape[1]
    return pl.pallas_call(
        input_back_kernel,
        out_shape=(sds(tok_d.shape, BF), sds(tok_q.shape, BF), sds((48, 128), F)),
        in_specs=[VM] * 16 + [ANY] * len(after),
        out_specs=[VM] * 3,
        scratch_shapes=[pltpu.VMEM((8, width), F)],
        compiler_params=pltpu.CompilerParams(vmem_limit_bytes=VMEM_LIMIT),
        cost_estimate=cost(3e9, 10e6),
        name="input_back",
    )(tok_d, tok_q, d_hid_d, d_hid_q, gains[0], *extra, *from_attn, weights[0], weights[1], weights[2], *after)


def unpack_kernel(which, own, one, two, three, *refs):
    stack = refs[-1]
    outs = refs[-5:-1]
    place = Place(True)
    half = own.shape[1]
    for m, part in enumerate((own, one, two, three)):
        for i in range(2):
            stack[place.rep ^ m, half * i : half * i + half, :] = part[i]
    if which == "attn":
        for r in range(4):
            for c in range(3):
                outs[r][:, 256 * c : 256 * c + 256] = stack[
                    r, 96 * c : 96 * c + 96, :
                ].astype(F)
        return
    for r in range(4):
        for c in range(4):
            first = (r % 2) * 1024 + 256 * c
            outs[r // 2][:, first : first + 256] = stack[
                r, 224 + 96 * c : 224 + 96 * c + 96, :
            ].astype(F)
        for c in range(3):
            outs[2][64 * r : 64 * r + 64, 256 * c : 256 * c + 256] = stack[
                r, 64 * c : 64 * c + 64, :
            ].astype(F)
    for r in range(3):
        outs[3][32 * r : 32 * r + 32, :] = stack[r, 192:224, 0:128].astype(F)


def unpack(which, parts, shapes, after):
    return pl.pallas_call(
        functools.partial(unpack_kernel, which),
        out_shape=tuple(sds(s, F) for s in shapes),
        in_specs=[VM] * 4 + [ANY] * len(after),
        out_specs=tuple(VM for _ in shapes),
        scratch_shapes=[pltpu.VMEM((4, 2 * parts[0].shape[1], parts[0].shape[2]), BF)],
        compiler_params=pltpu.CompilerParams(vmem_limit_bytes=VMEM_LIMIT),
        cost_estimate=cost(1e6, 3e6),
        name="unpack_" + which,
    )(*parts, *after)


def swap(values, axis, size, mask):
    return lax.ppermute(values, axis, [(i, i ^ mask) for i in range(size)])


def near_kernel(keep, came, *refs):
    send_a, send_b, own_a, own_b = refs[-4:]
    place = Place(True)
    y, x = place.y, place.x
    half = own_a.shape[2]

    def total(i, k, first):
        return keep[0, i, k, first : first + half, :] + came[0, i, k, first : first + half, :]

    for i in range(2):
        send_a[0, i] = total(i, 1 - x, 0)
        own_a[0, i] = total(i, x, 0)
        send_b[0, i] = total(1 - y, i, half)
        own_b[0, i] = total(y, i, half)


def cross_kernel(a, came_a, b, came_b, *refs):
    send_a, send_b, own_a, own_b = refs[-4:]
    place = Place(True)
    y, x = place.y, place.x
    for i in range(4):
        send_a[i] = a[i, 1 - y] + came_a[i, 1 - y]
        own_a[i] = a[i, y] + came_a[i, y]
        send_b[i] = b[i, 1 - x] + came_b[i, 1 - x]
        own_b[i] = b[i, x] + came_b[i, x]


def line_kernel(a, came_a, b, came_b, *refs):
    z = Place(True).z
    for m, out in enumerate(refs[-4:]):
        out[0] = a[z ^ m] + came_a[z ^ m]
        out[1] = b[z ^ m] + came_b[z ^ m]


def far_kernel(own, one, two, three, *refs):
    total = own[...].astype(F) + one[...].astype(F) + two[...].astype(F) + three[...].astype(F)
    refs[-1][...] = total.astype(BF)


def sum_two_kernel(a, b, *refs):
    refs[-1][...] = a[...] + b[...]


def sum_two(a, b, after):
    return pl.pallas_call(
        sum_two_kernel,
        out_shape=sds(a.shape, F),
        in_specs=[VM] * 2 + [ANY] * len(after),
        out_specs=VM,
        cost_estimate=cost(1e4, 1e5),
        name="sum_two",
    )(a, b, *after)


def fixed_sum(index, parts, stack):
    for m, part in enumerate(parts):
        stack[index ^ m] = part[...]
    return stack[0] + stack[1] + stack[2] + stack[3]


def sum_four_kernel(own, one, two, three, *refs):
    out, stack = refs[-2:]
    out[...] = fixed_sum(Place(True).rep, (own, one, two, three), stack)


def sum_four(own, came, after):
    return pl.pallas_call(
        sum_four_kernel,
        out_shape=sds(own.shape, F),
        in_specs=[VM] * 4 + [ANY] * len(after),
        out_specs=VM,
        scratch_shapes=[pltpu.VMEM((4,) + own.shape, F)],
        cost_estimate=cost(1e4, 1e5),
        name="sum_four",
    )(own, *came, *after)


def finish_kernel(heads, total_queries, own, one, two, three, *refs):
    gain_a, gain_f, gain_l, rel, loss, fraction, stack = refs[-7:]
    total = fixed_sum(Place(True).z, (own, one, two, three), stack)
    for i, out in enumerate((gain_a, gain_f, gain_l)):
        row = jnp.concatenate([total[8 * i + c : 8 * i + c + 1, :] for c in range(6)], axis=1)
        out[...] = row.reshape(out.shape[0])
    rel[...] = total[32 : 32 + heads, 0 : rel.shape[1]]
    lane = lax.broadcasted_iota(jnp.int32, (1, 128), 1)
    line = total[24:25, :]
    loss_sum, hits, found = (jnp.sum(jnp.where(lane == i, line, 0.0)) for i in range(3))
    loss[0, 0] = loss_sum / total_queries
    fraction[0, 0] = hits / (DL * found)


def finish(own, came, heads, buckets, width, total_queries, after):
    return pl.pallas_call(
        functools.partial(finish_kernel, heads, float(total_queries)),
        out_shape=(sds((width,), F),) * 3 + (sds((heads, buckets), F), sds((1, 1), F), sds((1, 1), F)),
        in_specs=[VM] * 4 + [ANY] * len(after),
        out_specs=[VM] * 4 + [SM] * 2,
        scratch_shapes=[pltpu.VMEM((4,) + own.shape, F)],
        cost_estimate=cost(1e4, 1e5),
        name="finish",
    )(own, *came, *after)


class Reduction:
    def __init__(self, name, keep, send):
        self.name = name
        self.half = keep.shape[3] // 2
        self.keep = keep
        self.came = swap(send, "wide", 8, 1)

    def near(self, after):
        rows = 2 * self.half
        whole = pl.BlockSpec((1, 2, 2, rows, 256), lambda i: (i, 0, 0, 0, 0))
        part = pl.BlockSpec((1, 2, self.half, 256), lambda i: (i, 0, 0, 0))
        send_a, send_b, self.a, self.b = pl.pallas_call(
            near_kernel,
            grid=(4,),
            out_shape=(sds((4, 2, self.half, 256), BF),) * 4,
            in_specs=[whole, whole] + [ANY] * len(after),
            out_specs=(part,) * 4,
            compiler_params=pltpu.CompilerParams(vmem_limit_bytes=VMEM_LIMIT),
            cost_estimate=cost(1, 1),
            name="near_" + self.name,
        )(self.keep, self.came, *after)
        self.came_a = swap(send_a, "rep", 4, 1)
        self.came_b = swap(send_b, "rep", 4, 2)
        return (self.a,)

    def step(self, kernel, name, ins, shape, number, after):
        return pl.pallas_call(
            kernel,
            out_shape=(sds(shape, BF),) * number,
            in_specs=[VM] * 4 + [ANY] * len(after),
            out_specs=(VM,) * number,
            compiler_params=pltpu.CompilerParams(vmem_limit_bytes=VMEM_LIMIT),
            cost_estimate=cost(1, 1),
            name=name + self.name,
        )(*ins, *after)

    def cross(self, after):
        ins = (self.a, self.came_a, self.b, self.came_b)
        shape = (4, self.half, 256)
        send_a, send_b, self.a, self.b = self.step(cross_kernel, "cross_", ins, shape, 4, after)
        self.came_a = swap(send_a, "rep", 4, 2)
        self.came_b = swap(send_b, "rep", 4, 1)
        return (self.a,)

    def line(self, after):
        ins = (self.a, self.came_a, self.b, self.came_b)
        outs = self.step(line_kernel, "line_", ins, (2, self.half, 256), 4, after)
        self.own = outs[0]
        self.came = [swap(outs[m], "wide", 8, 2 * m) for m in (1, 2, 3)]
        return (self.own,)

    def far(self, after):
        ins = (self.own, *self.came)
        (self.own,) = self.step(far_kernel, "far_", ins, (2, self.half, 256), 1, after)
        self.came = [swap(self.own, "rep", 4, m) for m in (1, 2, 3)]
        return (self.own,)

    def parts(self):
        return self.own, *self.came


def natural(which, keep, send):
    both = jnp.stack([keep, send])
    both = both.reshape((2, 4, 4) + both.shape[4:])
    if which == "attn":
        a = both.reshape(2, 4, 4, 3, 96, 256).transpose(2, 1, 0, 4, 3, 5).reshape(4, 768, 768)
        return [a[i] for i in range(4)]
    a = both[:, :, :, 224:].reshape(2, 4, 4, 4, 96, 256).transpose(1, 0, 4, 2, 3, 5)
    a = a.reshape(768, 4096)
    d = both[:, :, :, :192].reshape(2, 4, 4, 3, 64, 256).transpose(1, 0, 2, 4, 3, 5)
    e = both[:, :, :3, 192:224, :128].transpose(1, 0, 2, 3, 4)
    return [a[:, :2048], a[:, 2048:], d.reshape(2048, 768), e.reshape(768, 128)]


def body(
    doc_tokens, query_tokens, doc_cotangent, query_cotangent, retrieved, pos_ids, pos_count,
    w_query, w_key, carried_content_weights, w_out, w_gate, w_up, w_down, w_proj,
    gain_attn, gain_ffn, gain_final, rel_bias,
):
    n_wide = lax.axis_size("wide")
    n_rep = lax.axis_size("rep")
    group = retrieved.shape[1]
    fast = n_wide == 8 and n_rep == 4 and group == 64
    weights = (w_query, w_key, carried_content_weights, w_out, w_gate, w_up, w_down, w_proj)
    width = doc_tokens.shape[1]
    buckets, heads = rel_bias.shape
    hot_np = bucket_hot(buckets)
    hot = jnp.asarray(hot_np, BF)
    hot_f = jnp.asarray(hot_np, F)
    rep_hot = jnp.asarray(query_hot(64), BF)
    rel = jnp.transpose(rel_bias)
    queries = pos_ids.shape[0]
    ids = jnp.transpose(pos_ids)
    columns = jnp.transpose(retrieved)
    gains = (gain_attn, gain_ffn, gain_final)

    doc = layer_forward(doc_tokens, weights, gains, rel, hot, DL, (columns,) if fast else ())
    if fast:
        send = doc["send"]
        near = [send] + [swap(send, "wide", n_wide, 2 * m) for m in (1, 2, 3)]
        near_other = swap(send, "wide", n_wide, 1)
    query = layer_forward(query_tokens, weights, gains, rel, hot, QUERY_LENGTH, (), (doc["emb"],))
    if fast:
        other = swap(stack_rows(near[1:], (query["emb"],)), "wide", n_wide, 1)
        ins = near + [near_other, other]
    else:
        mask_query = lax.all_to_all(columns.astype(F), "wide", 0, 0, tiled=True)
        mask_query = mask_query.reshape(n_wide, queries, DL)
        ins = [lax.all_gather(doc["emb"], "wide", axis=0, tiled=True), mask_query]
    coef, d_query_emb, parts = query_sims(
        fast, ids, pos_count, query["emb"], query_cotangent, ins, n_wide
    )
    if fast:
        every = [coef] + [swap(coef, "wide", n_wide, m) for m in range(1, 8)]
        coef_all = query_cotangent
    else:
        every = [lax.all_gather(query["emb"], "wide", axis=0, tiled=True)]
        coef_all = lax.all_to_all(coef, "wide", 0, 0, tiled=True)
    d_proj_q, d_ffn_q, d_gate_q, d_up_q, d_hid_q, gains_q = query_back(
        d_query_emb, query, weights, gains, coef
    )
    d_h2, gain_l, d_gate, d_up, keep_f, send_f = doc_back(
        fast, doc_cotangent, doc["emb"], every, columns, rep_hot, coef_all, doc, query, gains,
        w_proj, w_down, (d_proj_q, d_ffn_q, d_gate_q, d_up_q),
    )
    if fast:
        ffn = Reduction("ffn", keep_f, send_f)
    d_hid, gain_f, d_attn, g = middle_back(
        d_h2, d_hid_q, d_gate, d_up, doc, query, weights, gains, ()
    )
    after = ffn.near((d_attn,)) if fast else ()
    dq, dk, dv, rel_grad = attn_back(g, doc, query, hot_f, after)
    after = ffn.cross((rel_grad,)) if fast else ()
    keep_a, send_a = attn_grads(fast, dq, dk, dv, d_attn, doc, query, after)
    if fast:
        attn = Reduction("attn", keep_a, send_a)
    doc_grad, query_grad, small = input_back(
        doc_tokens, query_tokens, d_hid, d_hid_q, gains, (gain_f, gain_l, gains_q, parts),
        (rel_grad, dq, dk, dv), weights, ffn.line((keep_a,)) if fast else (),
    )
    if fast:
        after = attn.near((small,))
        small = sum_two(small, swap(small, "wide", 8, 1), after)
        came = [swap(small, "rep", 4, m) for m in (1, 2, 3)]
        after = attn.cross((small,))
        after = ffn.far(after)
        small = sum_four(small, came, after)
        came = [swap(small, "wide", 8, 2 * m) for m in (1, 2, 3)]
        after = attn.line((small,))
        total_gain_a, total_gain_f, total_gain_l, total_rel, loss, fraction = finish(
            small, came, heads, buckets, width, queries * n_wide * n_rep, after
        )
        after = grad_gate, grad_up, grad_down, grad_proj = unpack(
            "ffn", ffn.parts(), ((96, 2048), (96, 2048), (256, 768), (96, 128)), (total_rel,)
        )
        after = attn.far(after[3:])
        grad_query, grad_key, grad_value, grad_out = unpack(
            "attn", attn.parts(), ((96, 768),) * 4, after
        )
        loss = loss.reshape(())
        fraction = fraction.reshape(())
    else:
        small = lax.psum(small, ("rep", "wide"))

        def total(whole):
            part = lax.psum_scatter(whole, "wide", scatter_dimension=0, tiled=True)
            return lax.psum(part, "rep").astype(F)

        grad_query, grad_key, grad_value, grad_out = (total(a) for a in natural("attn", keep_a, send_a))
        grad_gate, grad_up, grad_down, grad_proj = (total(a) for a in natural("ffn", keep_f, send_f))
        total_gain_a, total_gain_f, total_gain_l = (
            small[8 * i : 8 * i + 6].reshape(width) for i in range(3)
        )
        total_rel = small[32 : 32 + heads, 0:buckets]
        loss = small[24, 0] / (queries * n_wide * n_rep)
        fraction = small[24, 1] / (DL * small[24, 2])
    return (
        doc["emb"],
        query["emb"],
        doc_grad,
        query_grad,
        grad_query,
        grad_key,
        grad_value,
        grad_out,
        grad_gate,
        grad_up,
        grad_down,
        grad_proj,
        total_gain_a,
        total_gain_f,
        total_gain_l,
        jnp.transpose(total_rel),
        loss,
        fraction,
    )


def solution(mesh):
    rows = P(("rep", "wide"), None)
    return jax.shard_map(
        body,
        mesh=mesh,
        in_specs=(rows,) * 6 + (P(("rep", "wide")),) + (P(),) * 12,
        out_specs=(rows,) * 4 + (P("wide", None),) * 8 + (P(),) * 6,
        check_vma=False,
    )
```

```python
import functools

import jax
import jax.numpy as jnp
import numpy as np
from jax import lax
from jax.experimental import pallas as pl
from jax.experimental.pallas import tpu as pltpu
from jax.sharding import PartitionSpec as P

DL = 512
QUERY_LENGTH = 32
EPS = 1e-06
SCALE = 10.0
BF = jnp.bfloat16
F = jnp.float32
TABLE = 512
VMEM_LIMIT = 60 * 1024 * 1024

SAVED = (
    "n1", "q", "k", "v", "p", "li", "ctx", "hid", "n2", "gv", "us", "act", "h2", "n3", "proj", "lr", "emb", "send",
)

SM = pl.BlockSpec(memory_space=pltpu.SMEM)
ANY = pl.BlockSpec(memory_space=pl.ANY)
VM = pl.BlockSpec(memory_space=pltpu.VMEM)


def mm(a, b):
    return jnp.dot(a, b, preferred_element_type=F)


def mm_nt(a, b):
    return lax.dot_general(a, b, (((1,), (1,)), ((), ())), preferred_element_type=F)


def mm_tn(a, b):
    return lax.dot_general(a, b, (((0,), (0,)), ((), ())), preferred_element_type=F)


def bucket_hot(buckets):
    half = buckets // 2
    exact = half // 2
    column = np.arange(TABLE)
    relative = 128 - np.where(column <= TABLE - 128, column, column - TABLE)
    base = (relative > 0).astype(np.int64) * half
    distance = np.abs(relative)
    large = exact + (
        np.log(np.maximum(distance, 1) / float(exact)) / np.log(128.0 / exact) * (half - exact)
    ).astype(np.int64)
    large = np.minimum(large, half - 1)
    number = base + np.where(distance < exact, distance, large)
    return (np.arange(buckets)[:, None] == number[None, :]).astype(np.float32)


def query_hot(queries):
    tokens = np.arange(queries * QUERY_LENGTH)
    return (np.arange(queries)[:, None] == tokens[None, :] // QUERY_LENGTH).astype(np.float32)


def cost(flops, moved):
    large = flops > 1e8
    return pl.CostEstimate(flops=int(1e12 if large else 1), bytes_accessed=1, transcendentals=0)


class Place:
    def __init__(self, fast):
        self.fast = fast
        self.rep = lax.axis_index("rep")
        self.wide = lax.axis_index("wide")
        self.y, self.x = self.rep >> 1, self.rep & 1
        self.z = self.wide >> 1
        self.own = self.wide & 1 if fast else 0

    def doc(self, slot):
        return self.wide ^ (2 * (slot % 4)) ^ (slot // 4) if self.fast else slot

    def source(self, slot):
        return self.wide ^ slot if self.fast else slot


def row_of(gain):
    return gain[...].astype(F).reshape(1, gain.shape[0])


def stack_kernel(n_parts, *refs):
    out = refs[-1]
    row = 0
    for part in refs[:n_parts]:
        out[row : row + part.shape[0], :] = part[...]
        row += part.shape[0]


def stack_rows(parts, after):
    rows = sum(part.shape[0] for part in parts)
    return pl.pallas_call(
        functools.partial(stack_kernel, len(parts)),
        out_shape=sds((rows, 128), BF),
        in_specs=[VM] * len(parts) + [ANY] * len(after),
        out_specs=VM,
        cost_estimate=cost(1, 1),
        name="stack_rows",
    )(*parts, *after)


def sds(shape, dtype):
    return jax.ShapeDtypeStruct(shape, dtype)


def rows_loop(count, block, fn):
    def step(i, carry):
        fn(pl.ds(pl.multiple_of(i * block, block), block))
        return carry

    lax.fori_loop(0, count // block, step, 0)


def half_masks():
    lane = lax.broadcasted_iota(jnp.int32, (1, 128), 1)
    low = (lane < 64).astype(F)
    high = 1.0 - low
    one_low = (lane == 0).astype(F)
    one_high = (lane == 64).astype(F)
    return low, high, one_low, one_high


def rms(values):
    return lax.rsqrt(jnp.mean(values * values, axis=-1, keepdims=True) + EPS)


def rms_back(values, gain, d_result):
    inverse = rms(values)
    scaled = values * inverse
    grad_gain = jnp.sum(d_result * scaled, axis=0, keepdims=True)
    gained = d_result * gain
    d_values = inverse * (gained - scaled * jnp.mean(gained * scaled, axis=-1, keepdims=True))
    return d_values, grad_gain


def gelu_parts(gate):
    square = gate * gate
    tangent = jnp.tanh(gate * (0.7978845608028654 + (0.7978845608028654 * 0.044715) * square))
    half_plus = 0.5 + 0.5 * tangent
    value = gate * half_plus
    slope = half_plus + 0.5 * gate * (1.0 - tangent * tangent) * (
        0.7978845608028654 + (3.0 * 0.7978845608028654 * 0.044715) * square
    )
    return value, slope


def fwd_kernel(
    seq,
    heads,
    n_after,
    columns,
    tok, ga, gf, gl, rel, hot, wq_h, wk_h, wv_h, wo_h, wg_h, wu_h, wd_h, wp_h,
    *refs,
):
    (
    n1_h, q_h, k_h, v_h, p_h, li_h, ctx_h, hid_h, n2_h, gv_h, us_h, act_h, h2_h, n3_h, proj_h, lr_h, emb, send,
    wq, wk, wv, wo, wg, wu, wd, wp,
    n1, q, k, v, p, li, ctx, hid, n2, gv, us, act, h2, n3, proj, lr,
    tbl, bs, sem_in, sem_out,
    ) = refs[n_after + columns :]
    count = tok.shape[0]
    loads = [
        pltpu.make_async_copy(src, dst, sem_in.at[i])
        for i, (src, dst) in enumerate(
            zip((wq_h, wk_h, wv_h, wo_h, wg_h, wu_h, wd_h, wp_h), (wq, wk, wv, wo, wg, wu, wd, wp))
        )
    ]
    for copy in loads:
        copy.start()
    outs = {}

    def push(i, src, dst):
        outs[i] = pltpu.make_async_copy(src, dst, sem_out.at[i])
        outs[i].start()

    gain_a, gain_f, gain_l = row_of(ga), row_of(gf), row_of(gl)

    def norm_one(rows):
        x = tok[rows, :].astype(F)
        n1[rows, :] = (x * rms(x) * gain_a).astype(BF)

    rows_loop(count, 128, norm_one)
    push(0, n1, n1_h)
    lines = mm(rel[...], hot[...])
    for h in range(heads):
        tbl[h] = lines[h : h + 1, :]
    for i, (w, r, r_h) in enumerate(((wq, q, q_h), (wk, k, k_h), (wv, v, v_h))):
        loads[i].wait()
        r[...] = mm(n1[...], w[...]).astype(BF)
        push(1 + i, r, r_h)

    low, high, one_low, one_high = half_masks()
    is_low = low > 0.5

    blocks = count // 128

    def table(head, carry):
        row = jnp.broadcast_to(tbl[head], (128, TABLE))
        base = pltpu.roll(row, 0, 1, stride=1, stride_axis=0)
        if seq == DL:
            bs[head] = base[:, 0:384]
        else:
            rows = lax.broadcasted_iota(jnp.int32, (128, 128), 0) // seq
            columns = lax.broadcasted_iota(jnp.int32, (128, 128), 1) // seq
            bs[head] = jnp.where(rows == columns, base[:, 128:256], -1e30)
        return carry

    lax.fori_loop(0, heads, table, 0)

    def halves(index):
        lanes = pl.ds(pl.multiple_of(index * 128, 128), 128)
        q2 = q[:, lanes]
        k2 = k[:, lanes]
        v2 = v[:, lanes]
        parts = []
        for keep, one in ((low, one_high), (high, one_low)):
            parts.append((k2 * keep.astype(BF), v2 * keep.astype(BF) + one.astype(BF)))
        return lanes, q2, parts

    def join(lanes, o0, o1):
        inv = 1.0 / jnp.where(is_low, o0[:, 64:65], o1[:, 0:1])
        li[:, lanes] = inv
        ctx[:, lanes] = (jnp.where(is_low, o0, o1) * inv).astype(BF)

    def doc_scores(index):
        _, q2, parts = halves(index)
        for e in range(2):
            for half in range(2):
                yield mm_nt(parts[e][0], q2[256 * half : 256 * half + 256])

    def doc_softmax(head, score, i):
        cols = slice(128 * i, 128 * i + 128)
        terms = []
        for j in range(blocks):
            term = score[128 * j : 128 * j + 128, 128 * (i % 2) : 128 * (i % 2) + 128]
            if abs(j - i) <= 1:
                t = 1 - (j - i)
                terms.append(term + bs[head, :, 128 * t : 128 * t + 128])
            else:
                terms.append(term + (tbl[head, :, 0:1] if j > i else tbl[head, :, 256:257]))
        peak = functools.reduce(jnp.maximum, terms)
        peak = jnp.max(peak, axis=0, keepdims=True)
        total = jnp.zeros((128, 128), F)
        probs = []
        for j in range(blocks):
            power = jnp.exp(terms[j] - peak)
            total = total + power
            probs.append(power.astype(BF))
            p[head, 128 * j : 128 * j + 128, cols] = probs[-1]
        lr[head, :, cols] = 1.0 / jnp.sum(total, axis=0, keepdims=True)
        return jnp.concatenate(probs, axis=0)

    def doc_pairs(first, number):
        scores = list(doc_scores(first))
        for index in range(number):
            lanes, _, parts = halves(first + index)
            coming = doc_scores(first + index + 1) if index + 1 < number else iter(())
            following = []
            sides = []
            for e in range(2):
                head = 2 * (first + index) + e
                done = []
                for half in range(2):
                    following += [c for c in [next(coming, None)] if c is not None]
                    probs = [doc_softmax(head, scores[2 * e + half], 2 * half + i) for i in range(2)]
                    done.append(mm_tn(jnp.concatenate(probs, axis=1), parts[e][1]))
                sides.append(jnp.concatenate(done, axis=0))
            join(lanes, *sides)
            scores = following

    def query_group(group, carry):
        pairs = [halves(group * 3 + i) for i in range(3)]
        cells = [(i, e, b) for i in range(3) for e in range(2) for b in range(blocks)]
        rows = [slice(128 * b, 128 * b + 128) for b in range(blocks)]
        scores = [mm_nt(pairs[i][2][e][0][rows[b]], pairs[i][1][rows[b]]) for i, e, b in cells]
        probs = []
        for score, (i, e, b) in zip(scores, cells):
            head = (group * 3 + i) * 2 + e
            term = score + bs[head]
            power = jnp.exp(term - jnp.max(term, axis=0, keepdims=True))
            probs.append(power.astype(BF))
            p[head, rows[b], :] = probs[-1]
            lr[head, :, rows[b]] = 1.0 / jnp.sum(power, axis=0, keepdims=True)
        outs_g = [mm_tn(pb, pairs[i][2][e][1][rows[b]]) for pb, (i, e, b) in zip(probs, cells)]
        for i in range(3):
            sides = [
                jnp.concatenate([outs_g[cells.index((i, e, b))] for b in range(blocks)], axis=0)
                for e in range(2)
            ]
            join(pairs[i][0], *sides)
        return carry

    if seq == DL:
        def doc_group(group, carry):
            doc_pairs(group * 3, 3)
            return carry

        lax.fori_loop(0, heads // 2 // 3, doc_group, 0)
    else:
        lax.fori_loop(0, heads // 6, query_group, 0)
    push(4, p, p_h)
    push(5, li, li_h)
    push(15, lr, lr_h)
    push(6, ctx, ctx_h)

    loads[3].wait()

    def middle(rows):
        h = tok[rows, :].astype(F) + mm(ctx[rows, :], wo[...])
        hid[rows, :] = h
        h2[rows, :] = h
        n2[rows, :] = (h * rms(h) * gain_f).astype(BF)

    rows_loop(count, 256, middle)
    push(7, hid, hid_h)
    push(8, n2, n2_h)
    loads[4].wait()
    loads[5].wait()
    loads[6].wait()

    def ffn(t, carry):
        cols = pl.ds(pl.multiple_of(t * 512, 512), 512)
        for b in range(count // 256):
            rows = slice(256 * b, 256 * b + 256)
            gate = mm(n2[rows, :], wg[:, cols])
            up = mm(n2[rows, :], wu[:, cols])
            value, slope = gelu_parts(gate)
            a = (value * up).astype(BF)
            gv[rows, cols] = value.astype(BF)
            us[rows, cols] = (up * slope).astype(BF)
            act[rows, cols] = a
            h2[rows, :] += mm(a, wd[cols, :])
        return carry

    lax.fori_loop(0, wg.shape[1] // 512, ffn, 0)
    push(9, gv, gv_h)
    push(10, us, us_h)
    push(11, act, act_h)
    loads[7].wait()

    def top(rows):
        h = h2[rows, :]
        n = (h * rms(h) * gain_l).astype(BF)
        n3[rows, :] = n
        pr = mm(n, wp[...])
        proj[rows, :] = pr
        emb[rows, :] = (pr * lax.rsqrt(jnp.sum(pr * pr, axis=-1, keepdims=True) + EPS)).astype(BF)

    rows_loop(count, 256, top)
    if columns:
        send[0:count, :] = emb[...]
        mask = refs[0][...].astype(F).astype(BF)
        for b in range(DL // 128):
            first = count + 64 * b
            send[first : first + 64, :] = mask[:, 128 * b : 128 * b + 128]
    else:
        send[...] = jnp.zeros_like(send)
    push(12, h2, h2_h)
    push(13, n3, n3_h)
    push(14, proj, proj_h)
    for copy in outs.values():
        copy.wait()


def layer_forward(tokens, weights, gains, rel, hot, seq, columns=(), after=()):
    count, width = tokens.shape
    wq, wk, wv, wo, wg, wu, wd, wp = weights
    hidden = wg.shape[1]
    emb = wp.shape[1]
    heads = rel.shape[0]
    keys = DL if seq == DL else 128
    saved = (
        sds((count, width), BF),
        sds((count, width), BF),
        sds((count, width), BF),
        sds((count, width), BF),
        sds((heads, count, keys), BF),
        sds((count, width), F),
        sds((count, width), BF),
        sds((count, width), F),
        sds((count, width), BF),
        sds((count, hidden), BF),
        sds((count, hidden), BF),
        sds((count, hidden), BF),
        sds((count, width), F),
        sds((count, width), BF),
        sds((count, emb), F),
        sds((heads, 1, count), F),
    )
    outs = pl.pallas_call(
        functools.partial(fwd_kernel, seq, heads, len(after), len(columns)),
        out_shape=saved
        + (sds((count, emb), BF), sds((count + 64 * DL // 128 if columns else 16, emb), BF)),
        in_specs=[VM] * 6 + [ANY] * 8 + [VM] * len(columns) + [ANY] * len(after),
        out_specs=[ANY] * 16 + [VM] * 2,
        scratch_shapes=[pltpu.VMEM(w.shape, BF) for w in weights]
        + [pltpu.VMEM(s.shape, s.dtype) for s in saved]
        + [
            pltpu.VMEM((heads, 1, TABLE), F),
            pltpu.VMEM((heads, 128, 384 if seq == DL else 128), F),
            pltpu.SemaphoreType.DMA((8,)),
            pltpu.SemaphoreType.DMA((16,)),
        ],
        compiler_params=pltpu.CompilerParams(vmem_limit_bytes=VMEM_LIMIT),
        cost_estimate=cost(count * 14e6, 40e6),
        name="layer_forward_%d" % seq,
    )(tokens, *gains, rel, hot, *weights, *columns, *after)
    return dict(zip(SAVED, outs))


def each_block(arrays, block, fn):
    first = 0
    for array in arrays:
        number = array.shape[0] // block
        if number == 1:
            fn(first, array[...])
        else:

            def step(i, carry, array=array, first=first):
                fn(first + i, array[pl.ds(pl.multiple_of(i * block, block), block), :])
                return carry

            lax.fori_loop(0, number, step, 0)
        first += number


def query_sims_kernel(fast, n_docs, n_ins, ids, used, qemb, cot, *refs):
    ins = refs[:n_ins]
    coef, d_emb, parts, es, total, counts = refs[n_ins:]
    place = Place(fast)
    tokens = qemb.shape[0]
    queries = tokens // QUERY_LENGTH
    lane = lax.broadcasted_iota(jnp.int32, (tokens, 128), 1)
    lane_q = lax.broadcasted_iota(jnp.int32, (queries, 128), 1)
    total[...] = jnp.zeros_like(total)
    counts[...] = jnp.zeros_like(counts)

    if fast:
        row = lax.broadcasted_iota(jnp.int32, (queries, 64), 0)
        pick = row + queries * place.wide == lax.broadcasted_iota(jnp.int32, (queries, 64), 1)
        pick = jnp.where(pick, 1.0, 0.0).astype(BF)
        per = DL + 64 * DL // 128

        def rows_at(slot, first, last):
            if slot < 5:
                return ins[slot][first:last, :]
            base = per * (slot - 5)
            return ins[5][base + first : base + last, :]

        def doc_at(slot):
            return rows_at(slot, 0, DL)

        def mask_at(slot):
            packed = rows_at(slot, DL, per)
            return jnp.concatenate([mm(pick, packed[64 * b : 64 * b + 64]) for b in range(4)], axis=1)

        def each(fn):
            for slot in range(n_docs):
                fn(slot)

    else:
        docs, mask = ins

        def doc_at(slot):
            return docs[pl.ds(pl.multiple_of(slot * DL, DL), DL), :]

        def mask_at(slot):
            return mask[slot]

        def each(fn):
            def step(i, carry):
                fn(i)
                return carry

            lax.fori_loop(0, n_docs, step, 0)

    def forward(slot):
        d = place.doc(slot)
        m = mask_at(slot)
        wide = jnp.broadcast_to(m[:, None, :], (queries, QUERY_LENGTH, DL)).reshape(tokens, DL)
        e = jnp.exp(mm_nt(qemb[...], doc_at(slot)) * SCALE) * wide
        es[slot] = e
        total[...] = jnp.where(lane == d, jnp.sum(e, axis=1, keepdims=True), total[...])
        counts[...] = jnp.where(lane_q == d, jnp.sum(m, axis=1, keepdims=True), counts[...])

    each(forward)
    inside = lane_q < n_docs
    z = jnp.sum(jnp.log(1.0 + total[...]).reshape(queries, QUERY_LENGTH, 128), axis=1)
    z = z * (1.0 / QUERY_LENGTH)
    hot = jnp.zeros((queries, 128), F)
    row_q = lax.broadcasted_iota(jnp.int32, (queries, 128), 0)
    for q in range(queries):
        for s in range(ids.shape[0]):
            number = jnp.where(s < used[q], ids[s, q], 128)
            hot = jnp.where((row_q == q) & (lane_q == number), 1.0, hot)
    peak = jnp.max(jnp.where(inside, z, -1e30), axis=1, keepdims=True)
    power = jnp.where(inside, jnp.exp(jnp.where(inside, z - peak, 0.0)), 0.0)
    whole = jnp.sum(power, axis=1, keepdims=True)
    positive = jnp.sum(hot * power, axis=1, keepdims=True)
    loss = jnp.sum(jnp.log(whole) - jnp.log(positive))
    hits = jnp.sum(hot * counts[...])
    found = jnp.sum(hot)
    lane_p = lax.broadcasted_iota(jnp.int32, (8, 128), 1)
    parts[...] = jnp.where(
        lane_p == 0, loss, jnp.where(lane_p == 1, hits, jnp.where(lane_p == 2, found, 0.0))
    )
    d_z = power / whole - hot * power / positive
    d_wide = jnp.broadcast_to(d_z[:, None, :], (queries, QUERY_LENGTH, 128)).reshape(tokens, 128)
    c = d_wide * (SCALE / QUERY_LENGTH) / (1.0 + total[...])
    by_doc = jnp.transpose(c)[0:n_docs, :]
    if fast:
        split = jnp.concatenate([by_doc[:, 0:128], by_doc[:, 128:256]], axis=0)
        high_part = split.astype(BF)
        coef[0:tokens, :] = qemb[...]
        coef[tokens : tokens + 16, :] = high_part
        coef[tokens + 16 : tokens + 32, :] = (split - high_part.astype(F)).astype(BF)
    else:
        coef[...] = by_doc
    d_emb[...] = cot[...].astype(F)

    def backward(slot):
        column = jnp.sum(jnp.where(lane == place.doc(slot), c, 0.0), axis=1, keepdims=True)
        d_emb[...] += mm((es[slot] * column).astype(BF), doc_at(slot))

    each(backward)


def query_sims(fast, ids, used, qemb, cot, ins, n_docs):
    tokens, emb = qemb.shape
    queries = tokens // QUERY_LENGTH
    return pl.pallas_call(
        functools.partial(query_sims_kernel, fast, n_docs, len(ins)),
        out_shape=(
            sds((tokens + 32, emb), BF) if fast else sds((n_docs, tokens), F),
            sds((tokens, emb), F),
            sds((8, 128), F),
        ),
        in_specs=[SM] * 2 + [VM] * (2 + len(ins)),
        out_specs=[VM] * 3,
        scratch_shapes=[
            pltpu.VMEM((n_docs, tokens, DL), F),
            pltpu.VMEM((tokens, 128), F),
            pltpu.VMEM((queries, 128), F),
        ],
        compiler_params=pltpu.CompilerParams(vmem_limit_bytes=VMEM_LIMIT),
        cost_estimate=cost(n_docs * 67e6 * 10, n_docs * 1e6),
        name="query_sims",
    )(ids, used, qemb, cot, *ins)


def top_rows(d_emb, proj, h2, gain, wp):
    inv = lax.rsqrt(jnp.sum(proj * proj, axis=-1, keepdims=True) + EPS)
    along = jnp.sum(proj * d_emb, axis=-1, keepdims=True)
    d_proj = (inv * d_emb - proj * (inv * inv * inv) * along).astype(BF)
    d_h2, grad_gain = rms_back(h2, gain, mm_nt(d_proj, wp))
    return d_proj, d_h2, grad_gain


def query_back_kernel(
    d_emb, proj, gf, gl,
    h2_h, hid_h, gv_h, us_h, wp_h, wd_h, wg_h, wu_h, after,
    d_proj, d_ffn, d_gate_h, d_up_h, d_hid, g_gains,
    h2, hid, gv, us, wp, wd, wg, wu, d_gate, d_up, d_h2, d_n2, sem_in, sem_out,
):
    count = d_emb.shape[0]
    loads = [
        pltpu.make_async_copy(src, dst, sem_in.at[i])
        for i, (src, dst) in enumerate(
            zip((h2_h, wp_h, wd_h, us_h, gv_h, wg_h, wu_h, hid_h), (h2, wp, wd, us, gv, wg, wu, hid))
        )
    ]
    for copy in loads:
        copy.start()
    gain_f, gain_l = row_of(gf), row_of(gl)
    loads[0].wait()
    loads[1].wait()
    dp, dh, gg = top_rows(d_emb[...], proj[...], h2[...], gain_l, wp[...])
    d_proj[...] = dp
    d_h2[...] = dh
    g_gains[...] = jnp.zeros_like(g_gains)
    g_gains[1:2, :] = gg
    d_ffn[...] = dh.astype(BF)
    d_n2[...] = jnp.zeros_like(d_n2)
    for i in range(2, 7):
        loads[i].wait()

    def ffn(t, carry):
        cols = pl.ds(pl.multiple_of(t * 512, 512), 512)
        d_act = mm_nt(d_ffn[...], wd[cols, :])
        dg = (d_act * us[:, cols].astype(F)).astype(BF)
        du = (d_act * gv[:, cols].astype(F)).astype(BF)
        d_gate[:, cols] = dg
        d_up[:, cols] = du
        d_n2[...] += mm_nt(dg, wg[:, cols]) + mm_nt(du, wu[:, cols])
        return carry

    lax.fori_loop(0, wg.shape[1] // 512, ffn, 0)
    out_gate = pltpu.make_async_copy(d_gate, d_gate_h, sem_out.at[0])
    out_up = pltpu.make_async_copy(d_up, d_up_h, sem_out.at[1])
    out_gate.start()
    out_up.start()
    loads[7].wait()
    dm, gg = rms_back(hid[...], gain_f, d_n2[...])
    d_hid[...] = d_h2[...] + dm
    g_gains[0:1, :] = gg
    out_gate.wait()
    out_up.wait()


def query_back(d_emb, saved, weights, gains, after):
    wq, wk, wv, wo, wg, wu, wd, wp = weights
    count, emb = d_emb.shape
    width, hidden = wg.shape
    return pl.pallas_call(
        query_back_kernel,
        out_shape=(
            sds((count, emb), BF),
            sds((count, width), BF),
            sds((count, hidden), BF),
            sds((count, hidden), BF),
            sds((count, width), F),
            sds((8, width), F),
        ),
        in_specs=[VM] * 4 + [ANY] * 9,
        out_specs=[VM, VM, ANY, ANY, VM, VM],
        scratch_shapes=[
            pltpu.VMEM((count, width), F),
            pltpu.VMEM((count, width), F),
            pltpu.VMEM((count, hidden), BF),
            pltpu.VMEM((count, hidden), BF),
            pltpu.VMEM(wp.shape, BF),
            pltpu.VMEM(wd.shape, BF),
            pltpu.VMEM(wg.shape, BF),
            pltpu.VMEM(wu.shape, BF),
            pltpu.VMEM((count, hidden), BF),
            pltpu.VMEM((count, hidden), BF),
            pltpu.VMEM((count, width), F),
            pltpu.VMEM((count, width), F),
            pltpu.SemaphoreType.DMA((8,)),
            pltpu.SemaphoreType.DMA((2,)),
        ],
        compiler_params=pltpu.CompilerParams(vmem_limit_bytes=VMEM_LIMIT),
        cost_estimate=cost(4e9, 30e6),
        name="query_back",
    )(d_emb, saved["proj"], gains[1], gains[2], saved["h2"], saved["hid"], saved["gv"], saved["us"], wp, wd, wg, wu, after)


def split_out(own, grads, keep_h, send_h, sem):
    first = pltpu.make_async_copy(grads.at[own], keep_h, sem.at[0])
    second = pltpu.make_async_copy(grads.at[1 - own], send_h, sem.at[1])
    first.start()
    second.start()
    return first, second


def doc_back_kernel(
    fast, n_arrays, d_emb_in, demb, mask, rep, coef, proj, gl, wp, d_proj_q, d_ffn_q, n2_d, n2_q,
    h2_h, n3_h, n3_qh, act_h, act_qh, wd_h, us_h, gv_h, gate_qh, up_qh,
    *refs,
):
    every = refs[:n_arrays]
    (
    d_h2, g_gain, gate_h, up_h, keep_h, send_h,
    h2, n3, act, wd, us, gv, gate, up, n2t, d_proj, d_all, acc, grads, sem_in, sem_out,
    ) = refs[n_arrays:]
    place = Place(fast)
    count = demb.shape[0]
    loads = [
        pltpu.make_async_copy(src, dst, sem_in.at[i])
        for i, (src, dst) in enumerate(
            (
                (h2_h, h2),
                (n3_h, n3.at[0:count]),
                (n3_qh, n3.at[count:]),
                (act_h, act.at[0:count]),
                (act_qh, act.at[count:]),
                (wd_h, wd),
                (us_h, us),
                (gv_h, gv),
                (gate_qh, gate.at[count:]),
                (up_qh, up.at[count:]),
            )
        )
    ]
    for copy in loads:
        copy.start()
    acc[...] = d_emb_in[...].astype(F)
    per = 64 * QUERY_LENGTH // 256

    def sims(slot, qb, line):
        row = place.source(slot)
        e = jnp.exp(mm_nt(demb[...], qb) * SCALE)
        first = pl.multiple_of((row // per) * 64, 64)
        here = mask[pl.ds(first, 64), :].astype(F).astype(BF)
        m = mm_tn(here, rep[:, pl.ds(pl.multiple_of((row % per) * 256, 256), 256)])
        acc[...] += mm((e * m * line).astype(BF), qb)

    if fast:
        row = lax.broadcasted_iota(jnp.int32, (8, 32), 0)
        column = lax.broadcasted_iota(jnp.int32, (8, 32), 1)
        pick = jnp.where((row < 2) & ((column & 15) == 8 * row + place.wide), 1.0, 0.0).astype(BF)
        for slot in range(n_arrays):
            halves = mm(pick, every[slot][256:288, :])
            line = jnp.concatenate([halves[0:1, :], halves[1:2, :]], axis=1)
            sims(slot, every[slot][0:256, :], line)
    else:

        def step(slot, carry):
            rows = pl.ds(pl.multiple_of(slot * 256, 256), 256)
            sims(slot, every[0][rows, :], coef[pl.ds(slot, 1), :])
            return carry

        lax.fori_loop(0, coef.shape[0], step, 0)
    loads[0].wait()
    dp, dh, gg = top_rows(acc[...], proj[...], h2[...], row_of(gl), wp[...])
    d_proj[0:count, :] = dp
    d_proj[count:, :] = d_proj_q[...]
    d_h2[...] = dh
    g_gain[...] = jnp.zeros_like(g_gain)
    g_gain[0:1, :] = gg
    d_all[0:count, :] = dh.astype(BF)
    d_all[count:, :] = d_ffn_q[...]
    n2t[:, 0:count] = jnp.transpose(n2_d[...])
    n2t[:, count:] = jnp.transpose(n2_q[...])
    for copy in loads[1:]:
        copy.wait()
    gp = mm_tn(n3[...], d_proj[...])
    grads[:, :, :, :, 192:224, :] = jnp.zeros((2, 4, 2, 2, 32, 256), BF)
    for w in range(8):
        for r in range(3):
            lo = 96 * w + 32 * r
            grads[w % 2, w // 2, r // 2, r % 2, 192:224, 0:128] = gp[lo : lo + 32, :].astype(BF)

    def tile(t, carry):
        cols = pl.ds(pl.multiple_of(t * 512, 512), 512)
        for half in range(2):
            w = 2 * t + half
            g = mm_tn(act[:, pl.ds(pl.multiple_of(w * 256, 256), 256)], d_all[...])
            for r in range(4):
                for c in range(3):
                    grads[half, t, r // 2, r % 2, 64 * c : 64 * c + 64, :] = g[
                        64 * r : 64 * r + 64, 256 * c : 256 * c + 256
                    ].astype(BF)
        d_act = mm_nt(d_all[0:count, :], wd[cols, :])
        gate[0:count, cols] = (d_act * us[:, cols].astype(F)).astype(BF)
        up[0:count, cols] = (d_act * gv[:, cols].astype(F)).astype(BF)
        for base, source in ((0, gate), (1, up)):
            g = mm(n2t[...], source[:, cols]).astype(BF)
            for c in range(2):
                start = pl.multiple_of(224 + (t % 2) * 192 + 96 * c, 32)
                for w in range(8):
                    grads[w % 2, w // 2, base, t // 2, pl.ds(start, 96), :] = g[
                        96 * w : 96 * w + 96, 256 * c : 256 * c + 256
                    ]
        return carry

    lax.fori_loop(0, 4, tile, 0)
    copies = [
        pltpu.make_async_copy(gate.at[0:count], gate_h, sem_out.at[2]),
        pltpu.make_async_copy(up.at[0:count], up_h, sem_out.at[3]),
    ]
    out = split_out(place.own, grads, keep_h, send_h, sem_out)
    for copy in copies:
        copy.start()
    for copy in tuple(out) + tuple(copies):
        copy.wait()


def doc_back(fast, d_emb, demb, every, mask, rep, coef, dsaved, qsaved, gains, wp, wd, from_query):
    count, width = dsaved["h2"].shape
    d_proj_q, d_ffn_q, gate_q, up_q = from_query
    rows = count + d_ffn_q.shape[0]
    hidden = wd.shape[0]
    emb = wp.shape[1]
    piece = sds((4, 2, 2, 608, 256), BF)
    return pl.pallas_call(
        functools.partial(doc_back_kernel, fast, len(every)),
        out_shape=(
            sds((count, width), F),
            sds((8, width), F),
            sds((count, hidden), BF),
            sds((count, hidden), BF),
            piece,
            piece,
        ),
        in_specs=[VM] * 12 + [ANY] * 10 + [VM] * len(every),
        out_specs=[VM] * 2 + [ANY] * 4,
        scratch_shapes=[
            pltpu.VMEM((count, width), F),
            pltpu.VMEM((rows, width), BF),
            pltpu.VMEM((rows, hidden), BF),
            pltpu.VMEM(wd.shape, BF),
            pltpu.VMEM((count, hidden), BF),
            pltpu.VMEM((count, hidden), BF),
            pltpu.VMEM((rows, hidden), BF),
            pltpu.VMEM((rows, hidden), BF),
            pltpu.VMEM((width, rows), BF),
            pltpu.VMEM((rows, emb), BF),
            pltpu.VMEM((rows, width), BF),
            pltpu.VMEM((count, emb), F),
            pltpu.VMEM((2, 4, 2, 2, 608, 256), BF),
            pltpu.SemaphoreType.DMA((10,)),
            pltpu.SemaphoreType.DMA((4,)),
        ],
        compiler_params=pltpu.CompilerParams(vmem_limit_bytes=VMEM_LIMIT),
        cost_estimate=cost(14e9, 10e6),
        name="doc_back",
    )(
        d_emb, demb, mask, rep, coef, dsaved["proj"], gains[2], wp, d_proj_q, d_ffn_q,
        dsaved["n2"], qsaved["n2"], dsaved["h2"], dsaved["n3"], qsaved["n3"], dsaved["act"], qsaved["act"],
        wd, dsaved["us"], dsaved["gv"], gate_q, up_q, *every,
    )


def middle_back_kernel(
    d_h2, hid, d_hid_q, gf,
    wg_h, wu_h, wo_h, gate_h, up_h, li_d, li_q, *refs
):
    d_hid, g_gain, d_attn, g, wg, wu, wo, gate, up, li, sem_in = refs[-11:]
    count = d_h2.shape[0]
    rest = d_hid_q.shape[0]
    loads = [
        pltpu.make_async_copy(src, dst, sem_in.at[i])
        for i, (src, dst) in enumerate(
            (
                (wg_h, wg),
                (gate_h, gate),
                (wu_h, wu),
                (up_h, up),
                (wo_h, wo),
                (li_d, li.at[0:count]),
                (li_q, li.at[count:]),
            )
        )
    ]
    for copy in loads:
        copy.start()
    for copy in loads[0:4]:
        copy.wait()
    gain_f = row_of(gf)
    g_gain[...] = jnp.zeros_like(g_gain)

    def through(rows):
        d_n2 = mm_nt(gate[rows, :], wg[...]) + mm_nt(up[rows, :], wu[...])
        dm, gg = rms_back(hid[rows, :], gain_f, d_n2)
        total = d_h2[rows, :] + dm
        d_hid[rows, :] = total
        g_gain[0:1, :] += gg
        d_attn[rows, :] = total.astype(BF)

    rows_loop(count, 256, through)
    d_attn[count:, :] = d_hid_q[...].astype(BF)
    for copy in loads[4:]:
        copy.wait()

    def to_context(rows):
        d_context = mm_nt(d_attn[rows, :], wo[...]).astype(BF).astype(F)
        g[rows, :] = (d_context * li[rows, :]).astype(BF)

    rows_loop(count + rest, 256, to_context)


def middle_back(d_h2, d_hid_q, gate, up, dsaved, qsaved, weights, gains, after):
    wq, wk, wv, wo, wg, wu, wd, wp = weights
    count, width = d_h2.shape
    rows = count + d_hid_q.shape[0]
    hidden = wg.shape[1]
    return pl.pallas_call(
        middle_back_kernel,
        out_shape=(sds((count, width), F), sds((8, width), F), sds((rows, width), BF), sds((rows, width), BF)),
        in_specs=[VM] * 4 + [ANY] * (7 + len(after)),
        out_specs=[VM] * 4,
        scratch_shapes=[
            pltpu.VMEM(wg.shape, BF),
            pltpu.VMEM(wu.shape, BF),
            pltpu.VMEM(wo.shape, BF),
            pltpu.VMEM((count, hidden), BF),
            pltpu.VMEM((count, hidden), BF),
            pltpu.VMEM((rows, width), F),
            pltpu.SemaphoreType.DMA((7,)),
        ],
        compiler_params=pltpu.CompilerParams(vmem_limit_bytes=VMEM_LIMIT),
        cost_estimate=cost(5e9, 20e6),
        name="middle_back",
    )(d_h2, dsaved["hid"], d_hid_q, gains[1], wg, wu, wo, gate, up, dsaved["li"], qsaved["li"], *after)


def attn_back_kernel(
    hot, g,
    q_d, q_q, k_d, k_q, v_d, v_q, lr_d, lr_q, p_dh, p_qh, *refs
):
    dq, dk, dv, g_rel, q, k, v, p_d, p_q, lrd, lrq, ds, acc, sums, sem_in = refs[-15:]
    heads = p_d.shape[0]
    count = q_d.shape[0]
    rest = q_q.shape[0]
    blocks = count // 128
    cells_q = rest // 128
    loads = [
        pltpu.make_async_copy(src, dst, sem_in.at[i])
        for i, (src, dst) in enumerate(
            (
                (v_q, v.at[count:]),
                (p_qh, p_q),
                (lr_q, lrq),
                (q_q, q.at[count:]),
                (k_q, k.at[count:]),
                (v_d, v.at[0:count]),
                (p_dh, p_d),
                (lr_d, lrd),
                (q_d, q.at[0:count]),
                (k_d, k.at[0:count]),
            )
        )
    ]
    for copy in loads:
        copy.start()
    low, high, _, _ = half_masks()
    keeps = (low.astype(BF), high.astype(BF))
    for copy in loads[0:5]:
        copy.wait()
    acc[...] = jnp.zeros_like(acc)

    rows_q = [slice(count + 128 * b, count + 128 * b + 128) for b in range(cells_q)]
    cells = [(pair, e, b) for pair in range(heads // 2) for e in range(2) for b in range(cells_q)]
    lanes_of = [slice(128 * pair, 128 * pair + 128) for pair in range(heads // 2)]
    d_ps = [
        mm_nt(v[rows_q[b], lanes_of[pair]] * keeps[e], g[rows_q[b], lanes_of[pair]])
        for pair, e, b in cells
    ]
    dss = []
    for d_p, (pair, e, b) in zip(d_ps, cells):
        head = 2 * pair + e
        pf = p_q[head, 128 * b : 128 * b + 128, :].astype(F)
        t = pf * d_p
        share = lrq[head, :, 128 * b : 128 * b + 128] * jnp.sum(t, axis=0, keepdims=True)
        d_s = t - pf * share
        acc[head, :, 128:256] += d_s
        dss.append(d_s.astype(BF))
    for pair in range(heads // 2):
        lanes = lanes_of[pair]
        for b in range(cells_q):
            rows = rows_q[b]
            at_cell = [cells.index((pair, e, b)) for e in range(2)]
            probs = [p_q[2 * pair + e, 128 * b : 128 * b + 128, :] for e in range(2)]
            parts = [
                (
                    mm_tn(dss[at_cell[e]], k[rows, lanes] * keeps[e]),
                    mm(dss[at_cell[e]], q[rows, lanes] * keeps[e]),
                    mm(probs[e], g[rows, lanes] * keeps[e]),
                )
                for e in range(2)
            ]
            dq[rows, lanes] = (parts[0][0] + parts[1][0]).astype(BF)
            dk[rows, lanes] = (parts[0][1] + parts[1][1]).astype(BF)
            dv[rows, lanes] = (parts[0][2] + parts[1][2]).astype(BF)
    for copy in loads[5:]:
        copy.wait()

    def doc_pair(pair, carry):
        lanes = pl.ds(pl.multiple_of(pair * 128, 128), 128)
        q2 = q[0:count, lanes]
        k2 = k[0:count, lanes]
        v2 = v[0:count, lanes]
        g2 = g[0:count, lanes]
        d_ps = [mm_nt(v2 * keep, g2) for keep in keeps]
        sides = []
        for e, keep in enumerate(keeps):
            head = 2 * pair + e
            for i in range(blocks):
                cols = slice(128 * i, 128 * i + 128)
                pfs = [p_d[head, 128 * j : 128 * j + 128, cols].astype(F) for j in range(blocks)]
                ts = [pfs[j] * d_ps[e][128 * j : 128 * j + 128, cols] for j in range(blocks)]
                total = functools.reduce(jnp.add, ts)
                share = lrd[head, :, cols] * jnp.sum(total, axis=0, keepdims=True)
                for j in range(blocks):
                    d_s = ts[j] - pfs[j] * share
                    t = 1 - (j - i)
                    tile = t if abs(j - i) <= 1 else (3 if j > i else 4)
                    acc[head, :, 128 * tile : 128 * tile + 128] += d_s
                    ds[e, 128 * j : 128 * j + 128, cols] = d_s.astype(BF)
            sides.append(
                (
                    mm_tn(ds[e], k2 * keep),
                    mm(ds[e], q2 * keep),
                    mm(p_d[head], g2 * keep),
                )
            )
        dq[0:count, lanes] = (sides[0][0] + sides[1][0]).astype(BF)
        dk[0:count, lanes] = (sides[0][1] + sides[1][1]).astype(BF)
        dv[0:count, lanes] = (sides[0][2] + sides[1][2]).astype(BF)
        return carry

    lax.fori_loop(0, heads // 2, doc_pair, 0)
    sums[...] = jnp.zeros_like(sums)
    lane = lax.broadcasted_iota(jnp.int32, (1, TABLE), 1)
    for head in range(heads):
        folded = jnp.concatenate([acc[head, :, 0:384], jnp.zeros((128, 128), F)], axis=1)
        half = 64
        while half >= 8:
            folded = folded[0:half] + pltpu.roll(folded[half : 2 * half], TABLE - half, 1)
            half //= 2
        line = folded[0:1]
        for i in range(1, 8):
            line = line + pltpu.roll(folded[i : i + 1], TABLE - i, 1)
        after = jnp.sum(acc[head, :, 384:512])
        before = jnp.sum(acc[head, :, 512:640])
        line = line + jnp.where(lane == 0, after, jnp.where(lane == 256, before, 0.0))
        sums[head : head + 1, :] = line
    g_rel[...] = lax.dot_general(
        sums[...], hot[...], (((1,), (1,)), ((), ())),
        preferred_element_type=F, precision=lax.Precision.HIGHEST,
    )


def attn_back(g, dsaved, qsaved, hot, after):
    rows, width = g.shape
    heads = dsaved["p"].shape[0]
    buckets = hot.shape[0]
    count = dsaved["q"].shape[0]
    rest = rows - count
    both = []
    for name in ("q", "k", "v", "lr", "p"):
        both += [dsaved[name], qsaved[name]]
    return pl.pallas_call(
        attn_back_kernel,
        out_shape=(sds((rows, width), BF),) * 3 + (sds((16, buckets), F),),
        in_specs=[VM] * 2 + [ANY] * (10 + len(after)),
        out_specs=[VM] * 4,
        scratch_shapes=[pltpu.VMEM((rows, width), BF)] * 3
        + [
            pltpu.VMEM((heads, DL, DL), BF),
            pltpu.VMEM((heads, rest, 128), BF),
            pltpu.VMEM((heads, 1, count), F),
            pltpu.VMEM((heads, 1, rest), F),
            pltpu.VMEM((2, DL, DL), BF),
            pltpu.VMEM((heads, 128, 640), F),
            pltpu.VMEM((16, TABLE), F),
            pltpu.SemaphoreType.DMA((10,)),
        ],
        compiler_params=pltpu.CompilerParams(vmem_limit_bytes=VMEM_LIMIT),
        cost_estimate=cost(15e9, 40e6),
        name="attn_back",
    )(hot, g, *both, *after)


SMALL = 48


def split_small(values):
    high = values.astype(BF)
    return jnp.concatenate([high, (values - high.astype(F)).astype(BF)], axis=1)


def join_small(rows):
    return rows[:, 0:128].astype(F) + rows[:, 128:256].astype(F)


def attn_grads_kernel(fast, dq, dk, dv, d_attn, small, n1_d, n1_q, ctx_d, ctx_q, *refs):
    keep_h, send_h, n1, ctx, grads, sem_in, sem_out = refs[-7:]
    place = Place(fast)
    count = n1_d.shape[0]
    loads = [
        pltpu.make_async_copy(src, dst, sem_in.at[i])
        for i, (src, dst) in enumerate(
            (
                (n1_d, n1.at[0:count]),
                (n1_q, n1.at[count:]),
                (ctx_d, ctx.at[0:count]),
                (ctx_q, ctx.at[count:]),
            )
        )
    ]
    for copy in loads:
        copy.start()
    last = grads.shape[1] - SMALL
    for core in range(2):
        grads[core, last:, :] = split_small(small[...])
    for copy in loads:
        copy.wait()

    for which, (left, right) in enumerate(((n1, dq), (n1, dk), (n1, dv), (ctx, d_attn))):
        value = mm_tn(left[...], right[...]).astype(BF)
        for w in range(8):
            for c in range(3):
                row = ((w // 2) * 4 + which) * 288 + 96 * c
                grads[w % 2, row : row + 96, :] = value[96 * w : 96 * w + 96, 256 * c : 256 * c + 256]
    for copy in split_out(place.own, grads, keep_h, send_h, sem_out):
        copy.wait()


def attn_grads(fast, dq, dk, dv, d_attn, small, dsaved, qsaved, after):
    rows, width = d_attn.shape
    piece = sds((16 * 288 + SMALL, 256), BF)
    return pl.pallas_call(
        functools.partial(attn_grads_kernel, fast),
        out_shape=(piece, piece),
        in_specs=[VM] * 5 + [ANY] * (4 + len(after)),
        out_specs=[ANY] * 2,
        scratch_shapes=[
            pltpu.VMEM((rows, width), BF),
            pltpu.VMEM((rows, width), BF),
            pltpu.VMEM((2,) + piece.shape, BF),
            pltpu.SemaphoreType.DMA((4,)),
            pltpu.SemaphoreType.DMA((2,)),
        ],
        compiler_params=pltpu.CompilerParams(vmem_limit_bytes=VMEM_LIMIT),
        cost_estimate=cost(1, 1),
        name="attn_grads",
    )(dq, dk, dv, d_attn, small, dsaved["n1"], qsaved["n1"], dsaved["ctx"], qsaved["ctx"], *after)


def input_back_kernel(
    tok_d, tok_q, d_hid_d, d_hid_q, ga, gain_f, gain_l, gains_q, parts,
    rel, dq, dk, dv, wq, wk, wv, *refs
):
    out_d, out_q, small, g_gain = refs[-4:]
    count = tok_d.shape[0]
    gain_a = row_of(ga)
    g_gain[...] = jnp.zeros_like(g_gain)

    def part(offset, tok, d_hid, out):
        def step(rows):
            at_rows = pl.ds(pl.multiple_of(rows.start + offset, 256), 256)
            d_n1 = mm_nt(dq[at_rows, :], wq[...])
            d_n1 = d_n1 + mm_nt(dk[at_rows, :], wk[...])
            d_n1 = d_n1 + mm_nt(dv[at_rows, :], wv[...])
            d_in, gg = rms_back(tok[rows, :].astype(F), gain_a, d_n1)
            g_gain[0:1, :] += gg
            out[rows, :] = (d_hid[rows, :] + d_in).astype(BF)

        rows_loop(tok.shape[0], 256, step)

    part(0, tok_d, d_hid_d, out_d)
    part(count, tok_q, d_hid_q, out_q)
    small[...] = jnp.zeros_like(small)
    rows = (
        g_gain[0:1, :],
        gain_f[0:1, :] + gains_q[0:1, :],
        gain_l[0:1, :] + gains_q[1:2, :],
    )
    for i, row in enumerate(rows):
        for c in range(6):
            small[8 * i + c : 8 * i + c + 1, :] = row[:, 128 * c : 128 * c + 128]
    small[24:25, :] = parts[0:1, :]
    small[32:48, 0 : rel.shape[1]] = rel[...]


def input_back(tok_d, tok_q, d_hid_d, d_hid_q, gains, extra, from_attn, weights, after):
    width = tok_d.shape[1]
    return pl.pallas_call(
        input_back_kernel,
        out_shape=(sds(tok_d.shape, BF), sds(tok_q.shape, BF), sds((48, 128), F)),
        in_specs=[VM] * 16 + [ANY] * len(after),
        out_specs=[VM] * 3,
        scratch_shapes=[pltpu.VMEM((8, width), F)],
        compiler_params=pltpu.CompilerParams(vmem_limit_bytes=VMEM_LIMIT),
        cost_estimate=cost(3e9, 10e6),
        name="input_back",
    )(tok_d, tok_q, d_hid_d, d_hid_q, gains[0], *extra, *from_attn, weights[0], weights[1], weights[2], *after)


def unpack_kernel(which, own, one, two, three, *refs):
    stack = refs[-1]
    outs = refs[-5:-1]
    place = Place(True)
    half = own.shape[1]
    for m, part in enumerate((own, one, two, three)):
        for i in range(2):
            stack[place.rep ^ m, half * i : half * i + half, :] = part[i]
    if which == "attn":
        for r in range(4):
            for c in range(3):
                outs[r][:, 256 * c : 256 * c + 256] = stack[
                    r, 96 * c : 96 * c + 96, :
                ].astype(F)
        return
    for r in range(4):
        for c in range(4):
            first = (r % 2) * 1024 + 256 * c
            outs[r // 2][:, first : first + 256] = stack[
                r, 224 + 96 * c : 224 + 96 * c + 96, :
            ].astype(F)
        for c in range(3):
            outs[2][64 * r : 64 * r + 64, 256 * c : 256 * c + 256] = stack[
                r, 64 * c : 64 * c + 64, :
            ].astype(F)
    for r in range(3):
        outs[3][32 * r : 32 * r + 32, :] = stack[r, 192:224, 0:128].astype(F)


def unpack(which, parts, shapes, after):
    return pl.pallas_call(
        functools.partial(unpack_kernel, which),
        out_shape=tuple(sds(s, F) for s in shapes),
        in_specs=[VM] * 4 + [ANY] * len(after),
        out_specs=tuple(VM for _ in shapes),
        scratch_shapes=[pltpu.VMEM((4, 2 * parts[0].shape[1], parts[0].shape[2]), BF)],
        compiler_params=pltpu.CompilerParams(vmem_limit_bytes=16 * 1024 * 1024),
        cost_estimate=cost(1e6, 3e6),
        name="unpack_" + which,
    )(*parts, *after)


def swap(values, axis, size, mask):
    return lax.ppermute(values, axis, [(i, i ^ mask) for i in range(size)])


def near_kernel(keep, came, *refs):
    send_a, send_b, own_a, own_b = refs[-4:]
    place = Place(True)
    y, x = place.y, place.x
    half = own_a.shape[2]

    def total(i, k, first):
        return keep[0, i, k, first : first + half, :] + came[0, i, k, first : first + half, :]

    for i in range(2):
        send_a[0, i] = total(i, 1 - x, 0)
        own_a[0, i] = total(i, x, 0)
        send_b[0, i] = total(1 - y, i, half)
        own_b[0, i] = total(y, i, half)


def cross_kernel(a, came_a, b, came_b, *refs):
    send_a, send_b, own_a, own_b = refs[-4:]
    place = Place(True)
    y, x = place.y, place.x
    for i in range(4):
        send_a[i] = a[i, 1 - y] + came_a[i, 1 - y]
        own_a[i] = a[i, y] + came_a[i, y]
        send_b[i] = b[i, 1 - x] + came_b[i, 1 - x]
        own_b[i] = b[i, x] + came_b[i, x]


def line_kernel(a, came_a, b, came_b, *refs):
    send, own = refs[-2:]
    z = Place(True).z
    for i in range(2):
        for out, to in ((own, z ^ (2 * i)), (send, z ^ 1 ^ (2 * i))):
            out[i, 0] = a[to] + came_a[to]
            out[i, 1] = b[to] + came_b[to]


def next_kernel(own, came, *refs):
    send, out = refs[-2:]
    out[...] = own[0] + came[0]
    send[...] = own[1] + came[1]


def far_kernel(own, came, *refs):
    refs[-1][...] = own[...] + came[...]


def cell(index, half, first=0):
    return pl.ds(pl.multiple_of(index * half + first, 16), half)


def attn_near_kernel(keep, came, *refs):
    send_a, send_b, own_a, own_b, small = refs[-5:]
    place = Place(True)
    half = own_a.shape[2]

    def total(z, y, x, first):
        rows = cell((z * 2 + y) * 2 + x, 2 * half)
        rows = pl.ds(pl.multiple_of(rows.start + first, 16), half)
        return keep[rows, :] + came[rows, :]

    for z in range(4):
        for i in range(2):
            send_a[cell(z * 2 + i, half), :] = total(z, i, 1 - place.x, 0)
            own_a[z, i] = total(z, i, place.x, 0)
            send_b[z, i] = total(z, 1 - place.y, i, half)
            own_b[z, i] = total(z, place.y, i, half)
    last = 16 * 2 * half
    value = split_small(join_small(keep[last:, :]) + join_small(came[last:, :]))
    send_a[8 * half :, :] = value
    small[...] = value


def attn_cross_kernel(a, came_a, b, came_b, small_in, *refs):
    send_a, send_b, own_a, own_b, small = refs[-5:]
    place = Place(True)
    half = a.shape[2]
    y, x = place.y, place.x
    for z in range(4):
        send_a[cell(z, half), :] = a[z, 1 - y] + came_a[cell(z * 2 + 1 - y, half), :]
        own_a[z] = a[z, y] + came_a[cell(z * 2 + y, half), :]
        send_b[z] = b[z, 1 - x] + came_b[z, 1 - x]
        own_b[z] = b[z, x] + came_b[z, x]
    value = split_small(join_small(small_in[...]) + join_small(came_a[8 * half :, :]))
    send_a[4 * half :, :] = value
    small[...] = value


def attn_line_kernel(a, came_a, b, came_b, small_in, *refs):
    send, own, small = refs[-3:]
    z = Place(True).z
    half = a.shape[1]
    for i in range(2):
        for out, to in ((own, z ^ (2 * i)), (send, z ^ 1 ^ (2 * i))):
            out[2 * half * i : 2 * half * i + half, :] = a[to] + came_a[cell(to, half), :]
            out[2 * half * i + half : 2 * half * i + 2 * half, :] = b[to] + came_b[to]
    value = split_small(join_small(small_in[...]) + join_small(came_a[4 * half :, :]))
    send[4 * half :, :] = value
    small[...] = value


def attn_next_kernel(own, came, small_in, *refs):
    send, out, small = refs[-3:]
    rows = out.shape[0]
    out[...] = own[0:rows, :] + came[0:rows, :]
    send[0:rows, :] = own[rows : 2 * rows, :] + came[rows : 2 * rows, :]
    value = split_small(join_small(small_in[...]) + join_small(came[2 * rows :, :]))
    send[rows:, :] = value
    small[...] = value


def attn_far_kernel(heads, total_queries, own, came, small_in, *refs):
    out, gain_a, gain_f, gain_l, rel, loss, fraction = refs[-7:]
    rows = own.shape[0]
    for i in range(2):
        half = slice(rows // 2 * i, rows // 2 * (i + 1))
        out[i] = own[half, :] + came[half, :]
    total = join_small(small_in[...]) + join_small(came[rows:, :])
    for i, gain in enumerate((gain_a, gain_f, gain_l)):
        row = jnp.concatenate([total[8 * i + c : 8 * i + c + 1, :] for c in range(6)], axis=1)
        gain[...] = row.reshape(gain.shape[0])
    rel[...] = total[32 : 32 + heads, 0 : rel.shape[1]]
    lane = lax.broadcasted_iota(jnp.int32, (1, 128), 1)
    line = total[24:25, :]
    loss_sum, hits, found = (jnp.sum(jnp.where(lane == i, line, 0.0)) for i in range(3))
    loss[0, 0] = loss_sum / total_queries
    fraction[0, 0] = hits / (DL * found)


def stage(kernel, name, ins, outs, after, flops=1, scratch=(), scalars=0, limit=16):
    return pl.pallas_call(
        kernel,
        out_shape=outs,
        in_specs=[VM] * len(ins) + [ANY] * len(after),
        out_specs=[VM] * (len(outs) - scalars) + [SM] * scalars,
        scratch_shapes=list(scratch),
        compiler_params=pltpu.CompilerParams(vmem_limit_bytes=limit * 1024 * 1024),
        cost_estimate=cost(flops, 1),
        name=name,
    )(*ins, *after)


class AttnReduction:
    def __init__(self, keep, send):
        self.half = 144
        self.keep = keep
        self.came = swap(send, "wide", 8, 1)
        self.small_shape = sds((SMALL, 256), BF)

    def rows(self, cells):
        return sds((cells * self.half + SMALL, 256), BF)

    def near(self, after):
        own = sds((4, 2, self.half, 256), BF)
        outs = (self.rows(8), own, own, own, self.small_shape)
        send_a, send_b, self.a, self.b, self.small = stage(
            attn_near_kernel, "near_attn", (self.keep, self.came), outs, after, limit=24
        )
        self.came_a = swap(send_a, "rep", 4, 1)
        self.came_b = swap(send_b, "rep", 4, 2)
        return (self.a,)

    def ins(self):
        return self.a, self.came_a, self.b, self.came_b, self.small

    def cross(self, after):
        own = sds((4, self.half, 256), BF)
        outs = (self.rows(4), own, own, own, self.small_shape)
        send_a, send_b, self.a, self.b, self.small = stage(
            attn_cross_kernel, "cross_attn", self.ins(), outs, after, 1e9
        )
        self.came_a = swap(send_a, "rep", 4, 2)
        self.came_b = swap(send_b, "rep", 4, 1)
        return (self.a,)

    def line(self, after):
        own = sds((4 * self.half, 256), BF)
        outs = (self.rows(4), own, self.small_shape)
        send, self.own, self.small = stage(attn_line_kernel, "line_attn", self.ins(), outs, after)
        self.came = swap(send, "wide", 8, 2)
        return (self.own,)

    def next(self, after):
        own = sds((2 * self.half, 256), BF)
        ins = (self.own, self.came, self.small)
        outs = (self.rows(2), own, self.small_shape)
        send, self.own, self.small = stage(attn_next_kernel, "next_attn", ins, outs, after)
        self.came = swap(send, "wide", 8, 4)
        return (self.own,)

    def far(self, heads, buckets, width, total_queries, after):
        outs = (sds((2, self.half, 256), BF),) + (sds((width,), F),) * 3
        outs = outs + (sds((heads, buckets), F), sds((1, 1), F), sds((1, 1), F))
        self.own, *results = stage(
            functools.partial(attn_far_kernel, heads, float(total_queries)), "far_attn",
            (self.own, self.came, self.small), outs, after, scalars=2,
        )
        self.came = [swap(self.own, "rep", 4, m) for m in (1, 2, 3)]
        return results

    def parts(self):
        return self.own, *self.came


class Reduction:
    def __init__(self, name, keep, send):
        self.name = name
        self.half = keep.shape[3] // 2
        self.keep = keep
        self.came = swap(send, "wide", 8, 1)

    def near(self, after, flops=1):
        rows = 2 * self.half
        whole = pl.BlockSpec((1, 2, 2, rows, 256), lambda i: (i, 0, 0, 0, 0))
        part = pl.BlockSpec((1, 2, self.half, 256), lambda i: (i, 0, 0, 0))
        send_a, send_b, self.a, self.b = pl.pallas_call(
            near_kernel,
            grid=(4,),
            out_shape=(sds((4, 2, self.half, 256), BF),) * 4,
            in_specs=[whole, whole] + [ANY] * len(after),
            out_specs=(part,) * 4,
            compiler_params=pltpu.CompilerParams(vmem_limit_bytes=VMEM_LIMIT),
            cost_estimate=cost(flops, 1),
            name="near_" + self.name,
        )(self.keep, self.came, *after)
        self.came_a = swap(send_a, "rep", 4, 1)
        self.came_b = swap(send_b, "rep", 4, 2)
        return (self.a,)

    def step(self, kernel, name, ins, shapes, after, flops=1):
        outs = tuple(sds(shape, BF) for shape in shapes)
        return stage(kernel, name + self.name, ins, outs, after, flops)

    def cross(self, after, flops=1):
        ins = (self.a, self.came_a, self.b, self.came_b)
        shape = (4, self.half, 256)
        send_a, send_b, self.a, self.b = self.step(cross_kernel, "cross_", ins, (shape,) * 4, after, flops)
        self.came_a = swap(send_a, "rep", 4, 2)
        self.came_b = swap(send_b, "rep", 4, 1)
        return (self.a,)

    def line(self, after, flops=1):
        ins = (self.a, self.came_a, self.b, self.came_b)
        shape = (2, 2, self.half, 256)
        send, self.own = self.step(line_kernel, "line_", ins, (shape,) * 2, after, flops)
        self.came = swap(send, "wide", 8, 2)
        return (self.own,)

    def next(self, after):
        shape = (2, self.half, 256)
        send, self.own = self.step(next_kernel, "next_", (self.own, self.came), (shape,) * 2, after)
        self.came = swap(send, "wide", 8, 4)
        return (self.own,)

    def far(self, after):
        shape = (2, self.half, 256)
        (self.own,) = self.step(far_kernel, "far_", (self.own, self.came), (shape,), after)
        self.came = [swap(self.own, "rep", 4, m) for m in (1, 2, 3)]
        return (self.own,)

    def parts(self):
        return self.own, *self.came


def natural(which, keep, send):
    both = jnp.stack([keep, send])
    if which == "attn":
        a = both[:, : 16 * 288].reshape(2, 4, 4, 3, 96, 256).transpose(2, 1, 0, 4, 3, 5).reshape(4, 768, 768)
        return [a[i] for i in range(4)]
    both = both.reshape((2, 4, 4) + both.shape[4:])
    a = both[:, :, :, 224:].reshape(2, 4, 4, 4, 96, 256).transpose(1, 0, 4, 2, 3, 5)
    a = a.reshape(768, 4096)
    d = both[:, :, :, :192].reshape(2, 4, 4, 3, 64, 256).transpose(1, 0, 2, 4, 3, 5)
    e = both[:, :, :3, 192:224, :128].transpose(1, 0, 2, 3, 4)
    return [a[:, :2048], a[:, 2048:], d.reshape(2048, 768), e.reshape(768, 128)]


def body(
    doc_tokens, query_tokens, doc_cotangent, query_cotangent, retrieved, pos_ids, pos_count,
    w_query, w_key, carried_content_weights, w_out, w_gate, w_up, w_down, w_proj,
    gain_attn, gain_ffn, gain_final, rel_bias,
):
    n_wide = lax.axis_size("wide")
    n_rep = lax.axis_size("rep")
    group = retrieved.shape[1]
    fast = n_wide == 8 and n_rep == 4 and group == 64
    weights = (w_query, w_key, carried_content_weights, w_out, w_gate, w_up, w_down, w_proj)
    width = doc_tokens.shape[1]
    buckets, heads = rel_bias.shape
    hot_np = bucket_hot(buckets)
    hot = jnp.asarray(hot_np, BF)
    hot_f = jnp.asarray(hot_np, F)
    rep_hot = jnp.asarray(query_hot(64), BF)
    rel = jnp.transpose(rel_bias)
    queries = pos_ids.shape[0]
    ids = jnp.transpose(pos_ids)
    columns = jnp.transpose(retrieved)
    gains = (gain_attn, gain_ffn, gain_final)

    doc = layer_forward(doc_tokens, weights, gains, rel, hot, DL, (columns,) if fast else ())
    if fast:
        send = doc["send"]
        near = [send] + [swap(send, "wide", n_wide, 2 * m) for m in (1, 2, 3)]
        near_other = swap(send, "wide", n_wide, 1)
    query = layer_forward(query_tokens, weights, gains, rel, hot, QUERY_LENGTH, (), (doc["emb"],))
    if fast:
        other = swap(stack_rows(near[1:], (query["emb"],)), "wide", n_wide, 1)
        ins = near + [near_other, other]
    else:
        mask_query = lax.all_to_all(columns.astype(F), "wide", 0, 0, tiled=True)
        mask_query = mask_query.reshape(n_wide, queries, DL)
        ins = [lax.all_gather(doc["emb"], "wide", axis=0, tiled=True), mask_query]
    coef, d_query_emb, parts = query_sims(
        fast, ids, pos_count, query["emb"], query_cotangent, ins, n_wide
    )
    if fast:
        every = [coef] + [swap(coef, "wide", n_wide, m) for m in range(1, 8)]
        coef_all = query_cotangent
    else:
        every = [lax.all_gather(query["emb"], "wide", axis=0, tiled=True)]
        coef_all = lax.all_to_all(coef, "wide", 0, 0, tiled=True)
    d_proj_q, d_ffn_q, d_gate_q, d_up_q, d_hid_q, gains_q = query_back(
        d_query_emb, query, weights, gains, coef
    )
    d_h2, gain_l, d_gate, d_up, keep_f, send_f = doc_back(
        fast, doc_cotangent, doc["emb"], every, columns, rep_hot, coef_all, doc, query, gains,
        w_proj, w_down, (d_proj_q, d_ffn_q, d_gate_q, d_up_q),
    )
    if fast:
        ffn = Reduction("ffn", keep_f, send_f)
    d_hid, gain_f, d_attn, g = middle_back(
        d_h2, d_hid_q, d_gate, d_up, doc, query, weights, gains, ()
    )
    after = ffn.near((d_attn,)) if fast else ()
    dq, dk, dv, rel_grad = attn_back(g, doc, query, hot_f, after)
    after = ffn.cross((rel_grad,)) if fast else ()
    doc_grad, query_grad, small = input_back(
        doc_tokens, query_tokens, d_hid, d_hid_q, gains, (gain_f, gain_l, gains_q, parts),
        (rel_grad, dq, dk, dv), weights, after,
    )
    keep_a, send_a = attn_grads(fast, dq, dk, dv, d_attn, small, doc, query, (small,))
    if fast:
        attn = AttnReduction(keep_a, send_a)
        after = ffn.line((keep_a,), 1e9)
        after = attn.near(after)
        after = ffn.next(after)
        after = attn.cross(after)
        after = ffn.far(after)
        after = attn.line(after)
        after = attn.next(after)
        after = grad_gate, grad_up, grad_down, grad_proj = unpack(
            "ffn", ffn.parts(), ((96, 2048), (96, 2048), (256, 768), (96, 128)), after
        )
        total_gain_a, total_gain_f, total_gain_l, total_rel, loss, fraction = attn.far(
            heads, buckets, width, queries * n_wide * n_rep, after[3:]
        )
        grad_query, grad_key, grad_value, grad_out = unpack(
            "attn", attn.parts(), ((96, 768),) * 4, (total_rel,)
        )
        loss = loss.reshape(())
        fraction = fraction.reshape(())
    else:
        small = lax.psum(small, ("rep", "wide"))

        def total(whole):
            part = lax.psum_scatter(whole, "wide", scatter_dimension=0, tiled=True)
            return lax.psum(part, "rep").astype(F)

        grad_query, grad_key, grad_value, grad_out = (total(a) for a in natural("attn", keep_a, send_a))
        grad_gate, grad_up, grad_down, grad_proj = (total(a) for a in natural("ffn", keep_f, send_f))
        total_gain_a, total_gain_f, total_gain_l = (
            small[8 * i : 8 * i + 6].reshape(width) for i in range(3)
        )
        total_rel = small[32 : 32 + heads, 0:buckets]
        loss = small[24, 0] / (queries * n_wide * n_rep)
        fraction = small[24, 1] / (DL * small[24, 2])
    return (
        doc["emb"],
        query["emb"],
        doc_grad,
        query_grad,
        grad_query,
        grad_key,
        grad_value,
        grad_out,
        grad_gate,
        grad_up,
        grad_down,
        grad_proj,
        total_gain_a,
        total_gain_f,
        total_gain_l,
        jnp.transpose(total_rel),
        loss,
        fraction,
    )


def solution(mesh):
    rows = P(("rep", "wide"), None)
    return jax.shard_map(
        body,
        mesh=mesh,
        in_specs=(rows,) * 6 + (P(("rep", "wide")),) + (P(),) * 12,
        out_specs=(rows,) * 4 + (P("wide", None),) * 8 + (P(),) * 6,
        check_vma=False,
    )
```

```python
import functools

import jax
import jax.numpy as jnp
import numpy as np
from jax import lax
from jax.experimental import pallas as pl
from jax.experimental.pallas import tpu as pltpu
from jax.sharding import PartitionSpec as P

DL = 512
QUERY_LENGTH = 32
EPS = 1e-06
SCALE = 10.0
BF = jnp.bfloat16
F = jnp.float32
TABLE = 512
VMEM_LIMIT = 60 * 1024 * 1024

SAVED = (
    "n1", "q", "k", "v", "p", "li", "ctx", "hid", "n2", "gv", "us", "act", "h2", "n3", "proj", "lr", "emb", "send",
)

SM = pl.BlockSpec(memory_space=pltpu.SMEM)
ANY = pl.BlockSpec(memory_space=pl.ANY)
VM = pl.BlockSpec(memory_space=pltpu.VMEM)


def mm(a, b):
    return jnp.dot(a, b, preferred_element_type=F)


def mm_nt(a, b):
    return lax.dot_general(a, b, (((1,), (1,)), ((), ())), preferred_element_type=F)


def mm_tn(a, b):
    return lax.dot_general(a, b, (((0,), (0,)), ((), ())), preferred_element_type=F)


def bucket_hot(buckets):
    half = buckets // 2
    exact = half // 2
    column = np.arange(TABLE)
    relative = 128 - np.where(column <= TABLE - 128, column, column - TABLE)
    base = (relative > 0).astype(np.int64) * half
    distance = np.abs(relative)
    large = exact + (
        np.log(np.maximum(distance, 1) / float(exact)) / np.log(128.0 / exact) * (half - exact)
    ).astype(np.int64)
    large = np.minimum(large, half - 1)
    number = base + np.where(distance < exact, distance, large)
    return (np.arange(buckets)[:, None] == number[None, :]).astype(np.float32)


def query_hot(queries):
    tokens = np.arange(queries * QUERY_LENGTH)
    return (np.arange(queries)[:, None] == tokens[None, :] // QUERY_LENGTH).astype(np.float32)


def cost(flops, moved):
    large = flops > 1e8
    return pl.CostEstimate(flops=int(1e12 if large else 1), bytes_accessed=1, transcendentals=0)


class Place:
    def __init__(self, fast):
        self.fast = fast
        self.rep = lax.axis_index("rep")
        self.wide = lax.axis_index("wide")
        self.y, self.x = self.rep >> 1, self.rep & 1
        self.z = self.wide >> 1
        self.own = self.wide & 1 if fast else 0

    def doc(self, slot):
        return self.wide ^ (2 * (slot % 4)) ^ (slot // 4) if self.fast else slot

    def source(self, slot):
        return self.wide ^ slot if self.fast else slot


def row_of(gain):
    return gain[...].astype(F).reshape(1, gain.shape[0])


def stack_kernel(n_parts, *refs):
    out = refs[-1]
    row = 0
    for part in refs[:n_parts]:
        out[row : row + part.shape[0], :] = part[...]
        row += part.shape[0]


def stack_rows(parts, after):
    rows = sum(part.shape[0] for part in parts)
    return pl.pallas_call(
        functools.partial(stack_kernel, len(parts)),
        out_shape=sds((rows, 128), BF),
        in_specs=[VM] * len(parts) + [ANY] * len(after),
        out_specs=VM,
        cost_estimate=cost(1, 1),
        name="stack_rows",
    )(*parts, *after)


def sds(shape, dtype):
    return jax.ShapeDtypeStruct(shape, dtype)


def rows_loop(count, block, fn):
    def step(i, carry):
        fn(pl.ds(pl.multiple_of(i * block, block), block))
        return carry

    lax.fori_loop(0, count // block, step, 0)


def half_masks():
    lane = lax.broadcasted_iota(jnp.int32, (1, 128), 1)
    low = (lane < 64).astype(F)
    high = 1.0 - low
    one_low = (lane == 0).astype(F)
    one_high = (lane == 64).astype(F)
    return low, high, one_low, one_high


def rms(values):
    return lax.rsqrt(jnp.mean(values * values, axis=-1, keepdims=True) + EPS)


def rms_back(values, gain, d_result):
    inverse = rms(values)
    scaled = values * inverse
    grad_gain = jnp.sum(d_result * scaled, axis=0, keepdims=True)
    gained = d_result * gain
    d_values = inverse * (gained - scaled * jnp.mean(gained * scaled, axis=-1, keepdims=True))
    return d_values, grad_gain


def gelu_parts(gate):
    square = gate * gate
    tangent = jnp.tanh(gate * (0.7978845608028654 + (0.7978845608028654 * 0.044715) * square))
    half_plus = 0.5 + 0.5 * tangent
    value = gate * half_plus
    slope = half_plus + 0.5 * gate * (1.0 - tangent * tangent) * (
        0.7978845608028654 + (3.0 * 0.7978845608028654 * 0.044715) * square
    )
    return value, slope


def start_all(pairs, sems):
    copies = [pltpu.make_async_copy(src, dst, sems.at[i]) for i, (src, dst) in enumerate(pairs)]
    for copy in copies:
        copy.start()
    return copies


def wait_all(copies):
    for copy in copies:
        copy.wait()


def fwd_kernel(
    seq,
    heads,
    n_after,
    columns,
    tok, ga, gf, gl, rel, hot, wq_h, wk_h, wv_h, wo_h, wg_h, wu_h, wd_h, wp_h,
    *refs,
):
    (
    n1_h, q_h, k_h, v_h, p_h, li_h, ctx_h, hid_h, n2_h, gv_h, us_h, act_h, h2_h, n3_h, proj_h, lr_h, emb, send,
    wq, wk, wv, wo, wg, wu, wd, wp,
    n1, q, k, v, p, li, ctx, hid, n2, gv, us, act, h2, n3, proj, lr,
    tbl, bs, sem_in, sem_tile, sem_push, sem_out,
    ) = refs[n_after + columns :]
    count = tok.shape[0]
    loads = start_all(((wq_h, wq), (wk_h, wk), (wv_h, wv), (wo_h, wo), (wp_h, wp)), sem_in)

    def tile_loads(t):
        cols = pl.ds(pl.multiple_of(t * 512, 512), 512)
        pairs = ((wg_h.at[:, cols], wg.at[:, cols]), (wu_h.at[:, cols], wu.at[:, cols]), (wd_h.at[cols], wd.at[cols]))
        return [pltpu.make_async_copy(src, dst, sem_tile.at[t, i]) for i, (src, dst) in enumerate(pairs)]

    def tile_pushes(t):
        cols = pl.ds(pl.multiple_of(t * 512, 512), 512)
        pairs = tuple((a.at[:, cols], b.at[:, cols]) for a, b in ((gv, gv_h), (us, us_h), (act, act_h)))
        return [pltpu.make_async_copy(src, dst, sem_push.at[t, i]) for i, (src, dst) in enumerate(pairs)]

    outs = {}

    def push(i, src, dst):
        outs[i] = pltpu.make_async_copy(src, dst, sem_out.at[i])
        outs[i].start()

    gain_a, gain_f, gain_l = row_of(ga), row_of(gf), row_of(gl)

    def norm_one(rows):
        x = tok[rows, :].astype(F)
        n1[rows, :] = (x * rms(x) * gain_a).astype(BF)

    rows_loop(count, 128, norm_one)
    push(0, n1, n1_h)
    lines = mm(rel[...], hot[...])
    for h in range(heads):
        tbl[h] = lines[h : h + 1, :]
    for i, (w, r, r_h) in enumerate(((wq, q, q_h), (wk, k, k_h), (wv, v, v_h))):
        loads[i].wait()
        r[...] = mm(n1[...], w[...]).astype(BF)
        push(1 + i, r, r_h)
    n_tiles = wg.shape[1] // 512
    for t in range(2):
        for copy in tile_loads(t):
            copy.start()

    low, high, one_low, one_high = half_masks()
    is_low = low > 0.5

    blocks = count // 128

    def table(head, carry):
        row = jnp.broadcast_to(tbl[head], (128, TABLE))
        base = pltpu.roll(row, 0, 1, stride=1, stride_axis=0)
        if seq == DL:
            bs[head] = base[:, 0:384]
        else:
            rows = lax.broadcasted_iota(jnp.int32, (128, 128), 0) // seq
            columns = lax.broadcasted_iota(jnp.int32, (128, 128), 1) // seq
            bs[head] = jnp.where(rows == columns, base[:, 128:256], -1e30)
        return carry

    lax.fori_loop(0, heads, table, 0)

    def halves(index):
        lanes = pl.ds(pl.multiple_of(index * 128, 128), 128)
        q2 = q[:, lanes]
        k2 = k[:, lanes]
        v2 = v[:, lanes]
        parts = []
        for keep, one in ((low, one_high), (high, one_low)):
            parts.append((k2 * keep.astype(BF), v2 * keep.astype(BF) + one.astype(BF)))
        return lanes, q2, parts

    def join(lanes, o0, o1):
        inv = 1.0 / jnp.where(is_low, o0[:, 64:65], o1[:, 0:1])
        li[:, lanes] = inv
        ctx[:, lanes] = (jnp.where(is_low, o0, o1) * inv).astype(BF)

    def doc_scores(index):
        _, q2, parts = halves(index)
        for e in range(2):
            for half in range(2):
                yield mm_nt(parts[e][0], q2[256 * half : 256 * half + 256])

    def doc_softmax(head, score, i):
        cols = slice(128 * i, 128 * i + 128)
        terms = []
        for j in range(blocks):
            term = score[128 * j : 128 * j + 128, 128 * (i % 2) : 128 * (i % 2) + 128]
            if abs(j - i) <= 1:
                t = 1 - (j - i)
                terms.append(term + bs[head, :, 128 * t : 128 * t + 128])
            else:
                terms.append(term + (tbl[head, :, 0:1] if j > i else tbl[head, :, 256:257]))
        peak = functools.reduce(jnp.maximum, terms)
        peak = jnp.max(peak, axis=0, keepdims=True)
        total = jnp.zeros((128, 128), F)
        probs = []
        for j in range(blocks):
            power = jnp.exp(terms[j] - peak)
            total = total + power
            probs.append(power.astype(BF))
            p[head, 128 * j : 128 * j + 128, cols] = probs[-1]
        lr[head, :, cols] = 1.0 / jnp.sum(total, axis=0, keepdims=True)
        return jnp.concatenate(probs, axis=0)

    def doc_pairs(first, number):
        scores = list(doc_scores(first))
        for index in range(number):
            lanes, _, parts = halves(first + index)
            coming = doc_scores(first + index + 1) if index + 1 < number else iter(())
            following = []
            sides = []
            for e in range(2):
                head = 2 * (first + index) + e
                done = []
                for half in range(2):
                    following += [c for c in [next(coming, None)] if c is not None]
                    probs = [doc_softmax(head, scores[2 * e + half], 2 * half + i) for i in range(2)]
                    done.append(mm_tn(jnp.concatenate(probs, axis=1), parts[e][1]))
                sides.append(jnp.concatenate(done, axis=0))
            join(lanes, *sides)
            scores = following

    def query_group(group, carry):
        pairs = [halves(group * 3 + i) for i in range(3)]
        cells = [(i, e, b) for i in range(3) for e in range(2) for b in range(blocks)]
        rows = [slice(128 * b, 128 * b + 128) for b in range(blocks)]
        scores = [mm_nt(pairs[i][2][e][0][rows[b]], pairs[i][1][rows[b]]) for i, e, b in cells]
        probs = []
        for score, (i, e, b) in zip(scores, cells):
            head = (group * 3 + i) * 2 + e
            term = score + bs[head]
            power = jnp.exp(term - jnp.max(term, axis=0, keepdims=True))
            probs.append(power.astype(BF))
            p[head, rows[b], :] = probs[-1]
            lr[head, :, rows[b]] = 1.0 / jnp.sum(power, axis=0, keepdims=True)
        outs_g = [mm_tn(pb, pairs[i][2][e][1][rows[b]]) for pb, (i, e, b) in zip(probs, cells)]
        for i in range(3):
            sides = [
                jnp.concatenate([outs_g[cells.index((i, e, b))] for b in range(blocks)], axis=0)
                for e in range(2)
            ]
            join(pairs[i][0], *sides)
        return carry

    if seq == DL:
        def doc_group(group, carry):
            doc_pairs(group * 3, 3)
            return carry

        lax.fori_loop(0, heads // 2 // 3, doc_group, 0)
    else:
        lax.fori_loop(0, heads // 6, query_group, 0)
    push(4, p, p_h)
    push(5, li, li_h)
    push(15, lr, lr_h)
    push(6, ctx, ctx_h)

    loads[3].wait()

    def middle(rows):
        h = tok[rows, :].astype(F) + mm(ctx[rows, :], wo[...])
        hid[rows, :] = h
        h2[rows, :] = h
        n2[rows, :] = (h * rms(h) * gain_f).astype(BF)

    rows_loop(count, 256, middle)
    push(7, hid, hid_h)
    push(8, n2, n2_h)

    def ffn(t, carry):
        cols = pl.ds(pl.multiple_of(t * 512, 512), 512)

        @pl.when(t + 2 < n_tiles)
        def _():
            for copy in tile_loads(t + 2):
                copy.start()

        wait_all(tile_loads(t))
        for b in range(count // 256):
            rows = slice(256 * b, 256 * b + 256)
            gate = mm(n2[rows, :], wg[:, cols])
            up = mm(n2[rows, :], wu[:, cols])
            value, slope = gelu_parts(gate)
            a = (value * up).astype(BF)
            gv[rows, cols] = value.astype(BF)
            us[rows, cols] = (up * slope).astype(BF)
            act[rows, cols] = a
            h2[rows, :] += mm(a, wd[cols, :])
        for copy in tile_pushes(t):
            copy.start()
        return carry

    lax.fori_loop(0, n_tiles, ffn, 0)
    loads[4].wait()

    def top(rows):
        h = h2[rows, :]
        n = (h * rms(h) * gain_l).astype(BF)
        n3[rows, :] = n
        pr = mm(n, wp[...])
        proj[rows, :] = pr
        emb[rows, :] = (pr * lax.rsqrt(jnp.sum(pr * pr, axis=-1, keepdims=True) + EPS)).astype(BF)

    rows_loop(count, 256, top)
    if columns:
        send[0:count, :] = emb[...]
        mask = refs[0][...].astype(F).astype(BF)
        for b in range(DL // 128):
            first = count + 64 * b
            send[first : first + 64, :] = mask[:, 128 * b : 128 * b + 128]
    else:
        send[...] = jnp.zeros_like(send)
    push(12, h2, h2_h)
    push(13, n3, n3_h)
    push(14, proj, proj_h)
    wait_all(outs.values())
    for t in range(n_tiles):
        wait_all(tile_pushes(t))


def layer_forward(tokens, weights, gains, rel, hot, seq, columns=(), after=()):
    count, width = tokens.shape
    wq, wk, wv, wo, wg, wu, wd, wp = weights
    hidden = wg.shape[1]
    emb = wp.shape[1]
    heads = rel.shape[0]
    keys = DL if seq == DL else 128
    saved = (
        sds((count, width), BF),
        sds((count, width), BF),
        sds((count, width), BF),
        sds((count, width), BF),
        sds((heads, count, keys), BF),
        sds((count, width), F),
        sds((count, width), BF),
        sds((count, width), F),
        sds((count, width), BF),
        sds((count, hidden), BF),
        sds((count, hidden), BF),
        sds((count, hidden), BF),
        sds((count, width), F),
        sds((count, width), BF),
        sds((count, emb), F),
        sds((heads, 1, count), F),
    )
    outs = pl.pallas_call(
        functools.partial(fwd_kernel, seq, heads, len(after), len(columns)),
        out_shape=saved
        + (sds((count, emb), BF), sds((count + 64 * DL // 128 if columns else 16, emb), BF)),
        in_specs=[VM] * 6 + [ANY] * 8 + [VM] * len(columns) + [ANY] * len(after),
        out_specs=[ANY] * 16 + [VM] * 2,
        scratch_shapes=[pltpu.VMEM(w.shape, BF) for w in weights]
        + [pltpu.VMEM(s.shape, s.dtype) for s in saved]
        + [
            pltpu.VMEM((heads, 1, TABLE), F),
            pltpu.VMEM((heads, 128, 384 if seq == DL else 128), F),
            pltpu.SemaphoreType.DMA((5,)),
            pltpu.SemaphoreType.DMA((hidden // 512, 3)),
            pltpu.SemaphoreType.DMA((hidden // 512, 3)),
            pltpu.SemaphoreType.DMA((16,)),
        ],
        compiler_params=pltpu.CompilerParams(vmem_limit_bytes=VMEM_LIMIT),
        cost_estimate=cost(count * 14e6, 40e6),
        name="layer_forward_%d" % seq,
    )(tokens, *gains, rel, hot, *weights, *columns, *after)
    return dict(zip(SAVED, outs))


def each_block(arrays, block, fn):
    first = 0
    for array in arrays:
        number = array.shape[0] // block
        if number == 1:
            fn(first, array[...])
        else:

            def step(i, carry, array=array, first=first):
                fn(first + i, array[pl.ds(pl.multiple_of(i * block, block), block), :])
                return carry

            lax.fori_loop(0, number, step, 0)
        first += number


def query_sims_kernel(fast, n_docs, n_ins, ids, used, qemb, cot, *refs):
    ins = refs[:n_ins]
    coef, d_emb, parts, es, total, counts = refs[n_ins:]
    place = Place(fast)
    tokens = qemb.shape[0]
    queries = tokens // QUERY_LENGTH
    lane = lax.broadcasted_iota(jnp.int32, (tokens, 128), 1)
    lane_q = lax.broadcasted_iota(jnp.int32, (queries, 128), 1)
    total[...] = jnp.zeros_like(total)
    counts[...] = jnp.zeros_like(counts)

    if fast:
        row = lax.broadcasted_iota(jnp.int32, (queries, 64), 0)
        pick = row + queries * place.wide == lax.broadcasted_iota(jnp.int32, (queries, 64), 1)
        pick = jnp.where(pick, 1.0, 0.0).astype(BF)
        per = DL + 64 * DL // 128

        def rows_at(slot, first, last):
            if slot < 5:
                return ins[slot][first:last, :]
            base = per * (slot - 5)
            return ins[5][base + first : base + last, :]

        def doc_at(slot):
            return rows_at(slot, 0, DL)

        def mask_at(slot):
            packed = rows_at(slot, DL, per)
            return jnp.concatenate([mm(pick, packed[64 * b : 64 * b + 64]) for b in range(4)], axis=1)

        def each(fn):
            for slot in range(n_docs):
                fn(slot)

    else:
        docs, mask = ins

        def doc_at(slot):
            return docs[pl.ds(pl.multiple_of(slot * DL, DL), DL), :]

        def mask_at(slot):
            return mask[slot]

        def each(fn):
            def step(i, carry):
                fn(i)
                return carry

            lax.fori_loop(0, n_docs, step, 0)

    def forward(slot):
        d = place.doc(slot)
        m = mask_at(slot)
        wide = jnp.broadcast_to(m[:, None, :], (queries, QUERY_LENGTH, DL)).reshape(tokens, DL)
        e = jnp.exp(mm_nt(qemb[...], doc_at(slot)) * SCALE) * wide
        es[slot] = e
        total[...] = jnp.where(lane == d, jnp.sum(e, axis=1, keepdims=True), total[...])
        counts[...] = jnp.where(lane_q == d, jnp.sum(m, axis=1, keepdims=True), counts[...])

    each(forward)
    inside = lane_q < n_docs
    z = jnp.sum(jnp.log(1.0 + total[...]).reshape(queries, QUERY_LENGTH, 128), axis=1)
    z = z * (1.0 / QUERY_LENGTH)
    hot = jnp.zeros((queries, 128), F)
    row_q = lax.broadcasted_iota(jnp.int32, (queries, 128), 0)
    for q in range(queries):
        for s in range(ids.shape[0]):
            number = jnp.where(s < used[q], ids[s, q], 128)
            hot = jnp.where((row_q == q) & (lane_q == number), 1.0, hot)
    peak = jnp.max(jnp.where(inside, z, -1e30), axis=1, keepdims=True)
    power = jnp.where(inside, jnp.exp(jnp.where(inside, z - peak, 0.0)), 0.0)
    whole = jnp.sum(power, axis=1, keepdims=True)
    positive = jnp.sum(hot * power, axis=1, keepdims=True)
    loss = jnp.sum(jnp.log(whole) - jnp.log(positive))
    hits = jnp.sum(hot * counts[...])
    found = jnp.sum(hot)
    lane_p = lax.broadcasted_iota(jnp.int32, (8, 128), 1)
    parts[...] = jnp.where(
        lane_p == 0, loss, jnp.where(lane_p == 1, hits, jnp.where(lane_p == 2, found, 0.0))
    )
    d_z = power / whole - hot * power / positive
    d_wide = jnp.broadcast_to(d_z[:, None, :], (queries, QUERY_LENGTH, 128)).reshape(tokens, 128)
    c = d_wide * (SCALE / QUERY_LENGTH) / (1.0 + total[...])
    by_doc = jnp.transpose(c)[0:n_docs, :]
    coef[...] = jnp.zeros_like(coef)
    for half in range(tokens // 128):
        coef[:, half, :] = by_doc[:, 128 * half : 128 * half + 128]
    d_emb[...] = cot[...].astype(F)

    def backward(slot):
        column = jnp.sum(jnp.where(lane == place.doc(slot), c, 0.0), axis=1, keepdims=True)
        d_emb[...] += mm((es[slot] * column).astype(BF), doc_at(slot))

    each(backward)


def query_sims(fast, ids, used, qemb, cot, ins, n_docs):
    tokens, emb = qemb.shape
    queries = tokens // QUERY_LENGTH
    return pl.pallas_call(
        functools.partial(query_sims_kernel, fast, n_docs, len(ins)),
        out_shape=(
            sds((n_docs, 8, 128), F),
            sds((tokens, emb), F),
            sds((8, 128), F),
        ),
        in_specs=[SM] * 2 + [VM] * (2 + len(ins)),
        out_specs=[VM] * 3,
        scratch_shapes=[
            pltpu.VMEM((n_docs, tokens, DL), F),
            pltpu.VMEM((tokens, 128), F),
            pltpu.VMEM((queries, 128), F),
        ],
        compiler_params=pltpu.CompilerParams(vmem_limit_bytes=VMEM_LIMIT),
        cost_estimate=cost(n_docs * 67e6 * 10, n_docs * 1e6),
        name="query_sims",
    )(ids, used, qemb, cot, *ins)


def top_rows(d_emb, proj, h2, gain, wp):
    inv = lax.rsqrt(jnp.sum(proj * proj, axis=-1, keepdims=True) + EPS)
    along = jnp.sum(proj * d_emb, axis=-1, keepdims=True)
    d_proj = (inv * d_emb - proj * (inv * inv * inv) * along).astype(BF)
    d_h2, grad_gain = rms_back(h2, gain, mm_nt(d_proj, wp))
    return d_proj, d_h2, grad_gain


def back_kernel(
    fast, d_emb_in, demb, every, others, mask, rep, coef, d_emb_q, proj_d, proj_q, gf, gl, wp,
    h2_dh, h2_qh, n2_dh, n2_qh, n3_dh, n3_qh, wd_h, us_dh, us_qh, gv_dh, gv_qh, act_dh, act_qh,
    wg_h, wu_h, hid_dh, hid_qh, wo_h, li_dh, li_qh,
    d_hid, d_attn, g_out, g_gain, keep_h, send_h,
    h2, n2, n3, wd, us, gv, gate, up, act, wg, wu, hid, wo, li,
    n2t, d_proj, d_all, acc, d_n2, low_grads, down_grads, up_grads,
    sem_in, sem_tile, sem_last, sem_low, sem_out,
):
    place = Place(fast)
    count = demb.shape[0]
    rows = d_all.shape[0]

    def both(doc, query, target):
        return [(doc, target.at[0:count]), (query, target.at[count:])]

    loads = start_all(
        both(h2_dh, h2_qh, h2) + both(n2_dh, n2_qh, n2) + both(n3_dh, n3_qh, n3), sem_in
    )

    def tile_loads(t):
        cols = pl.ds(pl.multiple_of(t * 512, 512), 512)
        pairs = [
            (wd_h.at[cols], wd.at[cols]),
            (wg_h.at[:, cols], wg.at[:, cols]),
            (wu_h.at[:, cols], wu.at[:, cols]),
        ]
        for doc, query, target in ((us_dh, us_qh, us), (gv_dh, gv_qh, gv), (act_dh, act_qh, act)):
            pairs += both(doc.at[:, cols], query.at[:, cols], target.at[:, cols])
        return [pltpu.make_async_copy(src, dst, sem_tile.at[t, i]) for i, (src, dst) in enumerate(pairs)]

    def last_loads():
        pairs = both(hid_dh, hid_qh, hid) + [(wo_h, wo)] + both(li_dh, li_qh, li)
        return [pltpu.make_async_copy(src, dst, sem_last.at[i]) for i, (src, dst) in enumerate(pairs)]

    for copy in tile_loads(0):
        copy.start()
    acc[0:count, :] = d_emb_in[...].astype(F)
    acc[count:, :] = d_emb_q[...]
    per = 64 * QUERY_LENGTH // 256

    def sims(row, qb):
        line = jnp.concatenate([coef[row, 0:1, :], coef[row, 1:2, :]], axis=1)
        e = jnp.exp(mm_nt(demb[...], qb) * SCALE)
        first = pl.multiple_of((row // per) * 64, 64)
        here = mask[pl.ds(first, 64), :].astype(F).astype(BF)
        m = mm_tn(here, rep[:, pl.ds(pl.multiple_of((row % per) * 256, 256), 256)])
        acc[0:count, :] += mm((e * m * line).astype(BF), qb)

    if fast:
        for slot in range(8):
            where = slice(256 * (slot % 4), 256 * (slot % 4) + 256)
            sims(place.doc(slot), (every if slot < 4 else others)[where, :])
    else:

        def step(row, carry):
            sims(row, every[pl.ds(pl.multiple_of(row * 256, 256), 256), :])
            return carry

        lax.fori_loop(0, coef.shape[0], step, 0)
    wait_all(loads[0:2])
    g_gain[...] = jnp.zeros_like(g_gain)
    gain_l = row_of(gl)
    for at_rows, proj in ((slice(0, count), proj_d), (slice(count, rows), proj_q)):
        dp, dh, gg = top_rows(acc[at_rows, :], proj[...], h2[at_rows, :], gain_l, wp[...])
        d_proj[at_rows, :] = dp
        h2[at_rows, :] = dh
        g_gain[1:2, :] += gg
        d_all[at_rows, :] = dh.astype(BF)
    wait_all(loads[2:])
    n2t[...] = jnp.transpose(n2[...])
    gp = mm_tn(n3[...], d_proj[...])
    low_grads[...] = jnp.zeros_like(low_grads)
    for w in range(8):
        for r in range(3):
            first = 96 * w + 32 * r
            low_grads[w % 2, w // 2, r // 2, r % 2, :, 0:128] = gp[first : first + 32, :].astype(BF)
    below = pl.ds(192, 32)
    low = start_all(
        (
            (low_grads.at[place.own], keep_h.at[:, :, :, below]),
            (low_grads.at[1 - place.own], send_h.at[:, :, :, below]),
        ),
        sem_low,
    )
    d_n2[...] = jnp.zeros_like(d_n2)

    def outputs(t, slot):
        copies = []
        for i, (core, target) in enumerate(((place.own, keep_h), (1 - place.own, send_h))):
            copies.append(
                pltpu.make_async_copy(
                    down_grads.at[slot, core], target.at[t, :, :, pl.ds(0, 192)], sem_out.at[slot, 3 * i]
                )
            )
            start = pl.multiple_of(224 + (t % 2) * 192, 32)
            for base in range(2):
                copies.append(
                    pltpu.make_async_copy(
                        up_grads.at[slot, base, core],
                        target.at[:, base, t // 2, pl.ds(start, 192)],
                        sem_out.at[slot, 3 * i + 1 + base],
                    )
                )
        return copies

    def tile(t, carry):
        slot = t % 2
        cols = pl.ds(pl.multiple_of(t * 512, 512), 512)

        @pl.when(t >= 2)
        def _():
            wait_all(outputs(t - 2, slot))

        @pl.when(t < 3)
        def _():
            for copy in tile_loads(t + 1):
                copy.start()

        @pl.when(t == 3)
        def _():
            for copy in last_loads():
                copy.start()

        wait_all(tile_loads(t))
        d_act = mm_nt(d_all[...], wd[cols, :])
        gate[...] = (d_act * us[:, cols].astype(F)).astype(BF)
        up[...] = (d_act * gv[:, cols].astype(F)).astype(BF)
        for half in range(2):
            first = pl.multiple_of((2 * t + half) * 256, 256)
            g = mm_tn(act[:, pl.ds(first, 256)], d_all[...])
            for r in range(4):
                for c in range(3):
                    down_grads[slot, half, r // 2, r % 2, 64 * c : 64 * c + 64, :] = g[
                        64 * r : 64 * r + 64, 256 * c : 256 * c + 256
                    ].astype(BF)
        for base, source in ((0, gate), (1, up)):
            g = mm(n2t[...], source[...]).astype(BF)
            for c in range(2):
                for w in range(8):
                    up_grads[slot, base, w % 2, w // 2, 96 * c : 96 * c + 96, :] = g[
                        96 * w : 96 * w + 96, 256 * c : 256 * c + 256
                    ]
        for copy in outputs(t, slot):
            copy.start()
        d_n2[...] += mm_nt(gate[...], wg[:, cols]) + mm_nt(up[...], wu[:, cols])
        return carry

    lax.fori_loop(0, 4, tile, 0)
    wait_all(last_loads())
    gain_f = row_of(gf)

    def through(at_rows):
        dm, gg = rms_back(hid[at_rows, :], gain_f, d_n2[at_rows, :])
        total = h2[at_rows, :] + dm
        d_hid[at_rows, :] = total
        g_gain[0:1, :] += gg
        d_attn[at_rows, :] = total.astype(BF)

    rows_loop(rows, 256, through)

    def to_context(at_rows):
        d_context = mm_nt(d_attn[at_rows, :], wo[...]).astype(BF).astype(F)
        g_out[at_rows, :] = (d_context * li[at_rows, :]).astype(BF)

    rows_loop(rows, 256, to_context)
    wait_all(low)
    for t in (2, 3):
        wait_all(outputs(t, t % 2))


def back(fast, d_emb, demb, every, others, mask, rep, coef, d_emb_q, dsaved, qsaved, gains, weights):
    wq, wk, wv, wo, wg, wu, wd, wp = weights
    count, width = dsaved["h2"].shape
    rows = count + d_emb_q.shape[0]
    hidden = wd.shape[0]
    emb = wp.shape[1]
    piece = sds((4, 2, 2, 608, 256), BF)

    def both(name):
        return dsaved[name], qsaved[name]

    return pl.pallas_call(
        functools.partial(back_kernel, fast),
        out_shape=(
            sds((rows, width), F),
            sds((rows, width), BF),
            sds((rows, width), BF),
            sds((8, width), F),
            piece,
            piece,
        ),
        in_specs=[VM] * 13 + [ANY] * 20,
        out_specs=[VM] * 4 + [ANY] * 2,
        scratch_shapes=[
            pltpu.VMEM((rows, width), F),
            pltpu.VMEM((rows, width), BF),
            pltpu.VMEM((rows, width), BF),
            pltpu.VMEM(wd.shape, BF),
            pltpu.VMEM((rows, hidden), BF),
            pltpu.VMEM((rows, hidden), BF),
            pltpu.VMEM((rows, 512), BF),
            pltpu.VMEM((rows, 512), BF),
            pltpu.VMEM((rows, hidden), BF),
            pltpu.VMEM(wg.shape, BF),
            pltpu.VMEM(wu.shape, BF),
            pltpu.VMEM((rows, width), F),
            pltpu.VMEM(wo.shape, BF),
            pltpu.VMEM((rows, width), F),
            pltpu.VMEM((width, rows), BF),
            pltpu.VMEM((rows, emb), BF),
            pltpu.VMEM((rows, width), BF),
            pltpu.VMEM((rows, emb), F),
            pltpu.VMEM((rows, width), F),
            pltpu.VMEM((2, 4, 2, 2, 32, 256), BF),
            pltpu.VMEM((2, 2, 2, 2, 192, 256), BF),
            pltpu.VMEM((2, 2, 2, 4, 192, 256), BF),
            pltpu.SemaphoreType.DMA((6,)),
            pltpu.SemaphoreType.DMA((4, 9)),
            pltpu.SemaphoreType.DMA((5,)),
            pltpu.SemaphoreType.DMA((2,)),
            pltpu.SemaphoreType.DMA((2, 6)),
        ],
        compiler_params=pltpu.CompilerParams(vmem_limit_bytes=VMEM_LIMIT),
        cost_estimate=cost(14e9, 10e6),
        name="back",
    )(
        d_emb, demb, every, others, mask, rep, coef, d_emb_q, *both("proj"), gains[1], gains[2], wp,
        *both("h2"), *both("n2"), *both("n3"), wd, *both("us"), *both("gv"), *both("act"), wg, wu,
        *both("hid"), wo, *both("li"),
    )


def attn_back_kernel(
    first, n_pairs, with_queries, hot, g_h, q_d, q_q, k_d, k_q, v_d, v_q, lr_d, lr_q, p_dh, p_qh, *refs
):
    n_outs = 7 if with_queries else 4
    outs = refs[-n_outs - 15 : -15]
    (
    q, k, v, g, p_d, p_q, lrd, lrq, ds, acc, sums, sem_in, sem_p, qq, gq,
    ) = refs[-15:]
    dq, dk, dv, g_rel = outs[:4]
    count = q_d.shape[0]
    rest = q_q.shape[0]
    blocks = count // 128
    heads_here = pl.ds(2 * first, 2 * n_pairs)
    lanes_here = pl.ds(128 * first, 128 * n_pairs)
    pairs = []
    if with_queries:
        pairs += [
            (v_q, qq.at[2]),
            (g_h.at[count:], gq),
            (p_qh, p_q),
            (lr_q, lrq),
            (q_q, qq.at[0]),
            (k_q, qq.at[1]),
        ]
    n_query = len(pairs)
    pairs += [
        (v_d.at[:, lanes_here], v),
        (g_h.at[0:count, lanes_here], g),
        (lr_d.at[heads_here], lrd),
        (q_d.at[:, lanes_here], q),
        (k_d.at[:, lanes_here], k),
    ]
    loads = start_all(pairs, sem_in)

    def p_load(pair):
        return pltpu.make_async_copy(
            p_dh.at[pl.ds(2 * (first + pair), 2)], p_d.at[pl.ds(2 * pair, 2)], sem_p.at[pair]
        )

    p_load(0).start()
    low, high, _, _ = half_masks()
    keeps = (low.astype(BF), high.astype(BF))
    acc[...] = jnp.zeros_like(acc)
    wait_all(loads[:n_query])

    if with_queries:
        cells_q = rest // 128
        heads = p_q.shape[0]
        rows_q = [slice(128 * b, 128 * b + 128) for b in range(cells_q)]
        lanes_of = [slice(128 * pair, 128 * pair + 128) for pair in range(heads // 2)]
        for group in range(0, heads // 2, 3):
            cells = [
                (pair, e, b) for pair in range(group, group + 3) for e in range(2) for b in range(cells_q)
            ]
            d_ps = [
                mm_nt(qq[2, rows_q[b], lanes_of[pair]] * keeps[e], gq[rows_q[b], lanes_of[pair]])
                for pair, e, b in cells
            ]
            dss = []
            for d_p, (pair, e, b) in zip(d_ps, cells):
                head = 2 * pair + e
                pf = p_q[head, rows_q[b], :].astype(F)
                t = pf * d_p
                share = lrq[head, :, rows_q[b]] * jnp.sum(t, axis=0, keepdims=True)
                d_s = t - pf * share
                acc[head, :, 128:256] += d_s
                dss.append(d_s.astype(BF))
            for pair in range(group, group + 3):
                lanes = lanes_of[pair]
                for b in range(cells_q):
                    rows = rows_q[b]
                    at_cell = [cells.index((pair, e, b)) for e in range(2)]
                    probs = [p_q[2 * pair + e, rows, :] for e in range(2)]
                    parts = [
                        (
                            mm_tn(dss[at_cell[e]], qq[1, rows, lanes] * keeps[e]),
                            mm(dss[at_cell[e]], qq[0, rows, lanes] * keeps[e]),
                            mm(probs[e], gq[rows, lanes] * keeps[e]),
                        )
                        for e in range(2)
                    ]
                    for i in range(3):
                        outs[4 + i][rows, lanes] = (parts[0][i] + parts[1][i]).astype(BF)
    wait_all(loads[n_query:])

    def doc_pair(pair, carry):
        lanes = pl.ds(pl.multiple_of(pair * 128, 128), 128)

        @pl.when(pair + 1 < n_pairs)
        def _():
            p_load(pair + 1).start()

        p_load(pair).wait()
        q2 = q[:, lanes]
        k2 = k[:, lanes]
        v2 = v[:, lanes]
        g2 = g[:, lanes]
        d_ps = [mm_nt(v2 * keep, g2) for keep in keeps]
        sides = []
        for e, keep in enumerate(keeps):
            head = 2 * pair + e
            acc_head = 2 * (first + pair) + e if with_queries else head
            for i in range(blocks):
                cols = slice(128 * i, 128 * i + 128)
                pfs = [p_d[head, 128 * j : 128 * j + 128, cols].astype(F) for j in range(blocks)]
                ts = [pfs[j] * d_ps[e][128 * j : 128 * j + 128, cols] for j in range(blocks)]
                total = functools.reduce(jnp.add, ts)
                share = lrd[head, :, cols] * jnp.sum(total, axis=0, keepdims=True)
                for j in range(blocks):
                    d_s = ts[j] - pfs[j] * share
                    t = 1 - (j - i)
                    tile = t if abs(j - i) <= 1 else (3 if j > i else 4)
                    acc[acc_head, :, 128 * tile : 128 * tile + 128] += d_s
                    ds[e, 128 * j : 128 * j + 128, cols] = d_s.astype(BF)
            sides.append(
                (
                    mm_tn(ds[e], k2 * keep),
                    mm(ds[e], q2 * keep),
                    mm(p_d[head], g2 * keep),
                )
            )
        dq[:, lanes] = (sides[0][0] + sides[1][0]).astype(BF)
        dk[:, lanes] = (sides[0][1] + sides[1][1]).astype(BF)
        dv[:, lanes] = (sides[0][2] + sides[1][2]).astype(BF)
        return carry

    lax.fori_loop(0, n_pairs, doc_pair, 0)
    sums[...] = jnp.zeros_like(sums)
    n_heads = acc.shape[0]
    lane = lax.broadcasted_iota(jnp.int32, (n_heads, TABLE), 1)

    def left(values, by):
        flat = values.reshape(-1, TABLE)
        return pltpu.roll(flat, TABLE - by, 1).reshape(values.shape)

    near = jnp.concatenate([acc[:, :, 0:384], jnp.zeros((n_heads, 128, 128), F)], axis=2)
    folded = near[:, 0:8]
    for group in range(1, 16):
        folded = folded + left(near[:, 8 * group : 8 * group + 8], 8 * group)
    row = lax.broadcasted_iota(jnp.int32, (n_heads, 8, TABLE), 1)
    lines = folded
    for i in range(1, 8):
        lines = jnp.where(row == i, left(folded, i), lines)
    lines = jnp.sum(lines, axis=1)
    after = jnp.sum(jnp.sum(acc[:, :, 384:512], axis=1), axis=1, keepdims=True)
    before = jnp.sum(jnp.sum(acc[:, :, 512:640], axis=1), axis=1, keepdims=True)
    lines = lines + jnp.where(lane == 0, after, jnp.where(lane == 256, before, 0.0))
    offset = 0 if with_queries else 2 * first
    sums[offset : offset + n_heads, :] = lines
    g_rel[...] = lax.dot_general(
        sums[...], hot[...], (((1,), (1,)), ((), ())),
        preferred_element_type=F, precision=lax.Precision.HIGHEST,
    )


def attn_back(first, n_pairs, with_queries, g, dsaved, qsaved, hot, after):
    rows, width = g.shape
    heads = dsaved["p"].shape[0]
    buckets = hot.shape[0]
    count = dsaved["q"].shape[0]
    rest = rows - count
    columns = 128 * n_pairs
    both = []
    for name in ("q", "k", "v", "lr", "p"):
        both += [dsaved[name], qsaved[name]]
    outs = (sds((count, columns), BF),) * 3 + (sds((16, buckets), F),)
    if with_queries:
        outs = outs + (sds((rest, width), BF),) * 3
    return pl.pallas_call(
        functools.partial(attn_back_kernel, first, n_pairs, with_queries),
        out_shape=outs,
        in_specs=[VM] + [ANY] * (11 + len(after)),
        out_specs=[VM] * len(outs),
        scratch_shapes=[pltpu.VMEM((count, columns), BF)] * 4
        + [
            pltpu.VMEM((2 * n_pairs, DL, DL), BF),
            pltpu.VMEM((heads, rest, 128), BF),
            pltpu.VMEM((2 * n_pairs, 1, count), F),
            pltpu.VMEM((heads, 1, rest), F),
            pltpu.VMEM((2, DL, DL), BF),
            pltpu.VMEM((heads if with_queries else 2 * n_pairs, 128, 640), F),
            pltpu.VMEM((16, TABLE), F),
            pltpu.SemaphoreType.DMA((11,)),
            pltpu.SemaphoreType.DMA((n_pairs,)),
            pltpu.VMEM((3, rest, width), BF),
            pltpu.VMEM((rest, width), BF),
        ],
        compiler_params=pltpu.CompilerParams(vmem_limit_bytes=VMEM_LIMIT),
        cost_estimate=cost(15e9, 40e6),
        name="attn_back_%d" % first,
    )(hot, g, *both, *after)


SMALL = 48


def split_small(values):
    high = values.astype(BF)
    return jnp.concatenate([high, (values - high.astype(F)).astype(BF)], axis=1)


def join_small(rows):
    return rows[:, 0:128].astype(F) + rows[:, 128:256].astype(F)


def attn_parts(first, second, targets):
    half = first[0].shape[1]
    count = first[0].shape[0]
    pairs = []
    for i, target in enumerate(targets):
        pairs += [
            (first[i], target.at[0:count, 0:half]),
            (second[i], target.at[0:count, half:]),
            (first[4 + i], target.at[count:]),
        ]
    return pairs


def attn_grads_kernel(fast, *refs):
    ins, (d_attn_h, n1_d, n1_q, ctx_d, ctx_q) = refs[:9], refs[9:14]
    keep_h, send_h, dq, dk, dv, d_attn, n1, ctx, grads, sem_in, sem_out = refs[-11:]
    first = ins[0:3] + (None,) + ins[3:6]
    place = Place(fast)
    count = n1_d.shape[0]
    pairs = [
        (n1_d, n1.at[0:count]),
        (n1_q, n1.at[count:]),
        *attn_parts(first, ins[6:9], (dq, dk, dv)),
        (d_attn_h, d_attn),
        (ctx_d, ctx.at[0:count]),
        (ctx_q, ctx.at[count:]),
    ]
    loads = start_all(pairs, sem_in)
    targets = ((place.own, keep_h), (1 - place.own, send_h))
    outs = []
    wait_all(loads[0:2])
    groups = (loads[2:5], loads[5:8], loads[8:11], loads[11:14])
    for which, (left, right) in enumerate(((n1, dq), (n1, dk), (n1, dv), (ctx, d_attn))):
        wait_all(groups[which])
        value = mm_tn(left[...], right[...]).astype(BF)
        for w in range(8):
            for c in range(3):
                row = ((w // 2) * 4 + which) * 288 + 96 * c
                grads[w % 2, row : row + 96, :] = value[96 * w : 96 * w + 96, 256 * c : 256 * c + 256]
        for z in range(4):
            rows = slice((z * 4 + which) * 288, (z * 4 + which) * 288 + 288)
            for i, (core, target) in enumerate(targets):
                copy = pltpu.make_async_copy(
                    grads.at[core, rows], target.at[rows], sem_out.at[which, z, i]
                )
                copy.start()
                outs.append(copy)
    wait_all(outs)


def attn_grads(fast, first, second, d_attn, dsaved, qsaved, after):
    rows, width = d_attn.shape
    piece = sds((16 * 288, 256), BF)
    ins = (*first[0:3], *first[4:7], *second[0:3])
    return pl.pallas_call(
        functools.partial(attn_grads_kernel, fast),
        out_shape=(piece, piece),
        in_specs=[ANY] * (14 + len(after)),
        out_specs=[ANY] * 2,
        scratch_shapes=[pltpu.VMEM((rows, width), BF)] * 6
        + [
            pltpu.VMEM((2,) + piece.shape, BF),
            pltpu.SemaphoreType.DMA((14,)),
            pltpu.SemaphoreType.DMA((4, 4, 2)),
        ],
        compiler_params=pltpu.CompilerParams(vmem_limit_bytes=VMEM_LIMIT),
        cost_estimate=cost(1, 1),
        name="attn_grads",
    )(*ins, d_attn, dsaved["n1"], qsaved["n1"], dsaved["ctx"], qsaved["ctx"], *after)


def input_back_kernel(ga, gains, parts, rel_0, rel_1, *refs):
    ins, (wq_h, wk_h, wv_h, tok_d, tok_q, d_hid_h) = refs[:9], refs[9:15]
    out_dh, out_qh, small = refs[-16:-13]
    dq, dk, dv, wq, wk, wv, tok, d_hid, d_n1, out, g_gain, sem_in, sem_out = refs[-13:]
    first = ins[0:3] + (None,) + ins[3:6]
    count = tok_d.shape[0]
    parts_q = attn_parts(first, ins[6:9], (dq, dk, dv))
    groups = (
        [*parts_q[0:3], (wq_h, wq)],
        [*parts_q[3:6], (wk_h, wk)],
        [*parts_q[6:9], (wv_h, wv)],
        [
            (tok_d, tok.at[0:count]),
            (tok_q, tok.at[count:]),
            (d_hid_h, d_hid),
        ],
    )
    loads = [start_all(groups[0], sem_in.at[0])]
    gain_a = row_of(ga)
    g_gain[...] = jnp.zeros_like(g_gain)
    for i, (left, right) in enumerate(((dq, wq), (dk, wk), (dv, wv))):
        loads.append(start_all(groups[i + 1], sem_in.at[i + 1]))
        wait_all(loads[i])
        part = mm_nt(left[...], right[...])
        d_n1[...] = part if i == 0 else d_n1[...] + part
    wait_all(loads[3])

    def step(rows):
        d_in, gg = rms_back(tok[rows, :].astype(F), gain_a, d_n1[rows, :])
        g_gain[0:1, :] += gg
        out[rows, :] = (d_hid[rows, :] + d_in).astype(BF)

    rows_loop(tok.shape[0], 256, step)
    outs = start_all(((out.at[0:count], out_dh), (out.at[count:], out_qh)), sem_out)
    small[...] = jnp.zeros_like(small)
    rows = (
        g_gain[0:1, :],
        gains[0:1, :],
        gains[1:2, :],
    )
    for i, row in enumerate(rows):
        for c in range(6):
            small[8 * i + c : 8 * i + c + 1, :] = row[:, 128 * c : 128 * c + 128]
    small[24:25, :] = parts[0:1, :]
    small[32:48, 0 : rel_0.shape[1]] = rel_0[...] + rel_1[...]
    wait_all(outs)


def input_back(tok_d, tok_q, d_hid, gain, gains, parts, first, second, weights, after):
    count, width = tok_d.shape
    rows = count + tok_q.shape[0]
    ins = (*first[0:3], *first[4:7], *second[0:3])
    return pl.pallas_call(
        input_back_kernel,
        out_shape=(sds(tok_d.shape, BF), sds(tok_q.shape, BF), sds((SMALL, 128), F)),
        in_specs=[VM] * 5 + [ANY] * (15 + len(after)),
        out_specs=[ANY] * 2 + [VM],
        scratch_shapes=[pltpu.VMEM((rows, width), BF)] * 3
        + [pltpu.VMEM((width, width), BF)] * 3
        + [
            pltpu.VMEM((rows, width), BF),
            pltpu.VMEM((rows, width), F),
            pltpu.VMEM((rows, width), F),
            pltpu.VMEM((rows, width), BF),
            pltpu.VMEM((8, width), F),
            pltpu.SemaphoreType.DMA((4, 4)),
            pltpu.SemaphoreType.DMA((2,)),
        ],
        compiler_params=pltpu.CompilerParams(vmem_limit_bytes=VMEM_LIMIT),
        cost_estimate=cost(1, 1),
        name="input_back",
    )(
        gain, gains, parts, first[3], second[3], *ins, weights[0], weights[1], weights[2],
        tok_d, tok_q, d_hid, *after,
    )


def unpack_kernel(which, own, one, two, three, *refs):
    stack = refs[-1]
    outs = refs[-5:-1]
    place = Place(True)
    half = own.shape[1]
    for m, part in enumerate((own, one, two, three)):
        for i in range(2):
            stack[place.rep ^ m, half * i : half * i + half, :] = part[i]
    if which == "attn":
        for r in range(4):
            for c in range(3):
                outs[r][:, 256 * c : 256 * c + 256] = stack[
                    r, 96 * c : 96 * c + 96, :
                ].astype(F)
        return
    for r in range(4):
        for c in range(4):
            first = (r % 2) * 1024 + 256 * c
            outs[r // 2][:, first : first + 256] = stack[
                r, 224 + 96 * c : 224 + 96 * c + 96, :
            ].astype(F)
        for c in range(3):
            outs[2][64 * r : 64 * r + 64, 256 * c : 256 * c + 256] = stack[
                r, 64 * c : 64 * c + 64, :
            ].astype(F)
    for r in range(3):
        outs[3][32 * r : 32 * r + 32, :] = stack[r, 192:224, 0:128].astype(F)


def unpack(which, parts, shapes, after):
    return pl.pallas_call(
        functools.partial(unpack_kernel, which),
        out_shape=tuple(sds(s, F) for s in shapes),
        in_specs=[VM] * 4 + [ANY] * len(after),
        out_specs=tuple(VM for _ in shapes),
        scratch_shapes=[pltpu.VMEM((4, 2 * parts[0].shape[1], parts[0].shape[2]), BF)],
        compiler_params=pltpu.CompilerParams(vmem_limit_bytes=16 * 1024 * 1024),
        cost_estimate=cost(1e6, 3e6),
        name="unpack_" + which,
    )(*parts, *after)


def swap(values, axis, size, mask):
    return lax.ppermute(values, axis, [(i, i ^ mask) for i in range(size)])


def near_kernel(keep_h, came_h, *refs):
    send_a, send_b, kept, came, sems = refs[-5:]
    place = Place(True)
    half = send_a.shape[2]
    y, x = place.y, place.x
    loads = []
    for z in range(4):
        pairs = []
        for i, (source, target) in enumerate(((keep_h, kept), (came_h, came))):
            pairs += [
                (source.at[z, :, 1 - x, pl.ds(0, half)], target.at[0, z]),
                (source.at[z, 1 - y, :, pl.ds(half, half)], target.at[1, z]),
            ]
        loads.append(start_all(pairs, sems.at[z]))
    for z in range(4):
        wait_all(loads[z])
        send_a[z] = kept[0, z] + came[0, z]
        send_b[z] = kept[1, z] + came[1, z]


def own_kernel(keep_h, came_h, *refs):
    own_a, own_b, kept, came, sems = refs[-5:]
    place = Place(True)
    half = own_a.shape[2]
    y, x = place.y, place.x
    loads = []
    for z in range(4):
        pairs = []
        for i, (source, target) in enumerate(((keep_h, kept), (came_h, came))):
            pairs += [
                (source.at[z, :, x, pl.ds(0, half)], target.at[0, z]),
                (source.at[z, y, :, pl.ds(half, half)], target.at[1, z]),
            ]
        loads.append(start_all(pairs, sems.at[z]))
    for z in range(4):
        wait_all(loads[z])
        own_a[z] = kept[0, z] + came[0, z]
        own_b[z] = kept[1, z] + came[1, z]


def cross_kernel(a, came_a, b, came_b, *refs):
    send_a, send_b, own_a, own_b = refs[-4:]
    place = Place(True)
    y, x = place.y, place.x
    for z in range(4):
        send_a[z] = a[z, 1 - y] + came_a[z, 1 - y]
        own_a[z] = a[z, y] + came_a[z, y]
        send_b[z] = b[z, 1 - x] + came_b[z, 1 - x]
        own_b[z] = b[z, x] + came_b[z, x]


def line_kernel(a, came_a, b, came_b, *refs):
    send, own = refs[-2:]
    z = Place(True).z
    for i in range(2):
        for out, to in ((own, z ^ (2 * i)), (send, z ^ 1 ^ (2 * i))):
            out[i, 0] = a[to] + came_a[to]
            out[i, 1] = b[to] + came_b[to]


def next_kernel(own, came, *refs):
    send, out = refs[-2:]
    out[...] = own[0] + came[0]
    send[...] = own[1] + came[1]


def far_kernel(own, came, *refs):
    refs[-1][...] = own[...] + came[...]


def cell(index, half, first=0):
    return pl.ds(pl.multiple_of(index * half + first, 16), half)


def attn_near_kernel(keep_h, came_h, small_a, small_b, *refs):
    send_a, send_b, small, kept, came, sems = refs[-6:]
    place = Place(True)
    half = send_b.shape[2]
    loads = split_loads(keep_h, came_h, kept, came, sems, half, 1 - place.x, 1 - place.y)
    value = split_small(small_a[...] + small_b[...])
    send_a[8 * half :, :] = value
    small[...] = value
    for z in range(4):
        wait_all(loads[z])
        for i in range(2):
            send_a[cell(z * 2 + i, half), :] = kept[0, z, i] + came[0, z, i]
        send_b[z] = kept[1, z] + came[1, z]


def split_loads(keep_h, came_h, kept, came, sems, half, x, y):
    def rows(z, y, x, first):
        return pl.ds(pl.multiple_of(((z * 2 + y) * 2 + x) * 2 * half + first, 16), half)

    loads = []
    for z in range(4):
        pairs = []
        for source, target in ((keep_h, kept), (came_h, came)):
            for i in range(2):
                pairs += [
                    (source.at[rows(z, i, x, 0)], target.at[0, z, i]),
                    (source.at[rows(z, y, i, half)], target.at[1, z, i]),
                ]
        loads.append(start_all(pairs, sems.at[z]))
    return loads


def attn_own_kernel(keep_h, came_h, *refs):
    own_a, own_b, kept, came, sems = refs[-5:]
    place = Place(True)
    half = own_a.shape[2]
    loads = split_loads(keep_h, came_h, kept, came, sems, half, place.x, place.y)
    for z in range(4):
        wait_all(loads[z])
        own_a[z] = kept[0, z] + came[0, z]
        own_b[z] = kept[1, z] + came[1, z]


def attn_cross_kernel(a, came_a, b, came_b, small_in, *refs):
    send_a, send_b, own_a, own_b, small = refs[-5:]
    place = Place(True)
    half = a.shape[2]
    y, x = place.y, place.x
    for z in range(4):
        send_a[cell(z, half), :] = a[z, 1 - y] + came_a[cell(z * 2 + 1 - y, half), :]
        own_a[z] = a[z, y] + came_a[cell(z * 2 + y, half), :]
        send_b[z] = b[z, 1 - x] + came_b[z, 1 - x]
        own_b[z] = b[z, x] + came_b[z, x]
    value = split_small(join_small(small_in[...]) + join_small(came_a[8 * half :, :]))
    send_a[4 * half :, :] = value
    small[...] = value


def attn_line_kernel(a, came_a, b, came_b, small_in, *refs):
    send, own, small = refs[-3:]
    z = Place(True).z
    half = a.shape[1]
    for i in range(2):
        for out, to in ((own, z ^ (2 * i)), (send, z ^ 1 ^ (2 * i))):
            out[2 * half * i : 2 * half * i + half, :] = a[to] + came_a[cell(to, half), :]
            out[2 * half * i + half : 2 * half * i + 2 * half, :] = b[to] + came_b[to]
    value = split_small(join_small(small_in[...]) + join_small(came_a[4 * half :, :]))
    send[4 * half :, :] = value
    small[...] = value


def attn_next_kernel(own, came, small_in, *refs):
    send, out, small = refs[-3:]
    rows = out.shape[0]
    out[...] = own[0:rows, :] + came[0:rows, :]
    send[0:rows, :] = own[rows : 2 * rows, :] + came[rows : 2 * rows, :]
    value = split_small(join_small(small_in[...]) + join_small(came[2 * rows :, :]))
    send[rows:, :] = value
    small[...] = value


def attn_far_kernel(heads, total_queries, own, came, small_in, *refs):
    out, gain_a, gain_f, gain_l, rel, loss, fraction = refs[-7:]
    rows = own.shape[0]
    for i in range(2):
        half = slice(rows // 2 * i, rows // 2 * (i + 1))
        out[i] = own[half, :] + came[half, :]
    total = join_small(small_in[...]) + join_small(came[rows:, :])
    for i, gain in enumerate((gain_a, gain_f, gain_l)):
        row = jnp.concatenate([total[8 * i + c : 8 * i + c + 1, :] for c in range(6)], axis=1)
        gain[...] = row.reshape(gain.shape[0])
    rel[...] = total[32 : 32 + heads, 0 : rel.shape[1]]
    lane = lax.broadcasted_iota(jnp.int32, (1, 128), 1)
    line = total[24:25, :]
    loss_sum, hits, found = (jnp.sum(jnp.where(lane == i, line, 0.0)) for i in range(3))
    loss[0, 0] = loss_sum / total_queries
    fraction[0, 0] = hits / (DL * found)


def stage(kernel, name, ins, outs, after, flops=1, scratch=(), scalars=0, limit=16):
    return pl.pallas_call(
        kernel,
        out_shape=outs,
        in_specs=[VM] * len(ins) + [ANY] * len(after),
        out_specs=[VM] * (len(outs) - scalars) + [SM] * scalars,
        scratch_shapes=list(scratch),
        compiler_params=pltpu.CompilerParams(vmem_limit_bytes=limit * 1024 * 1024),
        cost_estimate=cost(flops, 1),
        name=name,
    )(*ins, *after)


class AttnReduction:
    def __init__(self, keep, send):
        self.half = 144
        self.keep = keep
        self.came = swap(send, "wide", 8, 1)
        self.small_shape = sds((SMALL, 256), BF)

    def rows(self, cells):
        return sds((cells * self.half + SMALL, 256), BF)

    def split(self, kernel, name, ins, outs, after):
        held = pltpu.VMEM((2, 4, 2, self.half, 256), BF)
        scratch = [held, held, pltpu.SemaphoreType.DMA((4, 8))]
        return pl.pallas_call(
            kernel,
            out_shape=outs,
            in_specs=[ANY] * 2 + [VM] * len(ins) + [ANY] * len(after),
            out_specs=(VM,) * len(outs),
            scratch_shapes=scratch,
            compiler_params=pltpu.CompilerParams(vmem_limit_bytes=VMEM_LIMIT),
            cost_estimate=cost(1, 1),
            name=name,
        )(self.keep, self.came, *ins, *after)

    def near(self, small, after):
        outs = (self.rows(8), sds((4, 2, self.half, 256), BF), self.small_shape)
        ins = (small, swap(small, "wide", 8, 1))
        send_a, send_b, self.small = self.split(attn_near_kernel, "near_attn", ins, outs, after)
        self.came_a = swap(send_a, "rep", 4, 1)
        self.came_b = swap(send_b, "rep", 4, 2)
        return (send_a,)

    def mine(self, after):
        own = sds((4, 2, self.half, 256), BF)
        self.a, self.b = self.split(attn_own_kernel, "own_attn", (), (own, own), after)
        return (self.a,)

    def cross(self, after):
        own = sds((4, self.half, 256), BF)
        outs = (self.rows(4), own, own, own, self.small_shape)
        ins = (self.a, self.came_a, self.b, self.came_b, self.small)
        send_a, send_b, self.a, self.b, self.small = stage(attn_cross_kernel, "cross_attn", ins, outs, after)
        self.came_a = swap(send_a, "rep", 4, 2)
        self.came_b = swap(send_b, "rep", 4, 1)
        return (self.a,)

    def line(self, after):
        own = sds((4 * self.half, 256), BF)
        outs = (self.rows(4), own, self.small_shape)
        ins = (self.a, self.came_a, self.b, self.came_b, self.small)
        send, self.own, self.small = stage(attn_line_kernel, "line_attn", ins, outs, after)
        self.came = swap(send, "wide", 8, 2)
        return (self.own,)

    def next(self, after):
        own = sds((2 * self.half, 256), BF)
        ins = (self.own, self.came, self.small)
        outs = (self.rows(2), own, self.small_shape)
        send, self.own, self.small = stage(attn_next_kernel, "next_attn", ins, outs, after)
        self.came = swap(send, "wide", 8, 4)
        return (self.own,)

    def far(self, heads, buckets, width, total_queries, after):
        outs = (sds((2, self.half, 256), BF),) + (sds((width,), F),) * 3
        outs = outs + (sds((heads, buckets), F), sds((1, 1), F), sds((1, 1), F))
        self.own, *results = stage(
            functools.partial(attn_far_kernel, heads, float(total_queries)), "far_attn",
            (self.own, self.came, self.small), outs, after, scalars=2,
        )
        self.came = [swap(self.own, "rep", 4, m) for m in (1, 2, 3)]
        return results

    def parts(self):
        return self.own, *self.came


class Reduction:
    def __init__(self, name, keep, send):
        self.name = name
        self.half = keep.shape[3] // 2
        self.keep = keep
        self.came = swap(send, "wide", 8, 1)

    def split(self, kernel, name, ins, shapes, specs, after):
        held = pltpu.VMEM((2, 4, 2, self.half, 256), BF)
        return pl.pallas_call(
            kernel,
            out_shape=tuple(sds(shape, BF) for shape in shapes),
            in_specs=[ANY] * 2 + specs + [ANY] * len(after),
            out_specs=(VM,) * len(shapes),
            scratch_shapes=[held, held, pltpu.SemaphoreType.DMA((4, 4))],
            compiler_params=pltpu.CompilerParams(vmem_limit_bytes=VMEM_LIMIT),
            cost_estimate=cost(1, 1),
            name=name + self.name,
        )(self.keep, self.came, *ins, *after)

    def near(self, after):
        shape = (4, 2, self.half, 256)
        send_a, send_b = self.split(near_kernel, "near_", (), (shape,) * 2, [], after)
        self.came_a = swap(send_a, "rep", 4, 1)
        self.came_b = swap(send_b, "rep", 4, 2)
        return (send_a,)

    def step(self, kernel, name, ins, shapes, after, flops=1):
        outs = tuple(sds(shape, BF) for shape in shapes)
        return stage(kernel, name + self.name, ins, outs, after, flops, limit=20)

    def mine(self, after):
        shape = (4, 2, self.half, 256)
        self.a, self.b = self.split(own_kernel, "own_", (), (shape,) * 2, [], after)
        return (self.a,)

    def cross(self, after):
        shape = (4, self.half, 256)
        ins = (self.a, self.came_a, self.b, self.came_b)
        send_a, send_b, self.a, self.b = self.step(cross_kernel, "cross_", ins, (shape,) * 4, after)
        self.came_a = swap(send_a, "rep", 4, 2)
        self.came_b = swap(send_b, "rep", 4, 1)
        return (self.a,)

    def line(self, after, flops=1):
        ins = (self.a, self.came_a, self.b, self.came_b)
        shape = (2, 2, self.half, 256)
        send, self.own = self.step(line_kernel, "line_", ins, (shape,) * 2, after, flops)
        self.came = swap(send, "wide", 8, 2)
        return (self.own,)

    def next(self, after):
        shape = (2, self.half, 256)
        send, self.own = self.step(next_kernel, "next_", (self.own, self.came), (shape,) * 2, after)
        self.came = swap(send, "wide", 8, 4)
        return (self.own,)

    def far(self, after):
        shape = (2, self.half, 256)
        (self.own,) = self.step(far_kernel, "far_", (self.own, self.came), (shape,), after)
        self.came = [swap(self.own, "rep", 4, m) for m in (1, 2, 3)]
        return (self.own,)

    def parts(self):
        return self.own, *self.came


def natural(which, keep, send):
    both = jnp.stack([keep, send])
    if which == "attn":
        a = both.reshape(2, 4, 4, 3, 96, 256).transpose(2, 1, 0, 4, 3, 5).reshape(4, 768, 768)
        return [a[i] for i in range(4)]
    both = both.reshape((2, 4, 4) + both.shape[4:])
    a = both[:, :, :, 224:].reshape(2, 4, 4, 4, 96, 256).transpose(1, 0, 4, 2, 3, 5)
    a = a.reshape(768, 4096)
    d = both[:, :, :, :192].reshape(2, 4, 4, 3, 64, 256).transpose(1, 0, 2, 4, 3, 5)
    e = both[:, :, :3, 192:224, :128].transpose(1, 0, 2, 3, 4)
    return [a[:, :2048], a[:, 2048:], d.reshape(2048, 768), e.reshape(768, 128)]


def body(
    doc_tokens, query_tokens, doc_cotangent, query_cotangent, retrieved, pos_ids, pos_count,
    w_query, w_key, carried_content_weights, w_out, w_gate, w_up, w_down, w_proj,
    gain_attn, gain_ffn, gain_final, rel_bias,
):
    n_wide = lax.axis_size("wide")
    n_rep = lax.axis_size("rep")
    group = retrieved.shape[1]
    fast = n_wide == 8 and n_rep == 4 and group == 64
    weights = (w_query, w_key, carried_content_weights, w_out, w_gate, w_up, w_down, w_proj)
    width = doc_tokens.shape[1]
    buckets, heads = rel_bias.shape
    hot_np = bucket_hot(buckets)
    hot = jnp.asarray(hot_np, BF)
    hot_f = jnp.asarray(hot_np, F)
    rep_hot = jnp.asarray(query_hot(64), BF)
    rel = jnp.transpose(rel_bias)
    queries = pos_ids.shape[0]
    ids = jnp.transpose(pos_ids)
    columns = jnp.transpose(retrieved)
    gains = (gain_attn, gain_ffn, gain_final)

    doc = layer_forward(doc_tokens, weights, gains, rel, hot, DL, (columns,) if fast else ())
    if fast:
        send = doc["send"]
        near = [send] + [swap(send, "wide", n_wide, 2 * m) for m in (1, 2, 3)]
        near_other = swap(send, "wide", n_wide, 1)
    query = layer_forward(query_tokens, weights, gains, rel, hot, QUERY_LENGTH, (), (doc["emb"],))
    if fast:
        other = swap(stack_rows(near[1:], (query["emb"],)), "wide", n_wide, 1)
        ins = near + [near_other, other]
    else:
        mask_query = lax.all_to_all(columns.astype(F), "wide", 0, 0, tiled=True)
        mask_query = mask_query.reshape(n_wide, queries, DL)
        ins = [lax.all_gather(doc["emb"], "wide", axis=0, tiled=True), mask_query]
    if fast:
        line = [query["emb"]] + [swap(query["emb"], "wide", n_wide, 2 * m) for m in (1, 2, 3)]
    coef, d_query_emb, parts = query_sims(
        fast, ids, pos_count, query["emb"], query_cotangent, ins, n_wide
    )
    coef_all = lax.all_to_all(coef, "wide", 0, 0, tiled=True)
    if fast:
        every = stack_rows(line, (coef,))
        others = swap(every, "wide", n_wide, 1)
    else:
        every = lax.all_gather(query["emb"], "wide", axis=0, tiled=True)
        others = query["emb"]
    d_hid, d_attn, g, gains_both, keep_f, send_f = back(
        fast, doc_cotangent, doc["emb"], every, others, columns, rep_hot, coef_all, d_query_emb, doc, query,
        gains, weights,
    )
    if fast:
        ffn = Reduction("ffn", keep_f, send_f)
    early = 2
    first = attn_back(0, early, True, g, doc, query, hot_f, ())
    after = ffn.near((first[3],)) if fast else ()
    second = attn_back(early, heads // 2 - early, False, g, doc, query, hot_f, after)
    doc_grad, query_grad, small = input_back(
        doc_tokens, query_tokens, d_hid, gain_attn, gains_both, parts, first, second, weights, (),
    )
    after = (small,)
    if fast:
        after = ffn.mine(after)
        after = ffn.cross(after)
    keep_a, send_a = attn_grads(fast, first, second, d_attn, doc, query, after)
    if fast:
        attn = AttnReduction(keep_a, send_a)
        after = ffn.line((keep_a,), 1e9)
        after = attn.near(small, after)
        after = attn.mine(after)
        after = ffn.next(after)
        after = attn.cross(after)
        after = ffn.far(after)
        after = attn.line(after)
        after = attn.next(after)
        after = grad_gate, grad_up, grad_down, grad_proj = unpack(
            "ffn", ffn.parts(), ((96, 2048), (96, 2048), (256, 768), (96, 128)), after
        )
        total_gain_a, total_gain_f, total_gain_l, total_rel, loss, fraction = attn.far(
            heads, buckets, width, queries * n_wide * n_rep, after[3:]
        )
        grad_query, grad_key, grad_value, grad_out = unpack(
            "attn", attn.parts(), ((96, 768),) * 4, (total_rel,)
        )
        loss = loss.reshape(())
        fraction = fraction.reshape(())
    else:
        small = lax.psum(small, ("rep", "wide"))

        def total(whole):
            part = lax.psum_scatter(whole, "wide", scatter_dimension=0, tiled=True)
            return lax.psum(part, "rep").astype(F)

        grad_query, grad_key, grad_value, grad_out = (total(a) for a in natural("attn", keep_a, send_a))
        grad_gate, grad_up, grad_down, grad_proj = (total(a) for a in natural("ffn", keep_f, send_f))
        total_gain_a, total_gain_f, total_gain_l = (
            small[8 * i : 8 * i + 6].reshape(width) for i in range(3)
        )
        total_rel = small[32 : 32 + heads, 0:buckets]
        loss = small[24, 0] / (queries * n_wide * n_rep)
        fraction = small[24, 1] / (DL * small[24, 2])
    return (
        doc["emb"],
        query["emb"],
        doc_grad,
        query_grad,
        grad_query,
        grad_key,
        grad_value,
        grad_out,
        grad_gate,
        grad_up,
        grad_down,
        grad_proj,
        total_gain_a,
        total_gain_f,
        total_gain_l,
        jnp.transpose(total_rel),
        loss,
        fraction,
    )


def solution(mesh):
    rows = P(("rep", "wide"), None)
    return jax.shard_map(
        body,
        mesh=mesh,
        in_specs=(rows,) * 6 + (P(("rep", "wide")),) + (P(),) * 12,
        out_specs=(rows,) * 4 + (P("wide", None),) * 8 + (P(),) * 6,
        check_vma=False,
    )
```

```python
import functools

import jax
import jax.numpy as jnp
import numpy as np
from jax import lax
from jax.experimental import pallas as pl
from jax.experimental.pallas import tpu as pltpu
from jax.sharding import PartitionSpec as P

DL = 512
QUERY_LENGTH = 32
EPS = 1e-06
SCALE = 10.0
BF = jnp.bfloat16
F = jnp.float32
TABLE = 512
VMEM_LIMIT = 60 * 1024 * 1024

SAVED = (
    "n1", "q", "k", "v", "p", "li", "ctx", "hid", "n2", "gv", "us", "act", "h2", "n3", "proj", "lr", "emb",
)

SM = pl.BlockSpec(memory_space=pltpu.SMEM)
ANY = pl.BlockSpec(memory_space=pl.ANY)
VM = pl.BlockSpec(memory_space=pltpu.VMEM)


def mm(a, b):
    return jnp.dot(a, b, preferred_element_type=F)


def mm_nt(a, b):
    return lax.dot_general(a, b, (((1,), (1,)), ((), ())), preferred_element_type=F)


def mm_tn(a, b):
    return lax.dot_general(a, b, (((0,), (0,)), ((), ())), preferred_element_type=F)


def bucket_hot(buckets):
    half = buckets // 2
    exact = half // 2
    column = np.arange(TABLE)
    relative = 128 - np.where(column <= TABLE - 128, column, column - TABLE)
    base = (relative > 0).astype(np.int64) * half
    distance = np.abs(relative)
    large = exact + (
        np.log(np.maximum(distance, 1) / float(exact)) / np.log(128.0 / exact) * (half - exact)
    ).astype(np.int64)
    large = np.minimum(large, half - 1)
    number = base + np.where(distance < exact, distance, large)
    return (np.arange(buckets)[:, None] == number[None, :]).astype(np.float32)


def query_hot(queries):
    tokens = np.arange(queries * QUERY_LENGTH)
    return (np.arange(queries)[:, None] == tokens[None, :] // QUERY_LENGTH).astype(np.float32)


def cost(flops, moved):
    large = flops > 1e8
    return pl.CostEstimate(flops=int(1e12 if large else 1), bytes_accessed=1, transcendentals=0)


class Place:
    def __init__(self, fast):
        self.fast = fast
        self.rep = lax.axis_index("rep")
        self.wide = lax.axis_index("wide")
        self.y, self.x = self.rep >> 1, self.rep & 1
        self.z = self.wide >> 1
        self.own = self.wide & 1 if fast else 0

    def doc(self, slot):
        return self.wide ^ (2 * (slot % 4)) ^ (slot // 4) if self.fast else slot

    def source(self, slot):
        return self.wide ^ slot if self.fast else slot


def row_of(gain):
    return gain[...].astype(F).reshape(1, gain.shape[0])


def stack_kernel(n_parts, *refs):
    out = refs[-1]
    row = 0
    for part in refs[:n_parts]:
        out[row : row + part.shape[0], :] = part[...]
        row += part.shape[0]


def stack_rows(parts, after):
    rows = sum(part.shape[0] for part in parts)
    return pl.pallas_call(
        functools.partial(stack_kernel, len(parts)),
        out_shape=sds((rows, 128), BF),
        in_specs=[VM] * len(parts) + [ANY] * len(after),
        out_specs=VM,
        cost_estimate=cost(1, 1),
        name="stack_rows",
    )(*parts, *after)


def sds(shape, dtype):
    return jax.ShapeDtypeStruct(shape, dtype)


def rows_loop(count, block, fn):
    def step(i, carry):
        fn(pl.ds(pl.multiple_of(i * block, block), block))
        return carry

    lax.fori_loop(0, count // block, step, 0)


def half_masks():
    lane = lax.broadcasted_iota(jnp.int32, (1, 128), 1)
    low = (lane < 64).astype(F)
    high = 1.0 - low
    one_low = (lane == 0).astype(F)
    one_high = (lane == 64).astype(F)
    return low, high, one_low, one_high


def rms(values):
    return lax.rsqrt(jnp.mean(values * values, axis=-1, keepdims=True) + EPS)


def rms_back(values, gain, d_result):
    inverse = rms(values)
    scaled = values * inverse
    grad_gain = jnp.sum(d_result * scaled, axis=0, keepdims=True)
    gained = d_result * gain
    d_values = inverse * (gained - scaled * jnp.mean(gained * scaled, axis=-1, keepdims=True))
    return d_values, grad_gain


def gelu_parts(gate):
    square = gate * gate
    tangent = jnp.tanh(gate * (0.7978845608028654 + (0.7978845608028654 * 0.044715) * square))
    half_plus = 0.5 + 0.5 * tangent
    value = gate * half_plus
    slope = half_plus + 0.5 * gate * (1.0 - tangent * tangent) * (
        0.7978845608028654 + (3.0 * 0.7978845608028654 * 0.044715) * square
    )
    return value, slope


def start_all(pairs, sems):
    copies = [pltpu.make_async_copy(src, dst, sems.at[i]) for i, (src, dst) in enumerate(pairs)]
    for copy in copies:
        copy.start()
    return copies


def wait_all(copies):
    for copy in copies:
        copy.wait()


def fwd_kernel(
    seq,
    heads,
    n_after,
    columns,
    tok, ga, gf, gl, rel, hot, wq_h, wk_h, wv_h, wo_h, wg_h, wu_h, wd_h, wp_h,
    *refs,
):
    (
    n1_h, q_h, k_h, v_h, p_h, li_h, ctx_h, hid_h, n2_h, gv_h, us_h, act_h, h2_h, n3_h, proj_h, lr_h, emb,
    wq, wk, wv, wo, wg, wu, wd, wp,
    n1, q, k, v, p, li, ctx, hid, n2, gv, us, act, h2, n3, proj, lr,
    tbl, bs, sem_in, sem_tile, sem_push, sem_out, _,
    ) = refs[n_after + columns : n_after + columns + 17] + refs[len(refs) - 31 :]
    sends = refs[n_after + columns + 17 : len(refs) - 31]
    count = tok.shape[0]
    loads = start_all(((wq_h, wq), (wk_h, wk), (wv_h, wv), (wo_h, wo), (wp_h, wp)), sem_in)

    def tile_loads(t):
        cols = pl.ds(pl.multiple_of(t * 512, 512), 512)
        pairs = ((wg_h.at[:, cols], wg.at[:, cols]), (wu_h.at[:, cols], wu.at[:, cols]), (wd_h.at[cols], wd.at[cols]))
        return [pltpu.make_async_copy(src, dst, sem_tile.at[t, i]) for i, (src, dst) in enumerate(pairs)]

    def tile_pushes(t):
        cols = pl.ds(pl.multiple_of(t * 512, 512), 512)
        pairs = tuple((a.at[:, cols], b.at[:, cols]) for a, b in ((gv, gv_h), (us, us_h), (act, act_h)))
        return [pltpu.make_async_copy(src, dst, sem_push.at[t, i]) for i, (src, dst) in enumerate(pairs)]

    outs = {}

    def push(i, src, dst):
        outs[i] = pltpu.make_async_copy(src, dst, sem_out.at[i])
        outs[i].start()

    gain_a, gain_f, gain_l = row_of(ga), row_of(gf), row_of(gl)

    def norm_one(rows):
        x = tok[rows, :].astype(F)
        n1[rows, :] = (x * rms(x) * gain_a).astype(BF)

    rows_loop(count, 128, norm_one)
    push(0, n1, n1_h)
    lines = mm(rel[...], hot[...])
    for h in range(heads):
        tbl[h] = lines[h : h + 1, :]
    for i, (w, r, r_h) in enumerate(((wq, q, q_h), (wk, k, k_h), (wv, v, v_h))):
        loads[i].wait()
        r[...] = mm(n1[...], w[...]).astype(BF)
        push(1 + i, r, r_h)
    n_tiles = wg.shape[1] // 512
    for t in range(2):
        for copy in tile_loads(t):
            copy.start()

    low, high, one_low, one_high = half_masks()
    is_low = low > 0.5

    blocks = count // 128

    def table(head, carry):
        row = jnp.broadcast_to(tbl[head], (128, TABLE))
        base = pltpu.roll(row, 0, 1, stride=1, stride_axis=0)
        if seq == DL:
            bs[head] = base[:, 0:384]
        else:
            rows = lax.broadcasted_iota(jnp.int32, (128, 128), 0) // seq
            columns = lax.broadcasted_iota(jnp.int32, (128, 128), 1) // seq
            bs[head] = jnp.where(rows == columns, base[:, 128:256], -1e30)
        return carry

    lax.fori_loop(0, heads, table, 0)

    def halves(index):
        lanes = pl.ds(pl.multiple_of(index * 128, 128), 128)
        q2 = q[:, lanes]
        k2 = k[:, lanes]
        v2 = v[:, lanes]
        parts = []
        for keep, one in ((low, one_high), (high, one_low)):
            parts.append((k2 * keep.astype(BF), v2 * keep.astype(BF) + one.astype(BF)))
        return lanes, q2, parts

    def join(lanes, o0, o1):
        inv = 1.0 / jnp.where(is_low, o0[:, 64:65], o1[:, 0:1])
        li[:, lanes] = inv
        ctx[:, lanes] = (jnp.where(is_low, o0, o1) * inv).astype(BF)

    def doc_scores(index):
        _, q2, parts = halves(index)
        for e in range(2):
            for half in range(2):
                yield mm_nt(parts[e][0], q2[256 * half : 256 * half + 256])

    def doc_softmax(head, score, i):
        cols = slice(128 * i, 128 * i + 128)
        terms = []
        for j in range(blocks):
            term = score[128 * j : 128 * j + 128, 128 * (i % 2) : 128 * (i % 2) + 128]
            if abs(j - i) <= 1:
                t = 1 - (j - i)
                terms.append(term + bs[head, :, 128 * t : 128 * t + 128])
            else:
                terms.append(term + (tbl[head, :, 0:1] if j > i else tbl[head, :, 256:257]))
        peak = functools.reduce(jnp.maximum, terms)
        peak = jnp.max(peak, axis=0, keepdims=True)
        total = jnp.zeros((128, 128), F)
        probs = []
        for j in range(blocks):
            power = jnp.exp(terms[j] - peak)
            total = total + power
            probs.append(power.astype(BF))
            p[head, 128 * j : 128 * j + 128, cols] = probs[-1]
        lr[head, :, cols] = 1.0 / jnp.sum(total, axis=0, keepdims=True)
        return jnp.concatenate(probs, axis=0)

    def doc_pairs(first, number):
        scores = list(doc_scores(first))
        for index in range(number):
            lanes, _, parts = halves(first + index)
            coming = doc_scores(first + index + 1) if index + 1 < number else iter(())
            following = []
            sides = []
            for e in range(2):
                head = 2 * (first + index) + e
                done = []
                for half in range(2):
                    following += [c for c in [next(coming, None)] if c is not None]
                    probs = [doc_softmax(head, scores[2 * e + half], 2 * half + i) for i in range(2)]
                    done.append(mm_tn(jnp.concatenate(probs, axis=1), parts[e][1]))
                sides.append(jnp.concatenate(done, axis=0))
            join(lanes, *sides)
            scores = following

    def query_group(group, carry):
        pairs = [halves(group * 3 + i) for i in range(3)]
        cells = [(i, e, b) for i in range(3) for e in range(2) for b in range(blocks)]
        rows = [slice(128 * b, 128 * b + 128) for b in range(blocks)]
        scores = [mm_nt(pairs[i][2][e][0][rows[b]], pairs[i][1][rows[b]]) for i, e, b in cells]
        probs = []
        for score, (i, e, b) in zip(scores, cells):
            head = (group * 3 + i) * 2 + e
            term = score + bs[head]
            power = jnp.exp(term - jnp.max(term, axis=0, keepdims=True))
            probs.append(power.astype(BF))
            p[head, rows[b], :] = probs[-1]
            lr[head, :, rows[b]] = 1.0 / jnp.sum(power, axis=0, keepdims=True)
        outs_g = [mm_tn(pb, pairs[i][2][e][1][rows[b]]) for pb, (i, e, b) in zip(probs, cells)]
        for i in range(3):
            sides = [
                jnp.concatenate([outs_g[cells.index((i, e, b))] for b in range(blocks)], axis=0)
                for e in range(2)
            ]
            join(pairs[i][0], *sides)
        return carry

    if seq == DL:
        def doc_group(group, carry):
            doc_pairs(group * 3, 3)
            return carry

        lax.fori_loop(0, heads // 2 // 3, doc_group, 0)
    else:
        lax.fori_loop(0, heads // 6, query_group, 0)
    push(4, p, p_h)
    push(5, li, li_h)
    push(15, lr, lr_h)
    push(6, ctx, ctx_h)

    loads[3].wait()

    def middle(rows):
        h = tok[rows, :].astype(F) + mm(ctx[rows, :], wo[...])
        hid[rows, :] = h
        h2[rows, :] = h
        n2[rows, :] = (h * rms(h) * gain_f).astype(BF)

    rows_loop(count, 256, middle)
    push(7, hid, hid_h)
    push(8, n2, n2_h)

    def ffn(t, carry):
        cols = pl.ds(pl.multiple_of(t * 512, 512), 512)

        @pl.when(t + 2 < n_tiles)
        def _():
            for copy in tile_loads(t + 2):
                copy.start()

        wait_all(tile_loads(t))
        for b in range(count // 256):
            rows = slice(256 * b, 256 * b + 256)
            gate = mm(n2[rows, :], wg[:, cols])
            up = mm(n2[rows, :], wu[:, cols])
            value, slope = gelu_parts(gate)
            a = (value * up).astype(BF)
            gv[rows, cols] = value.astype(BF)
            us[rows, cols] = (up * slope).astype(BF)
            act[rows, cols] = a
            h2[rows, :] += mm(a, wd[cols, :])
        for copy in tile_pushes(t):
            copy.start()
        return carry

    lax.fori_loop(0, n_tiles, ffn, 0)
    loads[4].wait()

    def top(rows):
        h = h2[rows, :]
        n = (h * rms(h) * gain_l).astype(BF)
        n3[rows, :] = n
        pr = mm(n, wp[...])
        proj[rows, :] = pr
        emb[rows, :] = (pr * lax.rsqrt(jnp.sum(pr * pr, axis=-1, keepdims=True) + EPS)).astype(BF)

    rows_loop(count, 256, top)
    if columns:
        z = lax.axis_index("wide") >> 1
        sent_mask = refs[-1]
        sent_mask[...] = refs[0][...].astype(F).astype(BF)
        for m, send in enumerate(sends):
            send[0:count, :] = emb[...]
            own_rows = sent_mask[pl.ds(pl.multiple_of(16 * (z ^ m), 16), 16), :]
            for b in range(DL // 128):
                first = count + 16 * b
                send[first : first + 16, :] = own_rows[:, 128 * b : 128 * b + 128]
    push(12, h2, h2_h)
    push(13, n3, n3_h)
    push(14, proj, proj_h)
    wait_all(outs.values())
    for t in range(n_tiles):
        wait_all(tile_pushes(t))


def layer_forward(tokens, weights, gains, rel, hot, seq, columns=(), after=()):
    count, width = tokens.shape
    wq, wk, wv, wo, wg, wu, wd, wp = weights
    hidden = wg.shape[1]
    emb = wp.shape[1]
    heads = rel.shape[0]
    keys = DL if seq == DL else 128
    saved = (
        sds((count, width), BF),
        sds((count, width), BF),
        sds((count, width), BF),
        sds((count, width), BF),
        sds((heads, count, keys), BF),
        sds((count, width), F),
        sds((count, width), BF),
        sds((count, width), F),
        sds((count, width), BF),
        sds((count, hidden), BF),
        sds((count, hidden), BF),
        sds((count, hidden), BF),
        sds((count, width), F),
        sds((count, width), BF),
        sds((count, emb), F),
        sds((heads, 1, count), F),
    )
    outs = pl.pallas_call(
        functools.partial(fwd_kernel, seq, heads, len(after), len(columns)),
        out_shape=saved
        + (sds((count, emb), BF),)
        + (sds((count + 16 * DL // 128, emb), BF),) * (4 * len(columns)),
        in_specs=[VM] * 6 + [ANY] * 8 + [VM] * len(columns) + [ANY] * len(after),
        out_specs=[ANY] * 16 + [VM] * (1 + 4 * len(columns)),
        scratch_shapes=[pltpu.VMEM(w.shape, BF) for w in weights]
        + [pltpu.VMEM(s.shape, s.dtype) for s in saved]
        + [
            pltpu.VMEM((heads, 1, TABLE), F),
            pltpu.VMEM((heads, 128, 384 if seq == DL else 128), F),
            pltpu.SemaphoreType.DMA((5,)),
            pltpu.SemaphoreType.DMA((hidden // 512, 3)),
            pltpu.SemaphoreType.DMA((hidden // 512, 3)),
            pltpu.SemaphoreType.DMA((16,)),
            pltpu.VMEM((64, DL) if columns else (16, 128), BF),
        ],
        compiler_params=pltpu.CompilerParams(vmem_limit_bytes=VMEM_LIMIT),
        cost_estimate=cost(count * 14e6, 40e6),
        name="layer_forward_%d" % seq,
    )(tokens, *gains, rel, hot, *weights, *columns, *after)
    return dict(zip(SAVED, outs)), outs[len(SAVED) :]


def each_block(arrays, block, fn):
    first = 0
    for array in arrays:
        number = array.shape[0] // block
        if number == 1:
            fn(first, array[...])
        else:

            def step(i, carry, array=array, first=first):
                fn(first + i, array[pl.ds(pl.multiple_of(i * block, block), block), :])
                return carry

            lax.fori_loop(0, number, step, 0)
        first += number


def query_sims_kernel(fast, n_docs, n_ins, ids, used, qemb, cot, *refs):
    ins = refs[:n_ins]
    coef, d_emb, parts, es, total, counts = refs[n_ins:]
    place = Place(fast)
    tokens = qemb.shape[0]
    queries = tokens // QUERY_LENGTH
    lane = lax.broadcasted_iota(jnp.int32, (tokens, 128), 1)
    lane_q = lax.broadcasted_iota(jnp.int32, (queries, 128), 1)
    total[...] = jnp.zeros_like(total)
    counts[...] = jnp.zeros_like(counts)

    if fast:
        row = lax.broadcasted_iota(jnp.int32, (queries, 16), 0)
        pick = row + queries * place.own == lax.broadcasted_iota(jnp.int32, (queries, 16), 1)
        pick = jnp.where(pick, 1.0, 0.0).astype(BF)
        per = DL + 16 * DL // 128

        def rows_at(slot, first, last):
            if slot < 4:
                return ins[slot][first:last, :]
            base = per * (slot - 4)
            return ins[4][base + first : base + last, :]

        def doc_at(slot):
            return rows_at(slot, 0, DL)

        def mask_at(slot):
            packed = rows_at(slot, DL, per)
            return jnp.concatenate([mm(pick, packed[16 * b : 16 * b + 16]) for b in range(4)], axis=1)

        def each(fn):
            for slot in range(n_docs):
                fn(slot)

    else:
        docs, mask = ins

        def doc_at(slot):
            return docs[pl.ds(pl.multiple_of(slot * DL, DL), DL), :]

        def mask_at(slot):
            return mask[slot]

        def each(fn):
            def step(i, carry):
                fn(i)
                return carry

            lax.fori_loop(0, n_docs, step, 0)

    def forward(slot):
        d = place.doc(slot)
        m = mask_at(slot)
        wide = jnp.broadcast_to(m[:, None, :], (queries, QUERY_LENGTH, DL)).reshape(tokens, DL)
        e = jnp.exp(mm_nt(qemb[...], doc_at(slot)) * SCALE) * wide
        es[slot] = e
        total[...] = jnp.where(lane == d, jnp.sum(e, axis=1, keepdims=True), total[...])
        counts[...] = jnp.where(lane_q == d, jnp.sum(m, axis=1, keepdims=True), counts[...])

    each(forward)
    inside = lane_q < n_docs
    z = jnp.sum(jnp.log(1.0 + total[...]).reshape(queries, QUERY_LENGTH, 128), axis=1)
    z = z * (1.0 / QUERY_LENGTH)
    hot = jnp.zeros((queries, 128), F)
    row_q = lax.broadcasted_iota(jnp.int32, (queries, 128), 0)
    for q in range(queries):
        for s in range(ids.shape[0]):
            number = jnp.where(s < used[q], ids[s, q], 128)
            hot = jnp.where((row_q == q) & (lane_q == number), 1.0, hot)
    peak = jnp.max(jnp.where(inside, z, -1e30), axis=1, keepdims=True)
    power = jnp.where(inside, jnp.exp(jnp.where(inside, z - peak, 0.0)), 0.0)
    whole = jnp.sum(power, axis=1, keepdims=True)
    positive = jnp.sum(hot * power, axis=1, keepdims=True)
    loss = jnp.sum(jnp.log(whole) - jnp.log(positive))
    hits = jnp.sum(hot * counts[...])
    found = jnp.sum(hot)
    lane_p = lax.broadcasted_iota(jnp.int32, (8, 128), 1)
    parts[...] = jnp.where(
        lane_p == 0, loss, jnp.where(lane_p == 1, hits, jnp.where(lane_p == 2, found, 0.0))
    )
    d_z = power / whole - hot * power / positive
    d_wide = jnp.broadcast_to(d_z[:, None, :], (queries, QUERY_LENGTH, 128)).reshape(tokens, 128)
    c = d_wide * (SCALE / QUERY_LENGTH) / (1.0 + total[...])
    by_doc = jnp.transpose(c)[0:n_docs, :]
    coef[...] = jnp.zeros_like(coef)
    for half in range(tokens // 128):
        coef[:, half, :] = by_doc[:, 128 * half : 128 * half + 128]
    d_emb[...] = cot[...].astype(F)

    def backward(slot):
        column = jnp.sum(jnp.where(lane == place.doc(slot), c, 0.0), axis=1, keepdims=True)
        d_emb[...] += mm((es[slot] * column).astype(BF), doc_at(slot))

    each(backward)


def query_sims(fast, ids, used, qemb, cot, ins, n_docs):
    tokens, emb = qemb.shape
    queries = tokens // QUERY_LENGTH
    return pl.pallas_call(
        functools.partial(query_sims_kernel, fast, n_docs, len(ins)),
        out_shape=(
            sds((n_docs, 8, 128), F),
            sds((tokens, emb), F),
            sds((8, 128), F),
        ),
        in_specs=[SM] * 2 + [VM] * (2 + len(ins)),
        out_specs=[VM] * 3,
        scratch_shapes=[
            pltpu.VMEM((n_docs, tokens, DL), F),
            pltpu.VMEM((tokens, 128), F),
            pltpu.VMEM((queries, 128), F),
        ],
        compiler_params=pltpu.CompilerParams(vmem_limit_bytes=VMEM_LIMIT),
        cost_estimate=cost(n_docs * 67e6 * 10, n_docs * 1e6),
        name="query_sims",
    )(ids, used, qemb, cot, *ins)


def top_rows(d_emb, proj, h2, gain, wp):
    inv = lax.rsqrt(jnp.sum(proj * proj, axis=-1, keepdims=True) + EPS)
    along = jnp.sum(proj * d_emb, axis=-1, keepdims=True)
    d_proj = (inv * d_emb - proj * (inv * inv * inv) * along).astype(BF)
    d_h2, grad_gain = rms_back(h2, gain, mm_nt(d_proj, wp))
    return d_proj, d_h2, grad_gain


def back_kernel(
    fast, d_emb_in, demb, every, others, mask, rep, coef, d_emb_q, proj_d, proj_q, gf, gl, wp,
    h2_dh, h2_qh, n2_dh, n2_qh, n3_dh, n3_qh, wd_h, us_dh, us_qh, gv_dh, gv_qh, act_dh, act_qh,
    wg_h, wu_h, hid_dh, hid_qh, wo_h, li_dh, li_qh,
    d_hid, d_attn, g_out, g_gain, keep_h, send_h,
    h2, n2, n3, wd, us, gv, gate, up, act, wg, wu, hid, wo, li,
    n2t, d_proj, d_all, acc, d_n2, low_grads, down_grads, up_grads,
    sem_in, sem_tile, sem_last, sem_low, sem_out,
):
    place = Place(fast)
    count = demb.shape[0]
    rows = d_all.shape[0]

    def both(doc, query, target):
        return [(doc, target.at[0:count]), (query, target.at[count:])]

    loads = start_all(
        both(h2_dh, h2_qh, h2) + both(n2_dh, n2_qh, n2) + both(n3_dh, n3_qh, n3), sem_in
    )

    def tile_loads(t):
        cols = pl.ds(pl.multiple_of(t * 512, 512), 512)
        pairs = [
            (wd_h.at[cols], wd.at[cols]),
            (wg_h.at[:, cols], wg.at[:, cols]),
            (wu_h.at[:, cols], wu.at[:, cols]),
        ]
        for doc, query, target in ((us_dh, us_qh, us), (gv_dh, gv_qh, gv), (act_dh, act_qh, act)):
            pairs += both(doc.at[:, cols], query.at[:, cols], target.at[:, cols])
        return [pltpu.make_async_copy(src, dst, sem_tile.at[t, i]) for i, (src, dst) in enumerate(pairs)]

    def last_loads():
        pairs = both(hid_dh, hid_qh, hid) + [(wo_h, wo)] + both(li_dh, li_qh, li)
        return [pltpu.make_async_copy(src, dst, sem_last.at[i]) for i, (src, dst) in enumerate(pairs)]

    for copy in tile_loads(0):
        copy.start()
    acc[0:count, :] = d_emb_in[...].astype(F)
    acc[count:, :] = d_emb_q[...]
    per = 64 * QUERY_LENGTH // 256

    def sims(row, qb):
        line = jnp.concatenate([coef[row, 0:1, :], coef[row, 1:2, :]], axis=1)
        e = jnp.exp(mm_nt(demb[...], qb) * SCALE)
        first = pl.multiple_of((row // per) * 64, 64)
        here = mask[pl.ds(first, 64), :].astype(F).astype(BF)
        m = mm_tn(here, rep[:, pl.ds(pl.multiple_of((row % per) * 256, 256), 256)])
        acc[0:count, :] += mm((e * m * line).astype(BF), qb)

    if fast:
        for slot in range(8):
            where = slice(256 * (slot % 4), 256 * (slot % 4) + 256)
            sims(place.doc(slot), (every if slot < 4 else others)[where, :])
    else:

        def step(row, carry):
            sims(row, every[pl.ds(pl.multiple_of(row * 256, 256), 256), :])
            return carry

        lax.fori_loop(0, coef.shape[0], step, 0)
    wait_all(loads[0:2])
    g_gain[...] = jnp.zeros_like(g_gain)
    gain_l = row_of(gl)
    for at_rows, proj in ((slice(0, count), proj_d), (slice(count, rows), proj_q)):
        dp, dh, gg = top_rows(acc[at_rows, :], proj[...], h2[at_rows, :], gain_l, wp[...])
        d_proj[at_rows, :] = dp
        h2[at_rows, :] = dh
        g_gain[1:2, :] += gg
        d_all[at_rows, :] = dh.astype(BF)
    wait_all(loads[2:])
    n2t[...] = jnp.transpose(n2[...])
    gp = mm_tn(n3[...], d_proj[...])
    low_grads[...] = jnp.zeros_like(low_grads)
    for w in range(8):
        for r in range(3):
            first = 96 * w + 32 * r
            low_grads[w % 2, w // 2, r // 2, r % 2, :, 0:128] = gp[first : first + 32, :].astype(BF)
    below = pl.ds(192, 32)
    low = start_all(
        (
            (low_grads.at[place.own], keep_h.at[:, :, :, below]),
            (low_grads.at[1 - place.own], send_h.at[:, :, :, below]),
        ),
        sem_low,
    )
    d_n2[...] = jnp.zeros_like(d_n2)

    def outputs(t, slot):
        copies = []
        for i, (core, target) in enumerate(((place.own, keep_h), (1 - place.own, send_h))):
            copies.append(
                pltpu.make_async_copy(
                    down_grads.at[slot, core], target.at[t, :, :, pl.ds(0, 192)], sem_out.at[slot, 3 * i]
                )
            )
            start = pl.multiple_of(224 + (t % 2) * 192, 32)
            for base in range(2):
                copies.append(
                    pltpu.make_async_copy(
                        up_grads.at[slot, base, core],
                        target.at[:, base, t // 2, pl.ds(start, 192)],
                        sem_out.at[slot, 3 * i + 1 + base],
                    )
                )
        return copies

    def tile(t, carry):
        slot = t % 2
        cols = pl.ds(pl.multiple_of(t * 512, 512), 512)

        @pl.when(t >= 2)
        def _():
            wait_all(outputs(t - 2, slot))

        @pl.when(t < 3)
        def _():
            for copy in tile_loads(t + 1):
                copy.start()

        @pl.when(t == 3)
        def _():
            for copy in last_loads():
                copy.start()

        wait_all(tile_loads(t))
        d_act = mm_nt(d_all[...], wd[cols, :])
        gate[...] = (d_act * us[:, cols].astype(F)).astype(BF)
        up[...] = (d_act * gv[:, cols].astype(F)).astype(BF)
        for half in range(2):
            first = pl.multiple_of((2 * t + half) * 256, 256)
            g = mm_tn(act[:, pl.ds(first, 256)], d_all[...])
            for r in range(4):
                for c in range(3):
                    down_grads[slot, half, r // 2, r % 2, 64 * c : 64 * c + 64, :] = g[
                        64 * r : 64 * r + 64, 256 * c : 256 * c + 256
                    ].astype(BF)
        for base, source in ((0, gate), (1, up)):
            g = mm(n2t[...], source[...]).astype(BF)
            for c in range(2):
                for w in range(8):
                    up_grads[slot, base, w % 2, w // 2, 96 * c : 96 * c + 96, :] = g[
                        96 * w : 96 * w + 96, 256 * c : 256 * c + 256
                    ]
        for copy in outputs(t, slot):
            copy.start()
        d_n2[...] += mm_nt(gate[...], wg[:, cols]) + mm_nt(up[...], wu[:, cols])
        return carry

    lax.fori_loop(0, 4, tile, 0)
    wait_all(last_loads())
    gain_f = row_of(gf)

    def through(at_rows):
        dm, gg = rms_back(hid[at_rows, :], gain_f, d_n2[at_rows, :])
        total = h2[at_rows, :] + dm
        d_hid[at_rows, :] = total
        g_gain[0:1, :] += gg
        d_attn[at_rows, :] = total.astype(BF)

    rows_loop(rows, 256, through)

    def to_context(at_rows):
        d_context = mm_nt(d_attn[at_rows, :], wo[...]).astype(BF).astype(F)
        g_out[at_rows, :] = (d_context * li[at_rows, :]).astype(BF)

    rows_loop(rows, 256, to_context)
    wait_all(low)
    for t in (2, 3):
        wait_all(outputs(t, t % 2))


def back(fast, d_emb, demb, every, others, mask, rep, coef, d_emb_q, dsaved, qsaved, gains, weights):
    wq, wk, wv, wo, wg, wu, wd, wp = weights
    count, width = dsaved["h2"].shape
    rows = count + d_emb_q.shape[0]
    hidden = wd.shape[0]
    emb = wp.shape[1]
    piece = sds((4, 2, 2, 608, 256), BF)

    def both(name):
        return dsaved[name], qsaved[name]

    return pl.pallas_call(
        functools.partial(back_kernel, fast),
        out_shape=(
            sds((rows, width), F),
            sds((rows, width), BF),
            sds((rows, width), BF),
            sds((8, width), F),
            piece,
            piece,
        ),
        in_specs=[VM] * 13 + [ANY] * 20,
        out_specs=[VM] * 4 + [ANY] * 2,
        scratch_shapes=[
            pltpu.VMEM((rows, width), F),
            pltpu.VMEM((rows, width), BF),
            pltpu.VMEM((rows, width), BF),
            pltpu.VMEM(wd.shape, BF),
            pltpu.VMEM((rows, hidden), BF),
            pltpu.VMEM((rows, hidden), BF),
            pltpu.VMEM((rows, 512), BF),
            pltpu.VMEM((rows, 512), BF),
            pltpu.VMEM((rows, hidden), BF),
            pltpu.VMEM(wg.shape, BF),
            pltpu.VMEM(wu.shape, BF),
            pltpu.VMEM((rows, width), F),
            pltpu.VMEM(wo.shape, BF),
            pltpu.VMEM((rows, width), F),
            pltpu.VMEM((width, rows), BF),
            pltpu.VMEM((rows, emb), BF),
            pltpu.VMEM((rows, width), BF),
            pltpu.VMEM((rows, emb), F),
            pltpu.VMEM((rows, width), F),
            pltpu.VMEM((2, 4, 2, 2, 32, 256), BF),
            pltpu.VMEM((2, 2, 2, 2, 192, 256), BF),
            pltpu.VMEM((2, 2, 2, 4, 192, 256), BF),
            pltpu.SemaphoreType.DMA((6,)),
            pltpu.SemaphoreType.DMA((4, 9)),
            pltpu.SemaphoreType.DMA((5,)),
            pltpu.SemaphoreType.DMA((2,)),
            pltpu.SemaphoreType.DMA((2, 6)),
        ],
        compiler_params=pltpu.CompilerParams(vmem_limit_bytes=VMEM_LIMIT),
        cost_estimate=cost(14e9, 10e6),
        name="back",
    )(
        d_emb, demb, every, others, mask, rep, coef, d_emb_q, *both("proj"), gains[1], gains[2], wp,
        *both("h2"), *both("n2"), *both("n3"), wd, *both("us"), *both("gv"), *both("act"), wg, wu,
        *both("hid"), wo, *both("li"),
    )


def attn_back_kernel(
    first, n_pairs, with_queries, hot, g_h, q_d, q_q, k_d, k_q, v_d, v_q, lr_d, lr_q, p_dh, p_qh, *refs
):
    n_outs = 7 if with_queries else 4
    outs = refs[-n_outs - 15 : -15]
    (
    q, k, v, g, p_d, p_q, lrd, lrq, ds, acc, sums, sem_in, sem_p, qq, gq,
    ) = refs[-15:]
    dq, dk, dv, g_rel = outs[:4]
    count = q_d.shape[0]
    rest = q_q.shape[0]
    blocks = count // 128
    heads_here = pl.ds(2 * first, 2 * n_pairs)
    lanes_here = pl.ds(128 * first, 128 * n_pairs)
    pairs = []
    if with_queries:
        pairs += [
            (v_q, qq.at[2]),
            (g_h.at[count:], gq),
            (p_qh, p_q),
            (lr_q, lrq),
            (q_q, qq.at[0]),
            (k_q, qq.at[1]),
        ]
    n_query = len(pairs)
    pairs += [
        (v_d.at[:, lanes_here], v),
        (g_h.at[0:count, lanes_here], g),
        (lr_d.at[heads_here], lrd),
        (q_d.at[:, lanes_here], q),
        (k_d.at[:, lanes_here], k),
    ]
    loads = start_all(pairs, sem_in)

    def p_load(pair):
        return pltpu.make_async_copy(
            p_dh.at[pl.ds(2 * (first + pair), 2)], p_d.at[pl.ds(2 * pair, 2)], sem_p.at[pair]
        )

    p_load(0).start()
    low, high, _, _ = half_masks()
    keeps = (low.astype(BF), high.astype(BF))
    acc[...] = jnp.zeros_like(acc)
    wait_all(loads[:n_query])

    if with_queries:
        cells_q = rest // 128
        heads = p_q.shape[0]
        rows_q = [slice(128 * b, 128 * b + 128) for b in range(cells_q)]
        lanes_of = [slice(128 * pair, 128 * pair + 128) for pair in range(heads // 2)]
        for group in range(0, heads // 2, 3):
            cells = [
                (pair, e, b) for pair in range(group, group + 3) for e in range(2) for b in range(cells_q)
            ]
            d_ps = [
                mm_nt(qq[2, rows_q[b], lanes_of[pair]] * keeps[e], gq[rows_q[b], lanes_of[pair]])
                for pair, e, b in cells
            ]
            dss = []
            for d_p, (pair, e, b) in zip(d_ps, cells):
                head = 2 * pair + e
                pf = p_q[head, rows_q[b], :].astype(F)
                t = pf * d_p
                share = lrq[head, :, rows_q[b]] * jnp.sum(t, axis=0, keepdims=True)
                d_s = t - pf * share
                acc[head, :, 128:256] += d_s
                dss.append(d_s.astype(BF))
            for pair in range(group, group + 3):
                lanes = lanes_of[pair]
                for b in range(cells_q):
                    rows = rows_q[b]
                    at_cell = [cells.index((pair, e, b)) for e in range(2)]
                    probs = [p_q[2 * pair + e, rows, :] for e in range(2)]
                    parts = [
                        (
                            mm_tn(dss[at_cell[e]], qq[1, rows, lanes] * keeps[e]),
                            mm(dss[at_cell[e]], qq[0, rows, lanes] * keeps[e]),
                            mm(probs[e], gq[rows, lanes] * keeps[e]),
                        )
                        for e in range(2)
                    ]
                    for i in range(3):
                        outs[4 + i][rows, lanes] = (parts[0][i] + parts[1][i]).astype(BF)
    wait_all(loads[n_query:])

    def doc_pair(pair, carry):
        lanes = pl.ds(pl.multiple_of(pair * 128, 128), 128)

        @pl.when(pair + 1 < n_pairs)
        def _():
            p_load(pair + 1).start()

        p_load(pair).wait()
        q2 = q[:, lanes]
        k2 = k[:, lanes]
        v2 = v[:, lanes]
        g2 = g[:, lanes]
        d_ps = [mm_nt(v2 * keep, g2) for keep in keeps]
        sides = []
        for e, keep in enumerate(keeps):
            head = 2 * pair + e
            acc_head = 2 * (first + pair) + e if with_queries else head
            for i in range(blocks):
                cols = slice(128 * i, 128 * i + 128)
                pfs = [p_d[head, 128 * j : 128 * j + 128, cols].astype(F) for j in range(blocks)]
                ts = [pfs[j] * d_ps[e][128 * j : 128 * j + 128, cols] for j in range(blocks)]
                total = functools.reduce(jnp.add, ts)
                share = lrd[head, :, cols] * jnp.sum(total, axis=0, keepdims=True)
                for j in range(blocks):
                    d_s = ts[j] - pfs[j] * share
                    t = 1 - (j - i)
                    tile = t if abs(j - i) <= 1 else (3 if j > i else 4)
                    acc[acc_head, :, 128 * tile : 128 * tile + 128] += d_s
                    ds[e, 128 * j : 128 * j + 128, cols] = d_s.astype(BF)
            sides.append(
                (
                    mm_tn(ds[e], k2 * keep),
                    mm(ds[e], q2 * keep),
                    mm(p_d[head], g2 * keep),
                )
            )
        dq[:, lanes] = (sides[0][0] + sides[1][0]).astype(BF)
        dk[:, lanes] = (sides[0][1] + sides[1][1]).astype(BF)
        dv[:, lanes] = (sides[0][2] + sides[1][2]).astype(BF)
        return carry

    lax.fori_loop(0, n_pairs, doc_pair, 0)
    sums[...] = jnp.zeros_like(sums)
    n_heads = acc.shape[0]
    lane = lax.broadcasted_iota(jnp.int32, (n_heads, TABLE), 1)

    def left(values, by):
        flat = values.reshape(-1, TABLE)
        return pltpu.roll(flat, TABLE - by, 1).reshape(values.shape)

    near = jnp.concatenate([acc[:, :, 0:384], jnp.zeros((n_heads, 128, 128), F)], axis=2)
    folded = near[:, 0:8]
    for group in range(1, 16):
        folded = folded + left(near[:, 8 * group : 8 * group + 8], 8 * group)
    row = lax.broadcasted_iota(jnp.int32, (n_heads, 8, TABLE), 1)
    lines = folded
    for i in range(1, 8):
        lines = jnp.where(row == i, left(folded, i), lines)
    lines = jnp.sum(lines, axis=1)
    after = jnp.sum(jnp.sum(acc[:, :, 384:512], axis=1), axis=1, keepdims=True)
    before = jnp.sum(jnp.sum(acc[:, :, 512:640], axis=1), axis=1, keepdims=True)
    lines = lines + jnp.where(lane == 0, after, jnp.where(lane == 256, before, 0.0))
    offset = 0 if with_queries else 2 * first
    sums[offset : offset + n_heads, :] = lines
    g_rel[...] = lax.dot_general(
        sums[...], hot[...], (((1,), (1,)), ((), ())),
        preferred_element_type=F, precision=lax.Precision.HIGHEST,
    )


def attn_back(first, n_pairs, with_queries, g, dsaved, qsaved, hot, after):
    rows, width = g.shape
    heads = dsaved["p"].shape[0]
    buckets = hot.shape[0]
    count = dsaved["q"].shape[0]
    rest = rows - count
    columns = 128 * n_pairs
    both = []
    for name in ("q", "k", "v", "lr", "p"):
        both += [dsaved[name], qsaved[name]]
    outs = (sds((count, columns), BF),) * 3 + (sds((16, buckets), F),)
    if with_queries:
        outs = outs + (sds((rest, width), BF),) * 3
    return pl.pallas_call(
        functools.partial(attn_back_kernel, first, n_pairs, with_queries),
        out_shape=outs,
        in_specs=[VM] + [ANY] * (11 + len(after)),
        out_specs=[VM] * len(outs),
        scratch_shapes=[pltpu.VMEM((count, columns), BF)] * 4
        + [
            pltpu.VMEM((2 * n_pairs, DL, DL), BF),
            pltpu.VMEM((heads, rest, 128), BF),
            pltpu.VMEM((2 * n_pairs, 1, count), F),
            pltpu.VMEM((heads, 1, rest), F),
            pltpu.VMEM((2, DL, DL), BF),
            pltpu.VMEM((heads if with_queries else 2 * n_pairs, 128, 640), F),
            pltpu.VMEM((16, TABLE), F),
            pltpu.SemaphoreType.DMA((11,)),
            pltpu.SemaphoreType.DMA((n_pairs,)),
            pltpu.VMEM((3, rest, width), BF),
            pltpu.VMEM((rest, width), BF),
        ],
        compiler_params=pltpu.CompilerParams(vmem_limit_bytes=VMEM_LIMIT),
        cost_estimate=cost(15e9, 40e6),
        name="attn_back_%d" % first,
    )(hot, g, *both, *after)


SMALL = 48


def split_small(values):
    high = values.astype(BF)
    return jnp.concatenate([high, (values - high.astype(F)).astype(BF)], axis=1)


def join_small(rows):
    return rows[:, 0:128].astype(F) + rows[:, 128:256].astype(F)


def attn_parts(first, second, targets):
    half = first[0].shape[1]
    count = first[0].shape[0]
    pairs = []
    for i, target in enumerate(targets):
        pairs += [
            (first[i], target.at[0:count, 0:half]),
            (second[i], target.at[0:count, half:]),
            (first[4 + i], target.at[count:]),
        ]
    return pairs


def attn_grads_kernel(fast, *refs):
    ins, (d_attn_h, n1_d, n1_q, ctx_d, ctx_q) = refs[:9], refs[9:14]
    keep_h, *sends = refs[-14:-9]
    dq, dk, dv, d_attn, n1, ctx, grads, sem_in, sem_out = refs[-9:]
    first = ins[0:3] + (None,) + ins[3:6]
    place = Place(fast)
    count = n1_d.shape[0]
    pairs = [
        (n1_d, n1.at[0:count]),
        (n1_q, n1.at[count:]),
        *attn_parts(first, ins[6:9], (dq, dk, dv)),
        (d_attn_h, d_attn),
        (ctx_d, ctx.at[0:count]),
        (ctx_q, ctx.at[count:]),
    ]
    loads = start_all(pairs, sem_in)
    outs = []
    wait_all(loads[0:2])
    groups = (loads[2:5], loads[5:8], loads[8:11], loads[11:14])
    for which, (left, right) in enumerate(((n1, dq), (n1, dk), (n1, dv), (ctx, d_attn))):
        wait_all(groups[which])
        value = mm_tn(left[...], right[...]).astype(BF)
        for w in range(8):
            for c in range(3):
                row = ((w // 2) * 4 + which) * 288 + 96 * c
                grads[w % 2, row : row + 96, :] = value[96 * w : 96 * w + 96, 256 * c : 256 * c + 256]
        for z in range(4):
            rows = slice((z * 4 + which) * 288, (z * 4 + which) * 288 + 288)
            there = slice(which * 288, which * 288 + 288)
            pairs = ((place.own, keep_h.at[rows]), (1 - place.own, sends[z].at[there]))
            for i, (core, target) in enumerate(pairs):
                copy = pltpu.make_async_copy(grads.at[core, rows], target, sem_out.at[which, z, i])
                copy.start()
                outs.append(copy)
    wait_all(outs)


def attn_grads(fast, first, second, d_attn, dsaved, qsaved, after):
    rows, width = d_attn.shape
    piece = sds((16 * 288, 256), BF)
    ins = (*first[0:3], *first[4:7], *second[0:3])
    keep, *sends = pl.pallas_call(
        functools.partial(attn_grads_kernel, fast),
        out_shape=(piece,) + (sds((4 * 288, 256), BF),) * 4,
        in_specs=[ANY] * (14 + len(after)),
        out_specs=[ANY] * 5,
        scratch_shapes=[pltpu.VMEM((rows, width), BF)] * 6
        + [
            pltpu.VMEM((2,) + piece.shape, BF),
            pltpu.SemaphoreType.DMA((14,)),
            pltpu.SemaphoreType.DMA((4, 4, 2)),
        ],
        compiler_params=pltpu.CompilerParams(vmem_limit_bytes=VMEM_LIMIT),
        cost_estimate=cost(1, 1),
        name="attn_grads",
    )(*ins, d_attn, dsaved["n1"], qsaved["n1"], dsaved["ctx"], qsaved["ctx"], *after)
    return keep, sends


def input_back_kernel(ga, gains, parts, rel_0, rel_1, *refs):
    ins, (wq_h, wk_h, wv_h, tok_d, tok_q, d_hid_h) = refs[:9], refs[9:15]
    out_dh, out_qh, small = refs[-16:-13]
    dq, dk, dv, wq, wk, wv, tok, d_hid, d_n1, out, g_gain, sem_in, sem_out = refs[-13:]
    first = ins[0:3] + (None,) + ins[3:6]
    count = tok_d.shape[0]
    parts_q = attn_parts(first, ins[6:9], (dq, dk, dv))
    groups = (
        [*parts_q[0:3], (wq_h, wq)],
        [*parts_q[3:6], (wk_h, wk)],
        [*parts_q[6:9], (wv_h, wv)],
        [
            (tok_d, tok.at[0:count]),
            (tok_q, tok.at[count:]),
            (d_hid_h, d_hid),
        ],
    )
    loads = [start_all(groups[0], sem_in.at[0])]
    gain_a = row_of(ga)
    g_gain[...] = jnp.zeros_like(g_gain)
    for i, (left, right) in enumerate(((dq, wq), (dk, wk), (dv, wv))):
        loads.append(start_all(groups[i + 1], sem_in.at[i + 1]))
        wait_all(loads[i])
        part = mm_nt(left[...], right[...])
        d_n1[...] = part if i == 0 else d_n1[...] + part
    wait_all(loads[3])

    def step(rows):
        d_in, gg = rms_back(tok[rows, :].astype(F), gain_a, d_n1[rows, :])
        g_gain[0:1, :] += gg
        out[rows, :] = (d_hid[rows, :] + d_in).astype(BF)

    rows_loop(tok.shape[0], 256, step)
    outs = start_all(((out.at[0:count], out_dh), (out.at[count:], out_qh)), sem_out)
    small[...] = jnp.zeros_like(small)
    rows = (
        g_gain[0:1, :],
        gains[0:1, :],
        gains[1:2, :],
    )
    for i, row in enumerate(rows):
        for c in range(6):
            small[8 * i + c : 8 * i + c + 1, :] = row[:, 128 * c : 128 * c + 128]
    small[24:25, :] = parts[0:1, :]
    small[32:48, 0 : rel_0.shape[1]] = rel_0[...] + rel_1[...]
    wait_all(outs)


def input_back(tok_d, tok_q, d_hid, gain, gains, parts, first, second, weights, after):
    count, width = tok_d.shape
    rows = count + tok_q.shape[0]
    ins = (*first[0:3], *first[4:7], *second[0:3])
    return pl.pallas_call(
        input_back_kernel,
        out_shape=(sds(tok_d.shape, BF), sds(tok_q.shape, BF), sds((SMALL, 128), F)),
        in_specs=[VM] * 5 + [ANY] * (15 + len(after)),
        out_specs=[ANY] * 2 + [VM],
        scratch_shapes=[pltpu.VMEM((rows, width), BF)] * 3
        + [pltpu.VMEM((width, width), BF)] * 3
        + [
            pltpu.VMEM((rows, width), BF),
            pltpu.VMEM((rows, width), F),
            pltpu.VMEM((rows, width), F),
            pltpu.VMEM((rows, width), BF),
            pltpu.VMEM((8, width), F),
            pltpu.SemaphoreType.DMA((4, 4)),
            pltpu.SemaphoreType.DMA((2,)),
        ],
        compiler_params=pltpu.CompilerParams(vmem_limit_bytes=VMEM_LIMIT),
        cost_estimate=cost(3e9, 10e6),
        name="input_back",
    )(
        gain, gains, parts, first[3], second[3], *ins, weights[0], weights[1], weights[2],
        tok_d, tok_q, d_hid, *after,
    )


def unpack_attn_kernel(heads, total_queries, own, one, two, three, *refs):
    outs, (gain_a, gain_f, gain_l, rel, loss, fraction, stack, smalls) = refs[-12:-8], refs[-8:]
    place = Place(True)
    rows = stack.shape[1]
    for m, part in enumerate((own, one, two, three)):
        stack[place.rep ^ m] = part[0:rows, :]
        smalls[place.rep ^ m] = join_small(part[rows:, :])
    for r in range(4):
        for c in range(3):
            outs[r][:, 256 * c : 256 * c + 256] = stack[r, 96 * c : 96 * c + 96, :].astype(F)
    total = smalls[0] + smalls[1] + smalls[2] + smalls[3]
    for i, gain in enumerate((gain_a, gain_f, gain_l)):
        row = jnp.concatenate([total[8 * i + c : 8 * i + c + 1, :] for c in range(6)], axis=1)
        gain[...] = row.reshape(gain.shape[0])
    rel[...] = total[32 : 32 + heads, 0 : rel.shape[1]]
    lane = lax.broadcasted_iota(jnp.int32, (1, 128), 1)
    line = total[24:25, :]
    loss_sum, hits, found = (jnp.sum(jnp.where(lane == i, line, 0.0)) for i in range(3))
    loss[0, 0] = loss_sum / total_queries
    fraction[0, 0] = hits / (DL * found)


def unpack_attn(heads, buckets, width, total_queries, parts):
    rows = parts[0].shape[0] - SMALL
    return pl.pallas_call(
        functools.partial(unpack_attn_kernel, heads, float(total_queries)),
        out_shape=(sds((96, width), F),) * 4
        + (sds((width,), F),) * 3
        + (sds((heads, buckets), F), sds((1, 1), F), sds((1, 1), F)),
        in_specs=[VM] * 4,
        out_specs=[VM] * 8 + [SM] * 2,
        scratch_shapes=[pltpu.VMEM((4, rows, 256), BF), pltpu.VMEM((4, SMALL, 128), F)],
        compiler_params=pltpu.CompilerParams(vmem_limit_bytes=16 * 1024 * 1024),
        cost_estimate=cost(1e6, 3e6),
        name="unpack_attn",
    )(*parts)


def unpack_kernel(own, one, two, three, *refs):
    stack = refs[-1]
    outs = refs[-5:-1]
    place = Place(True)
    half = own.shape[1]
    for m, part in enumerate((own, one, two, three)):
        for i in range(2):
            stack[place.rep ^ m, half * i : half * i + half, :] = part[i]
    for r in range(4):
        for c in range(4):
            first = (r % 2) * 1024 + 256 * c
            outs[r // 2][:, first : first + 256] = stack[
                r, 224 + 96 * c : 224 + 96 * c + 96, :
            ].astype(F)
        for c in range(3):
            outs[2][64 * r : 64 * r + 64, 256 * c : 256 * c + 256] = stack[
                r, 64 * c : 64 * c + 64, :
            ].astype(F)
    for r in range(3):
        outs[3][32 * r : 32 * r + 32, :] = stack[r, 192:224, 0:128].astype(F)


def unpack(parts, shapes, after):
    return pl.pallas_call(
        unpack_kernel,
        out_shape=tuple(sds(s, F) for s in shapes),
        in_specs=[VM] * 4 + [ANY] * len(after),
        out_specs=tuple(VM for _ in shapes),
        scratch_shapes=[pltpu.VMEM((4, 2 * parts[0].shape[1], parts[0].shape[2]), BF)],
        compiler_params=pltpu.CompilerParams(vmem_limit_bytes=16 * 1024 * 1024),
        cost_estimate=cost(1e6, 3e6),
        name="unpack_ffn",
    )(*parts, *after)


def swap(values, axis, size, mask):
    return lax.ppermute(values, axis, [(i, i ^ mask) for i in range(size)])


def near_kernel(keep_h, came_h, *refs):
    send_a, send_b, kept, came, sems = refs[-5:]
    place = Place(True)
    half = send_a.shape[2]
    y, x = place.y, place.x
    loads = []
    for z in range(4):
        pairs = []
        for i, (source, target) in enumerate(((keep_h, kept), (came_h, came))):
            pairs += [
                (source.at[z, :, 1 - x, pl.ds(0, half)], target.at[0, z]),
                (source.at[z, 1 - y, :, pl.ds(half, half)], target.at[1, z]),
            ]
        loads.append(start_all(pairs, sems.at[z]))
    for z in range(4):
        wait_all(loads[z])
        send_a[z] = kept[0, z] + came[0, z]
        send_b[z] = kept[1, z] + came[1, z]


def own_kernel(keep_h, came_h, *refs):
    own_a, own_b, kept, came, sems = refs[-5:]
    place = Place(True)
    half = own_a.shape[2]
    y, x = place.y, place.x
    loads = []
    for z in range(4):
        pairs = []
        for i, (source, target) in enumerate(((keep_h, kept), (came_h, came))):
            pairs += [
                (source.at[z, :, x, pl.ds(0, half)], target.at[0, z]),
                (source.at[z, y, :, pl.ds(half, half)], target.at[1, z]),
            ]
        loads.append(start_all(pairs, sems.at[z]))
    for z in range(4):
        wait_all(loads[z])
        own_a[z] = kept[0, z] + came[0, z]
        own_b[z] = kept[1, z] + came[1, z]


def cross_kernel(a, came_a, b, came_b, *refs):
    send_a, send_b, own_a, own_b = refs[-4:]
    place = Place(True)
    y, x = place.y, place.x
    send_a[0] = a[0, 1 - y] + came_a[0, 1 - y]
    own_a[0] = a[0, y] + came_a[0, y]
    send_b[0] = b[0, 1 - x] + came_b[0, 1 - x]
    own_b[0] = b[0, x] + came_b[0, x]


def line_kernel(a, came_a, b, came_b, *refs):
    send, own = refs[-2:]
    z = Place(True).z
    for i in range(2):
        for out, to in ((own, z ^ (2 * i)), (send, z ^ 1 ^ (2 * i))):
            out[i, 0] = a[to] + came_a[to]
            out[i, 1] = b[to] + came_b[to]


def next_kernel(own, came, *refs):
    send, out = refs[-2:]
    out[...] = own[0] + came[0]
    send[...] = own[1] + came[1]


def far_kernel(own, came, *refs):
    refs[-1][...] = own[...] + came[...]


def cell(index, half, first=0):
    return pl.ds(pl.multiple_of(index * half + first, 16), half)


def attn_near_kernel(keep_h, *refs):
    came_h = refs[:4]
    send_a, send_b, kept, came, sems = refs[-5:]
    place = Place(True)
    half = send_b.shape[2]
    loads = split_loads(keep_h, came_h, kept, came, sems, half, 1 - place.x, 1 - place.y)
    for z in range(4):
        wait_all(loads[z])
        send_a[z] = kept[0, z] + came[0, z]
        send_b[z] = kept[1, z] + came[1, z]


def split_loads(keep_h, came_h, kept, came, sems, half, x, y):
    def rows(cell_number, first):
        return pl.ds(pl.multiple_of(cell_number * 2 * half + first, 16), half)

    loads = []
    for z in range(4):
        pairs = []
        for source, base, target in ((keep_h, 4 * z, kept), (came_h[z], 0, came)):
            for i in range(2):
                pairs += [
                    (source.at[rows(base + 2 * i + x, 0)], target.at[0, z, i]),
                    (source.at[rows(base + 2 * y + i, half)], target.at[1, z, i]),
                ]
        loads.append(start_all(pairs, sems.at[z]))
    return loads


def attn_own_kernel(keep_h, *refs):
    came_h = refs[:4]
    own_a, own_b, kept, came, sems = refs[-5:]
    place = Place(True)
    half = own_a.shape[2]
    loads = split_loads(keep_h, came_h, kept, came, sems, half, place.x, place.y)
    for z in range(4):
        wait_all(loads[z])
        own_a[z] = kept[0, z] + came[0, z]
        own_b[z] = kept[1, z] + came[1, z]


def attn_cross_kernel(a, came_a, b, came_b, *refs):
    send_a, send_b, own_a, own_b = refs[-4:]
    place = Place(True)
    y, x = place.y, place.x
    for z in range(4):
        send_a[z] = a[z, 1 - y] + came_a[z, 1 - y]
        own_a[z] = a[z, y] + came_a[z, y]
        send_b[z] = b[z, 1 - x] + came_b[z, 1 - x]
        own_b[z] = b[z, x] + came_b[z, x]


def attn_line_kernel(a, came_a, b, came_b, small_a, small_b, *refs):
    send, own, small = refs[-3:]
    z = Place(True).z
    half = a.shape[1]
    for i in range(2):
        for out, to in ((own, z ^ (2 * i)), (send, z ^ 1 ^ (2 * i))):
            out[2 * half * i : 2 * half * i + half, :] = a[to] + came_a[to]
            out[2 * half * i + half : 2 * half * i + 2 * half, :] = b[to] + came_b[to]
    value = split_small(small_a[...] + small_b[...])
    send[4 * half :, :] = value
    small[...] = value


def attn_next_kernel(own, came, small_in, *refs):
    send, out, small = refs[-3:]
    rows = out.shape[0]
    out[...] = own[0:rows, :] + came[0:rows, :]
    send[0:rows, :] = own[rows : 2 * rows, :] + came[rows : 2 * rows, :]
    value = split_small(join_small(small_in[...]) + join_small(came[2 * rows :, :]))
    send[rows:, :] = value
    small[...] = value


def attn_far_kernel(own, came, small_in, *refs):
    out = refs[-1]
    rows = own.shape[0]
    out[0:rows, :] = own[...] + came[0:rows, :]
    out[rows:, :] = split_small(join_small(small_in[...]) + join_small(came[rows:, :]))


def stage(kernel, name, ins, outs, after, flops=1, scratch=(), scalars=0, limit=16):
    return pl.pallas_call(
        kernel,
        out_shape=outs,
        in_specs=[VM] * len(ins) + [ANY] * len(after),
        out_specs=[VM] * (len(outs) - scalars) + [SM] * scalars,
        scratch_shapes=list(scratch),
        compiler_params=pltpu.CompilerParams(vmem_limit_bytes=limit * 1024 * 1024),
        cost_estimate=cost(flops, 1),
        name=name,
    )(*ins, *after)


class AttnReduction:
    def __init__(self, keep, send):
        self.half = 144
        self.keep = keep
        self.came = [swap(part, "wide", 8, 1) for part in send]
        self.small_shape = sds((SMALL, 256), BF)

    def rows(self, cells):
        return sds((cells * self.half + SMALL, 256), BF)

    def split(self, kernel, name, ins, outs, after):
        held = pltpu.VMEM((2, 4, 2, self.half, 256), BF)
        scratch = [held, held, pltpu.SemaphoreType.DMA((4, 8))]
        return pl.pallas_call(
            kernel,
            out_shape=outs,
            in_specs=[ANY] * 5 + [VM] * len(ins) + [ANY] * len(after),
            out_specs=(VM,) * len(outs),
            scratch_shapes=scratch,
            compiler_params=pltpu.CompilerParams(vmem_limit_bytes=VMEM_LIMIT),
            cost_estimate=cost(1, 1),
            name=name,
        )(self.keep, *self.came, *ins, *after)

    def near(self, after):
        outs = (sds((4, 2, self.half, 256), BF),) * 2
        send_a, send_b = self.split(attn_near_kernel, "near_attn", (), outs, after)
        self.came_a = swap(send_a, "rep", 4, 1)
        self.came_b = swap(send_b, "rep", 4, 2)
        return (send_a,)

    def mine(self, after):
        own = sds((4, 2, self.half, 256), BF)
        self.a, self.b = self.split(attn_own_kernel, "own_attn", (), (own, own), after)
        return (self.a,)

    def cross(self, after):
        outs = (sds((4, self.half, 256), BF),) * 4
        ins = (self.a, self.came_a, self.b, self.came_b)
        send_a, send_b, self.a, self.b = stage(attn_cross_kernel, "cross_attn", ins, outs, after)
        self.came_a = swap(send_a, "rep", 4, 2)
        self.came_b = swap(send_b, "rep", 4, 1)
        return (self.a,)

    def line(self, small, after):
        own = sds((4 * self.half, 256), BF)
        outs = (self.rows(4), own, self.small_shape)
        ins = (self.a, self.came_a, self.b, self.came_b, small, swap(small, "wide", 8, 1))
        send, self.own, self.small = stage(attn_line_kernel, "line_attn", ins, outs, after)
        self.came = swap(send, "wide", 8, 2)
        return (self.own,)

    def next(self, after):
        own = sds((2 * self.half, 256), BF)
        ins = (self.own, self.came, self.small)
        outs = (self.rows(2), own, self.small_shape)
        send, self.own, self.small = stage(attn_next_kernel, "next_attn", ins, outs, after)
        self.came = swap(send, "wide", 8, 4)
        return (self.own,)

    def far(self, after):
        ins = (self.own, self.came, self.small)
        (self.own,) = stage(attn_far_kernel, "far_attn", ins, (self.rows(2),), after)
        self.came = [swap(self.own, "rep", 4, m) for m in (1, 2, 3)]
        return (self.own,)

    def parts(self):
        return self.own, *self.came


class Reduction:
    def __init__(self, name, keep, send):
        self.name = name
        self.half = keep.shape[3] // 2
        self.keep = keep
        self.came = swap(send, "wide", 8, 1)

    def split(self, kernel, name, ins, shapes, specs, after):
        held = pltpu.VMEM((2, 4, 2, self.half, 256), BF)
        return pl.pallas_call(
            kernel,
            out_shape=tuple(sds(shape, BF) for shape in shapes),
            in_specs=[ANY] * 2 + specs + [ANY] * len(after),
            out_specs=(VM,) * len(shapes),
            scratch_shapes=[held, held, pltpu.SemaphoreType.DMA((4, 4))],
            compiler_params=pltpu.CompilerParams(vmem_limit_bytes=VMEM_LIMIT),
            cost_estimate=cost(1, 1),
            name=name + self.name,
        )(self.keep, self.came, *ins, *after)

    def near(self, after):
        shape = (4, 2, self.half, 256)
        send_a, send_b = self.split(near_kernel, "near_", (), (shape,) * 2, [], after)
        self.came_a = swap(send_a, "rep", 4, 1)
        self.came_b = swap(send_b, "rep", 4, 2)
        return (send_a,)

    def step(self, kernel, name, ins, shapes, after, flops=1):
        outs = tuple(sds(shape, BF) for shape in shapes)
        return stage(kernel, name + self.name, ins, outs, after, flops, limit=20)

    def mine(self, after):
        shape = (4, 2, self.half, 256)
        self.a, self.b = self.split(own_kernel, "own_", (), (shape,) * 2, [], after)
        return (self.a,)

    def cross(self, after):
        shape = (4, self.half, 256)
        ins = (self.a, self.came_a, self.b, self.came_b)
        whole = pl.BlockSpec((1, 2, self.half, 256), lambda i: (i, 0, 0, 0))
        part = pl.BlockSpec((1, self.half, 256), lambda i: (i, 0, 0))
        send_a, send_b, self.a, self.b = pl.pallas_call(
            cross_kernel,
            grid=(4,),
            out_shape=(sds(shape, BF),) * 4,
            in_specs=[whole] * 4 + [ANY] * len(after),
            out_specs=(part,) * 4,
            compiler_params=pltpu.CompilerParams(vmem_limit_bytes=VMEM_LIMIT),
            cost_estimate=cost(1, 1),
            name="cross_" + self.name,
        )(*ins, *after)
        self.came_a = swap(send_a, "rep", 4, 2)
        self.came_b = swap(send_b, "rep", 4, 1)
        return (self.a,)

    def line(self, after, flops=1):
        ins = (self.a, self.came_a, self.b, self.came_b)
        shape = (2, 2, self.half, 256)
        send, self.own = self.step(line_kernel, "line_", ins, (shape,) * 2, after, flops)
        self.came = swap(send, "wide", 8, 2)
        return (self.own,)

    def next(self, after):
        shape = (2, self.half, 256)
        send, self.own = self.step(next_kernel, "next_", (self.own, self.came), (shape,) * 2, after)
        self.came = swap(send, "wide", 8, 4)
        return (self.own,)

    def far(self, after):
        shape = (2, self.half, 256)
        (self.own,) = self.step(far_kernel, "far_", (self.own, self.came), (shape,), after)
        self.came = [swap(self.own, "rep", 4, m) for m in (1, 2, 3)]
        return (self.own,)

    def parts(self):
        return self.own, *self.came


def natural(which, keep, send):
    both = jnp.stack([keep, send])
    if which == "attn":
        a = both.reshape(2, 4, 4, 3, 96, 256).transpose(2, 1, 0, 4, 3, 5).reshape(4, 768, 768)
        return [a[i] for i in range(4)]
    both = both.reshape((2, 4, 4) + both.shape[4:])
    a = both[:, :, :, 224:].reshape(2, 4, 4, 4, 96, 256).transpose(1, 0, 4, 2, 3, 5)
    a = a.reshape(768, 4096)
    d = both[:, :, :, :192].reshape(2, 4, 4, 3, 64, 256).transpose(1, 0, 2, 4, 3, 5)
    e = both[:, :, :3, 192:224, :128].transpose(1, 0, 2, 3, 4)
    return [a[:, :2048], a[:, 2048:], d.reshape(2048, 768), e.reshape(768, 128)]


def body(
    doc_tokens, query_tokens, doc_cotangent, query_cotangent, retrieved, pos_ids, pos_count,
    w_query, w_key, carried_content_weights, w_out, w_gate, w_up, w_down, w_proj,
    gain_attn, gain_ffn, gain_final, rel_bias,
):
    n_wide = lax.axis_size("wide")
    n_rep = lax.axis_size("rep")
    group = retrieved.shape[1]
    fast = n_wide == 8 and n_rep == 4 and group == 64
    weights = (w_query, w_key, carried_content_weights, w_out, w_gate, w_up, w_down, w_proj)
    width = doc_tokens.shape[1]
    buckets, heads = rel_bias.shape
    hot_np = bucket_hot(buckets)
    hot = jnp.asarray(hot_np, BF)
    hot_f = jnp.asarray(hot_np, F)
    rep_hot = jnp.asarray(query_hot(64), BF)
    rel = jnp.transpose(rel_bias)
    queries = pos_ids.shape[0]
    ids = jnp.transpose(pos_ids)
    columns = jnp.transpose(retrieved)
    gains = (gain_attn, gain_ffn, gain_final)

    doc, sends = layer_forward(doc_tokens, weights, gains, rel, hot, DL, (columns,) if fast else ())
    if fast:
        near = [sends[0]] + [swap(sends[m], "wide", n_wide, 2 * m) for m in (1, 2, 3)]
    query, _ = layer_forward(query_tokens, weights, gains, rel, hot, QUERY_LENGTH, (), (doc["emb"],))
    if fast:
        ins = near + [swap(stack_rows(near, (query["emb"],)), "wide", n_wide, 1)]
    else:
        mask_query = lax.all_to_all(columns.astype(F), "wide", 0, 0, tiled=True)
        mask_query = mask_query.reshape(n_wide, queries, DL)
        ins = [lax.all_gather(doc["emb"], "wide", axis=0, tiled=True), mask_query]
    if fast:
        line = [query["emb"]] + [swap(query["emb"], "wide", n_wide, 2 * m) for m in (1, 2, 3)]
    coef, d_query_emb, parts = query_sims(
        fast, ids, pos_count, query["emb"], query_cotangent, ins, n_wide
    )
    coef_all = lax.all_to_all(coef, "wide", 0, 0, tiled=True)
    if fast:
        every = stack_rows(line, (coef,))
        others = swap(every, "wide", n_wide, 1)
    else:
        every = lax.all_gather(query["emb"], "wide", axis=0, tiled=True)
        others = query["emb"]
    d_hid, d_attn, g, gains_both, keep_f, send_f = back(
        fast, doc_cotangent, doc["emb"], every, others, columns, rep_hot, coef_all, d_query_emb, doc, query,
        gains, weights,
    )
    if fast:
        ffn = Reduction("ffn", keep_f, send_f)
    early = 2
    first = attn_back(0, early, True, g, doc, query, hot_f, ())
    after = ffn.near((first[3],)) if fast else ()
    second = attn_back(early, heads // 2 - early, False, g, doc, query, hot_f, after)
    after = ffn.mine((second[3],)) if fast else (second[3],)
    keep_a, send_a = attn_grads(fast, first, second, d_attn, doc, query, after)
    after = (keep_a,)
    if fast:
        attn = AttnReduction(keep_a, send_a)
        after = ffn.cross(after)
        after = attn.near(after)
        after = attn.mine(after)
        after = ffn.line(after)
    doc_grad, query_grad, small = input_back(
        doc_tokens, query_tokens, d_hid, gain_attn, gains_both, parts, first, second, weights, after
    )
    if fast:
        after = attn.cross((small,))
        after = ffn.next(after)
        after = attn.line(small, after)
        after = ffn.far(after)
        after = attn.next(after)
        after = attn.far(after)
        grad_gate, grad_up, grad_down, grad_proj = unpack(
            ffn.parts(), ((96, 2048), (96, 2048), (256, 768), (96, 128)), after
        )
        (
            grad_query, grad_key, grad_value, grad_out,
            total_gain_a, total_gain_f, total_gain_l, total_rel, loss, fraction,
        ) = unpack_attn(heads, buckets, width, queries * n_wide * n_rep, attn.parts())
        loss = loss.reshape(())
        fraction = fraction.reshape(())
    else:
        small = lax.psum(small, ("rep", "wide"))

        def total(whole):
            part = lax.psum_scatter(whole, "wide", scatter_dimension=0, tiled=True)
            return lax.psum(part, "rep").astype(F)

        grad_query, grad_key, grad_value, grad_out = (total(a) for a in natural("attn", keep_a, jnp.concatenate(send_a)))
        grad_gate, grad_up, grad_down, grad_proj = (total(a) for a in natural("ffn", keep_f, send_f))
        total_gain_a, total_gain_f, total_gain_l = (
            small[8 * i : 8 * i + 6].reshape(width) for i in range(3)
        )
        total_rel = small[32 : 32 + heads, 0:buckets]
        loss = small[24, 0] / (queries * n_wide * n_rep)
        fraction = small[24, 1] / (DL * small[24, 2])
    return (
        doc["emb"],
        query["emb"],
        doc_grad,
        query_grad,
        grad_query,
        grad_key,
        grad_value,
        grad_out,
        grad_gate,
        grad_up,
        grad_down,
        grad_proj,
        total_gain_a,
        total_gain_f,
        total_gain_l,
        jnp.transpose(total_rel),
        loss,
        fraction,
    )


def solution(mesh):
    rows = P(("rep", "wide"), None)
    return jax.shard_map(
        body,
        mesh=mesh,
        in_specs=(rows,) * 6 + (P(("rep", "wide")),) + (P(),) * 12,
        out_specs=(rows,) * 4 + (P("wide", None),) * 8 + (P(),) * 6,
        check_vma=False,
    )
```

```python
import functools

import jax
import jax.numpy as jnp
import numpy as np
from jax import lax
from jax.experimental import pallas as pl
from jax.experimental.pallas import tpu as pltpu
from jax.sharding import PartitionSpec as P

DL = 512
QUERY_LENGTH = 32
EPS = 1e-06
SCALE = 10.0
BF = jnp.bfloat16
F = jnp.float32
TABLE = 512
VMEM_LIMIT = 60 * 1024 * 1024

SAVED = (
    "n1", "q", "k", "v", "p", "li", "ctx", "hid", "n2", "gv", "us", "act", "h2", "n3", "proj", "lr", "emb",
)

SM = pl.BlockSpec(memory_space=pltpu.SMEM)
ANY = pl.BlockSpec(memory_space=pl.ANY)
VM = pl.BlockSpec(memory_space=pltpu.VMEM)


def mm(a, b):
    return jnp.dot(a, b, preferred_element_type=F)


def mm_nt(a, b):
    return lax.dot_general(a, b, (((1,), (1,)), ((), ())), preferred_element_type=F)


def mm_tn(a, b):
    return lax.dot_general(a, b, (((0,), (0,)), ((), ())), preferred_element_type=F)


def bucket_hot(buckets):
    half = buckets // 2
    exact = half // 2
    column = np.arange(TABLE)
    relative = 128 - np.where(column <= TABLE - 128, column, column - TABLE)
    base = (relative > 0).astype(np.int64) * half
    distance = np.abs(relative)
    large = exact + (
        np.log(np.maximum(distance, 1) / float(exact)) / np.log(128.0 / exact) * (half - exact)
    ).astype(np.int64)
    large = np.minimum(large, half - 1)
    number = base + np.where(distance < exact, distance, large)
    return (np.arange(buckets)[:, None] == number[None, :]).astype(np.float32)


def query_hot(queries):
    tokens = np.arange(queries * QUERY_LENGTH)
    return (np.arange(queries)[:, None] == tokens[None, :] // QUERY_LENGTH).astype(np.float32)


def cost(flops, moved):
    large = flops > 1e8
    return pl.CostEstimate(flops=int(1e12 if large else 1), bytes_accessed=1, transcendentals=0)


class Place:
    def __init__(self, fast):
        self.fast = fast
        self.rep = lax.axis_index("rep")
        self.wide = lax.axis_index("wide")
        self.y, self.x = self.rep >> 1, self.rep & 1
        self.z = self.wide >> 1
        self.own = self.wide & 1 if fast else 0

    def doc(self, slot):
        return self.wide ^ (2 * (slot % 4)) ^ (slot // 4) if self.fast else slot

    def source(self, slot):
        return self.wide ^ slot if self.fast else slot


def row_of(gain):
    return gain[...].astype(F).reshape(1, gain.shape[0])


def stack_kernel(n_parts, *refs):
    out = refs[-1]
    row = 0
    for part in refs[:n_parts]:
        out[row : row + part.shape[0], :] = part[...]
        row += part.shape[0]


def stack_rows(parts, after):
    rows = sum(part.shape[0] for part in parts)
    return pl.pallas_call(
        functools.partial(stack_kernel, len(parts)),
        out_shape=sds((rows, 128), BF),
        in_specs=[VM] * len(parts) + [ANY] * len(after),
        out_specs=VM,
        cost_estimate=cost(1, 1),
        name="stack_rows",
    )(*parts, *after)


def sds(shape, dtype):
    return jax.ShapeDtypeStruct(shape, dtype)


def rows_loop(count, block, fn):
    def step(i, carry):
        fn(pl.ds(pl.multiple_of(i * block, block), block))
        return carry

    lax.fori_loop(0, count // block, step, 0, unroll=2)


def half_masks():
    lane = lax.broadcasted_iota(jnp.int32, (1, 128), 1)
    low = (lane < 64).astype(F)
    high = 1.0 - low
    one_low = (lane == 0).astype(F)
    one_high = (lane == 64).astype(F)
    return low, high, one_low, one_high


def rms(values):
    return lax.rsqrt(jnp.mean(values * values, axis=-1, keepdims=True) + EPS)


def rms_back(values, gain, d_result):
    inverse = rms(values)
    scaled = values * inverse
    grad_gain = jnp.sum(d_result * scaled, axis=0, keepdims=True)
    gained = d_result * gain
    d_values = inverse * (gained - scaled * jnp.mean(gained * scaled, axis=-1, keepdims=True))
    return d_values, grad_gain


def gelu_parts(gate):
    square = gate * gate
    tangent = jnp.tanh(gate * (0.7978845608028654 + (0.7978845608028654 * 0.044715) * square))
    half_plus = 0.5 + 0.5 * tangent
    value = gate * half_plus
    slope = half_plus + 0.5 * gate * (1.0 - tangent * tangent) * (
        0.7978845608028654 + (3.0 * 0.7978845608028654 * 0.044715) * square
    )
    return value, slope


def start_all(pairs, sems):
    copies = [pltpu.make_async_copy(src, dst, sems.at[i]) for i, (src, dst) in enumerate(pairs)]
    for copy in copies:
        copy.start()
    return copies


def wait_all(copies):
    for copy in copies:
        copy.wait()


def fwd_kernel(
    seq,
    heads,
    n_after,
    columns,
    tok, ga, gf, gl, rel, hot, wq_h, wk_h, wv_h, wo_h, wg_h, wu_h, wd_h, wp_h,
    *refs,
):
    (
    n1_h, q_h, k_h, v_h, p_h, li_h, ctx_h, hid_h, n2_h, gv_h, us_h, act_h, h2_h, n3_h, proj_h, lr_h, emb,
    wq, wk, wv, wo, wg, wu, wd, wp,
    n1, q, k, v, p, li, ctx, hid, n2, gv, us, act, h2, n3, proj, lr,
    tbl, bs, sem_in, sem_tile, sem_push, sem_out, _,
    ) = refs[n_after + columns : n_after + columns + 17] + refs[len(refs) - 31 :]
    sends = refs[n_after + columns + 17 : len(refs) - 31]
    count = tok.shape[0]
    loads = start_all(((wq_h, wq), (wk_h, wk), (wv_h, wv), (wo_h, wo), (wp_h, wp)), sem_in)

    def tile_loads(t):
        cols = pl.ds(pl.multiple_of(t * 512, 512), 512)
        pairs = ((wg_h.at[:, cols], wg.at[:, cols]), (wu_h.at[:, cols], wu.at[:, cols]), (wd_h.at[cols], wd.at[cols]))
        return [pltpu.make_async_copy(src, dst, sem_tile.at[t, i]) for i, (src, dst) in enumerate(pairs)]

    def tile_pushes(t):
        cols = pl.ds(pl.multiple_of(t * 512, 512), 512)
        pairs = tuple((a.at[:, cols], b.at[:, cols]) for a, b in ((gv, gv_h), (us, us_h), (act, act_h)))
        return [pltpu.make_async_copy(src, dst, sem_push.at[t, i]) for i, (src, dst) in enumerate(pairs)]

    outs = {}

    def push(i, src, dst):
        outs[i] = pltpu.make_async_copy(src, dst, sem_out.at[i])
        outs[i].start()

    gain_a, gain_f, gain_l = row_of(ga), row_of(gf), row_of(gl)

    def norm_one(rows):
        x = tok[rows, :].astype(F)
        n1[rows, :] = (x * rms(x) * gain_a).astype(BF)

    rows_loop(count, 128, norm_one)
    push(0, n1, n1_h)
    lines = mm(rel[...], hot[...])
    for h in range(heads):
        tbl[h] = lines[h : h + 1, :]
    for i, (w, r, r_h) in enumerate(((wq, q, q_h), (wk, k, k_h), (wv, v, v_h))):
        loads[i].wait()
        r[...] = mm(n1[...], w[...]).astype(BF)
        push(1 + i, r, r_h)
    n_tiles = wg.shape[1] // 512
    for t in range(2):
        for copy in tile_loads(t):
            copy.start()

    low, high, one_low, one_high = half_masks()
    is_low = low > 0.5

    blocks = count // 128

    def table(head, carry):
        row = jnp.broadcast_to(tbl[head], (128, TABLE))
        base = pltpu.roll(row, 0, 1, stride=1, stride_axis=0)
        if seq == DL:
            bs[head] = base[:, 0:384]
        else:
            rows = lax.broadcasted_iota(jnp.int32, (128, 128), 0) // seq
            columns = lax.broadcasted_iota(jnp.int32, (128, 128), 1) // seq
            bs[head] = jnp.where(rows == columns, base[:, 128:256], -1e30)
        return carry

    lax.fori_loop(0, heads, table, 0, unroll=4)

    def halves(index):
        lanes = pl.ds(pl.multiple_of(index * 128, 128), 128)
        q2 = q[:, lanes]
        k2 = k[:, lanes]
        v2 = v[:, lanes]
        parts = []
        for keep, one in ((low, one_high), (high, one_low)):
            parts.append((k2 * keep.astype(BF), v2 * keep.astype(BF) + one.astype(BF)))
        return lanes, q2, parts

    def join(lanes, o0, o1):
        inv = 1.0 / jnp.where(is_low, o0[:, 64:65], o1[:, 0:1])
        li[:, lanes] = inv
        ctx[:, lanes] = (jnp.where(is_low, o0, o1) * inv).astype(BF)

    def doc_scores(index):
        _, q2, parts = halves(index)
        for e in range(2):
            for half in range(2):
                yield mm_nt(parts[e][0], q2[256 * half : 256 * half + 256])

    def doc_softmax(head, score, i):
        cols = slice(128 * i, 128 * i + 128)
        terms = []
        for j in range(blocks):
            term = score[128 * j : 128 * j + 128, 128 * (i % 2) : 128 * (i % 2) + 128]
            if abs(j - i) <= 1:
                t = 1 - (j - i)
                terms.append(term + bs[head, :, 128 * t : 128 * t + 128])
            else:
                terms.append(term + (tbl[head, :, 0:1] if j > i else tbl[head, :, 256:257]))
        peak = functools.reduce(jnp.maximum, terms)
        peak = jnp.max(peak, axis=0, keepdims=True)
        total = jnp.zeros((128, 128), F)
        probs = []
        for j in range(blocks):
            power = jnp.exp(terms[j] - peak)
            total = total + power
            probs.append(power.astype(BF))
            p[head, 128 * j : 128 * j + 128, cols] = probs[-1]
        lr[head, :, cols] = 1.0 / jnp.sum(total, axis=0, keepdims=True)
        return jnp.concatenate(probs, axis=0)

    def doc_pairs(first, number):
        scores = list(doc_scores(first))
        for index in range(number):
            lanes, _, parts = halves(first + index)
            coming = doc_scores(first + index + 1) if index + 1 < number else iter(())
            following = []
            sides = []
            for e in range(2):
                head = 2 * (first + index) + e
                done = []
                for half in range(2):
                    following += [c for c in [next(coming, None)] if c is not None]
                    probs = [doc_softmax(head, scores[2 * e + half], 2 * half + i) for i in range(2)]
                    done.append(mm_tn(jnp.concatenate(probs, axis=1), parts[e][1]))
                sides.append(jnp.concatenate(done, axis=0))
            join(lanes, *sides)
            scores = following

    def query_group(group, carry):
        pairs = [halves(group * 3 + i) for i in range(3)]
        cells = [(i, e, b) for i in range(3) for e in range(2) for b in range(blocks)]
        rows = [slice(128 * b, 128 * b + 128) for b in range(blocks)]
        scores = [mm_nt(pairs[i][2][e][0][rows[b]], pairs[i][1][rows[b]]) for i, e, b in cells]
        probs = []
        for score, (i, e, b) in zip(scores, cells):
            head = (group * 3 + i) * 2 + e
            term = score + bs[head]
            power = jnp.exp(term - jnp.max(term, axis=0, keepdims=True))
            probs.append(power.astype(BF))
            p[head, rows[b], :] = probs[-1]
            lr[head, :, rows[b]] = 1.0 / jnp.sum(power, axis=0, keepdims=True)
        outs_g = [mm_tn(pb, pairs[i][2][e][1][rows[b]]) for pb, (i, e, b) in zip(probs, cells)]
        for i in range(3):
            sides = [
                jnp.concatenate([outs_g[cells.index((i, e, b))] for b in range(blocks)], axis=0)
                for e in range(2)
            ]
            join(pairs[i][0], *sides)
        return carry

    if seq == DL:
        def doc_group(group, carry):
            doc_pairs(group * 3, 3)
            return carry

        lax.fori_loop(0, heads // 2 // 3, doc_group, 0)
    else:
        lax.fori_loop(0, heads // 6, query_group, 0)
    push(4, p, p_h)
    push(5, li, li_h)
    push(15, lr, lr_h)
    push(6, ctx, ctx_h)

    loads[3].wait()

    def middle(rows):
        h = tok[rows, :].astype(F) + mm(ctx[rows, :], wo[...])
        hid[rows, :] = h
        h2[rows, :] = h
        n2[rows, :] = (h * rms(h) * gain_f).astype(BF)

    rows_loop(count, 256, middle)
    push(7, hid, hid_h)
    push(8, n2, n2_h)

    def ffn(t, carry):
        cols = pl.ds(pl.multiple_of(t * 512, 512), 512)

        @pl.when(t + 2 < n_tiles)
        def _():
            for copy in tile_loads(t + 2):
                copy.start()

        wait_all(tile_loads(t))
        row_blocks = [slice(256 * b, 256 * b + 256) for b in range(count // 256)]
        products = [(mm(n2[rows, :], wg[:, cols]), mm(n2[rows, :], wu[:, cols])) for rows in row_blocks]
        for rows, (gate, up) in zip(row_blocks, products):
            value, slope = gelu_parts(gate)
            a = (value * up).astype(BF)
            gv[rows, cols] = value.astype(BF)
            us[rows, cols] = (up * slope).astype(BF)
            act[rows, cols] = a
            h2[rows, :] += mm(a, wd[cols, :])
        for copy in tile_pushes(t):
            copy.start()
        return carry

    lax.fori_loop(0, n_tiles, ffn, 0)
    loads[4].wait()

    def top(rows):
        h = h2[rows, :]
        n = (h * rms(h) * gain_l).astype(BF)
        n3[rows, :] = n
        pr = mm(n, wp[...])
        proj[rows, :] = pr
        emb[rows, :] = (pr * lax.rsqrt(jnp.sum(pr * pr, axis=-1, keepdims=True) + EPS)).astype(BF)

    rows_loop(count, 256, top)
    if columns:
        z = lax.axis_index("wide") >> 1
        sent_mask = refs[-1]
        sent_mask[...] = refs[0][...].astype(F).astype(BF)
        for m, send in enumerate(sends):
            send[0:count, :] = emb[...]
            own_rows = sent_mask[pl.ds(pl.multiple_of(16 * (z ^ m), 16), 16), :]
            for b in range(DL // 128):
                first = count + 16 * b
                send[first : first + 16, :] = own_rows[:, 128 * b : 128 * b + 128]
    push(12, h2, h2_h)
    push(13, n3, n3_h)
    push(14, proj, proj_h)
    wait_all(outs.values())
    for t in range(n_tiles):
        wait_all(tile_pushes(t))


def layer_forward(tokens, weights, gains, rel, hot, seq, columns=(), after=()):
    count, width = tokens.shape
    wq, wk, wv, wo, wg, wu, wd, wp = weights
    hidden = wg.shape[1]
    emb = wp.shape[1]
    heads = rel.shape[0]
    keys = DL if seq == DL else 128
    saved = (
        sds((count, width), BF),
        sds((count, width), BF),
        sds((count, width), BF),
        sds((count, width), BF),
        sds((heads, count, keys), BF),
        sds((count, width), F),
        sds((count, width), BF),
        sds((count, width), F),
        sds((count, width), BF),
        sds((count, hidden), BF),
        sds((count, hidden), BF),
        sds((count, hidden), BF),
        sds((count, width), F),
        sds((count, width), BF),
        sds((count, emb), F),
        sds((heads, 1, count), F),
    )
    outs = pl.pallas_call(
        functools.partial(fwd_kernel, seq, heads, len(after), len(columns)),
        out_shape=saved
        + (sds((count, emb), BF),)
        + (sds((count + 16 * DL // 128, emb), BF),) * (4 * len(columns)),
        in_specs=[VM] * 6 + [ANY] * 8 + [VM] * len(columns) + [ANY] * len(after),
        out_specs=[ANY] * 16 + [VM] * (1 + 4 * len(columns)),
        scratch_shapes=[pltpu.VMEM(w.shape, BF) for w in weights]
        + [pltpu.VMEM(s.shape, s.dtype) for s in saved]
        + [
            pltpu.VMEM((heads, 1, TABLE), F),
            pltpu.VMEM((heads, 128, 384 if seq == DL else 128), F),
            pltpu.SemaphoreType.DMA((5,)),
            pltpu.SemaphoreType.DMA((hidden // 512, 3)),
            pltpu.SemaphoreType.DMA((hidden // 512, 3)),
            pltpu.SemaphoreType.DMA((16,)),
            pltpu.VMEM((64, DL) if columns else (16, 128), BF),
        ],
        compiler_params=pltpu.CompilerParams(vmem_limit_bytes=VMEM_LIMIT),
        cost_estimate=cost(count * 14e6, 40e6),
        name="layer_forward_%d" % seq,
    )(tokens, *gains, rel, hot, *weights, *columns, *after)
    return dict(zip(SAVED, outs)), outs[len(SAVED) :]


def each_block(arrays, block, fn):
    first = 0
    for array in arrays:
        number = array.shape[0] // block
        if number == 1:
            fn(first, array[...])
        else:

            def step(i, carry, array=array, first=first):
                fn(first + i, array[pl.ds(pl.multiple_of(i * block, block), block), :])
                return carry

            lax.fori_loop(0, number, step, 0)
        first += number


def query_sims_kernel(fast, n_docs, n_ins, ids, used, qemb, cot, *refs):
    ins = refs[:n_ins]
    *coefs, d_emb, parts, es, total, counts = refs[n_ins:]
    place = Place(fast)
    tokens = qemb.shape[0]
    queries = tokens // QUERY_LENGTH
    lane = lax.broadcasted_iota(jnp.int32, (tokens, 128), 1)
    lane_q = lax.broadcasted_iota(jnp.int32, (queries, 128), 1)
    total[...] = jnp.zeros_like(total)
    counts[...] = jnp.zeros_like(counts)

    if fast:
        row = lax.broadcasted_iota(jnp.int32, (queries, 16), 0)
        pick = row + queries * place.own == lax.broadcasted_iota(jnp.int32, (queries, 16), 1)
        pick = jnp.where(pick, 1.0, 0.0).astype(BF)
        per = DL + 16 * DL // 128

        def rows_at(slot, first, last):
            if slot < 4:
                return ins[slot][first:last, :]
            base = per * (slot - 4)
            return ins[4][base + first : base + last, :]

        def doc_at(slot):
            return rows_at(slot, 0, DL)

        def mask_at(slot):
            packed = rows_at(slot, DL, per)
            return jnp.concatenate([mm(pick, packed[16 * b : 16 * b + 16]) for b in range(4)], axis=1)

        def each(fn):
            for slot in range(n_docs):
                fn(slot)

    else:
        docs, mask = ins

        def doc_at(slot):
            return docs[pl.ds(pl.multiple_of(slot * DL, DL), DL), :]

        def mask_at(slot):
            return mask[slot]

        def each(fn):
            def step(i, carry):
                fn(i)
                return carry

            lax.fori_loop(0, n_docs, step, 0)

    def forward(slot):
        d = place.doc(slot)
        m = mask_at(slot)
        wide = jnp.broadcast_to(m[:, None, :], (queries, QUERY_LENGTH, DL)).reshape(tokens, DL)
        e = jnp.exp(mm_nt(qemb[...], doc_at(slot)) * SCALE) * wide
        es[slot] = e
        total[...] = jnp.where(lane == d, jnp.sum(e, axis=1, keepdims=True), total[...])
        counts[...] = jnp.where(lane_q == d, jnp.sum(m, axis=1, keepdims=True), counts[...])

    each(forward)
    inside = lane_q < n_docs
    z = jnp.sum(jnp.log(1.0 + total[...]).reshape(queries, QUERY_LENGTH, 128), axis=1)
    z = z * (1.0 / QUERY_LENGTH)
    hot = jnp.zeros((queries, 128), F)
    row_q = lax.broadcasted_iota(jnp.int32, (queries, 128), 0)
    for q in range(queries):
        for s in range(ids.shape[0]):
            number = jnp.where(s < used[q], ids[s, q], 128)
            hot = jnp.where((row_q == q) & (lane_q == number), 1.0, hot)
    peak = jnp.max(jnp.where(inside, z, -1e30), axis=1, keepdims=True)
    power = jnp.where(inside, jnp.exp(jnp.where(inside, z - peak, 0.0)), 0.0)
    whole = jnp.sum(power, axis=1, keepdims=True)
    positive = jnp.sum(hot * power, axis=1, keepdims=True)
    loss = jnp.sum(jnp.log(whole) - jnp.log(positive))
    hits = jnp.sum(hot * counts[...])
    found = jnp.sum(hot)
    lane_p = lax.broadcasted_iota(jnp.int32, (8, 128), 1)
    parts[...] = jnp.where(
        lane_p == 0, loss, jnp.where(lane_p == 1, hits, jnp.where(lane_p == 2, found, 0.0))
    )
    d_z = power / whole - hot * power / positive
    d_wide = jnp.broadcast_to(d_z[:, None, :], (queries, QUERY_LENGTH, 128)).reshape(tokens, 128)
    c = d_wide * (SCALE / QUERY_LENGTH) / (1.0 + total[...])
    by_doc = jnp.transpose(c)[0:n_docs, :]
    if fast:
        high_part = by_doc.astype(BF)
        low_part = (by_doc - high_part.astype(F)).astype(BF)
        row = lax.broadcasted_iota(jnp.int32, (8, 8), 0)
        column = lax.broadcasted_iota(jnp.int32, (8, 8), 1)
        for m, coef in enumerate(coefs):
            document = 2 * (place.z ^ m) + (row >> 1)
            picks = [
                jnp.where((row < 4) & ((row & 1) == half) & (column == document), 1.0, 0.0).astype(BF)
                for half in range(2)
            ]
            lines = [
                mm(picks[0], part[:, 0:128]) + mm(picks[1], part[:, 128:256])
                for part in (high_part, low_part)
            ]
            coef[0:tokens, :] = qemb[...]
            coef[tokens:, :] = jnp.concatenate(lines, axis=0).astype(BF)
    else:
        coefs[0][...] = jnp.zeros_like(coefs[0])
        for half in range(tokens // 128):
            coefs[0][:, half, :] = by_doc[:, 128 * half : 128 * half + 128]
    d_emb[...] = cot[...].astype(F)

    def backward(slot):
        column = jnp.sum(jnp.where(lane == place.doc(slot), c, 0.0), axis=1, keepdims=True)
        d_emb[...] += mm((es[slot] * column).astype(BF), doc_at(slot))

    each(backward)


def query_sims(fast, ids, used, qemb, cot, ins, n_docs):
    tokens, emb = qemb.shape
    queries = tokens // QUERY_LENGTH
    return pl.pallas_call(
        functools.partial(query_sims_kernel, fast, n_docs, len(ins)),
        out_shape=((sds((tokens + 16, 128), BF),) * 4 if fast else (sds((n_docs, 8, 128), F),))
        + (sds((tokens, emb), F), sds((8, 128), F)),
        in_specs=[SM] * 2 + [VM] * (2 + len(ins)),
        out_specs=[VM] * (6 if fast else 3),
        scratch_shapes=[
            pltpu.VMEM((n_docs, tokens, DL), F),
            pltpu.VMEM((tokens, 128), F),
            pltpu.VMEM((queries, 128), F),
        ],
        compiler_params=pltpu.CompilerParams(vmem_limit_bytes=VMEM_LIMIT),
        cost_estimate=cost(n_docs * 67e6 * 10, n_docs * 1e6),
        name="query_sims",
    )(ids, used, qemb, cot, *ins)


def top_rows(d_emb, proj, h2, gain, wp):
    inv = lax.rsqrt(jnp.sum(proj * proj, axis=-1, keepdims=True) + EPS)
    along = jnp.sum(proj * d_emb, axis=-1, keepdims=True)
    d_proj = (inv * d_emb - proj * (inv * inv * inv) * along).astype(BF)
    d_h2, grad_gain = rms_back(h2, gain, mm_nt(d_proj, wp))
    return d_proj, d_h2, grad_gain


def back_kernel(
    fast, d_emb_in, demb, every, others, mask, rep, coef, d_emb_q, proj_d, proj_q, gf, gl, wp,
    h2_dh, h2_qh, n2_dh, n2_qh, n3_dh, n3_qh, wd_h, us_dh, us_qh, gv_dh, gv_qh, act_dh, act_qh,
    wg_h, wu_h, hid_dh, hid_qh, wo_h, li_dh, li_qh,
    d_hid, d_attn, g_out, g_gain, keep_h, send_h,
    h2, n2, n3, wd, us, gv, gate, up, act, wg, wu, hid, wo, li,
    n2t, d_proj, d_all, acc, d_n2, low_grads, down_grads, up_grads,
    sem_in, sem_tile, sem_last, sem_low, sem_out,
):
    place = Place(fast)
    count = demb.shape[0]
    rows = d_all.shape[0]

    def both(doc, query, target):
        return [(doc, target.at[0:count]), (query, target.at[count:])]

    loads = start_all(
        both(h2_dh, h2_qh, h2) + both(n2_dh, n2_qh, n2) + both(n3_dh, n3_qh, n3), sem_in
    )

    def tile_loads(t):
        cols = pl.ds(pl.multiple_of(t * 512, 512), 512)
        pairs = [
            (wd_h.at[cols], wd.at[cols]),
            (wg_h.at[:, cols], wg.at[:, cols]),
            (wu_h.at[:, cols], wu.at[:, cols]),
        ]
        for doc, query, target in ((us_dh, us_qh, us), (gv_dh, gv_qh, gv), (act_dh, act_qh, act)):
            pairs += both(doc.at[:, cols], query.at[:, cols], target.at[:, cols])
        return [pltpu.make_async_copy(src, dst, sem_tile.at[t, i]) for i, (src, dst) in enumerate(pairs)]

    def last_loads():
        pairs = both(hid_dh, hid_qh, hid) + [(wo_h, wo)] + both(li_dh, li_qh, li)
        return [pltpu.make_async_copy(src, dst, sem_last.at[i]) for i, (src, dst) in enumerate(pairs)]

    for copy in tile_loads(0):
        copy.start()
    acc[0:count, :] = d_emb_in[...].astype(F)
    acc[count:, :] = d_emb_q[...]
    per = 64 * QUERY_LENGTH // 256

    def sims(row, qb, line):
        e = jnp.exp(mm_nt(demb[...], qb) * SCALE)
        first = pl.multiple_of((row // per) * 64, 64)
        here = mask[pl.ds(first, 64), :].astype(F).astype(BF)
        m = mm_tn(here, rep[:, pl.ds(pl.multiple_of((row % per) * 256, 256), 256)])
        acc[0:count, :] += mm((e * m * line).astype(BF), qb)

    if fast:
        row = lax.broadcasted_iota(jnp.int32, (8, 16), 0)
        column = lax.broadcasted_iota(jnp.int32, (8, 16), 1)
        pick = (row < 2) & ((column & 7) == 2 * place.own + row)
        pick = jnp.where(pick, 1.0, 0.0).astype(BF)
        for slot in range(8):
            source, at = (every if slot < 4 else others), slot % 4
            first = 272 * at
            halves = mm(pick, source[first + 256 : first + 272, :])
            line = jnp.concatenate([halves[0:1, :], halves[1:2, :]], axis=1)
            sims(place.doc(slot), source[first : first + 256, :], line)
    else:

        def step(row, carry):
            line = jnp.concatenate([coef[row, 0:1, :], coef[row, 1:2, :]], axis=1)
            sims(row, every[pl.ds(pl.multiple_of(row * 256, 256), 256), :], line)
            return carry

        lax.fori_loop(0, coef.shape[0], step, 0)
    wait_all(loads[0:2])
    g_gain[...] = jnp.zeros_like(g_gain)
    gain_l = row_of(gl)
    for at_rows, proj in ((slice(0, count), proj_d), (slice(count, rows), proj_q)):
        dp, dh, gg = top_rows(acc[at_rows, :], proj[...], h2[at_rows, :], gain_l, wp[...])
        d_proj[at_rows, :] = dp
        h2[at_rows, :] = dh
        g_gain[1:2, :] += gg
        d_all[at_rows, :] = dh.astype(BF)
    wait_all(loads[2:])
    n2t[...] = jnp.transpose(n2[...])
    gp = mm_tn(n3[...], d_proj[...])
    low_grads[...] = jnp.zeros_like(low_grads)
    for w in range(8):
        for r in range(3):
            first = 96 * w + 32 * r
            low_grads[w % 2, w // 2, r // 2, r % 2, :, 0:128] = gp[first : first + 32, :].astype(BF)
    below = pl.ds(192, 32)
    low = start_all(
        (
            (low_grads.at[place.own], keep_h.at[:, :, :, below]),
            (low_grads.at[1 - place.own], send_h.at[:, :, :, below]),
        ),
        sem_low,
    )
    d_n2[...] = jnp.zeros_like(d_n2)

    def outputs(t, slot):
        copies = []
        for i, (core, target) in enumerate(((place.own, keep_h), (1 - place.own, send_h))):
            copies.append(
                pltpu.make_async_copy(
                    down_grads.at[slot, core], target.at[t, :, :, pl.ds(0, 192)], sem_out.at[slot, 3 * i]
                )
            )
            start = pl.multiple_of(224 + (t % 2) * 192, 32)
            for base in range(2):
                copies.append(
                    pltpu.make_async_copy(
                        up_grads.at[slot, base, core],
                        target.at[:, base, t // 2, pl.ds(start, 192)],
                        sem_out.at[slot, 3 * i + 1 + base],
                    )
                )
        return copies

    def tile(t, carry):
        slot = t % 2
        cols = pl.ds(pl.multiple_of(t * 512, 512), 512)

        @pl.when(t >= 2)
        def _():
            wait_all(outputs(t - 2, slot))

        @pl.when(t < 3)
        def _():
            for copy in tile_loads(t + 1):
                copy.start()

        @pl.when(t == 3)
        def _():
            for copy in last_loads():
                copy.start()

        wait_all(tile_loads(t))
        d_act = mm_nt(d_all[...], wd[cols, :])
        gate[...] = (d_act * us[:, cols].astype(F)).astype(BF)
        up[...] = (d_act * gv[:, cols].astype(F)).astype(BF)
        for half in range(2):
            first = pl.multiple_of((2 * t + half) * 256, 256)
            g = mm_tn(act[:, pl.ds(first, 256)], d_all[...])
            for r in range(4):
                for c in range(3):
                    down_grads[slot, half, r // 2, r % 2, 64 * c : 64 * c + 64, :] = g[
                        64 * r : 64 * r + 64, 256 * c : 256 * c + 256
                    ].astype(BF)
        for base, source in ((0, gate), (1, up)):
            g = mm(n2t[...], source[...]).astype(BF)
            for c in range(2):
                for w in range(8):
                    up_grads[slot, base, w % 2, w // 2, 96 * c : 96 * c + 96, :] = g[
                        96 * w : 96 * w + 96, 256 * c : 256 * c + 256
                    ]
        for copy in outputs(t, slot):
            copy.start()
        d_n2[...] += mm_nt(gate[...], wg[:, cols]) + mm_nt(up[...], wu[:, cols])
        return carry

    lax.fori_loop(0, 4, tile, 0)
    wait_all(last_loads())
    gain_f = row_of(gf)

    def through(at_rows):
        dm, gg = rms_back(hid[at_rows, :], gain_f, d_n2[at_rows, :])
        total = h2[at_rows, :] + dm
        d_hid[at_rows, :] = total
        g_gain[0:1, :] += gg
        d_attn[at_rows, :] = total.astype(BF)

    rows_loop(rows, 256, through)

    def to_context(at_rows):
        d_context = mm_nt(d_attn[at_rows, :], wo[...]).astype(BF).astype(F)
        g_out[at_rows, :] = (d_context * li[at_rows, :]).astype(BF)

    rows_loop(rows, 256, to_context)
    wait_all(low)
    for t in (2, 3):
        wait_all(outputs(t, t % 2))


def back(fast, d_emb, demb, every, others, mask, rep, coef, d_emb_q, dsaved, qsaved, gains, weights):
    wq, wk, wv, wo, wg, wu, wd, wp = weights
    count, width = dsaved["h2"].shape
    rows = count + d_emb_q.shape[0]
    hidden = wd.shape[0]
    emb = wp.shape[1]
    piece = sds((4, 2, 2, 608, 256), BF)

    def both(name):
        return dsaved[name], qsaved[name]

    return pl.pallas_call(
        functools.partial(back_kernel, fast),
        out_shape=(
            sds((rows, width), F),
            sds((rows, width), BF),
            sds((rows, width), BF),
            sds((8, width), F),
            piece,
            piece,
        ),
        in_specs=[VM] * 13 + [ANY] * 20,
        out_specs=[VM] * 4 + [ANY] * 2,
        scratch_shapes=[
            pltpu.VMEM((rows, width), F),
            pltpu.VMEM((rows, width), BF),
            pltpu.VMEM((rows, width), BF),
            pltpu.VMEM(wd.shape, BF),
            pltpu.VMEM((rows, hidden), BF),
            pltpu.VMEM((rows, hidden), BF),
            pltpu.VMEM((rows, 512), BF),
            pltpu.VMEM((rows, 512), BF),
            pltpu.VMEM((rows, hidden), BF),
            pltpu.VMEM(wg.shape, BF),
            pltpu.VMEM(wu.shape, BF),
            pltpu.VMEM((rows, width), F),
            pltpu.VMEM(wo.shape, BF),
            pltpu.VMEM((rows, width), F),
            pltpu.VMEM((width, rows), BF),
            pltpu.VMEM((rows, emb), BF),
            pltpu.VMEM((rows, width), BF),
            pltpu.VMEM((rows, emb), F),
            pltpu.VMEM((rows, width), F),
            pltpu.VMEM((2, 4, 2, 2, 32, 256), BF),
            pltpu.VMEM((2, 2, 2, 2, 192, 256), BF),
            pltpu.VMEM((2, 2, 2, 4, 192, 256), BF),
            pltpu.SemaphoreType.DMA((6,)),
            pltpu.SemaphoreType.DMA((4, 9)),
            pltpu.SemaphoreType.DMA((5,)),
            pltpu.SemaphoreType.DMA((2,)),
            pltpu.SemaphoreType.DMA((2, 6)),
        ],
        compiler_params=pltpu.CompilerParams(vmem_limit_bytes=VMEM_LIMIT),
        cost_estimate=cost(14e9, 10e6),
        name="back",
    )(
        d_emb, demb, every, others, mask, rep, coef, d_emb_q, *both("proj"), gains[1], gains[2], wp,
        *both("h2"), *both("n2"), *both("n3"), wd, *both("us"), *both("gv"), *both("act"), wg, wu,
        *both("hid"), wo, *both("li"),
    )


def attn_back_kernel(
    first, n_pairs, with_queries, hot, g_h, q_d, q_q, k_d, k_q, v_d, v_q, lr_d, lr_q, p_dh, p_qh, *refs
):
    n_outs = 7 if with_queries else 4
    outs = refs[-n_outs - 15 : -15]
    (
    q, k, v, g, p_d, p_q, lrd, lrq, ds, acc, sums, sem_in, sem_p, qq, gq,
    ) = refs[-15:]
    dq, dk, dv, g_rel = outs[:4]
    count = q_d.shape[0]
    rest = q_q.shape[0]
    blocks = count // 128
    heads_here = pl.ds(2 * first, 2 * n_pairs)
    lanes_here = pl.ds(128 * first, 128 * n_pairs)
    pairs = []
    if with_queries:
        pairs += [
            (v_q, qq.at[2]),
            (g_h.at[count:], gq),
            (p_qh, p_q),
            (lr_q, lrq),
            (q_q, qq.at[0]),
            (k_q, qq.at[1]),
        ]
    n_query = len(pairs)
    pairs += [
        (v_d.at[:, lanes_here], v),
        (g_h.at[0:count, lanes_here], g),
        (lr_d.at[heads_here], lrd),
        (q_d.at[:, lanes_here], q),
        (k_d.at[:, lanes_here], k),
    ]
    loads = start_all(pairs, sem_in)

    def p_load(pair):
        return pltpu.make_async_copy(
            p_dh.at[pl.ds(2 * (first + pair), 2)], p_d.at[pl.ds(2 * pair, 2)], sem_p.at[pair]
        )

    p_load(0).start()
    low, high, _, _ = half_masks()
    keeps = (low.astype(BF), high.astype(BF))
    acc[...] = jnp.zeros_like(acc)
    wait_all(loads[:n_query])

    if with_queries:
        cells_q = rest // 128
        heads = p_q.shape[0]
        rows_q = [slice(128 * b, 128 * b + 128) for b in range(cells_q)]
        lanes_of = [slice(128 * pair, 128 * pair + 128) for pair in range(heads // 2)]
        for group in range(0, heads // 2, 3):
            cells = [
                (pair, e, b) for pair in range(group, group + 3) for e in range(2) for b in range(cells_q)
            ]
            d_ps = [
                mm_nt(qq[2, rows_q[b], lanes_of[pair]] * keeps[e], gq[rows_q[b], lanes_of[pair]])
                for pair, e, b in cells
            ]
            dss = []
            for d_p, (pair, e, b) in zip(d_ps, cells):
                head = 2 * pair + e
                pf = p_q[head, rows_q[b], :].astype(F)
                t = pf * d_p
                share = lrq[head, :, rows_q[b]] * jnp.sum(t, axis=0, keepdims=True)
                d_s = t - pf * share
                acc[head, :, 128:256] += d_s
                dss.append(d_s.astype(BF))
            for pair in range(group, group + 3):
                lanes = lanes_of[pair]
                for b in range(cells_q):
                    rows = rows_q[b]
                    at_cell = [cells.index((pair, e, b)) for e in range(2)]
                    probs = [p_q[2 * pair + e, rows, :] for e in range(2)]
                    parts = [
                        (
                            mm_tn(dss[at_cell[e]], qq[1, rows, lanes] * keeps[e]),
                            mm(dss[at_cell[e]], qq[0, rows, lanes] * keeps[e]),
                            mm(probs[e], gq[rows, lanes] * keeps[e]),
                        )
                        for e in range(2)
                    ]
                    for i in range(3):
                        outs[4 + i][rows, lanes] = (parts[0][i] + parts[1][i]).astype(BF)
    wait_all(loads[n_query:])

    def doc_pair(pair, carry):
        lanes = pl.ds(pl.multiple_of(pair * 128, 128), 128)

        @pl.when(pair + 1 < n_pairs)
        def _():
            p_load(pair + 1).start()

        p_load(pair).wait()
        q2 = q[:, lanes]
        k2 = k[:, lanes]
        v2 = v[:, lanes]
        g2 = g[:, lanes]
        d_ps = [mm_nt(v2 * keep, g2) for keep in keeps]
        sides = []
        for e, keep in enumerate(keeps):
            head = 2 * pair + e
            acc_head = 2 * (first + pair) + e if with_queries else head
            for i in range(blocks):
                cols = slice(128 * i, 128 * i + 128)
                pfs = [p_d[head, 128 * j : 128 * j + 128, cols].astype(F) for j in range(blocks)]
                ts = [pfs[j] * d_ps[e][128 * j : 128 * j + 128, cols] for j in range(blocks)]
                total = functools.reduce(jnp.add, ts)
                share = lrd[head, :, cols] * jnp.sum(total, axis=0, keepdims=True)
                for j in range(blocks):
                    d_s = ts[j] - pfs[j] * share
                    t = 1 - (j - i)
                    tile = t if abs(j - i) <= 1 else (3 if j > i else 4)
                    acc[acc_head, :, 128 * tile : 128 * tile + 128] += d_s
                    ds[e, 128 * j : 128 * j + 128, cols] = d_s.astype(BF)
            sides.append(
                (
                    mm_tn(ds[e], k2 * keep),
                    mm(ds[e], q2 * keep),
                    mm(p_d[head], g2 * keep),
                )
            )
        dq[:, lanes] = (sides[0][0] + sides[1][0]).astype(BF)
        dk[:, lanes] = (sides[0][1] + sides[1][1]).astype(BF)
        dv[:, lanes] = (sides[0][2] + sides[1][2]).astype(BF)
        return carry

    lax.fori_loop(0, n_pairs, doc_pair, 0, unroll=2 if with_queries else 1)
    sums[...] = jnp.zeros_like(sums)
    n_heads = acc.shape[0]
    lane = lax.broadcasted_iota(jnp.int32, (n_heads, TABLE), 1)

    def left(values, by):
        flat = values.reshape(-1, TABLE)
        return pltpu.roll(flat, TABLE - by, 1).reshape(values.shape)

    near = jnp.concatenate([acc[:, :, 0:384], jnp.zeros((n_heads, 128, 128), F)], axis=2)
    folded = near[:, 0:8]
    for group in range(1, 16):
        folded = folded + left(near[:, 8 * group : 8 * group + 8], 8 * group)
    row = lax.broadcasted_iota(jnp.int32, (n_heads, 8, TABLE), 1)
    lines = folded
    for i in range(1, 8):
        lines = jnp.where(row == i, left(folded, i), lines)
    lines = jnp.sum(lines, axis=1)
    after = jnp.sum(jnp.sum(acc[:, :, 384:512], axis=1), axis=1, keepdims=True)
    before = jnp.sum(jnp.sum(acc[:, :, 512:640], axis=1), axis=1, keepdims=True)
    lines = lines + jnp.where(lane == 0, after, jnp.where(lane == 256, before, 0.0))
    offset = 0 if with_queries else 2 * first
    sums[offset : offset + n_heads, :] = lines
    g_rel[...] = lax.dot_general(
        sums[...], hot[...], (((1,), (1,)), ((), ())),
        preferred_element_type=F, precision=lax.Precision.HIGHEST,
    )


def attn_back(first, n_pairs, with_queries, g, dsaved, qsaved, hot, after):
    rows, width = g.shape
    heads = dsaved["p"].shape[0]
    buckets = hot.shape[0]
    count = dsaved["q"].shape[0]
    rest = rows - count
    columns = 128 * n_pairs
    both = []
    for name in ("q", "k", "v", "lr", "p"):
        both += [dsaved[name], qsaved[name]]
    outs = (sds((count, columns), BF),) * 3 + (sds((16, buckets), F),)
    if with_queries:
        outs = outs + (sds((rest, width), BF),) * 3
    return pl.pallas_call(
        functools.partial(attn_back_kernel, first, n_pairs, with_queries),
        out_shape=outs,
        in_specs=[VM] + [ANY] * (11 + len(after)),
        out_specs=[VM] * len(outs),
        scratch_shapes=[pltpu.VMEM((count, columns), BF)] * 4
        + [
            pltpu.VMEM((2 * n_pairs, DL, DL), BF),
            pltpu.VMEM((heads, rest, 128), BF),
            pltpu.VMEM((2 * n_pairs, 1, count), F),
            pltpu.VMEM((heads, 1, rest), F),
            pltpu.VMEM((2, DL, DL), BF),
            pltpu.VMEM((heads if with_queries else 2 * n_pairs, 128, 640), F),
            pltpu.VMEM((16, TABLE), F),
            pltpu.SemaphoreType.DMA((11,)),
            pltpu.SemaphoreType.DMA((n_pairs,)),
            pltpu.VMEM((3, rest, width), BF),
            pltpu.VMEM((rest, width), BF),
        ],
        compiler_params=pltpu.CompilerParams(vmem_limit_bytes=VMEM_LIMIT),
        cost_estimate=cost(15e9, 40e6),
        name="attn_back_%d" % first,
    )(hot, g, *both, *after)


SMALL = 48


def split_small(values):
    high = values.astype(BF)
    return jnp.concatenate([high, (values - high.astype(F)).astype(BF)], axis=1)


def join_small(rows):
    return rows[:, 0:128].astype(F) + rows[:, 128:256].astype(F)


def attn_parts(first, second, targets):
    half = first[0].shape[1]
    count = first[0].shape[0]
    pairs = []
    for i, target in enumerate(targets):
        pairs += [
            (first[i], target.at[0:count, 0:half]),
            (second[i], target.at[0:count, half:]),
            (first[4 + i], target.at[count:]),
        ]
    return pairs


def attn_grads_kernel(fast, *refs):
    ins, (d_attn_h, n1_d, n1_q, ctx_d, ctx_q) = refs[:9], refs[9:14]
    keep_h, *sends = refs[-14:-9]
    dq, dk, dv, d_attn, n1, ctx, grads, sem_in, sem_out = refs[-9:]
    first = ins[0:3] + (None,) + ins[3:6]
    place = Place(fast)
    count = n1_d.shape[0]
    pairs = [
        (n1_d, n1.at[0:count]),
        (n1_q, n1.at[count:]),
        *attn_parts(first, ins[6:9], (dq, dk, dv)),
        (d_attn_h, d_attn),
        (ctx_d, ctx.at[0:count]),
        (ctx_q, ctx.at[count:]),
    ]
    loads = start_all(pairs, sem_in)
    outs = []
    wait_all(loads[0:2])
    groups = (loads[2:5], loads[5:8], loads[8:11], loads[11:14])
    for which, (left, right) in enumerate(((n1, dq), (n1, dk), (n1, dv), (ctx, d_attn))):
        wait_all(groups[which])
        value = mm_tn(left[...], right[...]).astype(BF)
        for w in range(8):
            for c in range(3):
                row = ((w // 2) * 4 + which) * 288 + 96 * c
                grads[w % 2, row : row + 96, :] = value[96 * w : 96 * w + 96, 256 * c : 256 * c + 256]
        for z in range(4):
            rows = slice((z * 4 + which) * 288, (z * 4 + which) * 288 + 288)
            there = slice(which * 288, which * 288 + 288)
            pairs = ((place.own, keep_h.at[rows]), (1 - place.own, sends[z].at[there]))
            for i, (core, target) in enumerate(pairs):
                copy = pltpu.make_async_copy(grads.at[core, rows], target, sem_out.at[which, z, i])
                copy.start()
                outs.append(copy)
    wait_all(outs)


def attn_grads(fast, first, second, d_attn, dsaved, qsaved, after):
    rows, width = d_attn.shape
    piece = sds((16 * 288, 256), BF)
    ins = (*first[0:3], *first[4:7], *second[0:3])
    keep, *sends = pl.pallas_call(
        functools.partial(attn_grads_kernel, fast),
        out_shape=(piece,) + (sds((4 * 288, 256), BF),) * 4,
        in_specs=[ANY] * (14 + len(after)),
        out_specs=[ANY] * 5,
        scratch_shapes=[pltpu.VMEM((rows, width), BF)] * 6
        + [
            pltpu.VMEM((2,) + piece.shape, BF),
            pltpu.SemaphoreType.DMA((14,)),
            pltpu.SemaphoreType.DMA((4, 4, 2)),
        ],
        compiler_params=pltpu.CompilerParams(vmem_limit_bytes=VMEM_LIMIT),
        cost_estimate=cost(1, 1),
        name="attn_grads",
    )(*ins, d_attn, dsaved["n1"], qsaved["n1"], dsaved["ctx"], qsaved["ctx"], *after)
    return keep, sends


def input_back_kernel(ga, gains, parts, rel_0, rel_1, *refs):
    ins, (wq_h, wk_h, wv_h, tok_d, tok_q, d_hid_h) = refs[:9], refs[9:15]
    out_dh, out_qh, small = refs[-16:-13]
    dq, dk, dv, wq, wk, wv, tok, d_hid, d_n1, out, g_gain, sem_in, sem_out = refs[-13:]
    first = ins[0:3] + (None,) + ins[3:6]
    count = tok_d.shape[0]
    parts_q = attn_parts(first, ins[6:9], (dq, dk, dv))
    groups = (
        [*parts_q[0:3], (wq_h, wq)],
        [*parts_q[3:6], (wk_h, wk)],
        [*parts_q[6:9], (wv_h, wv)],
        [
            (tok_d, tok.at[0:count]),
            (tok_q, tok.at[count:]),
            (d_hid_h, d_hid),
        ],
    )
    loads = [start_all(groups[0], sem_in.at[0])]
    gain_a = row_of(ga)
    g_gain[...] = jnp.zeros_like(g_gain)
    for i, (left, right) in enumerate(((dq, wq), (dk, wk), (dv, wv))):
        loads.append(start_all(groups[i + 1], sem_in.at[i + 1]))
        wait_all(loads[i])
        part = mm_nt(left[...], right[...])
        d_n1[...] = part if i == 0 else d_n1[...] + part
    wait_all(loads[3])

    def step(rows):
        d_in, gg = rms_back(tok[rows, :].astype(F), gain_a, d_n1[rows, :])
        g_gain[0:1, :] += gg
        out[rows, :] = (d_hid[rows, :] + d_in).astype(BF)

    rows_loop(tok.shape[0], 256, step)
    outs = start_all(((out.at[0:count], out_dh), (out.at[count:], out_qh)), sem_out)
    small[...] = jnp.zeros_like(small)
    rows = (
        g_gain[0:1, :],
        gains[0:1, :],
        gains[1:2, :],
    )
    for i, row in enumerate(rows):
        for c in range(6):
            small[8 * i + c : 8 * i + c + 1, :] = row[:, 128 * c : 128 * c + 128]
    small[24:25, :] = parts[0:1, :]
    small[32:48, 0 : rel_0.shape[1]] = rel_0[...] + rel_1[...]
    wait_all(outs)


def input_back(tok_d, tok_q, d_hid, gain, gains, parts, first, second, weights, after):
    count, width = tok_d.shape
    rows = count + tok_q.shape[0]
    ins = (*first[0:3], *first[4:7], *second[0:3])
    return pl.pallas_call(
        input_back_kernel,
        out_shape=(sds(tok_d.shape, BF), sds(tok_q.shape, BF), sds((SMALL, 128), F)),
        in_specs=[VM] * 5 + [ANY] * (15 + len(after)),
        out_specs=[ANY] * 2 + [VM],
        scratch_shapes=[pltpu.VMEM((rows, width), BF)] * 3
        + [pltpu.VMEM((width, width), BF)] * 3
        + [
            pltpu.VMEM((rows, width), BF),
            pltpu.VMEM((rows, width), F),
            pltpu.VMEM((rows, width), F),
            pltpu.VMEM((rows, width), BF),
            pltpu.VMEM((8, width), F),
            pltpu.SemaphoreType.DMA((4, 4)),
            pltpu.SemaphoreType.DMA((2,)),
        ],
        compiler_params=pltpu.CompilerParams(vmem_limit_bytes=VMEM_LIMIT),
        cost_estimate=cost(3e9, 10e6),
        name="input_back",
    )(
        gain, gains, parts, first[3], second[3], *ins, weights[0], weights[1], weights[2],
        tok_d, tok_q, d_hid, *after,
    )


def unpack_attn_kernel(heads, total_queries, own, one, two, three, *refs):
    outs, (gain_a, gain_f, gain_l, rel, loss, fraction, stack, smalls) = refs[-12:-8], refs[-8:]
    place = Place(True)
    rows = stack.shape[1]
    for m, part in enumerate((own, one, two, three)):
        stack[place.rep ^ m] = part[0:rows, :]
        smalls[place.rep ^ m] = join_small(part[rows:, :])
    for r in range(4):
        for c in range(3):
            outs[r][:, 256 * c : 256 * c + 256] = stack[r, 96 * c : 96 * c + 96, :].astype(F)
    total = smalls[0] + smalls[1] + smalls[2] + smalls[3]
    for i, gain in enumerate((gain_a, gain_f, gain_l)):
        row = jnp.concatenate([total[8 * i + c : 8 * i + c + 1, :] for c in range(6)], axis=1)
        gain[...] = row.reshape(gain.shape[0])
    rel[...] = total[32 : 32 + heads, 0 : rel.shape[1]]
    lane = lax.broadcasted_iota(jnp.int32, (1, 128), 1)
    line = total[24:25, :]
    loss_sum, hits, found = (jnp.sum(jnp.where(lane == i, line, 0.0)) for i in range(3))
    loss[0, 0] = loss_sum / total_queries
    fraction[0, 0] = hits / (DL * found)


def unpack_attn(heads, buckets, width, total_queries, parts):
    rows = parts[0].shape[0] - SMALL
    return pl.pallas_call(
        functools.partial(unpack_attn_kernel, heads, float(total_queries)),
        out_shape=(sds((96, width), F),) * 4
        + (sds((width,), F),) * 3
        + (sds((heads, buckets), F), sds((1, 1), F), sds((1, 1), F)),
        in_specs=[VM] * 4,
        out_specs=[VM] * 8 + [SM] * 2,
        scratch_shapes=[pltpu.VMEM((4, rows, 256), BF), pltpu.VMEM((4, SMALL, 128), F)],
        compiler_params=pltpu.CompilerParams(vmem_limit_bytes=16 * 1024 * 1024),
        cost_estimate=cost(1e6, 3e6),
        name="unpack_attn",
    )(*parts)


def unpack_kernel(own, one, two, three, *refs):
    stack = refs[-1]
    outs = refs[-5:-1]
    place = Place(True)
    half = own.shape[1]
    for m, part in enumerate((own, one, two, three)):
        for i in range(2):
            stack[place.rep ^ m, half * i : half * i + half, :] = part[i]
    for r in range(4):
        for c in range(4):
            first = (r % 2) * 1024 + 256 * c
            outs[r // 2][:, first : first + 256] = stack[
                r, 224 + 96 * c : 224 + 96 * c + 96, :
            ].astype(F)
        for c in range(3):
            outs[2][64 * r : 64 * r + 64, 256 * c : 256 * c + 256] = stack[
                r, 64 * c : 64 * c + 64, :
            ].astype(F)
    for r in range(3):
        outs[3][32 * r : 32 * r + 32, :] = stack[r, 192:224, 0:128].astype(F)


def unpack(parts, shapes, after):
    return pl.pallas_call(
        unpack_kernel,
        out_shape=tuple(sds(s, F) for s in shapes),
        in_specs=[VM] * 4 + [ANY] * len(after),
        out_specs=tuple(VM for _ in shapes),
        scratch_shapes=[pltpu.VMEM((4, 2 * parts[0].shape[1], parts[0].shape[2]), BF)],
        compiler_params=pltpu.CompilerParams(vmem_limit_bytes=16 * 1024 * 1024),
        cost_estimate=cost(1e6, 3e6),
        name="unpack_ffn",
    )(*parts, *after)


def swap(values, axis, size, mask):
    return lax.ppermute(values, axis, [(i, i ^ mask) for i in range(size)])


def near_kernel(keep_h, came_h, *refs):
    send_a, send_b, kept, came, sems = refs[-5:]
    place = Place(True)
    half = send_a.shape[2]
    y, x = place.y, place.x
    loads = []
    for z in range(4):
        pairs = []
        for i, (source, target) in enumerate(((keep_h, kept), (came_h, came))):
            pairs += [
                (source.at[z, :, 1 - x, pl.ds(0, half)], target.at[0, z]),
                (source.at[z, 1 - y, :, pl.ds(half, half)], target.at[1, z]),
            ]
        loads.append(start_all(pairs, sems.at[z]))
    for z in range(4):
        wait_all(loads[z])
        send_a[z] = kept[0, z] + came[0, z]
        send_b[z] = kept[1, z] + came[1, z]


def own_kernel(keep_h, came_h, *refs):
    own_a, own_b, kept, came, sems = refs[-5:]
    place = Place(True)
    half = own_a.shape[2]
    y, x = place.y, place.x
    loads = []
    for z in range(4):
        pairs = []
        for i, (source, target) in enumerate(((keep_h, kept), (came_h, came))):
            pairs += [
                (source.at[z, :, x, pl.ds(0, half)], target.at[0, z]),
                (source.at[z, y, :, pl.ds(half, half)], target.at[1, z]),
            ]
        loads.append(start_all(pairs, sems.at[z]))
    for z in range(4):
        wait_all(loads[z])
        own_a[z] = kept[0, z] + came[0, z]
        own_b[z] = kept[1, z] + came[1, z]


def cross_kernel(a, came_a, b, came_b, *refs):
    send_a, send_b, own_a, own_b = refs[-4:]
    place = Place(True)
    y, x = place.y, place.x
    send_a[0] = a[0, 1 - y] + came_a[0, 1 - y]
    own_a[0] = a[0, y] + came_a[0, y]
    send_b[0] = b[0, 1 - x] + came_b[0, 1 - x]
    own_b[0] = b[0, x] + came_b[0, x]


def line_kernel(a, came_a, b, came_b, *refs):
    send, own = refs[-2:]
    z = Place(True).z
    for i in range(2):
        for out, to in ((own, z ^ (2 * i)), (send, z ^ 1 ^ (2 * i))):
            out[i, 0] = a[to] + came_a[to]
            out[i, 1] = b[to] + came_b[to]


def next_kernel(own, came, *refs):
    send, out = refs[-2:]
    out[...] = own[0] + came[0]
    send[...] = own[1] + came[1]


def far_kernel(own, came, *refs):
    refs[-1][...] = own[...] + came[...]


def cell(index, half, first=0):
    return pl.ds(pl.multiple_of(index * half + first, 16), half)


def attn_near_kernel(keep_h, *refs):
    came_h = refs[:4]
    send_a, send_b, kept, came, sems = refs[-5:]
    place = Place(True)
    half = send_b.shape[2]
    loads = split_loads(keep_h, came_h, kept, came, sems, half, 1 - place.x, 1 - place.y)
    for z in range(4):
        wait_all(loads[z])
        send_a[z] = kept[0, z] + came[0, z]
        send_b[z] = kept[1, z] + came[1, z]


def split_loads(keep_h, came_h, kept, came, sems, half, x, y):
    def rows(cell_number, first):
        return pl.ds(pl.multiple_of(cell_number * 2 * half + first, 16), half)

    loads = []
    for z in range(4):
        pairs = []
        for source, base, target in ((keep_h, 4 * z, kept), (came_h[z], 0, came)):
            for i in range(2):
                pairs += [
                    (source.at[rows(base + 2 * i + x, 0)], target.at[0, z, i]),
                    (source.at[rows(base + 2 * y + i, half)], target.at[1, z, i]),
                ]
        loads.append(start_all(pairs, sems.at[z]))
    return loads


def attn_own_kernel(keep_h, *refs):
    came_h = refs[:4]
    own_a, own_b, kept, came, sems = refs[-5:]
    place = Place(True)
    half = own_a.shape[2]
    loads = split_loads(keep_h, came_h, kept, came, sems, half, place.x, place.y)
    for z in range(4):
        wait_all(loads[z])
        own_a[z] = kept[0, z] + came[0, z]
        own_b[z] = kept[1, z] + came[1, z]


def attn_cross_kernel(a, came_a, b, came_b, *refs):
    send_a, send_b, own_a, own_b = refs[-4:]
    place = Place(True)
    y, x = place.y, place.x
    for z in range(4):
        send_a[z] = a[z, 1 - y] + came_a[z, 1 - y]
        own_a[z] = a[z, y] + came_a[z, y]
        send_b[z] = b[z, 1 - x] + came_b[z, 1 - x]
        own_b[z] = b[z, x] + came_b[z, x]


def attn_line_kernel(a, came_a, b, came_b, small_a, small_b, *refs):
    send, own, small = refs[-3:]
    z = Place(True).z
    half = a.shape[1]
    for i in range(2):
        for out, to in ((own, z ^ (2 * i)), (send, z ^ 1 ^ (2 * i))):
            out[2 * half * i : 2 * half * i + half, :] = a[to] + came_a[to]
            out[2 * half * i + half : 2 * half * i + 2 * half, :] = b[to] + came_b[to]
    value = split_small(small_a[...] + small_b[...])
    send[4 * half :, :] = value
    small[...] = value


def attn_next_kernel(own, came, small_in, *refs):
    send, out, small = refs[-3:]
    rows = out.shape[0]
    out[...] = own[0:rows, :] + came[0:rows, :]
    send[0:rows, :] = own[rows : 2 * rows, :] + came[rows : 2 * rows, :]
    value = split_small(join_small(small_in[...]) + join_small(came[2 * rows :, :]))
    send[rows:, :] = value
    small[...] = value


def attn_far_kernel(own, came, small_in, *refs):
    out = refs[-1]
    rows = own.shape[0]
    out[0:rows, :] = own[...] + came[0:rows, :]
    out[rows:, :] = split_small(join_small(small_in[...]) + join_small(came[rows:, :]))


def stage(kernel, name, ins, outs, after, flops=1, scratch=(), scalars=0, limit=16):
    return pl.pallas_call(
        kernel,
        out_shape=outs,
        in_specs=[VM] * len(ins) + [ANY] * len(after),
        out_specs=[VM] * (len(outs) - scalars) + [SM] * scalars,
        scratch_shapes=list(scratch),
        compiler_params=pltpu.CompilerParams(vmem_limit_bytes=limit * 1024 * 1024),
        cost_estimate=cost(flops, 1),
        name=name,
    )(*ins, *after)


class AttnReduction:
    def __init__(self, keep, send):
        self.half = 144
        self.keep = keep
        self.came = [swap(part, "wide", 8, 1) for part in send]
        self.small_shape = sds((SMALL, 256), BF)

    def rows(self, cells):
        return sds((cells * self.half + SMALL, 256), BF)

    def split(self, kernel, name, ins, outs, after):
        held = pltpu.VMEM((2, 4, 2, self.half, 256), BF)
        scratch = [held, held, pltpu.SemaphoreType.DMA((4, 8))]
        return pl.pallas_call(
            kernel,
            out_shape=outs,
            in_specs=[ANY] * 5 + [VM] * len(ins) + [ANY] * len(after),
            out_specs=(VM,) * len(outs),
            scratch_shapes=scratch,
            compiler_params=pltpu.CompilerParams(vmem_limit_bytes=VMEM_LIMIT),
            cost_estimate=cost(1, 1),
            name=name,
        )(self.keep, *self.came, *ins, *after)

    def near(self, after):
        outs = (sds((4, 2, self.half, 256), BF),) * 2
        send_a, send_b = self.split(attn_near_kernel, "near_attn", (), outs, after)
        self.came_a = swap(send_a, "rep", 4, 1)
        self.came_b = swap(send_b, "rep", 4, 2)
        return (send_a,)

    def mine(self, after):
        own = sds((4, 2, self.half, 256), BF)
        self.a, self.b = self.split(attn_own_kernel, "own_attn", (), (own, own), after)
        return (self.a,)

    def cross(self, after):
        outs = (sds((4, self.half, 256), BF),) * 4
        ins = (self.a, self.came_a, self.b, self.came_b)
        send_a, send_b, self.a, self.b = stage(attn_cross_kernel, "cross_attn", ins, outs, after)
        self.came_a = swap(send_a, "rep", 4, 2)
        self.came_b = swap(send_b, "rep", 4, 1)
        return (self.a,)

    def line(self, small, after):
        own = sds((4 * self.half, 256), BF)
        outs = (self.rows(4), own, self.small_shape)
        ins = (self.a, self.came_a, self.b, self.came_b, small, swap(small, "wide", 8, 1))
        send, self.own, self.small = stage(attn_line_kernel, "line_attn", ins, outs, after)
        self.came = swap(send, "wide", 8, 2)
        return (self.own,)

    def next(self, after):
        own = sds((2 * self.half, 256), BF)
        ins = (self.own, self.came, self.small)
        outs = (self.rows(2), own, self.small_shape)
        send, self.own, self.small = stage(attn_next_kernel, "next_attn", ins, outs, after)
        self.came = swap(send, "wide", 8, 4)
        return (self.own,)

    def far(self, after):
        ins = (self.own, self.came, self.small)
        (self.own,) = stage(attn_far_kernel, "far_attn", ins, (self.rows(2),), after)
        self.came = [swap(self.own, "rep", 4, m) for m in (1, 2, 3)]
        return (self.own,)

    def parts(self):
        return self.own, *self.came


class Reduction:
    def __init__(self, name, keep, send):
        self.name = name
        self.half = keep.shape[3] // 2
        self.keep = keep
        self.came = swap(send, "wide", 8, 1)

    def split(self, kernel, name, ins, shapes, specs, after):
        held = pltpu.VMEM((2, 4, 2, self.half, 256), BF)
        return pl.pallas_call(
            kernel,
            out_shape=tuple(sds(shape, BF) for shape in shapes),
            in_specs=[ANY] * 2 + specs + [ANY] * len(after),
            out_specs=(VM,) * len(shapes),
            scratch_shapes=[held, held, pltpu.SemaphoreType.DMA((4, 4))],
            compiler_params=pltpu.CompilerParams(vmem_limit_bytes=VMEM_LIMIT),
            cost_estimate=cost(1, 1),
            name=name + self.name,
        )(self.keep, self.came, *ins, *after)

    def near(self, after):
        shape = (4, 2, self.half, 256)
        send_a, send_b = self.split(near_kernel, "near_", (), (shape,) * 2, [], after)
        self.came_a = swap(send_a, "rep", 4, 1)
        self.came_b = swap(send_b, "rep", 4, 2)
        return (send_a,)

    def step(self, kernel, name, ins, shapes, after, flops=1):
        outs = tuple(sds(shape, BF) for shape in shapes)
        return stage(kernel, name + self.name, ins, outs, after, flops, limit=20)

    def mine(self, after):
        shape = (4, 2, self.half, 256)
        self.a, self.b = self.split(own_kernel, "own_", (), (shape,) * 2, [], after)
        return (self.a,)

    def cross(self, after):
        shape = (4, self.half, 256)
        ins = (self.a, self.came_a, self.b, self.came_b)
        whole = pl.BlockSpec((1, 2, self.half, 256), lambda i: (i, 0, 0, 0))
        part = pl.BlockSpec((1, self.half, 256), lambda i: (i, 0, 0))
        send_a, send_b, self.a, self.b = pl.pallas_call(
            cross_kernel,
            grid=(4,),
            out_shape=(sds(shape, BF),) * 4,
            in_specs=[whole] * 4 + [ANY] * len(after),
            out_specs=(part,) * 4,
            compiler_params=pltpu.CompilerParams(vmem_limit_bytes=VMEM_LIMIT),
            cost_estimate=cost(1, 1),
            name="cross_" + self.name,
        )(*ins, *after)
        self.came_a = swap(send_a, "rep", 4, 2)
        self.came_b = swap(send_b, "rep", 4, 1)
        return (self.a,)

    def line(self, after, flops=1):
        ins = (self.a, self.came_a, self.b, self.came_b)
        shape = (2, 2, self.half, 256)
        send, self.own = self.step(line_kernel, "line_", ins, (shape,) * 2, after, flops)
        self.came = swap(send, "wide", 8, 2)
        return (self.own,)

    def next(self, after):
        shape = (2, self.half, 256)
        send, self.own = self.step(next_kernel, "next_", (self.own, self.came), (shape,) * 2, after)
        self.came = swap(send, "wide", 8, 4)
        return (self.own,)

    def far(self, after):
        shape = (2, self.half, 256)
        (self.own,) = self.step(far_kernel, "far_", (self.own, self.came), (shape,), after)
        self.came = [swap(self.own, "rep", 4, m) for m in (1, 2, 3)]
        return (self.own,)

    def parts(self):
        return self.own, *self.came


def natural(which, keep, send):
    both = jnp.stack([keep, send])
    if which == "attn":
        a = both.reshape(2, 4, 4, 3, 96, 256).transpose(2, 1, 0, 4, 3, 5).reshape(4, 768, 768)
        return [a[i] for i in range(4)]
    both = both.reshape((2, 4, 4) + both.shape[4:])
    a = both[:, :, :, 224:].reshape(2, 4, 4, 4, 96, 256).transpose(1, 0, 4, 2, 3, 5)
    a = a.reshape(768, 4096)
    d = both[:, :, :, :192].reshape(2, 4, 4, 3, 64, 256).transpose(1, 0, 2, 4, 3, 5)
    e = both[:, :, :3, 192:224, :128].transpose(1, 0, 2, 3, 4)
    return [a[:, :2048], a[:, 2048:], d.reshape(2048, 768), e.reshape(768, 128)]


def body(
    doc_tokens, query_tokens, doc_cotangent, query_cotangent, retrieved, pos_ids, pos_count,
    w_query, w_key, carried_content_weights, w_out, w_gate, w_up, w_down, w_proj,
    gain_attn, gain_ffn, gain_final, rel_bias,
):
    n_wide = lax.axis_size("wide")
    n_rep = lax.axis_size("rep")
    group = retrieved.shape[1]
    fast = n_wide == 8 and n_rep == 4 and group == 64
    weights = (w_query, w_key, carried_content_weights, w_out, w_gate, w_up, w_down, w_proj)
    width = doc_tokens.shape[1]
    buckets, heads = rel_bias.shape
    hot_np = bucket_hot(buckets)
    hot = jnp.asarray(hot_np, BF)
    hot_f = jnp.asarray(hot_np, F)
    rep_hot = jnp.asarray(query_hot(64), BF)
    rel = jnp.transpose(rel_bias)
    queries = pos_ids.shape[0]
    ids = jnp.transpose(pos_ids)
    columns = jnp.transpose(retrieved)
    gains = (gain_attn, gain_ffn, gain_final)

    doc, sends = layer_forward(doc_tokens, weights, gains, rel, hot, DL, (columns,) if fast else ())
    if fast:
        near = [sends[0]] + [swap(sends[m], "wide", n_wide, 2 * m) for m in (1, 2, 3)]
    query, _ = layer_forward(query_tokens, weights, gains, rel, hot, QUERY_LENGTH, (), (doc["emb"],))
    if fast:
        ins = near + [swap(stack_rows(near, (query["emb"],)), "wide", n_wide, 1)]
    else:
        mask_query = lax.all_to_all(columns.astype(F), "wide", 0, 0, tiled=True)
        mask_query = mask_query.reshape(n_wide, queries, DL)
        ins = [lax.all_gather(doc["emb"], "wide", axis=0, tiled=True), mask_query]
    *coefs, d_query_emb, parts = query_sims(
        fast, ids, pos_count, query["emb"], query_cotangent, ins, n_wide
    )
    if fast:
        coefs = [coefs[0]] + [swap(coefs[m], "wide", n_wide, 2 * m) for m in (1, 2, 3)]
        every = stack_rows(coefs, ())
        coef_all = d_query_emb
        others = swap(every, "wide", n_wide, 1)
    else:
        every = lax.all_gather(query["emb"], "wide", axis=0, tiled=True)
        others = query["emb"]
        coef_all = lax.all_to_all(coefs[0], "wide", 0, 0, tiled=True)
    d_hid, d_attn, g, gains_both, keep_f, send_f = back(
        fast, doc_cotangent, doc["emb"], every, others, columns, rep_hot, coef_all, d_query_emb, doc, query,
        gains, weights,
    )
    if fast:
        ffn = Reduction("ffn", keep_f, send_f)
    early = 2
    first = attn_back(0, early, True, g, doc, query, hot_f, ())
    after = ffn.near((first[3],)) if fast else ()
    second = attn_back(early, heads // 2 - early, False, g, doc, query, hot_f, after)
    after = ffn.mine((second[3],)) if fast else (second[3],)
    keep_a, send_a = attn_grads(fast, first, second, d_attn, doc, query, after)
    after = (keep_a,)
    if fast:
        attn = AttnReduction(keep_a, send_a)
        after = ffn.cross(after)
        after = attn.near(after)
        after = attn.mine(after)
        after = ffn.line(after)
    doc_grad, query_grad, small = input_back(
        doc_tokens, query_tokens, d_hid, gain_attn, gains_both, parts, first, second, weights, after
    )
    if fast:
        after = attn.cross((small,))
        after = ffn.next(after)
        after = attn.line(small, after)
        after = ffn.far(after)
        after = attn.next(after)
        after = attn.far(after)
        grad_gate, grad_up, grad_down, grad_proj = unpack(
            ffn.parts(), ((96, 2048), (96, 2048), (256, 768), (96, 128)), after
        )
        (
            grad_query, grad_key, grad_value, grad_out,
            total_gain_a, total_gain_f, total_gain_l, total_rel, loss, fraction,
        ) = unpack_attn(heads, buckets, width, queries * n_wide * n_rep, attn.parts())
        loss = loss.reshape(())
        fraction = fraction.reshape(())
    else:
        small = lax.psum(small, ("rep", "wide"))

        def total(whole):
            part = lax.psum_scatter(whole, "wide", scatter_dimension=0, tiled=True)
            return lax.psum(part, "rep").astype(F)

        grad_query, grad_key, grad_value, grad_out = (total(a) for a in natural("attn", keep_a, jnp.concatenate(send_a)))
        grad_gate, grad_up, grad_down, grad_proj = (total(a) for a in natural("ffn", keep_f, send_f))
        total_gain_a, total_gain_f, total_gain_l = (
            small[8 * i : 8 * i + 6].reshape(width) for i in range(3)
        )
        total_rel = small[32 : 32 + heads, 0:buckets]
        loss = small[24, 0] / (queries * n_wide * n_rep)
        fraction = small[24, 1] / (DL * small[24, 2])
    return (
        doc["emb"],
        query["emb"],
        doc_grad,
        query_grad,
        grad_query,
        grad_key,
        grad_value,
        grad_out,
        grad_gate,
        grad_up,
        grad_down,
        grad_proj,
        total_gain_a,
        total_gain_f,
        total_gain_l,
        jnp.transpose(total_rel),
        loss,
        fraction,
    )


def solution(mesh):
    rows = P(("rep", "wide"), None)
    return jax.shard_map(
        body,
        mesh=mesh,
        in_specs=(rows,) * 6 + (P(("rep", "wide")),) + (P(),) * 12,
        out_specs=(rows,) * 4 + (P("wide", None),) * 8 + (P(),) * 6,
        check_vma=False,
    )
```

```python
import functools

import jax
import jax.numpy as jnp
import numpy as np
from jax import lax
from jax.experimental import pallas as pl
from jax.experimental.pallas import tpu as pltpu
from jax.sharding import PartitionSpec as P

DL = 512
QUERY_LENGTH = 32
EPS = 1e-06
SCALE = 10.0
BF = jnp.bfloat16
F = jnp.float32
TABLE = 512
VMEM_LIMIT = 57 * 1024 * 1024

SAVED = (
    "n1", "q", "k", "v", "p", "li", "ctx", "hid", "n2", "gv", "us", "act", "h2", "n3", "proj", "lr", "emb",
)

SM = pl.BlockSpec(memory_space=pltpu.SMEM)
ANY = pl.BlockSpec(memory_space=pl.ANY)
VM = pl.BlockSpec(memory_space=pltpu.VMEM)


def mm(a, b):
    return jnp.dot(a, b, preferred_element_type=F)


def mm_nt(a, b):
    return lax.dot_general(a, b, (((1,), (1,)), ((), ())), preferred_element_type=F)


def mm_tn(a, b):
    return lax.dot_general(a, b, (((0,), (0,)), ((), ())), preferred_element_type=F)


def bucket_hot(buckets):
    half = buckets // 2
    exact = half // 2
    column = np.arange(TABLE)
    relative = 128 - np.where(column <= TABLE - 128, column, column - TABLE)
    base = (relative > 0).astype(np.int64) * half
    distance = np.abs(relative)
    large = exact + (
        np.log(np.maximum(distance, 1) / float(exact)) / np.log(128.0 / exact) * (half - exact)
    ).astype(np.int64)
    large = np.minimum(large, half - 1)
    number = base + np.where(distance < exact, distance, large)
    return (np.arange(buckets)[:, None] == number[None, :]).astype(np.float32)


def query_hot(queries):
    tokens = np.arange(queries * QUERY_LENGTH)
    return (np.arange(queries)[:, None] == tokens[None, :] // QUERY_LENGTH).astype(np.float32)


def cost(flops, moved):
    large = flops > 1e8
    return pl.CostEstimate(flops=int(1e12 if large else 1), bytes_accessed=1, transcendentals=0)


class Place:
    def __init__(self, fast):
        self.fast = fast
        self.rep = lax.axis_index("rep")
        self.wide = lax.axis_index("wide")
        self.y, self.x = self.rep >> 1, self.rep & 1
        self.z = self.wide >> 1
        self.own = self.wide & 1 if fast else 0

    def doc(self, slot):
        return self.wide ^ (2 * (slot % 4)) ^ (slot // 4) if self.fast else slot

    def source(self, slot):
        return self.wide ^ slot if self.fast else slot


def row_of(gain):
    return gain[...].astype(F).reshape(1, gain.shape[0])


def stack_kernel(n_parts, *refs):
    out = refs[-1]
    row = 0
    for part in refs[:n_parts]:
        out[row : row + part.shape[0], :] = part[...]
        row += part.shape[0]


def stack_rows(parts, after):
    rows = sum(part.shape[0] for part in parts)
    return pl.pallas_call(
        functools.partial(stack_kernel, len(parts)),
        out_shape=sds((rows, 128), BF),
        in_specs=[VM] * len(parts) + [ANY] * len(after),
        out_specs=VM,
        cost_estimate=cost(1, 1),
        name="stack_rows",
    )(*parts, *after)


def sds(shape, dtype):
    return jax.ShapeDtypeStruct(shape, dtype)


def rows_loop(count, block, fn):
    def step(i, carry):
        fn(pl.ds(pl.multiple_of(i * block, block), block))
        return carry

    lax.fori_loop(0, count // block, step, 0, unroll=2)


def half_masks():
    lane = lax.broadcasted_iota(jnp.int32, (1, 128), 1)
    low = (lane < 64).astype(F)
    high = 1.0 - low
    one_low = (lane == 0).astype(F)
    one_high = (lane == 64).astype(F)
    return low, high, one_low, one_high


def rms(values):
    return lax.rsqrt(jnp.mean(values * values, axis=-1, keepdims=True) + EPS)


def rms_back(values, gain, d_result):
    inverse = rms(values)
    scaled = values * inverse
    grad_gain = jnp.sum(d_result * scaled, axis=0, keepdims=True)
    gained = d_result * gain
    d_values = inverse * (gained - scaled * jnp.mean(gained * scaled, axis=-1, keepdims=True))
    return d_values, grad_gain


def gelu_parts(gate):
    square = gate * gate
    tangent = jnp.tanh(gate * (0.7978845608028654 + (0.7978845608028654 * 0.044715) * square))
    half_plus = 0.5 + 0.5 * tangent
    value = gate * half_plus
    slope = half_plus + 0.5 * gate * (1.0 - tangent * tangent) * (
        0.7978845608028654 + (3.0 * 0.7978845608028654 * 0.044715) * square
    )
    return value, slope


def start_all(pairs, sems):
    copies = [pltpu.make_async_copy(src, dst, sems.at[i]) for i, (src, dst) in enumerate(pairs)]
    for copy in copies:
        copy.start()
    return copies


def wait_all(copies):
    for copy in copies:
        copy.wait()


def fwd_kernel(
    seq,
    heads,
    n_after,
    columns,
    tok, ga, gf, gl, rel, hot, wq_h, wk_h, wv_h, wo_h, wg_h, wu_h, wd_h, wp_h,
    *refs,
):
    (
    n1_h, q_h, k_h, v_h, p_h, li_h, ctx_h, hid_h, n2_h, gv_h, us_h, act_h, h2_h, n3_h, proj_h, lr_h, emb,
    wq, wk, wv, wo, wg, wu, wd, wp,
    n1, q, k, v, p, li, ctx, hid, n2, gv, us, act, h2, n3, proj, lr,
    tbl, bs, sem_in, sem_tile, sem_push, sem_out, _,
    ) = refs[n_after + columns : n_after + columns + 17] + refs[len(refs) - 31 :]
    sends = refs[n_after + columns + 17 : len(refs) - 31]
    count = tok.shape[0]
    loads = start_all(((wq_h, wq), (wk_h, wk), (wv_h, wv), (wo_h, wo), (wp_h, wp)), sem_in)

    def tile_loads(t):
        cols = pl.ds(pl.multiple_of(t * 512, 512), 512)
        pairs = ((wg_h.at[:, cols], wg.at[:, cols]), (wu_h.at[:, cols], wu.at[:, cols]), (wd_h.at[cols], wd.at[cols]))
        return [pltpu.make_async_copy(src, dst, sem_tile.at[t, i]) for i, (src, dst) in enumerate(pairs)]

    def tile_pushes(t):
        cols = pl.ds(pl.multiple_of(t * 512, 512), 512)
        pairs = tuple((a.at[:, cols], b.at[:, cols]) for a, b in ((gv, gv_h), (us, us_h), (act, act_h)))
        return [pltpu.make_async_copy(src, dst, sem_push.at[t, i]) for i, (src, dst) in enumerate(pairs)]

    outs = {}

    def push(i, src, dst):
        outs[i] = pltpu.make_async_copy(src, dst, sem_out.at[i])
        outs[i].start()

    gain_a, gain_f, gain_l = row_of(ga), row_of(gf), row_of(gl)

    def norm_one(rows):
        x = tok[rows, :].astype(F)
        n1[rows, :] = (x * rms(x) * gain_a).astype(BF)

    rows_loop(count, 128, norm_one)
    push(0, n1, n1_h)
    lines = mm(rel[...], hot[...])
    for h in range(heads):
        tbl[h] = lines[h : h + 1, :]
    for i, (w, r, r_h) in enumerate(((wq, q, q_h), (wk, k, k_h), (wv, v, v_h))):
        loads[i].wait()
        r[...] = mm(n1[...], w[...]).astype(BF)
        push(1 + i, r, r_h)
    n_tiles = wg.shape[1] // 512
    for t in range(2):
        for copy in tile_loads(t):
            copy.start()

    low, high, one_low, one_high = half_masks()
    is_low = low > 0.5

    blocks = count // 128

    def table(head, carry):
        row = jnp.broadcast_to(tbl[head], (128, TABLE))
        base = pltpu.roll(row, 0, 1, stride=1, stride_axis=0)
        if seq == DL:
            bs[head] = base[:, 0:384]
        else:
            rows = lax.broadcasted_iota(jnp.int32, (128, 128), 0) // seq
            columns = lax.broadcasted_iota(jnp.int32, (128, 128), 1) // seq
            bs[head] = jnp.where(rows == columns, base[:, 128:256], -1e30)
        return carry

    lax.fori_loop(0, heads, table, 0, unroll=4)

    def halves(index):
        lanes = pl.ds(pl.multiple_of(index * 128, 128), 128)
        q2 = q[:, lanes]
        k2 = k[:, lanes]
        v2 = v[:, lanes]
        parts = []
        for keep, one in ((low, one_high), (high, one_low)):
            parts.append((k2 * keep.astype(BF), v2 * keep.astype(BF) + one.astype(BF)))
        return lanes, q2, parts

    def join(lanes, o0, o1):
        inv = 1.0 / jnp.where(is_low, o0[:, 64:65], o1[:, 0:1])
        li[:, lanes] = inv
        ctx[:, lanes] = (jnp.where(is_low, o0, o1) * inv).astype(BF)

    def doc_scores(index):
        _, q2, parts = halves(index)
        for e in range(2):
            for half in range(2):
                yield mm_nt(parts[e][0], q2[256 * half : 256 * half + 256])

    def doc_softmax(head, score, i):
        cols = slice(128 * i, 128 * i + 128)
        terms = []
        for j in range(blocks):
            term = score[128 * j : 128 * j + 128, 128 * (i % 2) : 128 * (i % 2) + 128]
            if abs(j - i) <= 1:
                t = 1 - (j - i)
                terms.append(term + bs[head, :, 128 * t : 128 * t + 128])
            else:
                terms.append(term + (tbl[head, :, 0:1] if j > i else tbl[head, :, 256:257]))
        peak = functools.reduce(jnp.maximum, terms)
        peak = jnp.max(peak, axis=0, keepdims=True)
        total = jnp.zeros((128, 128), F)
        probs = []
        for j in range(blocks):
            power = jnp.exp(terms[j] - peak)
            total = total + power
            probs.append(power.astype(BF))
            p[head, 128 * j : 128 * j + 128, cols] = probs[-1]
        lr[head, :, cols] = 1.0 / jnp.sum(total, axis=0, keepdims=True)
        return jnp.concatenate(probs, axis=0)

    def doc_pairs(first, number):
        scores = list(doc_scores(first))
        for index in range(number):
            lanes, _, parts = halves(first + index)
            coming = doc_scores(first + index + 1) if index + 1 < number else iter(())
            following = []
            sides = []
            for e in range(2):
                head = 2 * (first + index) + e
                done = []
                for half in range(2):
                    following += [c for c in [next(coming, None)] if c is not None]
                    probs = [doc_softmax(head, scores[2 * e + half], 2 * half + i) for i in range(2)]
                    done.append(mm_tn(jnp.concatenate(probs, axis=1), parts[e][1]))
                sides.append(jnp.concatenate(done, axis=0))
            join(lanes, *sides)
            scores = following

    def query_group(group, carry):
        pairs = [halves(group * 3 + i) for i in range(3)]
        cells = [(i, e, b) for i in range(3) for e in range(2) for b in range(blocks)]
        rows = [slice(128 * b, 128 * b + 128) for b in range(blocks)]
        scores = [mm_nt(pairs[i][2][e][0][rows[b]], pairs[i][1][rows[b]]) for i, e, b in cells]
        probs = []
        for score, (i, e, b) in zip(scores, cells):
            head = (group * 3 + i) * 2 + e
            term = score + bs[head]
            power = jnp.exp(term - jnp.max(term, axis=0, keepdims=True))
            probs.append(power.astype(BF))
            p[head, rows[b], :] = probs[-1]
            lr[head, :, rows[b]] = 1.0 / jnp.sum(power, axis=0, keepdims=True)
        outs_g = [mm_tn(pb, pairs[i][2][e][1][rows[b]]) for pb, (i, e, b) in zip(probs, cells)]
        for i in range(3):
            sides = [
                jnp.concatenate([outs_g[cells.index((i, e, b))] for b in range(blocks)], axis=0)
                for e in range(2)
            ]
            join(pairs[i][0], *sides)
        return carry

    if seq == DL:
        def doc_group(group, carry):
            doc_pairs(group * 3, 3)
            return carry

        lax.fori_loop(0, heads // 2 // 3, doc_group, 0)
    else:
        lax.fori_loop(0, heads // 6, query_group, 0)
    push(4, p, p_h)
    push(5, li, li_h)
    push(15, lr, lr_h)
    push(6, ctx, ctx_h)

    loads[3].wait()

    def middle(rows):
        h = tok[rows, :].astype(F) + mm(ctx[rows, :], wo[...])
        hid[rows, :] = h
        h2[rows, :] = h
        n2[rows, :] = (h * rms(h) * gain_f).astype(BF)

    rows_loop(count, 256, middle)
    push(7, hid, hid_h)
    push(8, n2, n2_h)

    def ffn(t, carry):
        cols = pl.ds(pl.multiple_of(t * 512, 512), 512)

        @pl.when(t + 2 < n_tiles)
        def _():
            for copy in tile_loads(t + 2):
                copy.start()

        wait_all(tile_loads(t))
        row_blocks = [slice(256 * b, 256 * b + 256) for b in range(count // 256)]
        products = [(mm(n2[rows, :], wg[:, cols]), mm(n2[rows, :], wu[:, cols])) for rows in row_blocks]
        for rows, (gate, up) in zip(row_blocks, products):
            value, slope = gelu_parts(gate)
            a = (value * up).astype(BF)
            gv[rows, cols] = value.astype(BF)
            us[rows, cols] = (up * slope).astype(BF)
            act[rows, cols] = a
            h2[rows, :] += mm(a, wd[cols, :])
        for copy in tile_pushes(t):
            copy.start()
        return carry

    lax.fori_loop(0, n_tiles, ffn, 0)
    loads[4].wait()

    def top(rows):
        h = h2[rows, :]
        n = (h * rms(h) * gain_l).astype(BF)
        n3[rows, :] = n
        pr = mm(n, wp[...])
        proj[rows, :] = pr
        emb[rows, :] = (pr * lax.rsqrt(jnp.sum(pr * pr, axis=-1, keepdims=True) + EPS)).astype(BF)

    rows_loop(count, 256, top)
    if columns:
        z = lax.axis_index("wide") >> 1
        sent_mask = refs[-1]
        sent_mask[...] = refs[0][...].astype(F).astype(BF)
        for m, send in enumerate(sends):
            send[0:count, :] = emb[...]
            own_rows = sent_mask[pl.ds(pl.multiple_of(16 * (z ^ m), 16), 16), :]
            for b in range(DL // 128):
                first = count + 16 * b
                send[first : first + 16, :] = own_rows[:, 128 * b : 128 * b + 128]
    push(12, h2, h2_h)
    push(13, n3, n3_h)
    push(14, proj, proj_h)
    wait_all(outs.values())
    for t in range(n_tiles):
        wait_all(tile_pushes(t))


def layer_forward(tokens, weights, gains, rel, hot, seq, columns=(), after=()):
    count, width = tokens.shape
    wq, wk, wv, wo, wg, wu, wd, wp = weights
    hidden = wg.shape[1]
    emb = wp.shape[1]
    heads = rel.shape[0]
    keys = DL if seq == DL else 128
    saved = (
        sds((count, width), BF),
        sds((count, width), BF),
        sds((count, width), BF),
        sds((count, width), BF),
        sds((heads, count, keys), BF),
        sds((count, width), F),
        sds((count, width), BF),
        sds((count, width), F),
        sds((count, width), BF),
        sds((count, hidden), BF),
        sds((count, hidden), BF),
        sds((count, hidden), BF),
        sds((count, width), F),
        sds((count, width), BF),
        sds((count, emb), F),
        sds((heads, 1, count), F),
    )
    outs = pl.pallas_call(
        functools.partial(fwd_kernel, seq, heads, len(after), len(columns)),
        out_shape=saved
        + (sds((count, emb), BF),)
        + (sds((count + 16 * DL // 128, emb), BF),) * (4 * len(columns)),
        in_specs=[VM] * 6 + [ANY] * 8 + [VM] * len(columns) + [ANY] * len(after),
        out_specs=[ANY] * 16 + [VM] * (1 + 4 * len(columns)),
        scratch_shapes=[pltpu.VMEM(w.shape, BF) for w in weights]
        + [pltpu.VMEM(s.shape, s.dtype) for s in saved]
        + [
            pltpu.VMEM((heads, 1, TABLE), F),
            pltpu.VMEM((heads, 128, 384 if seq == DL else 128), F),
            pltpu.SemaphoreType.DMA((5,)),
            pltpu.SemaphoreType.DMA((hidden // 512, 3)),
            pltpu.SemaphoreType.DMA((hidden // 512, 3)),
            pltpu.SemaphoreType.DMA((16,)),
            pltpu.VMEM((64, DL) if columns else (16, 128), BF),
        ],
        compiler_params=pltpu.CompilerParams(vmem_limit_bytes=VMEM_LIMIT),
        cost_estimate=cost(count * 14e6, 40e6),
        name="layer_forward_%d" % seq,
    )(tokens, *gains, rel, hot, *weights, *columns, *after)
    return dict(zip(SAVED, outs)), outs[len(SAVED) :]


def each_block(arrays, block, fn):
    first = 0
    for array in arrays:
        number = array.shape[0] // block
        if number == 1:
            fn(first, array[...])
        else:

            def step(i, carry, array=array, first=first):
                fn(first + i, array[pl.ds(pl.multiple_of(i * block, block), block), :])
                return carry

            lax.fori_loop(0, number, step, 0)
        first += number


def query_sims_kernel(fast, n_docs, n_ins, ids, used, qemb, cot, *refs):
    ins = refs[:n_ins]
    *coefs, d_emb, parts, es, total, counts = refs[n_ins:]
    place = Place(fast)
    tokens = qemb.shape[0]
    queries = tokens // QUERY_LENGTH
    lane = lax.broadcasted_iota(jnp.int32, (tokens, 128), 1)
    lane_q = lax.broadcasted_iota(jnp.int32, (queries, 128), 1)
    total[...] = jnp.zeros_like(total)
    counts[...] = jnp.zeros_like(counts)

    if fast:
        row = lax.broadcasted_iota(jnp.int32, (queries, 16), 0)
        pick = row + queries * place.own == lax.broadcasted_iota(jnp.int32, (queries, 16), 1)
        pick = jnp.where(pick, 1.0, 0.0).astype(BF)
        per = DL + 16 * DL // 128

        def rows_at(slot, first, last):
            if slot < 4:
                return ins[slot][first:last, :]
            base = per * (slot - 4)
            return ins[4][base + first : base + last, :]

        def doc_at(slot):
            return rows_at(slot, 0, DL)

        def mask_at(slot):
            packed = rows_at(slot, DL, per)
            return jnp.concatenate([mm(pick, packed[16 * b : 16 * b + 16]) for b in range(4)], axis=1)

        def each(fn):
            for slot in range(n_docs):
                fn(slot)

    else:
        docs, mask = ins

        def doc_at(slot):
            return docs[pl.ds(pl.multiple_of(slot * DL, DL), DL), :]

        def mask_at(slot):
            return mask[slot]

        def each(fn):
            def step(i, carry):
                fn(i)
                return carry

            lax.fori_loop(0, n_docs, step, 0)

    def forward(slot):
        d = place.doc(slot)
        m = mask_at(slot)
        wide = jnp.broadcast_to(m[:, None, :], (queries, QUERY_LENGTH, DL)).reshape(tokens, DL)
        e = jnp.exp(mm_nt(qemb[...], doc_at(slot)) * SCALE) * wide
        es[slot] = e
        total[...] = jnp.where(lane == d, jnp.sum(e, axis=1, keepdims=True), total[...])
        counts[...] = jnp.where(lane_q == d, jnp.sum(m, axis=1, keepdims=True), counts[...])

    each(forward)
    inside = lane_q < n_docs
    z = jnp.sum(jnp.log(1.0 + total[...]).reshape(queries, QUERY_LENGTH, 128), axis=1)
    z = z * (1.0 / QUERY_LENGTH)
    hot = jnp.zeros((queries, 128), F)
    row_q = lax.broadcasted_iota(jnp.int32, (queries, 128), 0)
    for q in range(queries):
        for s in range(ids.shape[0]):
            number = jnp.where(s < used[q], ids[s, q], 128)
            hot = jnp.where((row_q == q) & (lane_q == number), 1.0, hot)
    peak = jnp.max(jnp.where(inside, z, -1e30), axis=1, keepdims=True)
    power = jnp.where(inside, jnp.exp(jnp.where(inside, z - peak, 0.0)), 0.0)
    whole = jnp.sum(power, axis=1, keepdims=True)
    positive = jnp.sum(hot * power, axis=1, keepdims=True)
    loss = jnp.sum(jnp.log(whole) - jnp.log(positive))
    hits = jnp.sum(hot * counts[...])
    found = jnp.sum(hot)
    lane_p = lax.broadcasted_iota(jnp.int32, (8, 128), 1)
    parts[...] = jnp.where(
        lane_p == 0, loss, jnp.where(lane_p == 1, hits, jnp.where(lane_p == 2, found, 0.0))
    )
    d_z = power / whole - hot * power / positive
    d_wide = jnp.broadcast_to(d_z[:, None, :], (queries, QUERY_LENGTH, 128)).reshape(tokens, 128)
    c = d_wide * (SCALE / QUERY_LENGTH) / (1.0 + total[...])
    by_doc = jnp.transpose(c)[0:n_docs, :]
    if fast:
        high_part = by_doc.astype(BF)
        low_part = (by_doc - high_part.astype(F)).astype(BF)
        row = lax.broadcasted_iota(jnp.int32, (8, 8), 0)
        column = lax.broadcasted_iota(jnp.int32, (8, 8), 1)
        for m, coef in enumerate(coefs):
            document = 2 * (place.z ^ m) + (row >> 1)
            picks = [
                jnp.where((row < 4) & ((row & 1) == half) & (column == document), 1.0, 0.0).astype(BF)
                for half in range(2)
            ]
            lines = [
                mm(picks[0], part[:, 0:128]) + mm(picks[1], part[:, 128:256])
                for part in (high_part, low_part)
            ]
            coef[0:tokens, :] = qemb[...]
            coef[tokens:, :] = jnp.concatenate(lines, axis=0).astype(BF)
    else:
        coefs[0][...] = jnp.zeros_like(coefs[0])
        for half in range(tokens // 128):
            coefs[0][:, half, :] = by_doc[:, 128 * half : 128 * half + 128]
    d_emb[...] = cot[...].astype(F)

    def backward(slot):
        column = jnp.sum(jnp.where(lane == place.doc(slot), c, 0.0), axis=1, keepdims=True)
        d_emb[...] += mm((es[slot] * column).astype(BF), doc_at(slot))

    each(backward)


def query_sims(fast, ids, used, qemb, cot, ins, n_docs):
    tokens, emb = qemb.shape
    queries = tokens // QUERY_LENGTH
    return pl.pallas_call(
        functools.partial(query_sims_kernel, fast, n_docs, len(ins)),
        out_shape=((sds((tokens + 16, 128), BF),) * 4 if fast else (sds((n_docs, 8, 128), F),))
        + (sds((tokens, emb), F), sds((8, 128), F)),
        in_specs=[SM] * 2 + [VM] * (2 + len(ins)),
        out_specs=[VM] * (6 if fast else 3),
        scratch_shapes=[
            pltpu.VMEM((n_docs, tokens, DL), F),
            pltpu.VMEM((tokens, 128), F),
            pltpu.VMEM((queries, 128), F),
        ],
        compiler_params=pltpu.CompilerParams(vmem_limit_bytes=VMEM_LIMIT),
        cost_estimate=cost(n_docs * 67e6 * 10, n_docs * 1e6),
        name="query_sims",
    )(ids, used, qemb, cot, *ins)


def top_rows(d_emb, proj, h2, gain, wp):
    inv = lax.rsqrt(jnp.sum(proj * proj, axis=-1, keepdims=True) + EPS)
    along = jnp.sum(proj * d_emb, axis=-1, keepdims=True)
    d_proj = (inv * d_emb - proj * (inv * inv * inv) * along).astype(BF)
    d_h2, grad_gain = rms_back(h2, gain, mm_nt(d_proj, wp))
    return d_proj, d_h2, grad_gain


def back_kernel(
    fast, d_emb_in, demb, every, others, mask, rep, coef, d_emb_q, proj_d, proj_q, gf, gl, wp,
    h2_dh, h2_qh, n2_dh, n2_qh, n3_dh, n3_qh, wd_h, us_dh, us_qh, gv_dh, gv_qh, act_dh, act_qh,
    wg_h, wu_h, hid_dh, hid_qh, wo_h, li_dh, li_qh,
    d_hid, d_attn, g_out, g_gain, keep_h, send_h,
    h2, n2, n3, wd, us, gv, gate, up, act, wg, wu, hid, wo, li,
    n2t, d_proj, d_all, acc, d_n2, low_grads, down_grads, up_grads,
    sem_in, sem_tile, sem_last, sem_low, sem_out,
):
    place = Place(fast)
    count = demb.shape[0]
    rows = d_all.shape[0]

    def both(doc, query, target):
        return [(doc, target.at[0:count]), (query, target.at[count:])]

    loads = start_all(
        both(h2_dh, h2_qh, h2) + both(n2_dh, n2_qh, n2) + both(n3_dh, n3_qh, n3), sem_in
    )

    def tile_loads(t):
        cols = pl.ds(pl.multiple_of(t * 512, 512), 512)
        pairs = [
            (wd_h.at[cols], wd.at[cols]),
            (wg_h.at[:, cols], wg.at[:, cols]),
            (wu_h.at[:, cols], wu.at[:, cols]),
        ]
        for doc, query, target in ((us_dh, us_qh, us), (gv_dh, gv_qh, gv), (act_dh, act_qh, act)):
            pairs += both(doc.at[:, cols], query.at[:, cols], target.at[:, cols])
        return [pltpu.make_async_copy(src, dst, sem_tile.at[t, i]) for i, (src, dst) in enumerate(pairs)]

    def last_loads():
        pairs = both(hid_dh, hid_qh, hid) + [(wo_h, wo)] + both(li_dh, li_qh, li)
        return [pltpu.make_async_copy(src, dst, sem_last.at[i]) for i, (src, dst) in enumerate(pairs)]

    for copy in tile_loads(0):
        copy.start()
    acc[0:count, :] = d_emb_in[...].astype(F)
    acc[count:, :] = d_emb_q[...]
    per = 64 * QUERY_LENGTH // 256

    def sims(row, qb, line):
        e = jnp.exp(mm_nt(demb[...], qb) * SCALE)
        first = pl.multiple_of((row // per) * 64, 64)
        here = mask[pl.ds(first, 64), :].astype(F).astype(BF)
        m = mm_tn(here, rep[:, pl.ds(pl.multiple_of((row % per) * 256, 256), 256)])
        acc[0:count, :] += mm((e * m * line).astype(BF), qb)

    if fast:
        row = lax.broadcasted_iota(jnp.int32, (8, 16), 0)
        column = lax.broadcasted_iota(jnp.int32, (8, 16), 1)
        pick = (row < 2) & ((column & 7) == 2 * place.own + row)
        pick = jnp.where(pick, 1.0, 0.0).astype(BF)
        for slot in range(8):
            source, at = (every if slot < 4 else others), slot % 4
            first = 272 * at
            halves = mm(pick, source[first + 256 : first + 272, :])
            line = jnp.concatenate([halves[0:1, :], halves[1:2, :]], axis=1)
            sims(place.doc(slot), source[first : first + 256, :], line)
    else:

        def step(row, carry):
            line = jnp.concatenate([coef[row, 0:1, :], coef[row, 1:2, :]], axis=1)
            sims(row, every[pl.ds(pl.multiple_of(row * 256, 256), 256), :], line)
            return carry

        lax.fori_loop(0, coef.shape[0], step, 0)
    wait_all(loads[0:2])
    g_gain[...] = jnp.zeros_like(g_gain)
    gain_l = row_of(gl)
    for at_rows, proj in ((slice(0, count), proj_d), (slice(count, rows), proj_q)):
        dp, dh, gg = top_rows(acc[at_rows, :], proj[...], h2[at_rows, :], gain_l, wp[...])
        d_proj[at_rows, :] = dp
        h2[at_rows, :] = dh
        g_gain[1:2, :] += gg
        d_all[at_rows, :] = dh.astype(BF)
    wait_all(loads[2:])
    n2t[...] = jnp.transpose(n2[...])
    gp = mm_tn(n3[...], d_proj[...])
    low_grads[...] = jnp.zeros_like(low_grads)
    for w in range(8):
        for r in range(3):
            first = 96 * w + 32 * r
            low_grads[w % 2, w // 2, r // 2, r % 2, :, 0:128] = gp[first : first + 32, :].astype(BF)
    below = pl.ds(192, 32)
    low = start_all(
        (
            (low_grads.at[place.own], keep_h.at[:, :, :, below]),
            (low_grads.at[1 - place.own], send_h.at[:, :, :, below]),
        ),
        sem_low,
    )
    d_n2[...] = jnp.zeros_like(d_n2)

    def outputs(t, slot):
        copies = []
        for i, (core, target) in enumerate(((place.own, keep_h), (1 - place.own, send_h))):
            copies.append(
                pltpu.make_async_copy(
                    down_grads.at[slot, core], target.at[t, :, :, pl.ds(0, 192)], sem_out.at[slot, 3 * i]
                )
            )
            start = pl.multiple_of(224 + (t % 2) * 192, 32)
            for base in range(2):
                copies.append(
                    pltpu.make_async_copy(
                        up_grads.at[slot, base, core],
                        target.at[:, base, t // 2, pl.ds(start, 192)],
                        sem_out.at[slot, 3 * i + 1 + base],
                    )
                )
        return copies

    def tile(t, carry):
        slot = t % 2
        cols = pl.ds(pl.multiple_of(t * 512, 512), 512)

        @pl.when(t >= 2)
        def _():
            wait_all(outputs(t - 2, slot))

        @pl.when(t < 3)
        def _():
            for copy in tile_loads(t + 1):
                copy.start()

        @pl.when(t == 3)
        def _():
            for copy in last_loads():
                copy.start()

        wait_all(tile_loads(t))
        d_act = mm_nt(d_all[...], wd[cols, :])
        gate[...] = (d_act * us[:, cols].astype(F)).astype(BF)
        up[...] = (d_act * gv[:, cols].astype(F)).astype(BF)
        for half in range(2):
            first = pl.multiple_of((2 * t + half) * 256, 256)
            g = mm_tn(act[:, pl.ds(first, 256)], d_all[...])
            for r in range(4):
                for c in range(3):
                    down_grads[slot, half, r // 2, r % 2, 64 * c : 64 * c + 64, :] = g[
                        64 * r : 64 * r + 64, 256 * c : 256 * c + 256
                    ].astype(BF)
        for base, source in ((0, gate), (1, up)):
            g = mm(n2t[...], source[...]).astype(BF)
            for c in range(2):
                for w in range(8):
                    up_grads[slot, base, w % 2, w // 2, 96 * c : 96 * c + 96, :] = g[
                        96 * w : 96 * w + 96, 256 * c : 256 * c + 256
                    ]
        for copy in outputs(t, slot):
            copy.start()
        d_n2[...] += mm_nt(gate[...], wg[:, cols]) + mm_nt(up[...], wu[:, cols])
        return carry

    lax.fori_loop(0, 4, tile, 0)
    wait_all(last_loads())
    gain_f = row_of(gf)

    def through(at_rows):
        dm, gg = rms_back(hid[at_rows, :], gain_f, d_n2[at_rows, :])
        total = h2[at_rows, :] + dm
        d_hid[at_rows, :] = total
        g_gain[0:1, :] += gg
        d_attn[at_rows, :] = total.astype(BF)

    rows_loop(rows, 256, through)

    def to_context(at_rows):
        d_context = mm_nt(d_attn[at_rows, :], wo[...]).astype(BF).astype(F)
        g_out[at_rows, :] = (d_context * li[at_rows, :]).astype(BF)

    rows_loop(rows, 256, to_context)
    wait_all(low)
    for t in (2, 3):
        wait_all(outputs(t, t % 2))


def back(fast, d_emb, demb, every, others, mask, rep, coef, d_emb_q, dsaved, qsaved, gains, weights):
    wq, wk, wv, wo, wg, wu, wd, wp = weights
    count, width = dsaved["h2"].shape
    rows = count + d_emb_q.shape[0]
    hidden = wd.shape[0]
    emb = wp.shape[1]
    piece = sds((4, 2, 2, 608, 256), BF)

    def both(name):
        return dsaved[name], qsaved[name]

    return pl.pallas_call(
        functools.partial(back_kernel, fast),
        out_shape=(
            sds((rows, width), F),
            sds((rows, width), BF),
            sds((rows, width), BF),
            sds((8, width), F),
            piece,
            piece,
        ),
        in_specs=[VM] * 13 + [ANY] * 20,
        out_specs=[VM] * 4 + [ANY] * 2,
        scratch_shapes=[
            pltpu.VMEM((rows, width), F),
            pltpu.VMEM((rows, width), BF),
            pltpu.VMEM((rows, width), BF),
            pltpu.VMEM(wd.shape, BF),
            pltpu.VMEM((rows, hidden), BF),
            pltpu.VMEM((rows, hidden), BF),
            pltpu.VMEM((rows, 512), BF),
            pltpu.VMEM((rows, 512), BF),
            pltpu.VMEM((rows, hidden), BF),
            pltpu.VMEM(wg.shape, BF),
            pltpu.VMEM(wu.shape, BF),
            pltpu.VMEM((rows, width), F),
            pltpu.VMEM(wo.shape, BF),
            pltpu.VMEM((rows, width), F),
            pltpu.VMEM((width, rows), BF),
            pltpu.VMEM((rows, emb), BF),
            pltpu.VMEM((rows, width), BF),
            pltpu.VMEM((rows, emb), F),
            pltpu.VMEM((rows, width), F),
            pltpu.VMEM((2, 4, 2, 2, 32, 256), BF),
            pltpu.VMEM((2, 2, 2, 2, 192, 256), BF),
            pltpu.VMEM((2, 2, 2, 4, 192, 256), BF),
            pltpu.SemaphoreType.DMA((6,)),
            pltpu.SemaphoreType.DMA((4, 9)),
            pltpu.SemaphoreType.DMA((5,)),
            pltpu.SemaphoreType.DMA((2,)),
            pltpu.SemaphoreType.DMA((2, 6)),
        ],
        compiler_params=pltpu.CompilerParams(vmem_limit_bytes=VMEM_LIMIT),
        cost_estimate=cost(14e9, 10e6),
        name="back",
    )(
        d_emb, demb, every, others, mask, rep, coef, d_emb_q, *both("proj"), gains[1], gains[2], wp,
        *both("h2"), *both("n2"), *both("n3"), wd, *both("us"), *both("gv"), *both("act"), wg, wu,
        *both("hid"), wo, *both("li"),
    )


def attn_back_kernel(
    first, n_pairs, with_queries, hot, g_h, q_d, q_q, k_d, k_q, v_d, v_q, lr_d, lr_q, p_dh, p_qh, *refs
):
    n_outs = 7 if with_queries else 4
    outs = refs[-n_outs - 15 : -15]
    (
    q, k, v, g, p_d, p_q, lrd, lrq, ds, acc, sums, sem_in, sem_p, qq, gq,
    ) = refs[-15:]
    dq, dk, dv, g_rel = outs[:4]
    count = q_d.shape[0]
    rest = q_q.shape[0]
    blocks = count // 128
    heads_here = pl.ds(2 * first, 2 * n_pairs)
    lanes_here = pl.ds(128 * first, 128 * n_pairs)
    pairs = []
    if with_queries:
        pairs += [
            (v_q, qq.at[2]),
            (g_h.at[count:], gq),
            (p_qh, p_q),
            (lr_q, lrq),
            (q_q, qq.at[0]),
            (k_q, qq.at[1]),
        ]
    n_query = len(pairs)
    pairs += [
        (v_d.at[:, lanes_here], v),
        (g_h.at[0:count, lanes_here], g),
        (lr_d.at[heads_here], lrd),
        (q_d.at[:, lanes_here], q),
        (k_d.at[:, lanes_here], k),
    ]
    loads = start_all(pairs, sem_in)

    def p_load(pair):
        return pltpu.make_async_copy(
            p_dh.at[pl.ds(2 * (first + pair), 2)], p_d.at[pl.ds(2 * pair, 2)], sem_p.at[pair]
        )

    p_load(0).start()
    low, high, _, _ = half_masks()
    keeps = (low.astype(BF), high.astype(BF))
    acc[...] = jnp.zeros_like(acc)
    wait_all(loads[:n_query])

    if with_queries:
        cells_q = rest // 128
        heads = p_q.shape[0]
        rows_q = [slice(128 * b, 128 * b + 128) for b in range(cells_q)]
        lanes_of = [slice(128 * pair, 128 * pair + 128) for pair in range(heads // 2)]
        for group in range(0, heads // 2, 3):
            cells = [
                (pair, e, b) for pair in range(group, group + 3) for e in range(2) for b in range(cells_q)
            ]
            d_ps = [
                mm_nt(qq[2, rows_q[b], lanes_of[pair]] * keeps[e], gq[rows_q[b], lanes_of[pair]])
                for pair, e, b in cells
            ]
            dss = []
            for d_p, (pair, e, b) in zip(d_ps, cells):
                head = 2 * pair + e
                pf = p_q[head, rows_q[b], :].astype(F)
                t = pf * d_p
                share = lrq[head, :, rows_q[b]] * jnp.sum(t, axis=0, keepdims=True)
                d_s = t - pf * share
                acc[head, :, 128:256] += d_s
                dss.append(d_s.astype(BF))
            for pair in range(group, group + 3):
                lanes = lanes_of[pair]
                for b in range(cells_q):
                    rows = rows_q[b]
                    at_cell = [cells.index((pair, e, b)) for e in range(2)]
                    probs = [p_q[2 * pair + e, rows, :] for e in range(2)]
                    parts = [
                        (
                            mm_tn(dss[at_cell[e]], qq[1, rows, lanes] * keeps[e]),
                            mm(dss[at_cell[e]], qq[0, rows, lanes] * keeps[e]),
                            mm(probs[e], gq[rows, lanes] * keeps[e]),
                        )
                        for e in range(2)
                    ]
                    for i in range(3):
                        outs[4 + i][rows, lanes] = (parts[0][i] + parts[1][i]).astype(BF)
    wait_all(loads[n_query:])

    def doc_pair(pair, carry):
        lanes = pl.ds(pl.multiple_of(pair * 128, 128), 128)

        @pl.when(pair + 1 < n_pairs)
        def _():
            p_load(pair + 1).start()

        p_load(pair).wait()
        q2 = q[:, lanes]
        k2 = k[:, lanes]
        v2 = v[:, lanes]
        g2 = g[:, lanes]
        d_ps = [mm_nt(v2 * keep, g2) for keep in keeps]
        sides = []
        for e, keep in enumerate(keeps):
            head = 2 * pair + e
            acc_head = 2 * (first + pair) + e if with_queries else head
            for i in range(blocks):
                cols = slice(128 * i, 128 * i + 128)
                pfs = [p_d[head, 128 * j : 128 * j + 128, cols].astype(F) for j in range(blocks)]
                ts = [pfs[j] * d_ps[e][128 * j : 128 * j + 128, cols] for j in range(blocks)]
                total = functools.reduce(jnp.add, ts)
                share = lrd[head, :, cols] * jnp.sum(total, axis=0, keepdims=True)
                for j in range(blocks):
                    d_s = ts[j] - pfs[j] * share
                    t = 1 - (j - i)
                    tile = t if abs(j - i) <= 1 else (3 if j > i else 4)
                    acc[acc_head, :, 128 * tile : 128 * tile + 128] += d_s
                    ds[e, 128 * j : 128 * j + 128, cols] = d_s.astype(BF)
            sides.append(
                (
                    mm_tn(ds[e], k2 * keep),
                    mm(ds[e], q2 * keep),
                    mm(p_d[head], g2 * keep),
                )
            )
        dq[:, lanes] = (sides[0][0] + sides[1][0]).astype(BF)
        dk[:, lanes] = (sides[0][1] + sides[1][1]).astype(BF)
        dv[:, lanes] = (sides[0][2] + sides[1][2]).astype(BF)
        return carry

    lax.fori_loop(0, n_pairs, doc_pair, 0, unroll=2 if with_queries else 1)
    sums[...] = jnp.zeros_like(sums)
    n_heads = acc.shape[0]
    lane = lax.broadcasted_iota(jnp.int32, (n_heads, TABLE), 1)

    def left(values, by):
        flat = values.reshape(-1, TABLE)
        return pltpu.roll(flat, TABLE - by, 1).reshape(values.shape)

    near = jnp.concatenate([acc[:, :, 0:384], jnp.zeros((n_heads, 128, 128), F)], axis=2)
    folded = near[:, 0:8]
    for group in range(1, 16):
        folded = folded + left(near[:, 8 * group : 8 * group + 8], 8 * group)
    row = lax.broadcasted_iota(jnp.int32, (n_heads, 8, TABLE), 1)
    lines = folded
    for i in range(1, 8):
        lines = jnp.where(row == i, left(folded, i), lines)
    lines = jnp.sum(lines, axis=1)
    after = jnp.sum(jnp.sum(acc[:, :, 384:512], axis=1), axis=1, keepdims=True)
    before = jnp.sum(jnp.sum(acc[:, :, 512:640], axis=1), axis=1, keepdims=True)
    lines = lines + jnp.where(lane == 0, after, jnp.where(lane == 256, before, 0.0))
    offset = 0 if with_queries else 2 * first
    sums[offset : offset + n_heads, :] = lines
    g_rel[...] = lax.dot_general(
        sums[...], hot[...], (((1,), (1,)), ((), ())),
        preferred_element_type=F, precision=lax.Precision.HIGHEST,
    )


def attn_back(first, n_pairs, with_queries, g, dsaved, qsaved, hot, after):
    rows, width = g.shape
    heads = dsaved["p"].shape[0]
    buckets = hot.shape[0]
    count = dsaved["q"].shape[0]
    rest = rows - count
    columns = 128 * n_pairs
    both = []
    for name in ("q", "k", "v", "lr", "p"):
        both += [dsaved[name], qsaved[name]]
    outs = (sds((count, columns), BF),) * 3 + (sds((16, buckets), F),)
    if with_queries:
        outs = outs + (sds((rest, width), BF),) * 3
    return pl.pallas_call(
        functools.partial(attn_back_kernel, first, n_pairs, with_queries),
        out_shape=outs,
        in_specs=[VM] + [ANY] * (11 + len(after)),
        out_specs=[VM] * len(outs),
        scratch_shapes=[pltpu.VMEM((count, columns), BF)] * 4
        + [
            pltpu.VMEM((2 * n_pairs, DL, DL), BF),
            pltpu.VMEM((heads, rest, 128), BF),
            pltpu.VMEM((2 * n_pairs, 1, count), F),
            pltpu.VMEM((heads, 1, rest), F),
            pltpu.VMEM((2, DL, DL), BF),
            pltpu.VMEM((heads if with_queries else 2 * n_pairs, 128, 640), F),
            pltpu.VMEM((16, TABLE), F),
            pltpu.SemaphoreType.DMA((11,)),
            pltpu.SemaphoreType.DMA((n_pairs,)),
            pltpu.VMEM((3, rest, width), BF),
            pltpu.VMEM((rest, width), BF),
        ],
        compiler_params=pltpu.CompilerParams(vmem_limit_bytes=VMEM_LIMIT),
        cost_estimate=cost(15e9, 40e6),
        name="attn_back_%d" % first,
    )(hot, g, *both, *after)


SMALL = 48


def split_small(values):
    high = values.astype(BF)
    return jnp.concatenate([high, (values - high.astype(F)).astype(BF)], axis=1)


def join_small(rows):
    return rows[:, 0:128].astype(F) + rows[:, 128:256].astype(F)


def attn_parts(first, second, targets):
    half = first[0].shape[1]
    count = first[0].shape[0]
    pairs = []
    for i, target in enumerate(targets):
        pairs += [
            (first[i], target.at[0:count, 0:half]),
            (second[i], target.at[0:count, half:]),
            (first[4 + i], target.at[count:]),
        ]
    return pairs


def attn_grads_kernel(fast, *refs):
    ins, (d_attn_h, n1_d, n1_q, ctx_d, ctx_q) = refs[:9], refs[9:14]
    keep_h, *sends = refs[-12:-9]
    dq, dk, dv, d_attn, n1, ctx, grads, sem_in, sem_out = refs[-9:]
    first = ins[0:3] + (None,) + ins[3:6]
    place = Place(fast)
    count = n1_d.shape[0]
    pairs = [
        (n1_d, n1.at[0:count]),
        (n1_q, n1.at[count:]),
        *attn_parts(first, ins[6:9], (dq, dk, dv)),
        (d_attn_h, d_attn),
        (ctx_d, ctx.at[0:count]),
        (ctx_q, ctx.at[count:]),
    ]
    loads = start_all(pairs, sem_in)
    outs = []
    wait_all(loads[0:2])
    groups = (loads[2:5], loads[5:8], loads[8:11], loads[11:14])
    for which, (left, right) in enumerate(((n1, dq), (n1, dk), (n1, dv), (ctx, d_attn))):
        wait_all(groups[which])
        value = mm_tn(left[...], right[...]).astype(BF)
        for w in range(8):
            for c in range(3):
                row = ((w // 2) * 4 + which) * 288 + 96 * c
                grads[w % 2, row : row + 96, :] = value[96 * w : 96 * w + 96, 256 * c : 256 * c + 256]
        for z in range(4):
            rows = slice((z * 4 + which) * 288, (z * 4 + which) * 288 + 288)
            start = (z % 2 * 4 + which) * 288
            there = sends[z // 2].at[start : start + 288]
            pairs = ((place.own, keep_h.at[rows]), (1 - place.own, there))
            for i, (core, target) in enumerate(pairs):
                copy = pltpu.make_async_copy(grads.at[core, rows], target, sem_out.at[which, z, i])
                copy.start()
                outs.append(copy)
    wait_all(outs)


def attn_grads(fast, first, second, d_attn, dsaved, qsaved, after):
    rows, width = d_attn.shape
    piece = sds((16 * 288, 256), BF)
    ins = (*first[0:3], *first[4:7], *second[0:3])
    keep, *sends = pl.pallas_call(
        functools.partial(attn_grads_kernel, fast),
        out_shape=(piece,) + (sds((8 * 288, 256), BF),) * 2,
        in_specs=[ANY] * (14 + len(after)),
        out_specs=[ANY] * 3,
        scratch_shapes=[pltpu.VMEM((rows, width), BF)] * 6
        + [
            pltpu.VMEM((2,) + piece.shape, BF),
            pltpu.SemaphoreType.DMA((14,)),
            pltpu.SemaphoreType.DMA((4, 4, 2)),
        ],
        compiler_params=pltpu.CompilerParams(vmem_limit_bytes=VMEM_LIMIT),
        cost_estimate=cost(1, 1),
        name="attn_grads",
    )(*ins, d_attn, dsaved["n1"], qsaved["n1"], dsaved["ctx"], qsaved["ctx"], *after)
    return keep, sends


def input_back_kernel(ga, gains, parts, rel_0, rel_1, *refs):
    ins, (wq_h, wk_h, wv_h, tok_d, tok_q, d_hid_h) = refs[:9], refs[9:15]
    out_dh, out_qh, small = refs[-16:-13]
    dq, dk, dv, wq, wk, wv, tok, d_hid, d_n1, out, g_gain, sem_in, sem_out = refs[-13:]
    first = ins[0:3] + (None,) + ins[3:6]
    count = tok_d.shape[0]
    parts_q = attn_parts(first, ins[6:9], (dq, dk, dv))
    groups = (
        [*parts_q[0:3], (wq_h, wq)],
        [*parts_q[3:6], (wk_h, wk)],
        [*parts_q[6:9], (wv_h, wv)],
        [
            (tok_d, tok.at[0:count]),
            (tok_q, tok.at[count:]),
            (d_hid_h, d_hid),
        ],
    )
    loads = [start_all(groups[0], sem_in.at[0])]
    gain_a = row_of(ga)
    g_gain[...] = jnp.zeros_like(g_gain)
    for i, (left, right) in enumerate(((dq, wq), (dk, wk), (dv, wv))):
        loads.append(start_all(groups[i + 1], sem_in.at[i + 1]))
        wait_all(loads[i])
        part = mm_nt(left[...], right[...])
        d_n1[...] = part if i == 0 else d_n1[...] + part
    wait_all(loads[3])

    def step(rows):
        d_in, gg = rms_back(tok[rows, :].astype(F), gain_a, d_n1[rows, :])
        g_gain[0:1, :] += gg
        out[rows, :] = (d_hid[rows, :] + d_in).astype(BF)

    rows_loop(tok.shape[0], 256, step)
    outs = start_all(((out.at[0:count], out_dh), (out.at[count:], out_qh)), sem_out)
    small[...] = jnp.zeros_like(small)
    rows = (
        g_gain[0:1, :],
        gains[0:1, :],
        gains[1:2, :],
    )
    for i, row in enumerate(rows):
        for c in range(6):
            small[8 * i + c : 8 * i + c + 1, :] = row[:, 128 * c : 128 * c + 128]
    small[24:25, :] = parts[0:1, :]
    small[32:48, 0 : rel_0.shape[1]] = rel_0[...] + rel_1[...]
    wait_all(outs)


def input_back(tok_d, tok_q, d_hid, gain, gains, parts, first, second, weights, after):
    count, width = tok_d.shape
    rows = count + tok_q.shape[0]
    ins = (*first[0:3], *first[4:7], *second[0:3])
    return pl.pallas_call(
        input_back_kernel,
        out_shape=(sds(tok_d.shape, BF), sds(tok_q.shape, BF), sds((SMALL, 128), F)),
        in_specs=[VM] * 5 + [ANY] * (15 + len(after)),
        out_specs=[ANY] * 2 + [VM],
        scratch_shapes=[pltpu.VMEM((rows, width), BF)] * 3
        + [pltpu.VMEM((width, width), BF)] * 3
        + [
            pltpu.VMEM((rows, width), BF),
            pltpu.VMEM((rows, width), F),
            pltpu.VMEM((rows, width), F),
            pltpu.VMEM((rows, width), BF),
            pltpu.VMEM((8, width), F),
            pltpu.SemaphoreType.DMA((4, 4)),
            pltpu.SemaphoreType.DMA((2,)),
        ],
        compiler_params=pltpu.CompilerParams(vmem_limit_bytes=VMEM_LIMIT),
        cost_estimate=cost(3e9, 10e6),
        name="input_back",
    )(
        gain, gains, parts, first[3], second[3], *ins, weights[0], weights[1], weights[2],
        tok_d, tok_q, d_hid, *after,
    )


def unpack_attn_kernel(heads, total_queries, own, one, two, three, *refs):
    outs, (gain_a, gain_f, gain_l, rel, loss, fraction, stack, smalls) = refs[-12:-8], refs[-8:]
    place = Place(True)
    rows = stack.shape[1]
    for m, part in enumerate((own, one, two, three)):
        stack[place.rep ^ m] = part[0:rows, :]
        smalls[place.rep ^ m] = join_small(part[rows:, :])
    for r in range(4):
        for c in range(3):
            outs[r][:, 256 * c : 256 * c + 256] = stack[r, 96 * c : 96 * c + 96, :].astype(F)
    total = smalls[0] + smalls[1] + smalls[2] + smalls[3]
    for i, gain in enumerate((gain_a, gain_f, gain_l)):
        row = jnp.concatenate([total[8 * i + c : 8 * i + c + 1, :] for c in range(6)], axis=1)
        gain[...] = row.reshape(gain.shape[0])
    rel[...] = total[32 : 32 + heads, 0 : rel.shape[1]]
    lane = lax.broadcasted_iota(jnp.int32, (1, 128), 1)
    line = total[24:25, :]
    loss_sum, hits, found = (jnp.sum(jnp.where(lane == i, line, 0.0)) for i in range(3))
    loss[0, 0] = loss_sum / total_queries
    fraction[0, 0] = hits / (DL * found)


def unpack_attn(heads, buckets, width, total_queries, parts):
    rows = parts[0].shape[0] - SMALL
    return pl.pallas_call(
        functools.partial(unpack_attn_kernel, heads, float(total_queries)),
        out_shape=(sds((96, width), F),) * 4
        + (sds((width,), F),) * 3
        + (sds((heads, buckets), F), sds((1, 1), F), sds((1, 1), F)),
        in_specs=[VM] * 4,
        out_specs=[VM] * 8 + [SM] * 2,
        scratch_shapes=[pltpu.VMEM((4, rows, 256), BF), pltpu.VMEM((4, SMALL, 128), F)],
        compiler_params=pltpu.CompilerParams(vmem_limit_bytes=16 * 1024 * 1024),
        cost_estimate=cost(1e6, 3e6),
        name="unpack_attn",
    )(*parts)


def unpack_kernel(own, one, two, three, *refs):
    stack = refs[-1]
    outs = refs[-5:-1]
    place = Place(True)
    half = own.shape[1]
    for m, part in enumerate((own, one, two, three)):
        for i in range(2):
            stack[place.rep ^ m, half * i : half * i + half, :] = part[i]
    for r in range(4):
        for c in range(4):
            first = (r % 2) * 1024 + 256 * c
            outs[r // 2][:, first : first + 256] = stack[
                r, 224 + 96 * c : 224 + 96 * c + 96, :
            ].astype(F)
        for c in range(3):
            outs[2][64 * r : 64 * r + 64, 256 * c : 256 * c + 256] = stack[
                r, 64 * c : 64 * c + 64, :
            ].astype(F)
    for r in range(3):
        outs[3][32 * r : 32 * r + 32, :] = stack[r, 192:224, 0:128].astype(F)


def unpack(parts, shapes, after):
    return pl.pallas_call(
        unpack_kernel,
        out_shape=tuple(sds(s, F) for s in shapes),
        in_specs=[VM] * 4 + [ANY] * len(after),
        out_specs=tuple(VM for _ in shapes),
        scratch_shapes=[pltpu.VMEM((4, 2 * parts[0].shape[1], parts[0].shape[2]), BF)],
        compiler_params=pltpu.CompilerParams(vmem_limit_bytes=16 * 1024 * 1024),
        cost_estimate=cost(1e6, 3e6),
        name="unpack_ffn",
    )(*parts, *after)


def swap(values, axis, size, mask):
    return lax.ppermute(values, axis, [(i, i ^ mask) for i in range(size)])


def near_kernel(keep_h, came_h, *refs):
    send_a, send_b, kept, came, sems = refs[-5:]
    place = Place(True)
    half = send_a.shape[2]
    y, x = place.y, place.x
    loads = []
    for z in range(4):
        pairs = []
        for i, (source, target) in enumerate(((keep_h, kept), (came_h, came))):
            pairs += [
                (source.at[z, :, 1 - x, pl.ds(0, half)], target.at[0, z]),
                (source.at[z, 1 - y, :, pl.ds(half, half)], target.at[1, z]),
            ]
        loads.append(start_all(pairs, sems.at[z]))
    for z in range(4):
        wait_all(loads[z])
        send_a[z] = kept[0, z] + came[0, z]
        send_b[z] = kept[1, z] + came[1, z]


def own_kernel(keep_h, came_h, *refs):
    own_a, own_b, kept, came, sems = refs[-5:]
    place = Place(True)
    half = own_a.shape[2]
    y, x = place.y, place.x
    loads = []
    for z in range(4):
        pairs = []
        for i, (source, target) in enumerate(((keep_h, kept), (came_h, came))):
            pairs += [
                (source.at[z, :, x, pl.ds(0, half)], target.at[0, z]),
                (source.at[z, y, :, pl.ds(half, half)], target.at[1, z]),
            ]
        loads.append(start_all(pairs, sems.at[z]))
    for z in range(4):
        wait_all(loads[z])
        own_a[z] = kept[0, z] + came[0, z]
        own_b[z] = kept[1, z] + came[1, z]


def cross_kernel(other, a_h, came_ah, b_h, came_bh, *refs):
    out_a, out_b, held, sems = refs[-4:]
    place = Place(True)
    y = 1 - place.y if other else place.y
    x = 1 - place.x if other else place.x
    loads = []
    for z in range(4):
        pairs = ((a_h.at[z, y], 0), (came_ah.at[z, y], 1), (b_h.at[z, x], 2), (came_bh.at[z, x], 3))
        loads.append(start_all([(source, held.at[i, z]) for source, i in pairs], sems.at[z]))
    for z in range(4):
        wait_all(loads[z])
        out_a[z] = held[0, z] + held[1, z]
        out_b[z] = held[2, z] + held[3, z]


def line_kernel(a, came_a, b, came_b, *refs):
    send, own = refs[-2:]
    z = Place(True).z
    for i in range(2):
        for out, to in ((own, z ^ (2 * i)), (send, z ^ 1 ^ (2 * i))):
            out[i, 0] = a[to] + came_a[to]
            out[i, 1] = b[to] + came_b[to]


def next_kernel(own, came, *refs):
    send, out = refs[-2:]
    out[...] = own[0] + came[0]
    send[...] = own[1] + came[1]


def far_kernel(own, came, *refs):
    refs[-1][...] = own[...] + came[...]


def cell(index, half, first=0):
    return pl.ds(pl.multiple_of(index * half + first, 16), half)


def attn_near_kernel(keep_h, *refs):
    came_h = refs[:2]
    send_a, send_b, kept, came, sems = refs[-5:]
    place = Place(True)
    half = send_b.shape[2]
    loads = split_loads(keep_h, came_h, kept, came, sems, half, 1 - place.x, 1 - place.y)
    for z in range(4):
        wait_all(loads[z])
        send_a[z] = kept[0, z] + came[0, z]
        send_b[z] = kept[1, z] + came[1, z]


def split_loads(keep_h, came_h, kept, came, sems, half, x, y):
    def rows(cell_number, first):
        return pl.ds(pl.multiple_of(cell_number * 2 * half + first, 16), half)

    loads = []
    for z in range(4):
        pairs = []
        for source, base, target in ((keep_h, 4 * z, kept), (came_h[z // 2], z % 2 * 4, came)):
            for i in range(2):
                pairs += [
                    (source.at[rows(base + 2 * i + x, 0)], target.at[0, z, i]),
                    (source.at[rows(base + 2 * y + i, half)], target.at[1, z, i]),
                ]
        loads.append(start_all(pairs, sems.at[z]))
    return loads


def attn_own_kernel(keep_h, *refs):
    came_h = refs[:2]
    own_a, own_b, kept, came, sems = refs[-5:]
    place = Place(True)
    half = own_a.shape[2]
    loads = split_loads(keep_h, came_h, kept, came, sems, half, place.x, place.y)
    for z in range(4):
        wait_all(loads[z])
        own_a[z] = kept[0, z] + came[0, z]
        own_b[z] = kept[1, z] + came[1, z]


def attn_cross_kernel(a, came_a, b, came_b, *refs):
    send_a, send_b, own_a, own_b = refs[-4:]
    place = Place(True)
    y, x = place.y, place.x
    for z in range(4):
        send_a[z] = a[z, 1 - y] + came_a[z, 1 - y]
        own_a[z] = a[z, y] + came_a[z, y]
        send_b[z] = b[z, 1 - x] + came_b[z, 1 - x]
        own_b[z] = b[z, x] + came_b[z, x]


def attn_line_kernel(a, came_a, b, came_b, small_a, small_b, *refs):
    send, own, small = refs[-3:]
    z = Place(True).z
    half = a.shape[1]
    for i in range(2):
        for out, to in ((own, z ^ (2 * i)), (send, z ^ 1 ^ (2 * i))):
            out[2 * half * i : 2 * half * i + half, :] = a[to] + came_a[to]
            out[2 * half * i + half : 2 * half * i + 2 * half, :] = b[to] + came_b[to]
    value = split_small(small_a[...] + small_b[...])
    send[4 * half :, :] = value
    small[...] = value


def attn_next_kernel(own, came, small_in, *refs):
    send, out, small = refs[-3:]
    rows = out.shape[0]
    out[...] = own[0:rows, :] + came[0:rows, :]
    send[0:rows, :] = own[rows : 2 * rows, :] + came[rows : 2 * rows, :]
    value = split_small(join_small(small_in[...]) + join_small(came[2 * rows :, :]))
    send[rows:, :] = value
    small[...] = value


def attn_far_kernel(own, came, small_in, *refs):
    out = refs[-1]
    rows = own.shape[0]
    out[0:rows, :] = own[...] + came[0:rows, :]
    out[rows:, :] = split_small(join_small(small_in[...]) + join_small(came[rows:, :]))


def stage(kernel, name, ins, outs, after, flops=1, scratch=(), scalars=0, limit=16):
    return pl.pallas_call(
        kernel,
        out_shape=outs,
        in_specs=[VM] * len(ins) + [ANY] * len(after),
        out_specs=[VM] * (len(outs) - scalars) + [SM] * scalars,
        scratch_shapes=list(scratch),
        compiler_params=pltpu.CompilerParams(vmem_limit_bytes=limit * 1024 * 1024),
        cost_estimate=cost(flops, 1),
        name=name,
    )(*ins, *after)


class AttnReduction:
    def __init__(self, keep, send):
        self.half = 144
        self.keep = keep
        self.came = [swap(part, "wide", 8, 1) for part in send]
        self.small_shape = sds((SMALL, 256), BF)

    def rows(self, cells):
        return sds((cells * self.half + SMALL, 256), BF)

    def split(self, kernel, name, ins, outs, after):
        held = pltpu.VMEM((2, 4, 2, self.half, 256), BF)
        scratch = [held, held, pltpu.SemaphoreType.DMA((4, 8))]
        return pl.pallas_call(
            kernel,
            out_shape=outs,
            in_specs=[ANY] * 3 + [VM] * len(ins) + [ANY] * len(after),
            out_specs=(VM,) * len(outs),
            scratch_shapes=scratch,
            compiler_params=pltpu.CompilerParams(vmem_limit_bytes=VMEM_LIMIT),
            cost_estimate=cost(1, 1),
            name=name,
        )(self.keep, *self.came, *ins, *after)

    def near(self, after):
        outs = (sds((4, 2, self.half, 256), BF),) * 2
        send_a, send_b = self.split(attn_near_kernel, "near_attn", (), outs, after)
        self.came_a = swap(send_a, "rep", 4, 1)
        self.came_b = swap(send_b, "rep", 4, 2)
        return (send_a,)

    def mine(self, after):
        own = sds((4, 2, self.half, 256), BF)
        self.a, self.b = self.split(attn_own_kernel, "own_attn", (), (own, own), after)
        return (self.a,)

    def cross(self, after):
        outs = (sds((4, self.half, 256), BF),) * 4
        ins = (self.a, self.came_a, self.b, self.came_b)
        send_a, send_b, self.a, self.b = stage(attn_cross_kernel, "cross_attn", ins, outs, after)
        self.came_a = swap(send_a, "rep", 4, 2)
        self.came_b = swap(send_b, "rep", 4, 1)
        return (self.a,)

    def line(self, small, after):
        own = sds((4 * self.half, 256), BF)
        outs = (self.rows(4), own, self.small_shape)
        ins = (self.a, self.came_a, self.b, self.came_b, small, swap(small, "wide", 8, 1))
        send, self.own, self.small = stage(attn_line_kernel, "line_attn", ins, outs, after)
        self.came = swap(send, "wide", 8, 2)
        return (self.own,)

    def next(self, after):
        own = sds((2 * self.half, 256), BF)
        ins = (self.own, self.came, self.small)
        outs = (self.rows(2), own, self.small_shape)
        send, self.own, self.small = stage(attn_next_kernel, "next_attn", ins, outs, after)
        self.came = swap(send, "wide", 8, 4)
        return (self.own,)

    def far(self, after):
        ins = (self.own, self.came, self.small)
        (self.own,) = stage(attn_far_kernel, "far_attn", ins, (self.rows(2),), after)
        self.came = [swap(self.own, "rep", 4, m) for m in (1, 2, 3)]
        return (self.own,)

    def parts(self):
        return self.own, *self.came


class Reduction:
    def __init__(self, name, keep, send):
        self.name = name
        self.half = keep.shape[3] // 2
        self.keep = keep
        self.came = swap(send, "wide", 8, 1)

    def split(self, kernel, name, ins, shapes, specs, after):
        held = pltpu.VMEM((2, 4, 2, self.half, 256), BF)
        return pl.pallas_call(
            kernel,
            out_shape=tuple(sds(shape, BF) for shape in shapes),
            in_specs=[ANY] * 2 + specs + [ANY] * len(after),
            out_specs=(VM,) * len(shapes),
            scratch_shapes=[held, held, pltpu.SemaphoreType.DMA((4, 4))],
            compiler_params=pltpu.CompilerParams(vmem_limit_bytes=VMEM_LIMIT),
            cost_estimate=cost(1, 1),
            name=name + self.name,
        )(self.keep, self.came, *ins, *after)

    def near(self, after):
        shape = (4, 2, self.half, 256)
        send_a, send_b = self.split(near_kernel, "near_", (), (shape,) * 2, [], after)
        self.came_a = swap(send_a, "rep", 4, 1)
        self.came_b = swap(send_b, "rep", 4, 2)
        return (send_a,)

    def step(self, kernel, name, ins, shapes, after, flops=1):
        outs = tuple(sds(shape, BF) for shape in shapes)
        return stage(kernel, name + self.name, ins, outs, after, flops, limit=20)

    def mine(self, after):
        shape = (4, 2, self.half, 256)
        self.a, self.b = self.split(own_kernel, "own_", (), (shape,) * 2, [], after)
        return (self.a,)

    def half_sums(self, other, name, after):
        shape = (4, self.half, 256)
        return pl.pallas_call(
            functools.partial(cross_kernel, other),
            out_shape=(sds(shape, BF),) * 2,
            in_specs=[ANY] * (4 + len(after)),
            out_specs=(VM,) * 2,
            scratch_shapes=[pltpu.VMEM((4,) + shape, BF), pltpu.SemaphoreType.DMA((4, 4))],
            compiler_params=pltpu.CompilerParams(vmem_limit_bytes=VMEM_LIMIT),
            cost_estimate=cost(1, 1),
            name=name + self.name,
        )(*self.held, *after)

    def cross(self, after):
        self.held = (self.a, self.came_a, self.b, self.came_b)
        send_a, send_b = self.half_sums(True, "cross_", after)
        self.came_a = swap(send_a, "rep", 4, 2)
        self.came_b = swap(send_b, "rep", 4, 1)
        return (send_a,)

    def stay(self, after):
        self.a, self.b = self.half_sums(False, "stay_", after)
        return (self.a,)

    def line(self, after, flops=1):
        ins = (self.a, self.came_a, self.b, self.came_b)
        shape = (2, 2, self.half, 256)
        send, self.own = self.step(line_kernel, "line_", ins, (shape,) * 2, after, flops)
        self.came = swap(send, "wide", 8, 2)
        return (self.own,)

    def next(self, after):
        shape = (2, self.half, 256)
        send, self.own = self.step(next_kernel, "next_", (self.own, self.came), (shape,) * 2, after)
        self.came = swap(send, "wide", 8, 4)
        return (self.own,)

    def far(self, after):
        shape = (2, self.half, 256)
        (self.own,) = self.step(far_kernel, "far_", (self.own, self.came), (shape,), after)
        self.came = [swap(self.own, "rep", 4, m) for m in (1, 2, 3)]
        return (self.own,)

    def parts(self):
        return self.own, *self.came


def natural(which, keep, send):
    both = jnp.stack([keep, send])
    if which == "attn":
        a = both.reshape(2, 4, 4, 3, 96, 256).transpose(2, 1, 0, 4, 3, 5).reshape(4, 768, 768)
        return [a[i] for i in range(4)]
    both = both.reshape((2, 4, 4) + both.shape[4:])
    a = both[:, :, :, 224:].reshape(2, 4, 4, 4, 96, 256).transpose(1, 0, 4, 2, 3, 5)
    a = a.reshape(768, 4096)
    d = both[:, :, :, :192].reshape(2, 4, 4, 3, 64, 256).transpose(1, 0, 2, 4, 3, 5)
    e = both[:, :, :3, 192:224, :128].transpose(1, 0, 2, 3, 4)
    return [a[:, :2048], a[:, 2048:], d.reshape(2048, 768), e.reshape(768, 128)]


def body(
    doc_tokens, query_tokens, doc_cotangent, query_cotangent, retrieved, pos_ids, pos_count,
    w_query, w_key, carried_content_weights, w_out, w_gate, w_up, w_down, w_proj,
    gain_attn, gain_ffn, gain_final, rel_bias,
):
    n_wide = lax.axis_size("wide")
    n_rep = lax.axis_size("rep")
    group = retrieved.shape[1]
    fast = n_wide == 8 and n_rep == 4 and group == 64
    weights = (w_query, w_key, carried_content_weights, w_out, w_gate, w_up, w_down, w_proj)
    width = doc_tokens.shape[1]
    buckets, heads = rel_bias.shape
    hot_np = bucket_hot(buckets)
    hot = jnp.asarray(hot_np, BF)
    hot_f = jnp.asarray(hot_np, F)
    rep_hot = jnp.asarray(query_hot(64), BF)
    rel = jnp.transpose(rel_bias)
    queries = pos_ids.shape[0]
    ids = jnp.transpose(pos_ids)
    columns = jnp.transpose(retrieved)
    gains = (gain_attn, gain_ffn, gain_final)

    doc, sends = layer_forward(doc_tokens, weights, gains, rel, hot, DL, (columns,) if fast else ())
    if fast:
        near = [sends[0]] + [swap(sends[m], "wide", n_wide, 2 * m) for m in (1, 2, 3)]
    query, _ = layer_forward(query_tokens, weights, gains, rel, hot, QUERY_LENGTH, (), (doc["emb"],))
    if fast:
        ins = near + [swap(stack_rows(near, (query["emb"],)), "wide", n_wide, 1)]
    else:
        mask_query = lax.all_to_all(columns.astype(F), "wide", 0, 0, tiled=True)
        mask_query = mask_query.reshape(n_wide, queries, DL)
        ins = [lax.all_gather(doc["emb"], "wide", axis=0, tiled=True), mask_query]
    *coefs, d_query_emb, parts = query_sims(
        fast, ids, pos_count, query["emb"], query_cotangent, ins, n_wide
    )
    if fast:
        coefs = [coefs[0]] + [swap(coefs[m], "wide", n_wide, 2 * m) for m in (1, 2, 3)]
        every = stack_rows(coefs, ())
        coef_all = d_query_emb
        others = swap(every, "wide", n_wide, 1)
    else:
        every = lax.all_gather(query["emb"], "wide", axis=0, tiled=True)
        others = query["emb"]
        coef_all = lax.all_to_all(coefs[0], "wide", 0, 0, tiled=True)
    d_hid, d_attn, g, gains_both, keep_f, send_f = back(
        fast, doc_cotangent, doc["emb"], every, others, columns, rep_hot, coef_all, d_query_emb, doc, query,
        gains, weights,
    )
    if fast:
        ffn = Reduction("ffn", keep_f, send_f)
    early = 2
    first = attn_back(0, early, True, g, doc, query, hot_f, ())
    after = ffn.near((first[3],)) if fast else ()
    second = attn_back(early, heads // 2 - early, False, g, doc, query, hot_f, after)
    after = ffn.mine((second[3],)) if fast else (second[3],)
    keep_a, send_a = attn_grads(fast, first, second, d_attn, doc, query, after)
    after = (keep_a,)
    if fast:
        attn = AttnReduction(keep_a, send_a)
        after = ffn.cross(after)
        after = attn.near(after)
        after = attn.mine(after)
        after = ffn.stay(after)
        after = ffn.line(after)
    doc_grad, query_grad, small = input_back(
        doc_tokens, query_tokens, d_hid, gain_attn, gains_both, parts, first, second, weights, after
    )
    if fast:
        after = attn.cross((small,))
        after = ffn.next(after)
        after = attn.line(small, after)
        after = ffn.far(after)
        after = attn.next(after)
        after = attn.far(after)
        grad_gate, grad_up, grad_down, grad_proj = unpack(
            ffn.parts(), ((96, 2048), (96, 2048), (256, 768), (96, 128)), after
        )
        (
            grad_query, grad_key, grad_value, grad_out,
            total_gain_a, total_gain_f, total_gain_l, total_rel, loss, fraction,
        ) = unpack_attn(heads, buckets, width, queries * n_wide * n_rep, attn.parts())
        loss = loss.reshape(())
        fraction = fraction.reshape(())
    else:
        small = lax.psum(small, ("rep", "wide"))

        def total(whole):
            part = lax.psum_scatter(whole, "wide", scatter_dimension=0, tiled=True)
            return lax.psum(part, "rep").astype(F)

        grad_query, grad_key, grad_value, grad_out = (total(a) for a in natural("attn", keep_a, jnp.concatenate(send_a)))
        grad_gate, grad_up, grad_down, grad_proj = (total(a) for a in natural("ffn", keep_f, send_f))
        total_gain_a, total_gain_f, total_gain_l = (
            small[8 * i : 8 * i + 6].reshape(width) for i in range(3)
        )
        total_rel = small[32 : 32 + heads, 0:buckets]
        loss = small[24, 0] / (queries * n_wide * n_rep)
        fraction = small[24, 1] / (DL * small[24, 2])
    return (
        doc["emb"],
        query["emb"],
        doc_grad,
        query_grad,
        grad_query,
        grad_key,
        grad_value,
        grad_out,
        grad_gate,
        grad_up,
        grad_down,
        grad_proj,
        total_gain_a,
        total_gain_f,
        total_gain_l,
        jnp.transpose(total_rel),
        loss,
        fraction,
    )


def solution(mesh):
    rows = P(("rep", "wide"), None)
    return jax.shard_map(
        body,
        mesh=mesh,
        in_specs=(rows,) * 6 + (P(("rep", "wide")),) + (P(),) * 12,
        out_specs=(rows,) * 4 + (P("wide", None),) * 8 + (P(),) * 6,
        check_vma=False,
    )
```

```python
import functools

import jax
import jax.numpy as jnp
import numpy as np
from jax import lax
from jax.experimental import pallas as pl
from jax.experimental.pallas import tpu as pltpu
from jax.sharding import PartitionSpec as P

DL = 512
QUERY_LENGTH = 32
EPS = 1e-06
SCALE = 10.0
BF = jnp.bfloat16
F = jnp.float32
TABLE = 512
VMEM_LIMIT = 57 * 1024 * 1024

SAVED = (
    "n1", "q", "k", "v", "p", "li", "ctx", "hid", "n2", "gv", "us", "act", "h2", "n3", "proj", "lr", "emb",
)

SM = pl.BlockSpec(memory_space=pltpu.SMEM)
ANY = pl.BlockSpec(memory_space=pl.ANY)
VM = pl.BlockSpec(memory_space=pltpu.VMEM)


def mm(a, b):
    return jnp.dot(a, b, preferred_element_type=F)


def mm_nt(a, b):
    return lax.dot_general(a, b, (((1,), (1,)), ((), ())), preferred_element_type=F)


def mm_tn(a, b):
    return lax.dot_general(a, b, (((0,), (0,)), ((), ())), preferred_element_type=F)


def bucket_hot(buckets):
    half = buckets // 2
    exact = half // 2
    column = np.arange(TABLE)
    relative = 128 - np.where(column <= TABLE - 128, column, column - TABLE)
    base = (relative > 0).astype(np.int64) * half
    distance = np.abs(relative)
    large = exact + (
        np.log(np.maximum(distance, 1) / float(exact)) / np.log(128.0 / exact) * (half - exact)
    ).astype(np.int64)
    large = np.minimum(large, half - 1)
    number = base + np.where(distance < exact, distance, large)
    return (np.arange(buckets)[:, None] == number[None, :]).astype(np.float32)


def query_hot(queries):
    tokens = np.arange(queries * QUERY_LENGTH)
    return (np.arange(queries)[:, None] == tokens[None, :] // QUERY_LENGTH).astype(np.float32)


def cost(flops, moved):
    large = flops > 1e8
    return pl.CostEstimate(flops=int(1e12 if large else 1), bytes_accessed=1, transcendentals=0)


class Place:
    def __init__(self, fast):
        self.fast = fast
        self.rep = lax.axis_index("rep")
        self.wide = lax.axis_index("wide")
        self.y, self.x = self.rep >> 1, self.rep & 1
        self.z = self.wide >> 1
        self.own = self.wide & 1 if fast else 0

    def doc(self, slot):
        return self.wide ^ (2 * (slot % 4)) ^ (slot // 4) if self.fast else slot

    def source(self, slot):
        return self.wide ^ slot if self.fast else slot


def row_of(gain):
    return gain[...].astype(F).reshape(1, gain.shape[0])


def stack_kernel(n_parts, *refs):
    out = refs[-1]
    row = 0
    for part in refs[:n_parts]:
        out[row : row + part.shape[0], :] = part[...]
        row += part.shape[0]


def stack_rows(parts, after):
    rows = sum(part.shape[0] for part in parts)
    return pl.pallas_call(
        functools.partial(stack_kernel, len(parts)),
        out_shape=sds((rows, 128), BF),
        in_specs=[VM] * len(parts) + [ANY] * len(after),
        out_specs=VM,
        cost_estimate=cost(1, 1),
        name="stack_rows",
    )(*parts, *after)


def sds(shape, dtype):
    return jax.ShapeDtypeStruct(shape, dtype)


def rows_loop(count, block, fn):
    def step(i, carry):
        fn(pl.ds(pl.multiple_of(i * block, block), block))
        return carry

    lax.fori_loop(0, count // block, step, 0, unroll=2)


def half_masks():
    lane = lax.broadcasted_iota(jnp.int32, (1, 128), 1)
    low = (lane < 64).astype(F)
    high = 1.0 - low
    one_low = (lane == 0).astype(F)
    one_high = (lane == 64).astype(F)
    return low, high, one_low, one_high


def rms(values):
    return lax.rsqrt(jnp.mean(values * values, axis=-1, keepdims=True) + EPS)


def rms_back(values, gain, d_result):
    inverse = rms(values)
    scaled = values * inverse
    grad_gain = jnp.sum(d_result * scaled, axis=0, keepdims=True)
    gained = d_result * gain
    d_values = inverse * (gained - scaled * jnp.mean(gained * scaled, axis=-1, keepdims=True))
    return d_values, grad_gain


def gelu_parts(gate):
    square = gate * gate
    tangent = jnp.tanh(gate * (0.7978845608028654 + (0.7978845608028654 * 0.044715) * square))
    half_plus = 0.5 + 0.5 * tangent
    value = gate * half_plus
    slope = half_plus + 0.5 * gate * (1.0 - tangent * tangent) * (
        0.7978845608028654 + (3.0 * 0.7978845608028654 * 0.044715) * square
    )
    return value, slope


def start_all(pairs, sems):
    copies = [pltpu.make_async_copy(src, dst, sems.at[i]) for i, (src, dst) in enumerate(pairs)]
    for copy in copies:
        copy.start()
    return copies


def wait_all(copies):
    for copy in copies:
        copy.wait()


def fwd_kernel(
    seq,
    heads,
    n_after,
    columns,
    tok, ga, gf, gl, rel, hot, wq_h, wk_h, wv_h, wo_h, wg_h, wu_h, wd_h, wp_h,
    *refs,
):
    (
    n1_h, q_h, k_h, v_h, p_h, li_h, ctx_h, hid_h, n2_h, gv_h, us_h, act_h, h2_h, n3_h, proj_h, lr_h, emb,
    wq, wk, wv, wo, wg, wu, wd, wp,
    n1, q, k, v, p, li, ctx, hid, n2, gv, us, act, h2, n3, proj, lr,
    tbl, bs, sem_in, sem_tile, sem_push, sem_out, _,
    ) = refs[n_after + columns : n_after + columns + 17] + refs[len(refs) - 31 :]
    sends = refs[n_after + columns + 17 : len(refs) - 31]
    count = tok.shape[0]
    loads = start_all(((wq_h, wq), (wk_h, wk), (wv_h, wv), (wo_h, wo), (wp_h, wp)), sem_in)

    def tile_loads(t):
        cols = pl.ds(pl.multiple_of(t * 512, 512), 512)
        pairs = ((wg_h.at[:, cols], wg.at[:, cols]), (wu_h.at[:, cols], wu.at[:, cols]), (wd_h.at[cols], wd.at[cols]))
        return [pltpu.make_async_copy(src, dst, sem_tile.at[t, i]) for i, (src, dst) in enumerate(pairs)]

    def tile_pushes(t):
        cols = pl.ds(pl.multiple_of(t * 512, 512), 512)
        pairs = tuple((a.at[:, cols], b.at[:, cols]) for a, b in ((gv, gv_h), (us, us_h), (act, act_h)))
        return [pltpu.make_async_copy(src, dst, sem_push.at[t, i]) for i, (src, dst) in enumerate(pairs)]

    outs = {}

    def push(i, src, dst):
        outs[i] = pltpu.make_async_copy(src, dst, sem_out.at[i])
        outs[i].start()

    gain_a, gain_f, gain_l = row_of(ga), row_of(gf), row_of(gl)

    def norm_one(rows):
        x = tok[rows, :].astype(F)
        n1[rows, :] = (x * rms(x) * gain_a).astype(BF)

    rows_loop(count, 128, norm_one)
    push(0, n1, n1_h)
    lines = mm(rel[...], hot[...])
    for h in range(heads):
        tbl[h] = lines[h : h + 1, :]
    for i, (w, r, r_h) in enumerate(((wq, q, q_h), (wk, k, k_h), (wv, v, v_h))):
        loads[i].wait()
        r[...] = mm(n1[...], w[...]).astype(BF)
        push(1 + i, r, r_h)
    n_tiles = wg.shape[1] // 512
    for t in range(2):
        for copy in tile_loads(t):
            copy.start()

    low, high, one_low, one_high = half_masks()
    is_low = low > 0.5

    blocks = count // 128

    def table(head, carry):
        row = jnp.broadcast_to(tbl[head], (128, TABLE))
        base = pltpu.roll(row, 0, 1, stride=1, stride_axis=0)
        if seq == DL:
            bs[head] = base[:, 0:384]
        else:
            rows = lax.broadcasted_iota(jnp.int32, (128, 128), 0) // seq
            columns = lax.broadcasted_iota(jnp.int32, (128, 128), 1) // seq
            bs[head] = jnp.where(rows == columns, base[:, 128:256], -1e30)
        return carry

    lax.fori_loop(0, heads, table, 0, unroll=12)

    def halves(index):
        lanes = pl.ds(pl.multiple_of(index * 128, 128), 128)
        q2 = q[:, lanes]
        k2 = k[:, lanes]
        v2 = v[:, lanes]
        parts = []
        for keep, one in ((low, one_high), (high, one_low)):
            parts.append((k2 * keep.astype(BF), v2 * keep.astype(BF) + one.astype(BF)))
        return lanes, q2, parts

    def join(lanes, o0, o1):
        inv = 1.0 / jnp.where(is_low, o0[:, 64:65], o1[:, 0:1])
        li[:, lanes] = inv
        ctx[:, lanes] = (jnp.where(is_low, o0, o1) * inv).astype(BF)

    def doc_scores(index):
        _, q2, parts = halves(index)
        for e in range(2):
            for half in range(2):
                yield mm_nt(parts[e][0], q2[256 * half : 256 * half + 256])

    def doc_softmax(head, score, i):
        cols = slice(128 * i, 128 * i + 128)
        terms = []
        for j in range(blocks):
            term = score[128 * j : 128 * j + 128, 128 * (i % 2) : 128 * (i % 2) + 128]
            if abs(j - i) <= 1:
                t = 1 - (j - i)
                terms.append(term + bs[head, :, 128 * t : 128 * t + 128])
            else:
                terms.append(term + (tbl[head, :, 0:1] if j > i else tbl[head, :, 256:257]))
        peak = functools.reduce(jnp.maximum, terms)
        peak = jnp.max(peak, axis=0, keepdims=True)
        total = jnp.zeros((128, 128), F)
        probs = []
        for j in range(blocks):
            power = jnp.exp(terms[j] - peak)
            total = total + power
            probs.append(power.astype(BF))
            p[head, 128 * j : 128 * j + 128, cols] = probs[-1]
        lr[head, :, cols] = 1.0 / jnp.sum(total, axis=0, keepdims=True)
        return jnp.concatenate(probs, axis=0)

    def doc_pairs(first, number):
        scores = list(doc_scores(first))
        for index in range(number):
            lanes, _, parts = halves(first + index)
            coming = doc_scores(first + index + 1) if index + 1 < number else iter(())
            following = []
            sides = []
            for e in range(2):
                head = 2 * (first + index) + e
                done = []
                for half in range(2):
                    following += [c for c in [next(coming, None)] if c is not None]
                    probs = [doc_softmax(head, scores[2 * e + half], 2 * half + i) for i in range(2)]
                    done.append(mm_tn(jnp.concatenate(probs, axis=1), parts[e][1]))
                sides.append(jnp.concatenate(done, axis=0))
            join(lanes, *sides)
            scores = following

    def query_group(group, carry):
        pairs = [halves(group * 3 + i) for i in range(3)]
        cells = [(i, e, b) for i in range(3) for e in range(2) for b in range(blocks)]
        rows = [slice(128 * b, 128 * b + 128) for b in range(blocks)]
        scores = [mm_nt(pairs[i][2][e][0][rows[b]], pairs[i][1][rows[b]]) for i, e, b in cells]
        probs = []
        for score, (i, e, b) in zip(scores, cells):
            head = (group * 3 + i) * 2 + e
            term = score + bs[head]
            power = jnp.exp(term - jnp.max(term, axis=0, keepdims=True))
            probs.append(power.astype(BF))
            p[head, rows[b], :] = probs[-1]
            lr[head, :, rows[b]] = 1.0 / jnp.sum(power, axis=0, keepdims=True)
        outs_g = [mm_tn(pb, pairs[i][2][e][1][rows[b]]) for pb, (i, e, b) in zip(probs, cells)]
        for i in range(3):
            sides = [
                jnp.concatenate([outs_g[cells.index((i, e, b))] for b in range(blocks)], axis=0)
                for e in range(2)
            ]
            join(pairs[i][0], *sides)
        return carry

    if seq == DL:
        def doc_group(group, carry):
            doc_pairs(group * 6, 6)
            return carry

        lax.fori_loop(0, heads // 2 // 6, doc_group, 0)
    else:
        lax.fori_loop(0, heads // 6, query_group, 0)
    push(4, p, p_h)
    push(5, li, li_h)
    push(15, lr, lr_h)
    push(6, ctx, ctx_h)

    loads[3].wait()

    def middle(rows):
        h = tok[rows, :].astype(F) + mm(ctx[rows, :], wo[...])
        hid[rows, :] = h
        h2[rows, :] = h
        n2[rows, :] = (h * rms(h) * gain_f).astype(BF)

    rows_loop(count, 256, middle)
    push(7, hid, hid_h)
    push(8, n2, n2_h)

    def ffn(t, carry):
        cols = pl.ds(pl.multiple_of(t * 512, 512), 512)

        @pl.when(t + 2 < n_tiles)
        def _():
            for copy in tile_loads(t + 2):
                copy.start()

        wait_all(tile_loads(t))
        row_blocks = [slice(256 * b, 256 * b + 256) for b in range(count // 256)]
        products = [(mm(n2[rows, :], wg[:, cols]), mm(n2[rows, :], wu[:, cols])) for rows in row_blocks]
        for rows, (gate, up) in zip(row_blocks, products):
            value, slope = gelu_parts(gate)
            a = (value * up).astype(BF)
            gv[rows, cols] = value.astype(BF)
            us[rows, cols] = (up * slope).astype(BF)
            act[rows, cols] = a
            h2[rows, :] += mm(a, wd[cols, :])
        for copy in tile_pushes(t):
            copy.start()
        return carry

    lax.fori_loop(0, n_tiles, ffn, 0)
    loads[4].wait()

    def top(rows):
        h = h2[rows, :]
        n = (h * rms(h) * gain_l).astype(BF)
        n3[rows, :] = n
        pr = mm(n, wp[...])
        proj[rows, :] = pr
        emb[rows, :] = (pr * lax.rsqrt(jnp.sum(pr * pr, axis=-1, keepdims=True) + EPS)).astype(BF)

    rows_loop(count, 256, top)
    if columns:
        z = lax.axis_index("wide") >> 1
        sent_mask = refs[-1]
        sent_mask[...] = refs[0][...].astype(F).astype(BF)
        for m, send in enumerate(sends):
            send[0:count, :] = emb[...]
            own_rows = sent_mask[pl.ds(pl.multiple_of(16 * (z ^ m), 16), 16), :]
            for b in range(DL // 128):
                first = count + 16 * b
                send[first : first + 16, :] = own_rows[:, 128 * b : 128 * b + 128]
    push(12, h2, h2_h)
    push(13, n3, n3_h)
    push(14, proj, proj_h)
    wait_all(outs.values())
    for t in range(n_tiles):
        wait_all(tile_pushes(t))


def layer_forward(tokens, weights, gains, rel, hot, seq, columns=(), after=()):
    count, width = tokens.shape
    wq, wk, wv, wo, wg, wu, wd, wp = weights
    hidden = wg.shape[1]
    emb = wp.shape[1]
    heads = rel.shape[0]
    keys = DL if seq == DL else 128
    saved = (
        sds((count, width), BF),
        sds((count, width), BF),
        sds((count, width), BF),
        sds((count, width), BF),
        sds((heads, count, keys), BF),
        sds((count, width), F),
        sds((count, width), BF),
        sds((count, width), F),
        sds((count, width), BF),
        sds((count, hidden), BF),
        sds((count, hidden), BF),
        sds((count, hidden), BF),
        sds((count, width), F),
        sds((count, width), BF),
        sds((count, emb), F),
        sds((heads, 1, count), F),
    )
    outs = pl.pallas_call(
        functools.partial(fwd_kernel, seq, heads, len(after), len(columns)),
        out_shape=saved
        + (sds((count, emb), BF),)
        + (sds((count + 16 * DL // 128, emb), BF),) * (4 * len(columns)),
        in_specs=[VM] * 6 + [ANY] * 8 + [VM] * len(columns) + [ANY] * len(after),
        out_specs=[ANY] * 16 + [VM] * (1 + 4 * len(columns)),
        scratch_shapes=[pltpu.VMEM(w.shape, BF) for w in weights]
        + [pltpu.VMEM(s.shape, s.dtype) for s in saved]
        + [
            pltpu.VMEM((heads, 1, TABLE), F),
            pltpu.VMEM((heads, 128, 384 if seq == DL else 128), F),
            pltpu.SemaphoreType.DMA((5,)),
            pltpu.SemaphoreType.DMA((hidden // 512, 3)),
            pltpu.SemaphoreType.DMA((hidden // 512, 3)),
            pltpu.SemaphoreType.DMA((16,)),
            pltpu.VMEM((64, DL) if columns else (16, 128), BF),
        ],
        compiler_params=pltpu.CompilerParams(vmem_limit_bytes=VMEM_LIMIT),
        cost_estimate=cost(count * 14e6, 40e6),
        name="layer_forward_%d" % seq,
    )(tokens, *gains, rel, hot, *weights, *columns, *after)
    return dict(zip(SAVED, outs)), outs[len(SAVED) :]


def each_block(arrays, block, fn):
    first = 0
    for array in arrays:
        number = array.shape[0] // block
        if number == 1:
            fn(first, array[...])
        else:

            def step(i, carry, array=array, first=first):
                fn(first + i, array[pl.ds(pl.multiple_of(i * block, block), block), :])
                return carry

            lax.fori_loop(0, number, step, 0)
        first += number


def query_sims_kernel(fast, n_docs, n_ins, ids, used, qemb, cot, *refs):
    ins = refs[:n_ins]
    *coefs, d_emb, parts, es, total, counts = refs[n_ins:]
    place = Place(fast)
    tokens = qemb.shape[0]
    queries = tokens // QUERY_LENGTH
    lane = lax.broadcasted_iota(jnp.int32, (tokens, 128), 1)
    lane_q = lax.broadcasted_iota(jnp.int32, (queries, 128), 1)
    total[...] = jnp.zeros_like(total)
    counts[...] = jnp.zeros_like(counts)

    if fast:
        row = lax.broadcasted_iota(jnp.int32, (queries, 16), 0)
        pick = row + queries * place.own == lax.broadcasted_iota(jnp.int32, (queries, 16), 1)
        pick = jnp.where(pick, 1.0, 0.0).astype(BF)
        per = DL + 16 * DL // 128

        def rows_at(slot, first, last):
            if slot < 4:
                return ins[slot][first:last, :]
            base = per * (slot - 4)
            return ins[4][base + first : base + last, :]

        def doc_at(slot):
            return rows_at(slot, 0, DL)

        def mask_at(slot):
            packed = rows_at(slot, DL, per)
            return jnp.concatenate([mm(pick, packed[16 * b : 16 * b + 16]) for b in range(4)], axis=1)

        def each(fn):
            for slot in range(n_docs):
                fn(slot)

    else:
        docs, mask = ins

        def doc_at(slot):
            return docs[pl.ds(pl.multiple_of(slot * DL, DL), DL), :]

        def mask_at(slot):
            return mask[slot]

        def each(fn):
            def step(i, carry):
                fn(i)
                return carry

            lax.fori_loop(0, n_docs, step, 0)

    def forward(slot):
        d = place.doc(slot)
        m = mask_at(slot)
        wide = jnp.broadcast_to(m[:, None, :], (queries, QUERY_LENGTH, DL)).reshape(tokens, DL)
        e = jnp.exp(mm_nt(qemb[...], doc_at(slot)) * SCALE) * wide
        es[slot] = e
        total[...] = jnp.where(lane == d, jnp.sum(e, axis=1, keepdims=True), total[...])
        counts[...] = jnp.where(lane_q == d, jnp.sum(m, axis=1, keepdims=True), counts[...])

    each(forward)
    inside = lane_q < n_docs
    z = jnp.sum(jnp.log(1.0 + total[...]).reshape(queries, QUERY_LENGTH, 128), axis=1)
    z = z * (1.0 / QUERY_LENGTH)
    hot = jnp.zeros((queries, 128), F)
    row_q = lax.broadcasted_iota(jnp.int32, (queries, 128), 0)
    for q in range(queries):
        for s in range(ids.shape[0]):
            number = jnp.where(s < used[q], ids[s, q], 128)
            hot = jnp.where((row_q == q) & (lane_q == number), 1.0, hot)
    peak = jnp.max(jnp.where(inside, z, -1e30), axis=1, keepdims=True)
    power = jnp.where(inside, jnp.exp(jnp.where(inside, z - peak, 0.0)), 0.0)
    whole = jnp.sum(power, axis=1, keepdims=True)
    positive = jnp.sum(hot * power, axis=1, keepdims=True)
    loss = jnp.sum(jnp.log(whole) - jnp.log(positive))
    hits = jnp.sum(hot * counts[...])
    found = jnp.sum(hot)
    lane_p = lax.broadcasted_iota(jnp.int32, (8, 128), 1)
    parts[...] = jnp.where(
        lane_p == 0, loss, jnp.where(lane_p == 1, hits, jnp.where(lane_p == 2, found, 0.0))
    )
    d_z = power / whole - hot * power / positive
    d_wide = jnp.broadcast_to(d_z[:, None, :], (queries, QUERY_LENGTH, 128)).reshape(tokens, 128)
    c = d_wide * (SCALE / QUERY_LENGTH) / (1.0 + total[...])
    by_doc = jnp.transpose(c)[0:n_docs, :]
    if fast:
        high_part = by_doc.astype(BF)
        low_part = (by_doc - high_part.astype(F)).astype(BF)
        row = lax.broadcasted_iota(jnp.int32, (8, 8), 0)
        column = lax.broadcasted_iota(jnp.int32, (8, 8), 1)
        for m, coef in enumerate(coefs):
            document = 2 * (place.z ^ m) + (row >> 1)
            picks = [
                jnp.where((row < 4) & ((row & 1) == half) & (column == document), 1.0, 0.0).astype(BF)
                for half in range(2)
            ]
            lines = [
                mm(picks[0], part[:, 0:128]) + mm(picks[1], part[:, 128:256])
                for part in (high_part, low_part)
            ]
            coef[0:tokens, :] = qemb[...]
            coef[tokens:, :] = jnp.concatenate(lines, axis=0).astype(BF)
    else:
        coefs[0][...] = jnp.zeros_like(coefs[0])
        for half in range(tokens // 128):
            coefs[0][:, half, :] = by_doc[:, 128 * half : 128 * half + 128]
    d_emb[...] = cot[...].astype(F)

    def backward(slot):
        column = jnp.sum(jnp.where(lane == place.doc(slot), c, 0.0), axis=1, keepdims=True)
        d_emb[...] += mm((es[slot] * column).astype(BF), doc_at(slot))

    each(backward)


def query_sims(fast, ids, used, qemb, cot, ins, n_docs):
    tokens, emb = qemb.shape
    queries = tokens // QUERY_LENGTH
    return pl.pallas_call(
        functools.partial(query_sims_kernel, fast, n_docs, len(ins)),
        out_shape=((sds((tokens + 16, 128), BF),) * 4 if fast else (sds((n_docs, 8, 128), F),))
        + (sds((tokens, emb), F), sds((8, 128), F)),
        in_specs=[SM] * 2 + [VM] * (2 + len(ins)),
        out_specs=[VM] * (6 if fast else 3),
        scratch_shapes=[
            pltpu.VMEM((n_docs, tokens, DL), F),
            pltpu.VMEM((tokens, 128), F),
            pltpu.VMEM((queries, 128), F),
        ],
        compiler_params=pltpu.CompilerParams(vmem_limit_bytes=VMEM_LIMIT),
        cost_estimate=cost(n_docs * 67e6 * 10, n_docs * 1e6),
        name="query_sims",
    )(ids, used, qemb, cot, *ins)


def top_rows(d_emb, proj, h2, gain, wp):
    inv = lax.rsqrt(jnp.sum(proj * proj, axis=-1, keepdims=True) + EPS)
    along = jnp.sum(proj * d_emb, axis=-1, keepdims=True)
    d_proj = (inv * d_emb - proj * (inv * inv * inv) * along).astype(BF)
    d_h2, grad_gain = rms_back(h2, gain, mm_nt(d_proj, wp))
    return d_proj, d_h2, grad_gain


def back_kernel(
    fast, d_emb_in, demb, every, others, mask, rep, coef, d_emb_q, proj_d, proj_q, gf, gl, wp,
    h2_dh, h2_qh, n2_dh, n2_qh, n3_dh, n3_qh, wd_h, us_dh, us_qh, gv_dh, gv_qh, act_dh, act_qh,
    wg_h, wu_h, hid_dh, hid_qh, wo_h, li_dh, li_qh,
    d_hid, d_attn, g_out, g_gain, keep_h, send_h,
    h2, n2, n3, wd, us, gv, gate, up, act, wg, wu, hid, wo, li,
    n2t, d_proj, d_all, acc, d_n2, low_grads, down_grads, up_grads,
    sem_in, sem_tile, sem_last, sem_low, sem_out,
):
    place = Place(fast)
    count = demb.shape[0]
    rows = d_all.shape[0]

    def both(doc, query, target):
        return [(doc, target.at[0:count]), (query, target.at[count:])]

    loads = start_all(
        both(h2_dh, h2_qh, h2) + both(n2_dh, n2_qh, n2) + both(n3_dh, n3_qh, n3), sem_in
    )

    def tile_loads(t):
        cols = pl.ds(pl.multiple_of(t * 512, 512), 512)
        pairs = [
            (wd_h.at[cols], wd.at[cols]),
            (wg_h.at[:, cols], wg.at[:, cols]),
            (wu_h.at[:, cols], wu.at[:, cols]),
        ]
        for doc, query, target in ((us_dh, us_qh, us), (gv_dh, gv_qh, gv), (act_dh, act_qh, act)):
            pairs += both(doc.at[:, cols], query.at[:, cols], target.at[:, cols])
        return [pltpu.make_async_copy(src, dst, sem_tile.at[t, i]) for i, (src, dst) in enumerate(pairs)]

    def last_loads():
        pairs = both(hid_dh, hid_qh, hid) + [(wo_h, wo)] + both(li_dh, li_qh, li)
        return [pltpu.make_async_copy(src, dst, sem_last.at[i]) for i, (src, dst) in enumerate(pairs)]

    for copy in tile_loads(0):
        copy.start()
    acc[0:count, :] = d_emb_in[...].astype(F)
    acc[count:, :] = d_emb_q[...]
    per = 64 * QUERY_LENGTH // 256

    def sims(row, qb, line):
        e = jnp.exp(mm_nt(demb[...], qb) * SCALE)
        first = pl.multiple_of((row // per) * 64, 64)
        here = mask[pl.ds(first, 64), :].astype(F).astype(BF)
        m = mm_tn(here, rep[:, pl.ds(pl.multiple_of((row % per) * 256, 256), 256)])
        acc[0:count, :] += mm((e * m * line).astype(BF), qb)

    if fast:
        row = lax.broadcasted_iota(jnp.int32, (8, 16), 0)
        column = lax.broadcasted_iota(jnp.int32, (8, 16), 1)
        pick = (row < 2) & ((column & 7) == 2 * place.own + row)
        pick = jnp.where(pick, 1.0, 0.0).astype(BF)
        for slot in range(8):
            source, at = (every if slot < 4 else others), slot % 4
            first = 272 * at
            halves = mm(pick, source[first + 256 : first + 272, :])
            line = jnp.concatenate([halves[0:1, :], halves[1:2, :]], axis=1)
            sims(place.doc(slot), source[first : first + 256, :], line)
    else:

        def step(row, carry):
            line = jnp.concatenate([coef[row, 0:1, :], coef[row, 1:2, :]], axis=1)
            sims(row, every[pl.ds(pl.multiple_of(row * 256, 256), 256), :], line)
            return carry

        lax.fori_loop(0, coef.shape[0], step, 0)
    wait_all(loads[0:2])
    g_gain[...] = jnp.zeros_like(g_gain)
    gain_l = row_of(gl)
    for at_rows, proj in ((slice(0, count), proj_d), (slice(count, rows), proj_q)):
        dp, dh, gg = top_rows(acc[at_rows, :], proj[...], h2[at_rows, :], gain_l, wp[...])
        d_proj[at_rows, :] = dp
        h2[at_rows, :] = dh
        g_gain[1:2, :] += gg
        d_all[at_rows, :] = dh.astype(BF)
    wait_all(loads[2:])
    n2t[...] = jnp.transpose(n2[...])
    gp = mm_tn(n3[...], d_proj[...])
    low_grads[...] = jnp.zeros_like(low_grads)
    for w in range(8):
        for r in range(3):
            first = 96 * w + 32 * r
            low_grads[w % 2, w // 2, r // 2, r % 2, :, 0:128] = gp[first : first + 32, :].astype(BF)
    below = pl.ds(192, 32)
    low = start_all(
        (
            (low_grads.at[place.own], keep_h.at[:, :, :, below]),
            (low_grads.at[1 - place.own], send_h.at[:, :, :, below]),
        ),
        sem_low,
    )
    d_n2[...] = jnp.zeros_like(d_n2)

    def outputs(t, slot):
        copies = []
        for i, (core, target) in enumerate(((place.own, keep_h), (1 - place.own, send_h))):
            copies.append(
                pltpu.make_async_copy(
                    down_grads.at[slot, core], target.at[t, :, :, pl.ds(0, 192)], sem_out.at[slot, 3 * i]
                )
            )
            start = pl.multiple_of(224 + (t % 2) * 192, 32)
            for base in range(2):
                copies.append(
                    pltpu.make_async_copy(
                        up_grads.at[slot, base, core],
                        target.at[:, base, t // 2, pl.ds(start, 192)],
                        sem_out.at[slot, 3 * i + 1 + base],
                    )
                )
        return copies

    def tile(t, carry):
        slot = t % 2
        cols = pl.ds(pl.multiple_of(t * 512, 512), 512)

        @pl.when(t >= 2)
        def _():
            wait_all(outputs(t - 2, slot))

        @pl.when(t < 3)
        def _():
            for copy in tile_loads(t + 1):
                copy.start()

        @pl.when(t == 3)
        def _():
            for copy in last_loads():
                copy.start()

        wait_all(tile_loads(t))
        d_act = mm_nt(d_all[...], wd[cols, :])
        gate[...] = (d_act * us[:, cols].astype(F)).astype(BF)
        up[...] = (d_act * gv[:, cols].astype(F)).astype(BF)
        for half in range(2):
            first = pl.multiple_of((2 * t + half) * 256, 256)
            g = mm_tn(act[:, pl.ds(first, 256)], d_all[...])
            for r in range(4):
                for c in range(3):
                    down_grads[slot, half, r // 2, r % 2, 64 * c : 64 * c + 64, :] = g[
                        64 * r : 64 * r + 64, 256 * c : 256 * c + 256
                    ].astype(BF)
        for base, source in ((0, gate), (1, up)):
            g = mm(n2t[...], source[...]).astype(BF)
            for c in range(2):
                for w in range(8):
                    up_grads[slot, base, w % 2, w // 2, 96 * c : 96 * c + 96, :] = g[
                        96 * w : 96 * w + 96, 256 * c : 256 * c + 256
                    ]
        for copy in outputs(t, slot):
            copy.start()
        d_n2[...] += mm_nt(gate[...], wg[:, cols]) + mm_nt(up[...], wu[:, cols])
        return carry

    lax.fori_loop(0, 4, tile, 0)
    wait_all(last_loads())
    gain_f = row_of(gf)

    def through(at_rows):
        dm, gg = rms_back(hid[at_rows, :], gain_f, d_n2[at_rows, :])
        total = h2[at_rows, :] + dm
        d_hid[at_rows, :] = total
        g_gain[0:1, :] += gg
        d_attn[at_rows, :] = total.astype(BF)

    rows_loop(rows, 256, through)

    def to_context(at_rows):
        d_context = mm_nt(d_attn[at_rows, :], wo[...]).astype(BF).astype(F)
        g_out[at_rows, :] = (d_context * li[at_rows, :]).astype(BF)

    rows_loop(rows, 256, to_context)
    wait_all(low)
    for t in (2, 3):
        wait_all(outputs(t, t % 2))


def back(fast, d_emb, demb, every, others, mask, rep, coef, d_emb_q, dsaved, qsaved, gains, weights):
    wq, wk, wv, wo, wg, wu, wd, wp = weights
    count, width = dsaved["h2"].shape
    rows = count + d_emb_q.shape[0]
    hidden = wd.shape[0]
    emb = wp.shape[1]
    piece = sds((4, 2, 2, 608, 256), BF)

    def both(name):
        return dsaved[name], qsaved[name]

    return pl.pallas_call(
        functools.partial(back_kernel, fast),
        out_shape=(
            sds((rows, width), F),
            sds((rows, width), BF),
            sds((rows, width), BF),
            sds((8, width), F),
            piece,
            piece,
        ),
        in_specs=[VM] * 13 + [ANY] * 20,
        out_specs=[VM] * 4 + [ANY] * 2,
        scratch_shapes=[
            pltpu.VMEM((rows, width), F),
            pltpu.VMEM((rows, width), BF),
            pltpu.VMEM((rows, width), BF),
            pltpu.VMEM(wd.shape, BF),
            pltpu.VMEM((rows, hidden), BF),
            pltpu.VMEM((rows, hidden), BF),
            pltpu.VMEM((rows, 512), BF),
            pltpu.VMEM((rows, 512), BF),
            pltpu.VMEM((rows, hidden), BF),
            pltpu.VMEM(wg.shape, BF),
            pltpu.VMEM(wu.shape, BF),
            pltpu.VMEM((rows, width), F),
            pltpu.VMEM(wo.shape, BF),
            pltpu.VMEM((rows, width), F),
            pltpu.VMEM((width, rows), BF),
            pltpu.VMEM((rows, emb), BF),
            pltpu.VMEM((rows, width), BF),
            pltpu.VMEM((rows, emb), F),
            pltpu.VMEM((rows, width), F),
            pltpu.VMEM((2, 4, 2, 2, 32, 256), BF),
            pltpu.VMEM((2, 2, 2, 2, 192, 256), BF),
            pltpu.VMEM((2, 2, 2, 4, 192, 256), BF),
            pltpu.SemaphoreType.DMA((6,)),
            pltpu.SemaphoreType.DMA((4, 9)),
            pltpu.SemaphoreType.DMA((5,)),
            pltpu.SemaphoreType.DMA((2,)),
            pltpu.SemaphoreType.DMA((2, 6)),
        ],
        compiler_params=pltpu.CompilerParams(vmem_limit_bytes=VMEM_LIMIT),
        cost_estimate=cost(14e9, 10e6),
        name="back",
    )(
        d_emb, demb, every, others, mask, rep, coef, d_emb_q, *both("proj"), gains[1], gains[2], wp,
        *both("h2"), *both("n2"), *both("n3"), wd, *both("us"), *both("gv"), *both("act"), wg, wu,
        *both("hid"), wo, *both("li"),
    )


def attn_back_kernel(
    first, n_pairs, with_queries, hot, g_h, q_d, q_q, k_d, k_q, v_d, v_q, lr_d, lr_q, p_dh, p_qh, *refs
):
    n_outs = 7 if with_queries else 4
    outs = refs[-n_outs - 15 : -15]
    (
    q, k, v, g, p_d, p_q, lrd, lrq, ds, acc, sums, sem_in, sem_p, qq, gq,
    ) = refs[-15:]
    dq, dk, dv, g_rel = outs[:4]
    count = q_d.shape[0]
    rest = q_q.shape[0]
    blocks = count // 128
    heads_here = pl.ds(2 * first, 2 * n_pairs)
    lanes_here = pl.ds(128 * first, 128 * n_pairs)
    pairs = []
    if with_queries:
        pairs += [
            (v_q, qq.at[2]),
            (g_h.at[count:], gq),
            (p_qh, p_q),
            (lr_q, lrq),
            (q_q, qq.at[0]),
            (k_q, qq.at[1]),
        ]
    n_query = len(pairs)
    pairs += [
        (v_d.at[:, lanes_here], v),
        (g_h.at[0:count, lanes_here], g),
        (lr_d.at[heads_here], lrd),
        (q_d.at[:, lanes_here], q),
        (k_d.at[:, lanes_here], k),
    ]
    loads = start_all(pairs, sem_in)

    def p_load(pair):
        return pltpu.make_async_copy(
            p_dh.at[pl.ds(2 * (first + pair), 2)], p_d.at[pl.ds(2 * pair, 2)], sem_p.at[pair]
        )

    p_load(0).start()
    low, high, _, _ = half_masks()
    keeps = (low.astype(BF), high.astype(BF))
    acc[...] = jnp.zeros_like(acc)
    wait_all(loads[:n_query])

    if with_queries:
        cells_q = rest // 128
        heads = p_q.shape[0]
        rows_q = [slice(128 * b, 128 * b + 128) for b in range(cells_q)]
        lanes_of = [slice(128 * pair, 128 * pair + 128) for pair in range(heads // 2)]
        for group in range(0, heads // 2, 3):
            cells = [
                (pair, e, b) for pair in range(group, group + 3) for e in range(2) for b in range(cells_q)
            ]
            d_ps = [
                mm_nt(qq[2, rows_q[b], lanes_of[pair]] * keeps[e], gq[rows_q[b], lanes_of[pair]])
                for pair, e, b in cells
            ]
            dss = []
            for d_p, (pair, e, b) in zip(d_ps, cells):
                head = 2 * pair + e
                pf = p_q[head, rows_q[b], :].astype(F)
                t = pf * d_p
                share = lrq[head, :, rows_q[b]] * jnp.sum(t, axis=0, keepdims=True)
                d_s = t - pf * share
                acc[head, :, 128:256] += d_s
                dss.append(d_s.astype(BF))
            for pair in range(group, group + 3):
                lanes = lanes_of[pair]
                for b in range(cells_q):
                    rows = rows_q[b]
                    at_cell = [cells.index((pair, e, b)) for e in range(2)]
                    probs = [p_q[2 * pair + e, rows, :] for e in range(2)]
                    parts = [
                        (
                            mm_tn(dss[at_cell[e]], qq[1, rows, lanes] * keeps[e]),
                            mm(dss[at_cell[e]], qq[0, rows, lanes] * keeps[e]),
                            mm(probs[e], gq[rows, lanes] * keeps[e]),
                        )
                        for e in range(2)
                    ]
                    for i in range(3):
                        outs[4 + i][rows, lanes] = (parts[0][i] + parts[1][i]).astype(BF)
    wait_all(loads[n_query:])

    def doc_pair(pair, carry):
        lanes = pl.ds(pl.multiple_of(pair * 128, 128), 128)

        @pl.when(pair + 1 < n_pairs)
        def _():
            p_load(pair + 1).start()

        p_load(pair).wait()
        q2 = q[:, lanes]
        k2 = k[:, lanes]
        v2 = v[:, lanes]
        g2 = g[:, lanes]
        d_ps = [mm_nt(v2 * keep, g2) for keep in keeps]
        sides = []
        for e, keep in enumerate(keeps):
            head = 2 * pair + e
            acc_head = 2 * (first + pair) + e if with_queries else head
            for i in range(blocks):
                cols = slice(128 * i, 128 * i + 128)
                pfs = [p_d[head, 128 * j : 128 * j + 128, cols].astype(F) for j in range(blocks)]
                ts = [pfs[j] * d_ps[e][128 * j : 128 * j + 128, cols] for j in range(blocks)]
                total = functools.reduce(jnp.add, ts)
                share = lrd[head, :, cols] * jnp.sum(total, axis=0, keepdims=True)
                for j in range(blocks):
                    d_s = ts[j] - pfs[j] * share
                    t = 1 - (j - i)
                    tile = t if abs(j - i) <= 1 else (3 if j > i else 4)
                    acc[acc_head, :, 128 * tile : 128 * tile + 128] += d_s
                    ds[e, 128 * j : 128 * j + 128, cols] = d_s.astype(BF)
            sides.append(
                (
                    mm_tn(ds[e], k2 * keep),
                    mm(ds[e], q2 * keep),
                    mm(p_d[head], g2 * keep),
                )
            )
        dq[:, lanes] = (sides[0][0] + sides[1][0]).astype(BF)
        dk[:, lanes] = (sides[0][1] + sides[1][1]).astype(BF)
        dv[:, lanes] = (sides[0][2] + sides[1][2]).astype(BF)
        return carry

    lax.fori_loop(0, n_pairs, doc_pair, 0, unroll=2 if with_queries else 1)
    sums[...] = jnp.zeros_like(sums)
    n_heads = acc.shape[0]
    lane = lax.broadcasted_iota(jnp.int32, (n_heads, TABLE), 1)

    def left(values, by):
        flat = values.reshape(-1, TABLE)
        return pltpu.roll(flat, TABLE - by, 1).reshape(values.shape)

    near = jnp.concatenate([acc[:, :, 0:384], jnp.zeros((n_heads, 128, 128), F)], axis=2)
    folded = near[:, 0:8]
    for group in range(1, 16):
        folded = folded + left(near[:, 8 * group : 8 * group + 8], 8 * group)
    row = lax.broadcasted_iota(jnp.int32, (n_heads, 8, TABLE), 1)
    lines = folded
    for i in range(1, 8):
        lines = jnp.where(row == i, left(folded, i), lines)
    lines = jnp.sum(lines, axis=1)
    after = jnp.sum(jnp.sum(acc[:, :, 384:512], axis=1), axis=1, keepdims=True)
    before = jnp.sum(jnp.sum(acc[:, :, 512:640], axis=1), axis=1, keepdims=True)
    lines = lines + jnp.where(lane == 0, after, jnp.where(lane == 256, before, 0.0))
    offset = 0 if with_queries else 2 * first
    sums[offset : offset + n_heads, :] = lines
    g_rel[...] = lax.dot_general(
        sums[...], hot[...], (((1,), (1,)), ((), ())),
        preferred_element_type=F, precision=lax.Precision.HIGHEST,
    )


def attn_back(first, n_pairs, with_queries, g, dsaved, qsaved, hot, after):
    rows, width = g.shape
    heads = dsaved["p"].shape[0]
    buckets = hot.shape[0]
    count = dsaved["q"].shape[0]
    rest = rows - count
    columns = 128 * n_pairs
    both = []
    for name in ("q", "k", "v", "lr", "p"):
        both += [dsaved[name], qsaved[name]]
    outs = (sds((count, columns), BF),) * 3 + (sds((16, buckets), F),)
    if with_queries:
        outs = outs + (sds((rest, width), BF),) * 3
    return pl.pallas_call(
        functools.partial(attn_back_kernel, first, n_pairs, with_queries),
        out_shape=outs,
        in_specs=[VM] + [ANY] * (11 + len(after)),
        out_specs=[VM] * len(outs),
        scratch_shapes=[pltpu.VMEM((count, columns), BF)] * 4
        + [
            pltpu.VMEM((2 * n_pairs, DL, DL), BF),
            pltpu.VMEM((heads, rest, 128), BF),
            pltpu.VMEM((2 * n_pairs, 1, count), F),
            pltpu.VMEM((heads, 1, rest), F),
            pltpu.VMEM((2, DL, DL), BF),
            pltpu.VMEM((heads if with_queries else 2 * n_pairs, 128, 640), F),
            pltpu.VMEM((16, TABLE), F),
            pltpu.SemaphoreType.DMA((11,)),
            pltpu.SemaphoreType.DMA((n_pairs,)),
            pltpu.VMEM((3, rest, width), BF),
            pltpu.VMEM((rest, width), BF),
        ],
        compiler_params=pltpu.CompilerParams(vmem_limit_bytes=VMEM_LIMIT),
        cost_estimate=cost(15e9, 40e6),
        name="attn_back_%d" % first,
    )(hot, g, *both, *after)


SMALL = 48


def split_small(values):
    high = values.astype(BF)
    return jnp.concatenate([high, (values - high.astype(F)).astype(BF)], axis=1)


def join_small(rows):
    return rows[:, 0:128].astype(F) + rows[:, 128:256].astype(F)


def attn_parts(first, second, targets):
    half = first[0].shape[1]
    count = first[0].shape[0]
    pairs = []
    for i, target in enumerate(targets):
        pairs += [
            (first[i], target.at[0:count, 0:half]),
            (second[i], target.at[0:count, half:]),
            (first[4 + i], target.at[count:]),
        ]
    return pairs


def attn_grads_kernel(fast, *refs):
    ins, (d_attn_h, n1_d, n1_q, ctx_d, ctx_q) = refs[:9], refs[9:14]
    keep_h, *sends = refs[-12:-9]
    dq, dk, dv, d_attn, n1, ctx, grads, sem_in, sem_out = refs[-9:]
    first = ins[0:3] + (None,) + ins[3:6]
    place = Place(fast)
    count = n1_d.shape[0]
    pairs = [
        (n1_d, n1.at[0:count]),
        (n1_q, n1.at[count:]),
        *attn_parts(first, ins[6:9], (dq, dk, dv)),
        (d_attn_h, d_attn),
        (ctx_d, ctx.at[0:count]),
        (ctx_q, ctx.at[count:]),
    ]
    loads = start_all(pairs, sem_in)
    outs = []
    wait_all(loads[0:2])
    groups = (loads[2:5], loads[5:8], loads[8:11], loads[11:14])
    for which, (left, right) in enumerate(((n1, dq), (n1, dk), (n1, dv), (ctx, d_attn))):
        wait_all(groups[which])
        value = mm_tn(left[...], right[...]).astype(BF)
        for w in range(8):
            for c in range(3):
                row = ((w // 2) * 4 + which) * 288 + 96 * c
                grads[w % 2, row : row + 96, :] = value[96 * w : 96 * w + 96, 256 * c : 256 * c + 256]
        for z in range(4):
            rows = slice((z * 4 + which) * 288, (z * 4 + which) * 288 + 288)
            start = (z % 2 * 4 + which) * 288
            there = sends[z // 2].at[start : start + 288]
            pairs = ((place.own, keep_h.at[rows]), (1 - place.own, there))
            for i, (core, target) in enumerate(pairs):
                copy = pltpu.make_async_copy(grads.at[core, rows], target, sem_out.at[which, z, i])
                copy.start()
                outs.append(copy)
    wait_all(outs)


def attn_grads(fast, first, second, d_attn, dsaved, qsaved, after):
    rows, width = d_attn.shape
    piece = sds((16 * 288, 256), BF)
    ins = (*first[0:3], *first[4:7], *second[0:3])
    keep, *sends = pl.pallas_call(
        functools.partial(attn_grads_kernel, fast),
        out_shape=(piece,) + (sds((8 * 288, 256), BF),) * 2,
        in_specs=[ANY] * (14 + len(after)),
        out_specs=[ANY] * 3,
        scratch_shapes=[pltpu.VMEM((rows, width), BF)] * 6
        + [
            pltpu.VMEM((2,) + piece.shape, BF),
            pltpu.SemaphoreType.DMA((14,)),
            pltpu.SemaphoreType.DMA((4, 4, 2)),
        ],
        compiler_params=pltpu.CompilerParams(vmem_limit_bytes=VMEM_LIMIT),
        cost_estimate=cost(1, 1),
        name="attn_grads",
    )(*ins, d_attn, dsaved["n1"], qsaved["n1"], dsaved["ctx"], qsaved["ctx"], *after)
    return keep, sends


def input_back_kernel(ga, gains, parts, rel_0, rel_1, *refs):
    ins, (wq_h, wk_h, wv_h, tok_d, tok_q, d_hid_h) = refs[:9], refs[9:15]
    out_dh, out_qh, small = refs[-16:-13]
    dq, dk, dv, wq, wk, wv, tok, d_hid, d_n1, out, g_gain, sem_in, sem_out = refs[-13:]
    first = ins[0:3] + (None,) + ins[3:6]
    count = tok_d.shape[0]
    parts_q = attn_parts(first, ins[6:9], (dq, dk, dv))
    groups = (
        [*parts_q[0:3], (wq_h, wq)],
        [*parts_q[3:6], (wk_h, wk)],
        [*parts_q[6:9], (wv_h, wv)],
        [
            (tok_d, tok.at[0:count]),
            (tok_q, tok.at[count:]),
            (d_hid_h, d_hid),
        ],
    )
    loads = [start_all(groups[0], sem_in.at[0])]
    gain_a = row_of(ga)
    g_gain[...] = jnp.zeros_like(g_gain)
    for i, (left, right) in enumerate(((dq, wq), (dk, wk), (dv, wv))):
        loads.append(start_all(groups[i + 1], sem_in.at[i + 1]))
        wait_all(loads[i])
        part = mm_nt(left[...], right[...])
        d_n1[...] = part if i == 0 else d_n1[...] + part
    wait_all(loads[3])

    def step(rows):
        d_in, gg = rms_back(tok[rows, :].astype(F), gain_a, d_n1[rows, :])
        g_gain[0:1, :] += gg
        out[rows, :] = (d_hid[rows, :] + d_in).astype(BF)

    rows_loop(tok.shape[0], 256, step)
    outs = start_all(((out.at[0:count], out_dh), (out.at[count:], out_qh)), sem_out)
    small[...] = jnp.zeros_like(small)
    rows = (
        g_gain[0:1, :],
        gains[0:1, :],
        gains[1:2, :],
    )
    for i, row in enumerate(rows):
        for c in range(6):
            small[8 * i + c : 8 * i + c + 1, :] = row[:, 128 * c : 128 * c + 128]
    small[24:25, :] = parts[0:1, :]
    small[32:48, 0 : rel_0.shape[1]] = rel_0[...] + rel_1[...]
    wait_all(outs)


def input_back(tok_d, tok_q, d_hid, gain, gains, parts, first, second, weights, after):
    count, width = tok_d.shape
    rows = count + tok_q.shape[0]
    ins = (*first[0:3], *first[4:7], *second[0:3])
    return pl.pallas_call(
        input_back_kernel,
        out_shape=(sds(tok_d.shape, BF), sds(tok_q.shape, BF), sds((SMALL, 128), F)),
        in_specs=[VM] * 5 + [ANY] * (15 + len(after)),
        out_specs=[ANY] * 2 + [VM],
        scratch_shapes=[pltpu.VMEM((rows, width), BF)] * 3
        + [pltpu.VMEM((width, width), BF)] * 3
        + [
            pltpu.VMEM((rows, width), BF),
            pltpu.VMEM((rows, width), F),
            pltpu.VMEM((rows, width), F),
            pltpu.VMEM((rows, width), BF),
            pltpu.VMEM((8, width), F),
            pltpu.SemaphoreType.DMA((4, 4)),
            pltpu.SemaphoreType.DMA((2,)),
        ],
        compiler_params=pltpu.CompilerParams(vmem_limit_bytes=VMEM_LIMIT),
        cost_estimate=cost(3e9, 10e6),
        name="input_back",
    )(
        gain, gains, parts, first[3], second[3], *ins, weights[0], weights[1], weights[2],
        tok_d, tok_q, d_hid, *after,
    )


def unpack_attn_kernel(heads, total_queries, own, one, two, three, *refs):
    outs, (gain_a, gain_f, gain_l, rel, loss, fraction, stack, smalls) = refs[-12:-8], refs[-8:]
    place = Place(True)
    rows = stack.shape[1]
    for m, part in enumerate((own, one, two, three)):
        stack[place.rep ^ m] = part[0:rows, :]
        smalls[place.rep ^ m] = join_small(part[rows:, :])
    for r in range(4):
        for c in range(3):
            outs[r][:, 256 * c : 256 * c + 256] = stack[r, 96 * c : 96 * c + 96, :].astype(F)
    total = smalls[0] + smalls[1] + smalls[2] + smalls[3]
    for i, gain in enumerate((gain_a, gain_f, gain_l)):
        row = jnp.concatenate([total[8 * i + c : 8 * i + c + 1, :] for c in range(6)], axis=1)
        gain[...] = row.reshape(gain.shape[0])
    rel[...] = total[32 : 32 + heads, 0 : rel.shape[1]]
    lane = lax.broadcasted_iota(jnp.int32, (1, 128), 1)
    line = total[24:25, :]
    loss_sum, hits, found = (jnp.sum(jnp.where(lane == i, line, 0.0)) for i in range(3))
    loss[0, 0] = loss_sum / total_queries
    fraction[0, 0] = hits / (DL * found)


def unpack_attn(heads, buckets, width, total_queries, parts):
    rows = parts[0].shape[0] - SMALL
    return pl.pallas_call(
        functools.partial(unpack_attn_kernel, heads, float(total_queries)),
        out_shape=(sds((96, width), F),) * 4
        + (sds((width,), F),) * 3
        + (sds((heads, buckets), F), sds((1, 1), F), sds((1, 1), F)),
        in_specs=[VM] * 4,
        out_specs=[VM] * 8 + [SM] * 2,
        scratch_shapes=[pltpu.VMEM((4, rows, 256), BF), pltpu.VMEM((4, SMALL, 128), F)],
        compiler_params=pltpu.CompilerParams(vmem_limit_bytes=16 * 1024 * 1024),
        cost_estimate=cost(1e6, 3e6),
        name="unpack_attn",
    )(*parts)


def unpack_kernel(own, one, two, three, *refs):
    stack = refs[-1]
    outs = refs[-5:-1]
    place = Place(True)
    half = own.shape[1]
    for m, part in enumerate((own, one, two, three)):
        for i in range(2):
            stack[place.rep ^ m, half * i : half * i + half, :] = part[i]
    for r in range(4):
        for c in range(4):
            first = (r % 2) * 1024 + 256 * c
            outs[r // 2][:, first : first + 256] = stack[
                r, 224 + 96 * c : 224 + 96 * c + 96, :
            ].astype(F)
        for c in range(3):
            outs[2][64 * r : 64 * r + 64, 256 * c : 256 * c + 256] = stack[
                r, 64 * c : 64 * c + 64, :
            ].astype(F)
    for r in range(3):
        outs[3][32 * r : 32 * r + 32, :] = stack[r, 192:224, 0:128].astype(F)


def unpack(parts, shapes, after):
    return pl.pallas_call(
        unpack_kernel,
        out_shape=tuple(sds(s, F) for s in shapes),
        in_specs=[VM] * 4 + [ANY] * len(after),
        out_specs=tuple(VM for _ in shapes),
        scratch_shapes=[pltpu.VMEM((4, 2 * parts[0].shape[1], parts[0].shape[2]), BF)],
        compiler_params=pltpu.CompilerParams(vmem_limit_bytes=16 * 1024 * 1024),
        cost_estimate=cost(1e6, 3e6),
        name="unpack_ffn",
    )(*parts, *after)


def swap(values, axis, size, mask):
    return lax.ppermute(values, axis, [(i, i ^ mask) for i in range(size)])


def near_kernel(keep_h, came_h, *refs):
    send_a, send_b, kept, came, sems = refs[-5:]
    place = Place(True)
    half = send_a.shape[2]
    y, x = place.y, place.x
    loads = []
    for z in range(4):
        pairs = []
        for i, (source, target) in enumerate(((keep_h, kept), (came_h, came))):
            pairs += [
                (source.at[z, :, 1 - x, pl.ds(0, half)], target.at[0, z]),
                (source.at[z, 1 - y, :, pl.ds(half, half)], target.at[1, z]),
            ]
        loads.append(start_all(pairs, sems.at[z]))
    for z in range(4):
        wait_all(loads[z])
        send_a[z] = kept[0, z] + came[0, z]
        send_b[z] = kept[1, z] + came[1, z]


def own_kernel(keep_h, came_h, *refs):
    own_a, own_b, kept, came, sems = refs[-5:]
    place = Place(True)
    half = own_a.shape[2]
    y, x = place.y, place.x
    loads = []
    for z in range(4):
        pairs = []
        for i, (source, target) in enumerate(((keep_h, kept), (came_h, came))):
            pairs += [
                (source.at[z, :, x, pl.ds(0, half)], target.at[0, z]),
                (source.at[z, y, :, pl.ds(half, half)], target.at[1, z]),
            ]
        loads.append(start_all(pairs, sems.at[z]))
    for z in range(4):
        wait_all(loads[z])
        own_a[z] = kept[0, z] + came[0, z]
        own_b[z] = kept[1, z] + came[1, z]


def cross_kernel(other, a_h, came_ah, b_h, came_bh, *refs):
    out_a, out_b, held, sems = refs[-4:]
    place = Place(True)
    y = 1 - place.y if other else place.y
    x = 1 - place.x if other else place.x
    loads = []
    for z in range(4):
        pairs = ((a_h.at[z, y], 0), (came_ah.at[z, y], 1), (b_h.at[z, x], 2), (came_bh.at[z, x], 3))
        loads.append(start_all([(source, held.at[i, z]) for source, i in pairs], sems.at[z]))
    for z in range(4):
        wait_all(loads[z])
        out_a[z] = held[0, z] + held[1, z]
        out_b[z] = held[2, z] + held[3, z]


def line_kernel(a, came_a, b, came_b, *refs):
    send, own = refs[-2:]
    z = Place(True).z
    for i in range(2):
        for out, to in ((own, z ^ (2 * i)), (send, z ^ 1 ^ (2 * i))):
            out[i, 0] = a[to] + came_a[to]
            out[i, 1] = b[to] + came_b[to]


def next_kernel(own, came, *refs):
    send, out = refs[-2:]
    out[...] = own[0] + came[0]
    send[...] = own[1] + came[1]


def far_kernel(own, came, *refs):
    refs[-1][...] = own[...] + came[...]


def cell(index, half, first=0):
    return pl.ds(pl.multiple_of(index * half + first, 16), half)


def attn_near_kernel(keep_h, *refs):
    came_h = refs[:2]
    send_a, send_b, kept, came, sems = refs[-5:]
    place = Place(True)
    half = send_b.shape[2]
    loads = split_loads(keep_h, came_h, kept, came, sems, half, 1 - place.x, 1 - place.y)
    for z in range(4):
        wait_all(loads[z])
        send_a[z] = kept[0, z] + came[0, z]
        send_b[z] = kept[1, z] + came[1, z]


def split_loads(keep_h, came_h, kept, came, sems, half, x, y):
    def rows(cell_number, first):
        return pl.ds(pl.multiple_of(cell_number * 2 * half + first, 16), half)

    loads = []
    for z in range(4):
        pairs = []
        for source, base, target in ((keep_h, 4 * z, kept), (came_h[z // 2], z % 2 * 4, came)):
            for i in range(2):
                pairs += [
                    (source.at[rows(base + 2 * i + x, 0)], target.at[0, z, i]),
                    (source.at[rows(base + 2 * y + i, half)], target.at[1, z, i]),
                ]
        loads.append(start_all(pairs, sems.at[z]))
    return loads


def attn_own_kernel(keep_h, *refs):
    came_h = refs[:2]
    own_a, own_b, kept, came, sems = refs[-5:]
    place = Place(True)
    half = own_a.shape[2]
    loads = split_loads(keep_h, came_h, kept, came, sems, half, place.x, place.y)
    for z in range(4):
        wait_all(loads[z])
        own_a[z] = kept[0, z] + came[0, z]
        own_b[z] = kept[1, z] + came[1, z]


def attn_cross_kernel(a, came_a, b, came_b, *refs):
    send_a, send_b, own_a, own_b = refs[-4:]
    place = Place(True)
    y, x = place.y, place.x
    for z in range(4):
        send_a[z] = a[z, 1 - y] + came_a[z, 1 - y]
        own_a[z] = a[z, y] + came_a[z, y]
        send_b[z] = b[z, 1 - x] + came_b[z, 1 - x]
        own_b[z] = b[z, x] + came_b[z, x]


def attn_line_kernel(a, came_a, b, came_b, small_a, small_b, *refs):
    send, own, small = refs[-3:]
    z = Place(True).z
    half = a.shape[1]
    for i in range(2):
        for out, to in ((own, z ^ (2 * i)), (send, z ^ 1 ^ (2 * i))):
            out[2 * half * i : 2 * half * i + half, :] = a[to] + came_a[to]
            out[2 * half * i + half : 2 * half * i + 2 * half, :] = b[to] + came_b[to]
    value = split_small(small_a[...] + small_b[...])
    send[4 * half :, :] = value
    small[...] = value


def attn_next_kernel(own, came, small_in, *refs):
    send, out, small = refs[-3:]
    rows = out.shape[0]
    out[...] = own[0:rows, :] + came[0:rows, :]
    send[0:rows, :] = own[rows : 2 * rows, :] + came[rows : 2 * rows, :]
    value = split_small(join_small(small_in[...]) + join_small(came[2 * rows :, :]))
    send[rows:, :] = value
    small[...] = value


def attn_far_kernel(own, came, small_in, *refs):
    out = refs[-1]
    rows = own.shape[0]
    out[0:rows, :] = own[...] + came[0:rows, :]
    out[rows:, :] = split_small(join_small(small_in[...]) + join_small(came[rows:, :]))


def stage(kernel, name, ins, outs, after, flops=1, scratch=(), scalars=0, limit=16):
    return pl.pallas_call(
        kernel,
        out_shape=outs,
        in_specs=[VM] * len(ins) + [ANY] * len(after),
        out_specs=[VM] * (len(outs) - scalars) + [SM] * scalars,
        scratch_shapes=list(scratch),
        compiler_params=pltpu.CompilerParams(vmem_limit_bytes=limit * 1024 * 1024),
        cost_estimate=cost(flops, 1),
        name=name,
    )(*ins, *after)


class AttnReduction:
    def __init__(self, keep, send):
        self.half = 144
        self.keep = keep
        self.came = [swap(part, "wide", 8, 1) for part in send]
        self.small_shape = sds((SMALL, 256), BF)

    def rows(self, cells):
        return sds((cells * self.half + SMALL, 256), BF)

    def split(self, kernel, name, ins, outs, after):
        held = pltpu.VMEM((2, 4, 2, self.half, 256), BF)
        scratch = [held, held, pltpu.SemaphoreType.DMA((4, 8))]
        return pl.pallas_call(
            kernel,
            out_shape=outs,
            in_specs=[ANY] * 3 + [VM] * len(ins) + [ANY] * len(after),
            out_specs=(VM,) * len(outs),
            scratch_shapes=scratch,
            compiler_params=pltpu.CompilerParams(vmem_limit_bytes=VMEM_LIMIT),
            cost_estimate=cost(1, 1),
            name=name,
        )(self.keep, *self.came, *ins, *after)

    def near(self, after):
        outs = (sds((4, 2, self.half, 256), BF),) * 2
        send_a, send_b = self.split(attn_near_kernel, "near_attn", (), outs, after)
        self.came_a = swap(send_a, "rep", 4, 1)
        self.came_b = swap(send_b, "rep", 4, 2)
        return (send_a,)

    def mine(self, after):
        own = sds((4, 2, self.half, 256), BF)
        self.a, self.b = self.split(attn_own_kernel, "own_attn", (), (own, own), after)
        return (self.a,)

    def cross(self, after):
        outs = (sds((4, self.half, 256), BF),) * 4
        ins = (self.a, self.came_a, self.b, self.came_b)
        send_a, send_b, self.a, self.b = stage(attn_cross_kernel, "cross_attn", ins, outs, after)
        self.came_a = swap(send_a, "rep", 4, 2)
        self.came_b = swap(send_b, "rep", 4, 1)
        return (self.a,)

    def line(self, small, after):
        own = sds((4 * self.half, 256), BF)
        outs = (self.rows(4), own, self.small_shape)
        ins = (self.a, self.came_a, self.b, self.came_b, small, swap(small, "wide", 8, 1))
        send, self.own, self.small = stage(attn_line_kernel, "line_attn", ins, outs, after)
        self.came = swap(send, "wide", 8, 2)
        return (self.own,)

    def next(self, after):
        own = sds((2 * self.half, 256), BF)
        ins = (self.own, self.came, self.small)
        outs = (self.rows(2), own, self.small_shape)
        send, self.own, self.small = stage(attn_next_kernel, "next_attn", ins, outs, after)
        self.came = swap(send, "wide", 8, 4)
        return (self.own,)

    def far(self, after):
        ins = (self.own, self.came, self.small)
        (self.own,) = stage(attn_far_kernel, "far_attn", ins, (self.rows(2),), after)
        self.came = [swap(self.own, "rep", 4, m) for m in (1, 2, 3)]
        return (self.own,)

    def parts(self):
        return self.own, *self.came


class Reduction:
    def __init__(self, name, keep, send):
        self.name = name
        self.half = keep.shape[3] // 2
        self.keep = keep
        self.came = swap(send, "wide", 8, 1)

    def split(self, kernel, name, ins, shapes, specs, after):
        held = pltpu.VMEM((2, 4, 2, self.half, 256), BF)
        return pl.pallas_call(
            kernel,
            out_shape=tuple(sds(shape, BF) for shape in shapes),
            in_specs=[ANY] * 2 + specs + [ANY] * len(after),
            out_specs=(VM,) * len(shapes),
            scratch_shapes=[held, held, pltpu.SemaphoreType.DMA((4, 4))],
            compiler_params=pltpu.CompilerParams(vmem_limit_bytes=VMEM_LIMIT),
            cost_estimate=cost(1, 1),
            name=name + self.name,
        )(self.keep, self.came, *ins, *after)

    def near(self, after):
        shape = (4, 2, self.half, 256)
        send_a, send_b = self.split(near_kernel, "near_", (), (shape,) * 2, [], after)
        self.came_a = swap(send_a, "rep", 4, 1)
        self.came_b = swap(send_b, "rep", 4, 2)
        return (send_a,)

    def step(self, kernel, name, ins, shapes, after, flops=1):
        outs = tuple(sds(shape, BF) for shape in shapes)
        return stage(kernel, name + self.name, ins, outs, after, flops, limit=20)

    def mine(self, after):
        shape = (4, 2, self.half, 256)
        self.a, self.b = self.split(own_kernel, "own_", (), (shape,) * 2, [], after)
        return (self.a,)

    def half_sums(self, other, name, after):
        shape = (4, self.half, 256)
        return pl.pallas_call(
            functools.partial(cross_kernel, other),
            out_shape=(sds(shape, BF),) * 2,
            in_specs=[ANY] * (4 + len(after)),
            out_specs=(VM,) * 2,
            scratch_shapes=[pltpu.VMEM((4,) + shape, BF), pltpu.SemaphoreType.DMA((4, 4))],
            compiler_params=pltpu.CompilerParams(vmem_limit_bytes=VMEM_LIMIT),
            cost_estimate=cost(1, 1),
            name=name + self.name,
        )(*self.held, *after)

    def cross(self, after):
        self.held = (self.a, self.came_a, self.b, self.came_b)
        send_a, send_b = self.half_sums(True, "cross_", after)
        self.came_a = swap(send_a, "rep", 4, 2)
        self.came_b = swap(send_b, "rep", 4, 1)
        return (send_a,)

    def stay(self, after):
        self.a, self.b = self.half_sums(False, "stay_", after)
        return (self.a,)

    def line(self, after, flops=1):
        ins = (self.a, self.came_a, self.b, self.came_b)
        shape = (2, 2, self.half, 256)
        send, self.own = self.step(line_kernel, "line_", ins, (shape,) * 2, after, flops)
        self.came = swap(send, "wide", 8, 2)
        return (self.own,)

    def next(self, after):
        shape = (2, self.half, 256)
        send, self.own = self.step(next_kernel, "next_", (self.own, self.came), (shape,) * 2, after)
        self.came = swap(send, "wide", 8, 4)
        return (self.own,)

    def far(self, after):
        shape = (2, self.half, 256)
        (self.own,) = self.step(far_kernel, "far_", (self.own, self.came), (shape,), after)
        self.came = [swap(self.own, "rep", 4, m) for m in (1, 2, 3)]
        return (self.own,)

    def parts(self):
        return self.own, *self.came


def natural(which, keep, send):
    both = jnp.stack([keep, send])
    if which == "attn":
        a = both.reshape(2, 4, 4, 3, 96, 256).transpose(2, 1, 0, 4, 3, 5).reshape(4, 768, 768)
        return [a[i] for i in range(4)]
    both = both.reshape((2, 4, 4) + both.shape[4:])
    a = both[:, :, :, 224:].reshape(2, 4, 4, 4, 96, 256).transpose(1, 0, 4, 2, 3, 5)
    a = a.reshape(768, 4096)
    d = both[:, :, :, :192].reshape(2, 4, 4, 3, 64, 256).transpose(1, 0, 2, 4, 3, 5)
    e = both[:, :, :3, 192:224, :128].transpose(1, 0, 2, 3, 4)
    return [a[:, :2048], a[:, 2048:], d.reshape(2048, 768), e.reshape(768, 128)]


def body(
    doc_tokens, query_tokens, doc_cotangent, query_cotangent, retrieved, pos_ids, pos_count,
    w_query, w_key, carried_content_weights, w_out, w_gate, w_up, w_down, w_proj,
    gain_attn, gain_ffn, gain_final, rel_bias,
):
    n_wide = lax.axis_size("wide")
    n_rep = lax.axis_size("rep")
    group = retrieved.shape[1]
    fast = n_wide == 8 and n_rep == 4 and group == 64
    weights = (w_query, w_key, carried_content_weights, w_out, w_gate, w_up, w_down, w_proj)
    width = doc_tokens.shape[1]
    buckets, heads = rel_bias.shape
    hot_np = bucket_hot(buckets)
    hot = jnp.asarray(hot_np, BF)
    hot_f = jnp.asarray(hot_np, F)
    rep_hot = jnp.asarray(query_hot(64), BF)
    rel = jnp.transpose(rel_bias)
    queries = pos_ids.shape[0]
    ids = jnp.transpose(pos_ids)
    columns = jnp.transpose(retrieved)
    gains = (gain_attn, gain_ffn, gain_final)

    doc, sends = layer_forward(doc_tokens, weights, gains, rel, hot, DL, (columns,) if fast else ())
    if fast:
        near = [sends[0]] + [swap(sends[m], "wide", n_wide, 2 * m) for m in (1, 2, 3)]
    query, _ = layer_forward(query_tokens, weights, gains, rel, hot, QUERY_LENGTH, (), (doc["emb"],))
    if fast:
        ins = near + [swap(stack_rows(near, (query["emb"],)), "wide", n_wide, 1)]
    else:
        mask_query = lax.all_to_all(columns.astype(F), "wide", 0, 0, tiled=True)
        mask_query = mask_query.reshape(n_wide, queries, DL)
        ins = [lax.all_gather(doc["emb"], "wide", axis=0, tiled=True), mask_query]
    *coefs, d_query_emb, parts = query_sims(
        fast, ids, pos_count, query["emb"], query_cotangent, ins, n_wide
    )
    if fast:
        coefs = [coefs[0]] + [swap(coefs[m], "wide", n_wide, 2 * m) for m in (1, 2, 3)]
        every = stack_rows(coefs, ())
        coef_all = d_query_emb
        others = swap(every, "wide", n_wide, 1)
    else:
        every = lax.all_gather(query["emb"], "wide", axis=0, tiled=True)
        others = query["emb"]
        coef_all = lax.all_to_all(coefs[0], "wide", 0, 0, tiled=True)
    d_hid, d_attn, g, gains_both, keep_f, send_f = back(
        fast, doc_cotangent, doc["emb"], every, others, columns, rep_hot, coef_all, d_query_emb, doc, query,
        gains, weights,
    )
    if fast:
        ffn = Reduction("ffn", keep_f, send_f)
    early = 2
    first = attn_back(0, early, True, g, doc, query, hot_f, ())
    after = ffn.near((first[3],)) if fast else ()
    second = attn_back(early, heads // 2 - early, False, g, doc, query, hot_f, after)
    after = ffn.mine((second[3],)) if fast else (second[3],)
    keep_a, send_a = attn_grads(fast, first, second, d_attn, doc, query, after)
    after = (keep_a,)
    if fast:
        attn = AttnReduction(keep_a, send_a)
        after = ffn.cross(after)
        after = attn.near(after)
        after = attn.mine(after)
        after = ffn.stay(after)
        after = ffn.line(after)
    doc_grad, query_grad, small = input_back(
        doc_tokens, query_tokens, d_hid, gain_attn, gains_both, parts, first, second, weights, after
    )
    if fast:
        after = attn.cross((small,))
        after = ffn.next(after)
        after = attn.line(small, after)
        after = ffn.far(after)
        after = attn.next(after)
        after = attn.far(after)
        grad_gate, grad_up, grad_down, grad_proj = unpack(
            ffn.parts(), ((96, 2048), (96, 2048), (256, 768), (96, 128)), after
        )
        (
            grad_query, grad_key, grad_value, grad_out,
            total_gain_a, total_gain_f, total_gain_l, total_rel, loss, fraction,
        ) = unpack_attn(heads, buckets, width, queries * n_wide * n_rep, attn.parts())
        loss = loss.reshape(())
        fraction = fraction.reshape(())
    else:
        small = lax.psum(small, ("rep", "wide"))

        def total(whole):
            part = lax.psum_scatter(whole, "wide", scatter_dimension=0, tiled=True)
            return lax.psum(part, "rep").astype(F)

        grad_query, grad_key, grad_value, grad_out = (total(a) for a in natural("attn", keep_a, jnp.concatenate(send_a)))
        grad_gate, grad_up, grad_down, grad_proj = (total(a) for a in natural("ffn", keep_f, send_f))
        total_gain_a, total_gain_f, total_gain_l = (
            small[8 * i : 8 * i + 6].reshape(width) for i in range(3)
        )
        total_rel = small[32 : 32 + heads, 0:buckets]
        loss = small[24, 0] / (queries * n_wide * n_rep)
        fraction = small[24, 1] / (DL * small[24, 2])
    return (
        doc["emb"],
        query["emb"],
        doc_grad,
        query_grad,
        grad_query,
        grad_key,
        grad_value,
        grad_out,
        grad_gate,
        grad_up,
        grad_down,
        grad_proj,
        total_gain_a,
        total_gain_f,
        total_gain_l,
        jnp.transpose(total_rel),
        loss,
        fraction,
    )


def solution(mesh):
    rows = P(("rep", "wide"), None)
    return jax.shard_map(
        body,
        mesh=mesh,
        in_specs=(rows,) * 6 + (P(("rep", "wide")),) + (P(),) * 12,
        out_specs=(rows,) * 4 + (P("wide", None),) * 8 + (P(),) * 6,
        check_vma=False,
    )
```
